32 devices in a mesh: groups: 2 (over x), tensor: 16 (over z, y, core).
Axes of the slice: x: 2, y: 2, z: 4, core: 2. Of those that a mesh axis runs over, the one named last changes fastest.
Arguments:
- hidden: bfloat16 [4, 4, 16384], P('groups', None, 'tensor'), parts along dimension 0, may hold values from -6 to 6
- queries: bfloat16 [4, 4, 16384], P('groups', None, 'tensor'), parts along dimension 0, may hold values from -160 to 160
- key_value_weight: bfloat16 [16384, 2048], P('tensor'), may hold values from -0.046875 to 0.046875
- adapter_down_weight: bfloat16 [16, 16384, 128], P('tensor'), may hold values from -0.046875 to 0.046875
- adapter_up_weight: bfloat16 [16, 128, 2048], P('tensor'), may hold values from -0.5 to 0.5
- cached_key_rows: bfloat16 [4, 2048, 1024], P('groups', 'tensor'), parts along dimension 0, may hold values from -5 to 5
- cached_value_rows: bfloat16 [4, 2048, 1024], P('groups', 'tensor'), parts along dimension 0, may hold values from -6 to 6
- request_adapter: int32 [4], P('groups'), parts along dimension 0, may hold values from 0 to 15
- adapter_rank_list: int32 [16], replicated, may hold values from 16 to 128, as said below
- adapter_pool_row: int32 [16], replicated, may hold values from 0 to 15, each once
- lengths: int32 [4], P('groups'), parts along dimension 0, may hold values from 2 to 2048
Outputs:
- attended: bfloat16 [4, 4, 16384], P('groups', None, 'tensor'), parts along dimension 0
The draws below stay inside these ranges and needn't reach their ends.
There are 2 independent parts, one for each index of `groups`. The reference program is written for one: setup_inputs(seed, part) draws one part's arguments, and reference() takes and returns one part's arrays. A program takes and returns all parts, laid end to end along the dimension named above; an argument that names none is the same for every part. Nothing has to cross between parts.
Inputs may be any that keep to these rules, and one draw needn't show every extreme that they name: `adapter_rank_list`: each a multiple of 16. `adapter_pool_row`: each pool row holds one adapter.
All inputs are finite; a program needn't handle non-finite values.
Results may differ from the reference program's by a relative error of at most 0.0095.
Values may be sent and summed in bfloat16 or wider, within the bound.
No kernel may reach another device: no remote copies, remote signals or barrier semaphores. Data moves between devices by JAX's collectives and lax.ppermute only.
A program may use at most 128 MiB of HBM per device.

```python
import math
import jax
import jax.numpy as jnp
import numpy as np
from jax import lax

MODEL_WIDTH = 16384
QUERY_HEADS = 128
KEY_HEADS = 8
HEAD_WIDTH = 128
PADDED_RANK = 128
NEW_TOKENS = 4
REQUEST_COUNT = 2
CACHE_LENGTH = 2048
ADAPTER_COUNT = 16


def shared_keys(key):
    return jnp.clip(jax.random.normal(key, (REQUEST_COUNT, CACHE_LENGTH, KEY_HEADS * HEAD_WIDTH), jnp.float32), -5.0, 5.0)


def draw_cached_key_rows(key, part):
    drawn_key_rows = shared_keys(key)
    return drawn_key_rows.astype(jnp.bfloat16)


def draw_queries(key, part):
    key = jax.random.fold_in(key, 23)
    out_shape = (REQUEST_COUNT, NEW_TOKENS, QUERY_HEADS * HEAD_WIDTH)
    return jnp.clip(jax.random.normal(key, out_shape, jnp.float32), -5.0, 5.0).astype(jnp.bfloat16)


def draw_lengths(key, part):
    key = jax.random.fold_in(key, 37)
    raw_values = jax.random.randint(jax.random.fold_in(key, 1), (REQUEST_COUNT,), 0, CACHE_LENGTH - 1)
    shifts = jax.random.randint(jax.random.fold_in(key, 2), (REQUEST_COUNT,), 0, 12)
    values = 2 + raw_values // jnp.left_shift(jnp.ones_like(shifts), shifts)
    shuffled = jax.random.permutation(jax.random.fold_in(key, 3), REQUEST_COUNT)
    short_length = jax.random.randint(jax.random.fold_in(key, 4), (), 2, 9)
    values = values.at[shuffled[0]].set(CACHE_LENGTH).at[shuffled[1]].set(short_length)
    return values.astype(jnp.int32)


def draw_adapter_rank_list(key, part):
    key = jax.random.fold_in(key, 53)
    rank_unit = PADDED_RANK // 8
    values = rank_unit * jax.random.randint(jax.random.fold_in(key, 1), (ADAPTER_COUNT,), 1, 9)
    shuffled = jax.random.permutation(jax.random.fold_in(key, 2), ADAPTER_COUNT)
    values = values.at[shuffled[0]].set(PADDED_RANK).at[shuffled[1]].set(rank_unit)
    return values.astype(jnp.int32)


def levels(stream_key, shape, pieces, least, top_value):
    loudness, own = 1.0, jax.random.fold_in(stream_key, 6)
    for axis_at, shards_of in pieces:
        steps = jnp.exp(jax.random.uniform(jax.random.fold_in(own, axis_at), (shards_of,), jnp.float32, least / len(pieces), top_value / len(pieces)))
        loudness = loudness * jnp.repeat(steps, shape[axis_at] // shards_of).reshape([-1 if axis == axis_at else 1 for axis in range(len(shape))])
    return loudness


def rank_table(count, lean):
    weights = [(1 << 20) // math.isqrt(rank ** lean) + 1 for rank in range(1, count + 1)]
    deviation = 1 + sum(weights) // (1 << 30)
    return np.cumsum(np.array([max(1, weight // deviation) for weight in weights]))


def ranked(key, dims, count, lean):
    table = rank_table(count, lean)
    ticket = jax.random.randint(jax.random.fold_in(key, 1), dims, 0, int(table[count - 1]))
    standing = jnp.searchsorted(jnp.asarray(table, jnp.int32), ticket, side="right")
    return jax.random.permutation(jax.random.fold_in(key, 2), count)[standing].astype(jnp.int32)


def gaussian(stream_key, shape, width, bound, pieces=(), kind=jnp.bfloat16):
    gain = levels(stream_key, shape, pieces, -0.22, 0.18) if pieces else 1.0
    drawn = jax.random.normal(stream_key, shape, jnp.float32) * width * gain
    return jnp.minimum(jnp.maximum(drawn, -bound), bound).astype(kind)


def setup_inputs(seed: int = 0, part: int = 0) -> dict:
    seeds = jax.random.split(jax.random.key(seed), 12)
    own_keys = jax.random.split(jax.random.fold_in(seeds[11], part), 12)
    return {
        "hidden": gaussian(own_keys[0], (REQUEST_COUNT, NEW_TOKENS, MODEL_WIDTH), 1.0, 6.0, ((2, 16),)),
        "queries": draw_queries(jax.random.fold_in(jax.random.fold_in(seeds[11], part), 71), part),
        "key_value_weight": gaussian(seeds[2], (MODEL_WIDTH, 2 * KEY_HEADS * HEAD_WIDTH), MODEL_WIDTH ** -0.5, 0.046875, ((0, 16),)),
        "adapter_down_weight": gaussian(seeds[3], (ADAPTER_COUNT, MODEL_WIDTH, PADDED_RANK), MODEL_WIDTH ** -0.5, 0.046875, ((0, 16),)),
        "adapter_up_weight": gaussian(seeds[4], (ADAPTER_COUNT, PADDED_RANK, 2 * KEY_HEADS * HEAD_WIDTH), PADDED_RANK ** -0.5, 0.5, ((0, 16),)),
        "cached_key_rows": draw_cached_key_rows(jax.random.fold_in(jax.random.fold_in(seeds[11], part), 71), part),
        "cached_value_rows": gaussian(own_keys[6], (REQUEST_COUNT, CACHE_LENGTH, KEY_HEADS * HEAD_WIDTH), 1.0, 6.0, ((1, 16),)),
        "request_adapter": ranked(own_keys[7], (REQUEST_COUNT,), ADAPTER_COUNT, 2),
        "adapter_rank_list": draw_adapter_rank_list(jax.random.fold_in(seeds[11], 71), part),
        "adapter_pool_row": jax.random.permutation(seeds[9], ADAPTER_COUNT).astype(jnp.int32),
        "lengths": draw_lengths(jax.random.fold_in(jax.random.fold_in(seeds[11], part), 71), part),
    }


ROPE_BASE = 500000.0
NEG_FILL = -1e+30

def apply_rotation(vectors, starts):
    half_width = vectors.shape[-1] // 2
    offsets = jnp.arange(vectors.shape[1], dtype=jnp.int32)
    places = (starts[:, None] + offsets[None, :]).astype(jnp.float32)
    inverse_freq = jnp.exp(jnp.arange(half_width, dtype=jnp.float32) * (-2.0 * math.log(ROPE_BASE) / vectors.shape[-1]))
    angles = places[:, :, None] * inverse_freq[None, None, :]
    cosine = jnp.cos(angles)[:, :, None, :]
    sine_part = jnp.sin(angles)[:, :, None, :]
    first_half = vectors[..., :half_width]
    second = vectors[..., half_width:]
    return jnp.concatenate([first_half * cosine - second * sine_part, second * cosine + first_half * sine_part], axis=-1)

def reference(hidden, queries, key_value_weight, adapter_down_weight, adapter_up_weight, cached_key_rows, cached_value_rows, request_adapter, adapter_rank_list, adapter_pool_row, lengths):
    pool_row_index = adapter_pool_row[request_adapter]
    request_ranks = adapter_rank_list[request_adapter]
    hidden_f = hidden.astype(jnp.float32)
    base_part = jnp.einsum('bnd,dk->bnk', hidden_f, key_value_weight.astype(jnp.float32))
    down_factor_rows = adapter_down_weight[pool_row_index].astype(jnp.float32)
    reduced_output = jnp.einsum('bnd,bdr->bnr', hidden_f, down_factor_rows)
    rank_mask = jnp.arange(PADDED_RANK, dtype=jnp.int32)[None, :] < request_ranks[:, None]
    reduced_output = jnp.where(rank_mask[:, None, :], reduced_output, 0.0).astype(jnp.bfloat16)
    raised_output = jnp.einsum('ywm,ymq->ywq', reduced_output.astype(jnp.float32), adapter_up_weight[pool_row_index].astype(jnp.float32))
    projected_rows = base_part + raised_output
    key_column_width = KEY_HEADS * HEAD_WIDTH
    incoming_keys = apply_rotation(projected_rows[:, :, :key_column_width].reshape(REQUEST_COUNT, NEW_TOKENS, KEY_HEADS, HEAD_WIDTH), lengths).astype(jnp.bfloat16)
    incoming_values = projected_rows[:, :, key_column_width:].reshape(REQUEST_COUNT, NEW_TOKENS, KEY_HEADS, HEAD_WIDTH).astype(jnp.bfloat16)
    query_group_width = QUERY_HEADS // KEY_HEADS
    score_scale = 1.0 / math.sqrt(HEAD_WIDTH)
    causal = jnp.arange(NEW_TOKENS)[:, None] >= jnp.arange(NEW_TOKENS)[None, :]

    def attend(request):
        query_matrix, earlier_keys, earlier_values, fresh_keys, fresh_values, length = request
        query_matrix = query_matrix.reshape(NEW_TOKENS, KEY_HEADS, query_group_width, HEAD_WIDTH).astype(jnp.float32)
        earlier_keys = earlier_keys.reshape(CACHE_LENGTH, KEY_HEADS, HEAD_WIDTH).astype(jnp.float32)
        earlier_values = earlier_values.reshape(CACHE_LENGTH, KEY_HEADS, HEAD_WIDTH).astype(jnp.float32)
        past_scores = jnp.einsum('nkgd,pkd->nkgp', query_matrix, earlier_keys) * score_scale
        fresh_scores = jnp.einsum('nkgd,jkd->nkgj', query_matrix, fresh_keys.astype(jnp.float32)) * score_scale
        past_valid = (jnp.arange(CACHE_LENGTH) < length)[None, None, None, :]
        fresh_valid = causal[:, None, None, :]
        peak = jnp.maximum(lax.optimization_barrier(jnp.max(jnp.where(past_valid, past_scores, NEG_FILL), axis=-1)), lax.optimization_barrier(jnp.max(jnp.where(fresh_valid, fresh_scores, NEG_FILL), axis=-1)))
        past_weights = jnp.where(past_valid, jnp.exp(past_scores - peak[..., None]), 0.0)
        fresh_weights = jnp.where(fresh_valid, jnp.exp(fresh_scores - peak[..., None]), 0.0)
        row_sum = lax.optimization_barrier(jnp.sum(past_weights, axis=-1)) + lax.optimization_barrier(jnp.sum(fresh_weights, axis=-1))
        past_rounded = lax.optimization_barrier(past_weights.astype(jnp.bfloat16)).astype(jnp.float32)
        fresh_rounded = lax.optimization_barrier(fresh_weights.astype(jnp.bfloat16)).astype(jnp.float32)
        mixture = jnp.einsum('nkgp,pkd->nkgd', past_rounded, earlier_values) + jnp.einsum('nkgj,jkd->nkgd', fresh_rounded, fresh_values.astype(jnp.float32))
        return (mixture / row_sum[..., None]).reshape(NEW_TOKENS, QUERY_HEADS * HEAD_WIDTH).astype(jnp.bfloat16)
    return lax.map(attend, (queries, cached_key_rows, cached_value_rows, incoming_keys, incoming_values, lengths))
```

```python
import functools
import math

import jax
import jax.numpy as jnp
from jax import lax
from jax.experimental import pallas as pl
from jax.experimental.pallas import tpu as pltpu
from jax.sharding import PartitionSpec as P

QUERY_HEADS = 128
KEY_HEADS = 8
HEAD_WIDTH = 128
ROPE_BASE = 500000.0
NEG_FILL = -1e30
SCALE = 1.0 / math.sqrt(HEAD_WIDTH)
PROJ_ROWS = 32
STAT_ROWS = 16


def dot(a, b, dims):
    return lax.dot_general(a, b, (dims, ((), ())), preferred_element_type=jnp.float32)


def partial_kernel(devices, requests, tokens, *refs):
    (index_ref, adapter_ref, rank_ref, pool_ref, length_ref) = refs[:5]
    base_ref, down_ref, up_ref, key_ref, value_ref, out_ref = refs[-6:]
    gathered = refs[5:-6]
    here = index_ref[0]
    rows = requests * tokens
    heads = QUERY_HEADS // devices
    per_key_head = devices // KEY_HEADS
    chunks = down_ref.shape[0] // devices // HEAD_WIDTH
    positions = key_ref.shape[0] // requests
    mix_rows = heads * rows

    flat = [ref.at[s] for ref in gathered for s in range(ref.shape[0])]
    bits = devices.bit_length() - 1
    slots = [flat[int(format(r, f"0{bits}b")[::-1], 2)] for r in range(devices)]

    lowered = jnp.zeros((rows, down_ref.shape[1]), jnp.float32)
    for r in range(devices):
        hidden = jnp.concatenate([slots[r][heads + c] for c in range(chunks)], axis=1)
        source = here ^ r
        depth = chunks * HEAD_WIDTH
        factor = down_ref[pl.ds(pl.multiple_of(source * depth, depth), depth), :]
        lowered += dot(hidden, factor, ((1,), (0,)))
    row_request = lax.broadcasted_iota(jnp.int32, (rows, 1), 0) // tokens
    ranks = jnp.zeros((rows, 1), jnp.int32)
    owners = jnp.zeros((rows, 1), jnp.int32)
    for b in range(requests):
        adapter = adapter_ref[b]
        ranks = jnp.where(row_request == b, rank_ref[adapter], ranks)
        owners = jnp.where(row_request == b, pool_ref[adapter], owners)
    lane = lax.broadcasted_iota(jnp.int32, lowered.shape, 1)
    lowered = jnp.where(lane < ranks, lowered, 0.0).astype(jnp.bfloat16)
    lifted = dot(lowered, up_ref[...], ((1,), (0,)))
    projected = base_ref[...] + jnp.where(owners == here, lifted, 0.0)
    high = projected.astype(jnp.bfloat16)
    low = (projected - high.astype(jnp.float32)).astype(jnp.bfloat16)
    split = KEY_HEADS * HEAD_WIDTH
    for head in range(KEY_HEADS):
        at = head * HEAD_WIDTH
        block = jnp.concatenate(
            [
                high[:, at : at + HEAD_WIDTH],
                high[:, split + at : split + at + HEAD_WIDTH],
                low[:, at : at + HEAD_WIDTH],
                low[:, split + at : split + at + HEAD_WIDTH],
            ],
            axis=0,
        )
        for t in range(per_key_head):
            out_ref[head * per_key_head + t, mix_rows : mix_rows + PROJ_ROWS, :] = block

    stacked = requests * positions
    place = lax.broadcasted_iota(jnp.int32, (stacked, HEAD_WIDTH), 0)
    column = lax.broadcasted_iota(jnp.int32, (stacked, HEAD_WIDTH), 1)
    place_request = place // positions
    limit = jnp.zeros_like(place)
    for b in range(requests):
        limit = jnp.where(place_request == b, length_ref[b], limit)
    allowed = (here * positions + place % positions < limit) & (
        place_request == (column // tokens) % requests
    )
    stat_row = lax.broadcasted_iota(jnp.int32, (STAT_ROWS, mix_rows), 0)
    pad = jnp.zeros((STAT_ROWS, HEAD_WIDTH - mix_rows), jnp.float32)
    for j in range(KEY_HEADS):
        key_head = (here // per_key_head) ^ j
        at = pl.multiple_of(key_head * HEAD_WIDTH, HEAD_WIDTH)
        query = jnp.concatenate(
            [
                slots[j * per_key_head + t][h]
                for t in range(per_key_head)
                for h in range(heads)
            ],
            axis=0,
        )
        scores = dot(key_ref[:, pl.ds(at, HEAD_WIDTH)], query, ((1,), (1,))) * SCALE
        peak = jnp.max(jnp.where(allowed, scores, NEG_FILL), axis=0, keepdims=True)
        peak = peak.astype(jnp.bfloat16).astype(jnp.float32)
        weights = jnp.where(allowed, jnp.exp(scores - peak), 0.0)
        total = jnp.sum(weights, axis=0, keepdims=True)
        total_high = total.astype(jnp.bfloat16).astype(jnp.float32)
        mix = dot(weights.astype(jnp.bfloat16), value_ref[:, pl.ds(at, HEAD_WIDTH)], ((0,), (0,)))
        mix = mix.astype(jnp.bfloat16)
        for t in range(per_key_head):
            owner = here ^ (j * per_key_head + t)
            own = slice(t * mix_rows, (t + 1) * mix_rows)
            out_ref[owner, 0:mix_rows, :] = mix[own]
            stats = jnp.where(
                stat_row == 0,
                peak[:, own],
                jnp.where(
                    stat_row == 1,
                    total_high[:, own],
                    jnp.where(stat_row == 2, (total - total_high)[:, own], 0.0),
                ),
            )
            out_ref[owner, mix_rows + PROJ_ROWS :, :] = jnp.concatenate([stats, pad], axis=1).astype(
                jnp.bfloat16
            )


def merge_kernel(devices, requests, tokens, query_ref, cos_ref, sin_ref, got_ref, out_ref):
    rows = requests * tokens
    heads = QUERY_HEADS // devices
    mix_rows = heads * rows
    projected = jnp.sum(got_ref[:, mix_rows : mix_rows + PROJ_ROWS, :].astype(jnp.float32), axis=0)
    projected = projected[: 2 * rows] + projected[2 * rows :]
    keys, values = projected[:rows], projected[rows:].astype(jnp.bfloat16)
    turned = pltpu.roll(keys, HEAD_WIDTH // 2, 1)
    keys = (keys * cos_ref[...] + turned * sin_ref[...]).astype(jnp.bfloat16)
    query = jnp.concatenate([query_ref[h] for h in range(heads)], axis=0)
    fresh = dot(keys, query, ((1,), (1,))) * SCALE
    source = lax.broadcasted_iota(jnp.int32, fresh.shape, 0)
    column = lax.broadcasted_iota(jnp.int32, fresh.shape, 1) % rows
    allowed = (source // tokens == column // tokens) & (source % tokens <= column % tokens)
    stats = got_ref[:, mix_rows + PROJ_ROWS :, :].astype(jnp.float32)[:, :, :mix_rows]
    peaks = stats[:, 0, :]
    totals = stats[:, 1, :] + stats[:, 2, :]
    peak = jnp.maximum(
        jnp.max(peaks, axis=0, keepdims=True),
        jnp.max(jnp.where(allowed, fresh, NEG_FILL), axis=0, keepdims=True),
    )
    weights = jnp.where(allowed, jnp.exp(fresh - peak), 0.0)
    factors = jnp.exp(peaks - peak)
    total = jnp.sum(factors * totals, axis=0, keepdims=True) + jnp.sum(
        weights, axis=0, keepdims=True
    )
    inverse = 1.0 / total
    filler = jnp.zeros((128 - devices - 8, mix_rows), jnp.float32)
    table = jnp.concatenate(
        [factors * inverse, jnp.broadcast_to(inverse, (8, mix_rows)), filler], axis=0
    )
    if mix_rows < 128:
        table = jnp.concatenate([table, jnp.zeros((128, 128 - mix_rows), jnp.float32)], axis=1)
    table = jnp.transpose(table)[:mix_rows]
    mix = dot(weights.astype(jnp.bfloat16), values, ((0,), (0,))) * table[:, devices : devices + 1]
    for s in range(devices):
        mix += got_ref[s, 0:mix_rows, :].astype(jnp.float32) * table[:, s : s + 1]
    for h in range(heads):
        out_ref[:, h * HEAD_WIDTH : (h + 1) * HEAD_WIDTH] = mix[h * rows : (h + 1) * rows].astype(
            jnp.bfloat16
        )


def rotation(lengths, tokens):
    half = HEAD_WIDTH // 2
    places = (lengths[:, None] + jnp.arange(tokens, dtype=jnp.int32)[None, :]).astype(jnp.float32)
    inverse_freq = jnp.exp(
        jnp.arange(half, dtype=jnp.float32) * (-2.0 * math.log(ROPE_BASE) / HEAD_WIDTH)
    )
    angles = places.reshape(-1, 1) * inverse_freq[None, :]
    cosine, sine = jnp.cos(angles), jnp.sin(angles)
    return jnp.concatenate([cosine, cosine], axis=1), jnp.concatenate([-sine, sine], axis=1)


def vmem():
    return pl.BlockSpec(memory_space=pltpu.VMEM)


def smem():
    return pl.BlockSpec(memory_space=pltpu.SMEM)


def per_device(
    hidden,
    queries,
    key_value_weight,
    adapter_down_weight,
    adapter_up_weight,
    cached_key_rows,
    cached_value_rows,
    request_adapter,
    adapter_rank_list,
    adapter_pool_row,
    lengths,
):
    requests, tokens, width = hidden.shape
    rows = requests * tokens
    devices = lax.axis_size("tensor")
    here = lax.axis_index("tensor")
    heads = QUERY_HEADS // devices
    chunks = width // HEAD_WIDTH

    def tiles(x):
        return x.reshape(rows, -1, HEAD_WIDTH).transpose(1, 0, 2)

    own_queries = tiles(queries)
    own = jnp.concatenate([own_queries, tiles(hidden)], axis=0)[None]
    gathered = [own]
    bit = devices // 2
    while bit:
        sent = gathered[0] if len(gathered) == 1 else jnp.concatenate(gathered, axis=0)
        pairs = [(d, d ^ bit) for d in range(devices)]
        gathered = [sent, lax.ppermute(sent, "tensor", pairs)]
        bit //= 2
    held = jnp.concatenate(gathered, axis=0)
    base = dot(hidden.reshape(rows, width), key_value_weight, ((1,), (0,)))
    flat = requests * cached_key_rows.shape[1]
    mix_rows = heads * rows
    packet_rows = mix_rows + PROJ_ROWS + STAT_ROWS
    packets = pl.pallas_call(
        functools.partial(partial_kernel, devices, requests, tokens),
        out_shape=jax.ShapeDtypeStruct((devices, packet_rows, HEAD_WIDTH), jnp.bfloat16),
        in_specs=[smem()] * 5 + [vmem()] * 6,
        out_specs=vmem(),
        compiler_params=pltpu.CompilerParams(vmem_limit_bytes=24 * 2**20),
        name="partial_states",
    )(
        here.reshape(1).astype(jnp.int32),
        request_adapter,
        adapter_rank_list,
        adapter_pool_row,
        lengths,
        held,
        base,
        adapter_down_weight[0],
        adapter_up_weight[0],
        cached_key_rows.reshape(flat, -1),
        cached_value_rows.reshape(flat, -1),
    )
    got = lax.all_to_all(packets, "tensor", split_axis=0, concat_axis=0, tiled=True)
    cosine, sine = rotation(lengths, tokens)
    out = pl.pallas_call(
        functools.partial(merge_kernel, devices, requests, tokens),
        out_shape=jax.ShapeDtypeStruct((rows, heads * HEAD_WIDTH), jnp.bfloat16),
        in_specs=[vmem()] * 4,
        out_specs=vmem(),
        compiler_params=pltpu.CompilerParams(vmem_limit_bytes=16 * 2**20),
        name="merge_states",
    )(own_queries, cosine, sine, got)
    return out.reshape(requests, tokens, -1)


def solution(mesh):
    in_specs = (
        P("groups", None, "tensor"),
        P("groups", None, "tensor"),
        P("tensor", None),
        P("tensor", None, None),
        P("tensor", None, None),
        P("groups", "tensor", None),
        P("groups", "tensor", None),
        P("groups"),
        P(),
        P(),
        P("groups"),
    )
    out_specs = P("groups", None, "tensor")
    return jax.shard_map(
        per_device, mesh=mesh, in_specs=in_specs, out_specs=out_specs, check_vma=False
    )
```

```python
import functools
import math

import jax
import jax.numpy as jnp
from jax import lax
from jax.experimental import pallas as pl
from jax.experimental.pallas import tpu as pltpu
from jax.sharding import PartitionSpec as P

QUERY_HEADS = 128
KEY_HEADS = 8
HEAD_WIDTH = 128
ROPE_BASE = 500000.0
NEG_FILL = -1e30
SCALE = 1.0 / math.sqrt(HEAD_WIDTH)
PAIRS = KEY_HEADS // 2
STAT_ROWS = 16
MIB = 2**20


def dot(a, b, dims):
    return lax.dot_general(a, b, (dims, ((), ())), preferred_element_type=jnp.float32)


def round_bf16(x):
    return x.astype(jnp.bfloat16).astype(jnp.float32)


def pack_kernel(requests, query_ref, hidden_ref, out_ref):
    at = 0
    for ref in (query_ref, hidden_ref):
        rows = jnp.concatenate([ref[b].astype(jnp.float32) for b in range(requests)], axis=0)
        for c in range(rows.shape[1] // HEAD_WIDTH):
            tile = rows[:, c * HEAD_WIDTH : (c + 1) * HEAD_WIDTH]
            out_ref[at] = tile.astype(jnp.bfloat16)
            at += 1


def base_kernel(heads, packed_ref, weight_ref, base_ref):
    chunks = weight_ref.shape[0] // HEAD_WIDTH
    hidden = jnp.concatenate([packed_ref[heads + c] for c in range(chunks)], axis=1)
    base_ref[...] = dot(hidden, weight_ref[...], ((1,), (0,)))


def partial_kernel(devices, requests, tokens, *refs):
    (index_ref, adapter_ref, rank_ref, pool_ref, length_ref) = refs[:5]
    (lane_ref, other_ref, base_ref, down_ref, up_ref, key_ref, value_ref) = refs[5:12]
    (send_ref, mix_ref, stat_ref, proj_ref, all_ref) = refs[12:]
    here = index_ref[0]
    rows = requests * tokens
    heads = QUERY_HEADS // devices
    lanes = devices // 2
    per_key_head = devices // KEY_HEADS
    per_lane = per_key_head // 2
    chunks = down_ref.shape[0] // devices // HEAD_WIDTH
    positions = key_ref.shape[0] // requests
    depth = chunks * HEAD_WIDTH

    lowered = jnp.zeros((rows, down_ref.shape[1]), jnp.float32)
    for side, ref in enumerate((lane_ref, other_ref)):
        for m in range(lanes):
            hidden = jnp.concatenate([ref[m, heads + c] for c in range(chunks)], axis=1)
            source = here ^ (2 * m + side)
            factor = down_ref[pl.ds(pl.multiple_of(source * depth, depth), depth), :]
            lowered += dot(hidden, factor, ((1,), (0,)))
    row_request = lax.broadcasted_iota(jnp.int32, (rows, 1), 0) // tokens
    ranks = jnp.zeros((rows, 1), jnp.int32)
    owners = jnp.zeros((rows, 1), jnp.int32)
    for b in range(requests):
        adapter = adapter_ref[b]
        ranks = jnp.where(row_request == b, rank_ref[adapter], ranks)
        owners = jnp.where(row_request == b, pool_ref[adapter], owners)
    column = lax.broadcasted_iota(jnp.int32, lowered.shape, 1)
    lowered = jnp.where(column < ranks, lowered, 0.0).astype(jnp.bfloat16)
    lifted = dot(lowered, up_ref[...], ((1,), (0,)))
    all_ref[...] = base_ref[...] + jnp.where(owners == here, lifted, 0.0)

    split = KEY_HEADS * HEAD_WIDTH
    mix_total = KEY_HEADS * 64
    for j in range(KEY_HEADS):
        at = ((here // per_key_head) ^ j) * HEAD_WIDTH
        keys = all_ref[:, pl.ds(pl.multiple_of(at, HEAD_WIDTH), HEAD_WIDTH)]
        values = all_ref[:, pl.ds(pl.multiple_of(split + at, HEAD_WIDTH), HEAD_WIDTH)]
        proj_ref[0, j] = keys
        proj_ref[1, j] = values
    keys = proj_ref[0].reshape(KEY_HEADS * rows, HEAD_WIDTH)
    high = keys.astype(jnp.bfloat16)
    step = KEY_HEADS * rows
    send_ref[mix_total : mix_total + step] = high
    send_ref[mix_total + step : mix_total + 2 * step] = (keys - high.astype(jnp.float32)).astype(
        jnp.bfloat16
    )
    send_ref[mix_total + 2 * step : mix_total + 3 * step] = (
        proj_ref[1].reshape(step, HEAD_WIDTH).astype(jnp.bfloat16)
    )

    stacked = requests * positions
    place = lax.broadcasted_iota(jnp.int32, (stacked, HEAD_WIDTH), 0)
    column = lax.broadcasted_iota(jnp.int32, (stacked, HEAD_WIDTH), 1)
    place_request = place // positions
    limit = jnp.zeros_like(place)
    for b in range(requests):
        limit = jnp.where(place_request == b, length_ref[b], limit)
    allowed = (here * positions + place % positions < limit) & (
        place_request == (column // tokens) % requests
    )
    first = column < 64
    stat_row = lax.broadcasted_iota(jnp.int32, (STAT_ROWS, HEAD_WIDTH), 0)
    for side, ref in enumerate((other_ref, lane_ref)):
        stats = jnp.zeros((STAT_ROWS, HEAD_WIDTH), jnp.float32)
        for p in range(PAIRS):
            spots = [
                pl.multiple_of(((here // per_key_head) ^ j) * HEAD_WIDTH, HEAD_WIDTH)
                for j in (2 * p, 2 * p + 1)
            ]
            query = jnp.concatenate(
                [ref[2 * p * per_lane + t, h] for t in range(2 * per_lane) for h in range(heads)],
                axis=0,
            )
            scores = [
                dot(key_ref[:, pl.ds(at, HEAD_WIDTH)], query, ((1,), (1,))) for at in spots
            ]
            scores = jnp.where(first, scores[0], scores[1]) * SCALE
            peak = jnp.max(jnp.where(allowed, scores, NEG_FILL), axis=0, keepdims=True)
            peak = round_bf16(peak)
            weights = jnp.where(allowed, jnp.exp(scores - peak), 0.0)
            total = jnp.sum(weights, axis=0, keepdims=True)
            weights = jnp.transpose(weights.astype(jnp.bfloat16))
            mix = [
                dot(weights[64 * i : 64 * i + 64], value_ref[:, pl.ds(at, HEAD_WIDTH)], ((1,), (0,)))
                for i, at in enumerate(spots)
            ]
            at = p * 128
            for i in range(2):
                if side == 0:
                    send_ref[at + 64 * i : at + 64 * i + 64] = mix[i].astype(jnp.bfloat16)
                else:
                    mix_ref[at + 64 * i : at + 64 * i + 64] = mix[i]
            stats = jnp.where(stat_row == p, peak, stats)
            high = round_bf16(total)
            if side == 0:
                stats = jnp.where(stat_row == PAIRS + p, high, stats)
                stats = jnp.where(stat_row == 2 * PAIRS + p, total - high, stats)
            else:
                stats = jnp.where(stat_row == PAIRS + p, total, stats)
        if side == 0:
            send_ref[mix_total + 3 * step :] = stats.astype(jnp.bfloat16)
        else:
            stat_ref[...] = stats


def join_kernel(devices, requests, tokens, mix_ref, stat_ref, proj_ref, got_ref, *out_refs):
    rows = requests * tokens
    heads = QUERY_HEADS // devices
    mix_rows = heads * rows
    per_lane = devices // KEY_HEADS // 2
    mix_total = KEY_HEADS * 64
    step = KEY_HEADS * rows
    got = got_ref[mix_total + 3 * step :, :].astype(jnp.float32)
    own = stat_ref[...]
    own_peak, got_peak = own[:PAIRS], got[:PAIRS]
    peak = jnp.maximum(own_peak, got_peak)
    own_factor = jnp.exp(own_peak - peak)
    got_factor = jnp.exp(got_peak - peak)
    total = own_factor * own[PAIRS : 2 * PAIRS] + got_factor * (
        got[PAIRS : 2 * PAIRS] + got[2 * PAIRS : 3 * PAIRS]
    )
    high = round_bf16(total)
    filler = jnp.zeros((128 - 2 * PAIRS, 128), jnp.float32)
    table = jnp.transpose(jnp.concatenate([own_factor, got_factor, filler], axis=0))
    keys = got_ref[mix_total : mix_total + step].astype(jnp.float32) + got_ref[
        mix_total + step : mix_total + 2 * step
    ].astype(jnp.float32)
    keys += proj_ref[0].reshape(step, HEAD_WIDTH)
    values = got_ref[mix_total + 2 * step : mix_total + 3 * step].astype(jnp.float32)
    values += proj_ref[1].reshape(step, HEAD_WIDTH)
    keys_high = round_bf16(keys)
    keys_low = keys - keys_high
    stat_row = lax.broadcasted_iota(jnp.int32, (rows, HEAD_WIDTH), 0)
    for p in range(PAIRS):
        mix = mix_ref[p * 128 : p * 128 + 128] * table[:, p : p + 1] + got_ref[
            p * 128 : p * 128 + 128
        ].astype(jnp.float32) * table[:, PAIRS + p : PAIRS + p + 1]
        stats = jnp.where(
            stat_row == 0,
            peak[p : p + 1],
            jnp.where(
                stat_row == 1,
                high[p : p + 1],
                jnp.where(stat_row == 2, (total - high)[p : p + 1], 0.0),
            ),
        )
        for t in range(2 * per_lane):
            j = 2 * p + t // per_lane
            out_ref = out_refs[2 * p * per_lane + t]
            out_ref[:mix_rows] = mix[t * mix_rows : (t + 1) * mix_rows].astype(jnp.bfloat16)
            shifted = stats if t == 0 else pltpu.roll(stats, HEAD_WIDTH - t * mix_rows, 1)
            own = slice(j * rows, (j + 1) * rows)
            out_ref[mix_rows:] = jnp.concatenate(
                [keys_high[own], keys_low[own], values[own], shifted], axis=0
            ).astype(jnp.bfloat16)


def merge_kernel(devices, requests, tokens, packed_ref, cos_ref, sin_ref, *refs):
    got_refs, out_ref = refs[:-1], refs[-1]
    rows = requests * tokens
    heads = QUERY_HEADS // devices
    mix_rows = heads * rows
    sources = len(got_refs)
    tails = [ref[mix_rows:].astype(jnp.float32) for ref in got_refs]
    sums = functools.reduce(jnp.add, [tail[: 3 * rows] for tail in tails])
    keys = sums[:rows] + sums[rows : 2 * rows]
    values = sums[2 * rows :].astype(jnp.bfloat16)
    turned = pltpu.roll(keys, HEAD_WIDTH // 2, 1)
    keys = (keys * cos_ref[...] + turned * sin_ref[...]).astype(jnp.bfloat16)
    query = jnp.concatenate([packed_ref[h] for h in range(heads)], axis=0)
    if mix_rows < 128:
        query = jnp.concatenate(
            [query, jnp.zeros((128 - mix_rows, HEAD_WIDTH), jnp.bfloat16)], axis=0
        )
    fresh = dot(keys, query, ((1,), (1,))) * SCALE
    source = lax.broadcasted_iota(jnp.int32, fresh.shape, 0)
    column = lax.broadcasted_iota(jnp.int32, fresh.shape, 1) % rows
    allowed = (source // tokens == column // tokens) & (source % tokens <= column % tokens)
    fresh_peak = jnp.max(jnp.where(allowed, fresh, NEG_FILL), axis=0, keepdims=True)
    stats = [tail[3 * rows :] for tail in tails]
    peak = functools.reduce(jnp.maximum, [stat[0:1] for stat in stats], fresh_peak)
    weights = jnp.where(allowed, jnp.exp(fresh - peak), 0.0)
    factors = [jnp.exp(stat[0:1] - peak) for stat in stats]
    total = functools.reduce(
        jnp.add,
        [factor * (stat[1:2] + stat[2:3]) for factor, stat in zip(factors, stats)],
        jnp.sum(weights, axis=0, keepdims=True),
    )
    inverse = 1.0 / total
    filler = jnp.zeros((128 - sources - 1, 128), jnp.float32)
    table = jnp.concatenate([factor * inverse for factor in factors] + [inverse, filler], axis=0)
    table = jnp.transpose(table)[:mix_rows]
    weights = jnp.transpose(
        jnp.concatenate([weights, jnp.zeros((128 - rows, 128), jnp.float32)], axis=0)
    )[:mix_rows].astype(jnp.bfloat16)
    values = jnp.concatenate(
        [values, jnp.zeros((128 - rows, HEAD_WIDTH), jnp.bfloat16)], axis=0
    )
    mix = dot(weights, values, ((1,), (0,))) * table[:, sources : sources + 1]
    for s, ref in enumerate(got_refs):
        mix += ref[:mix_rows].astype(jnp.float32) * table[:, s : s + 1]
    for h in range(heads):
        tile = mix[h * rows : (h + 1) * rows]
        for b in range(requests):
            out_ref[b, :, h * HEAD_WIDTH : (h + 1) * HEAD_WIDTH] = tile[
                b * tokens : (b + 1) * tokens
            ].astype(jnp.bfloat16)


def rotation(lengths, tokens):
    half = HEAD_WIDTH // 2
    places = (lengths[:, None] + jnp.arange(tokens, dtype=jnp.int32)[None, :]).astype(jnp.float32)
    inverse_freq = jnp.exp(
        jnp.arange(half, dtype=jnp.float32) * (-2.0 * math.log(ROPE_BASE) / HEAD_WIDTH)
    )
    angles = places.reshape(-1, 1) * inverse_freq[None, :]
    cosine, sine = jnp.cos(angles), jnp.sin(angles)
    return jnp.concatenate([cosine, cosine], axis=1), jnp.concatenate([-sine, sine], axis=1)


def vmem():
    return pl.BlockSpec(memory_space=pltpu.VMEM)


def smem():
    return pl.BlockSpec(memory_space=pltpu.SMEM)


def hbm():
    return pl.BlockSpec(memory_space=pltpu.HBM)


def cost(flops, moved):
    return pl.CostEstimate(flops=int(flops), bytes_accessed=int(moved), transcendentals=0)


def swap(x, devices, bit):
    return lax.ppermute(x, "tensor", [(d, d ^ bit) for d in range(devices)])


def per_device(
    hidden,
    queries,
    key_value_weight,
    adapter_down_weight,
    adapter_up_weight,
    cached_key_rows,
    cached_value_rows,
    request_adapter,
    adapter_rank_list,
    adapter_pool_row,
    lengths,
):
    requests, tokens, width = hidden.shape
    rows = requests * tokens
    devices = lax.axis_size("tensor")
    here = lax.axis_index("tensor")
    heads = QUERY_HEADS // devices
    chunks = width // HEAD_WIDTH
    lanes = devices // 2
    tiles = heads + chunks
    mix_rows = heads * rows

    packed = pl.pallas_call(
        functools.partial(pack_kernel, requests),
        out_shape=jax.ShapeDtypeStruct((tiles, rows, HEAD_WIDTH), jnp.bfloat16),
        in_specs=[vmem()] * 2,
        out_specs=vmem(),
        cost_estimate=cost(10**10, 0),
        name="pack",
    )(queries, hidden)
    lane = [packed] + [swap(packed, devices, 2 * m) for m in range(1, lanes)]
    lane = jnp.concatenate([x[None] for x in lane], axis=0)

    base = pl.pallas_call(
        functools.partial(base_kernel, heads),
        out_shape=jax.ShapeDtypeStruct((rows, key_value_weight.shape[1]), jnp.float32),
        in_specs=[vmem()] * 2,
        out_specs=vmem(),
        compiler_params=pltpu.CompilerParams(vmem_limit_bytes=16 * MIB),
        cost_estimate=cost(2 * rows * key_value_weight.size, 2 * key_value_weight.size),
        name="base",
    )(packed, key_value_weight)
    lane, base = lax.optimization_barrier((lane, base))
    other = swap(lane, devices, 1)

    flat = requests * cached_key_rows.shape[1]
    mix_total = KEY_HEADS * 64
    send_rows = mix_total + 3 * KEY_HEADS * rows + STAT_ROWS
    send, mix, stats, proj = pl.pallas_call(
        functools.partial(partial_kernel, devices, requests, tokens),
        out_shape=(
            jax.ShapeDtypeStruct((send_rows, HEAD_WIDTH), jnp.bfloat16),
            jax.ShapeDtypeStruct((mix_total, HEAD_WIDTH), jnp.float32),
            jax.ShapeDtypeStruct((STAT_ROWS, HEAD_WIDTH), jnp.float32),
            jax.ShapeDtypeStruct((2, KEY_HEADS, rows, HEAD_WIDTH), jnp.float32),
        ),
        in_specs=[smem()] * 5 + [vmem()] * 7,
        out_specs=(vmem(),) * 4,
        scratch_shapes=[pltpu.VMEM(base.shape, jnp.float32)],
        compiler_params=pltpu.CompilerParams(vmem_limit_bytes=20 * MIB),
        name="partial_states",
    )(
        here.reshape(1).astype(jnp.int32),
        request_adapter,
        adapter_rank_list,
        adapter_pool_row,
        lengths,
        lane,
        other,
        base,
        adapter_down_weight[0],
        adapter_up_weight[0],
        cached_key_rows.reshape(flat, -1),
        cached_value_rows.reshape(flat, -1),
    )
    got = swap(send, devices, 1)
    packet = jax.ShapeDtypeStruct((mix_rows + 4 * rows, HEAD_WIDTH), jnp.bfloat16)
    packets = pl.pallas_call(
        functools.partial(join_kernel, devices, requests, tokens),
        out_shape=(packet,) * lanes,
        in_specs=[vmem()] * 4,
        out_specs=(vmem(),) * lanes,
        name="join",
    )(mix, stats, proj, got)
    packets = [packets[0]] + [swap(packets[m], devices, 2 * m) for m in range(1, lanes)]
    cosine, sine = rotation(lengths, tokens)
    return pl.pallas_call(
        functools.partial(merge_kernel, devices, requests, tokens),
        out_shape=jax.ShapeDtypeStruct((requests, tokens, heads * HEAD_WIDTH), jnp.bfloat16),
        in_specs=[vmem()] * (3 + lanes),
        out_specs=vmem(),
        name="merge_states",
    )(packed, cosine, sine, *packets)


def solution(mesh):
    in_specs = (
        P("groups", None, "tensor"),
        P("groups", None, "tensor"),
        P("tensor", None),
        P("tensor", None, None),
        P("tensor", None, None),
        P("groups", "tensor", None),
        P("groups", "tensor", None),
        P("groups"),
        P(),
        P(),
        P("groups"),
    )
    out_specs = P("groups", None, "tensor")
    return jax.shard_map(
        per_device, mesh=mesh, in_specs=in_specs, out_specs=out_specs, check_vma=False
    )
```

```python
import functools
import math

import jax
import jax.numpy as jnp
from jax import lax
from jax.experimental import pallas as pl
from jax.experimental.pallas import tpu as pltpu
from jax.sharding import PartitionSpec as P

QUERY_HEADS = 128
KEY_HEADS = 8
HEAD_WIDTH = 128
ROPE_BASE = 500000.0
NEG_FILL = -1e30
SCALE = 1.0 / math.sqrt(HEAD_WIDTH)
PAIRS = KEY_HEADS // 2
STAT_ROWS = 16
MIB = 2**20


def dot(a, b, dims):
    return lax.dot_general(a, b, (dims, ((), ())), preferred_element_type=jnp.float32)


def round_bf16(x):
    return x.astype(jnp.bfloat16).astype(jnp.float32)


def pack_kernel(requests, query_ref, hidden_ref, out_ref):
    at = 0
    for ref in (query_ref, hidden_ref):
        rows = jnp.concatenate([ref[b].astype(jnp.float32) for b in range(requests)], axis=0)
        for c in range(rows.shape[1] // HEAD_WIDTH):
            tile = rows[:, c * HEAD_WIDTH : (c + 1) * HEAD_WIDTH]
            for copy in range(out_ref.shape[0]):
                out_ref[copy, at] = tile.astype(jnp.bfloat16)
            at += 1


def base_kernel(heads, packed_ref, weight_ref, base_ref):
    chunks = weight_ref.shape[0] // HEAD_WIDTH
    hidden = jnp.concatenate([packed_ref[0, heads + c] for c in range(chunks)], axis=1)
    base_ref[...] = dot(hidden, weight_ref[...], ((1,), (0,)))


def partial_kernel(devices, requests, tokens, *refs):
    (index_ref, adapter_ref, rank_ref, pool_ref, length_ref) = refs[:5]
    (lane_ref, other_ref, base_ref, down_ref, up_ref, key_ref, value_ref) = refs[5:12]
    (send_ref, mix_ref, stat_ref, proj_ref) = refs[12:]
    here = index_ref[0]
    rows = requests * tokens
    heads = QUERY_HEADS // devices
    lanes = devices // 2
    per_key_head = devices // KEY_HEADS
    per_lane = per_key_head // 2
    chunks = down_ref.shape[0] // devices // HEAD_WIDTH
    positions = key_ref.shape[0] // requests
    depth = chunks * HEAD_WIDTH

    lowered = jnp.zeros((rows, down_ref.shape[1]), jnp.float32)
    for side, ref in enumerate((lane_ref, other_ref)):
        for m in range(lanes):
            hidden = jnp.concatenate([ref[m, heads + c] for c in range(chunks)], axis=1)
            source = 2 * m + (here % 2 ^ side)
            factor = down_ref[pl.ds(pl.multiple_of(source * depth, depth), depth), :]
            lowered += dot(hidden, factor, ((1,), (0,)))
    row_request = lax.broadcasted_iota(jnp.int32, (rows, 1), 0) // tokens
    ranks = jnp.zeros((rows, 1), jnp.int32)
    owners = jnp.zeros((rows, 1), jnp.int32)
    for b in range(requests):
        adapter = adapter_ref[b]
        ranks = jnp.where(row_request == b, rank_ref[adapter], ranks)
        owners = jnp.where(row_request == b, pool_ref[adapter], owners)
    column = lax.broadcasted_iota(jnp.int32, lowered.shape, 1)
    lowered = jnp.where(column < ranks, lowered, 0.0).astype(jnp.bfloat16)
    lifted = dot(lowered, up_ref[...], ((1,), (0,)))
    projected = base_ref[...] + jnp.where(owners == here, lifted, 0.0)

    split = KEY_HEADS * HEAD_WIDTH
    mix_total = KEY_HEADS * 64
    for j in range(KEY_HEADS):
        at = j * HEAD_WIDTH
        proj_ref[0, j] = projected[:, at : at + HEAD_WIDTH]
        proj_ref[1, j] = projected[:, split + at : split + at + HEAD_WIDTH]
    keys = proj_ref[0].reshape(KEY_HEADS * rows, HEAD_WIDTH)
    high = keys.astype(jnp.bfloat16)
    step = KEY_HEADS * rows
    send_ref[mix_total : mix_total + step] = high
    send_ref[mix_total + step : mix_total + 2 * step] = (keys - high.astype(jnp.float32)).astype(
        jnp.bfloat16
    )
    send_ref[mix_total + 2 * step : mix_total + 3 * step] = (
        proj_ref[1].reshape(step, HEAD_WIDTH).astype(jnp.bfloat16)
    )

    stacked = requests * positions
    place = lax.broadcasted_iota(jnp.int32, (stacked, HEAD_WIDTH), 0)
    column = lax.broadcasted_iota(jnp.int32, (stacked, HEAD_WIDTH), 1)
    place_request = place // positions
    limit = jnp.zeros_like(place)
    for b in range(requests):
        limit = jnp.where(place_request == b, length_ref[b], limit)
    allowed = (here * positions + place % positions < limit) & (
        place_request == (column // tokens) % requests
    )
    first = column < 64
    stat_row = lax.broadcasted_iota(jnp.int32, (STAT_ROWS, HEAD_WIDTH), 0)
    for side, ref in enumerate((other_ref, lane_ref)):
        stats = jnp.zeros((STAT_ROWS, HEAD_WIDTH), jnp.float32)
        for p in range(PAIRS):
            spots = [2 * p * HEAD_WIDTH, (2 * p + 1) * HEAD_WIDTH]
            query = jnp.concatenate(
                [ref[2 * p * per_lane + t, h] for t in range(2 * per_lane) for h in range(heads)],
                axis=0,
            )
            scores = [
                dot(key_ref[:, at : at + HEAD_WIDTH], query, ((1,), (1,))) for at in spots
            ]
            scores = jnp.where(first, scores[0], scores[1]) * SCALE
            peak = jnp.max(jnp.where(allowed, scores, NEG_FILL), axis=0, keepdims=True)
            peak = round_bf16(peak)
            weights = jnp.where(allowed, jnp.exp(scores - peak), 0.0)
            total = jnp.sum(weights, axis=0, keepdims=True)
            weights = jnp.transpose(weights.astype(jnp.bfloat16))
            mix = [
                dot(weights[64 * i : 64 * i + 64], value_ref[:, at : at + HEAD_WIDTH], ((1,), (0,)))
                for i, at in enumerate(spots)
            ]
            at = p * 128
            for i in range(2):
                if side == 0:
                    send_ref[at + 64 * i : at + 64 * i + 64] = mix[i].astype(jnp.bfloat16)
                else:
                    mix_ref[at + 64 * i : at + 64 * i + 64] = mix[i]
            stats = jnp.where(stat_row == p, peak, stats)
            high = round_bf16(total)
            if side == 0:
                stats = jnp.where(stat_row == PAIRS + p, high, stats)
                stats = jnp.where(stat_row == 2 * PAIRS + p, total - high, stats)
            else:
                stats = jnp.where(stat_row == PAIRS + p, total, stats)
        if side == 0:
            send_ref[mix_total + 3 * step :] = stats.astype(jnp.bfloat16)
        else:
            stat_ref[...] = stats


def join_kernel(devices, requests, tokens, mix_ref, stat_ref, proj_ref, got_ref, packet_ref):
    rows = requests * tokens
    heads = QUERY_HEADS // devices
    mix_rows = heads * rows
    per_lane = devices // KEY_HEADS // 2
    mix_total = KEY_HEADS * 64
    step = KEY_HEADS * rows
    got = got_ref[mix_total + 3 * step :, :].astype(jnp.float32)
    own = stat_ref[...]
    own_peak, got_peak = own[:PAIRS], got[:PAIRS]
    peak = jnp.maximum(own_peak, got_peak)
    own_factor = jnp.exp(own_peak - peak)
    got_factor = jnp.exp(got_peak - peak)
    total = own_factor * own[PAIRS : 2 * PAIRS] + got_factor * (
        got[PAIRS : 2 * PAIRS] + got[2 * PAIRS : 3 * PAIRS]
    )
    high = round_bf16(total)
    filler = jnp.zeros((128 - 2 * PAIRS, 128), jnp.float32)
    table = jnp.transpose(jnp.concatenate([own_factor, got_factor, filler], axis=0))
    keys = got_ref[mix_total : mix_total + step].astype(jnp.float32) + got_ref[
        mix_total + step : mix_total + 2 * step
    ].astype(jnp.float32)
    keys += proj_ref[0].reshape(step, HEAD_WIDTH)
    values = got_ref[mix_total + 2 * step : mix_total + 3 * step].astype(jnp.float32)
    values += proj_ref[1].reshape(step, HEAD_WIDTH)
    keys_high = round_bf16(keys)
    keys_low = keys - keys_high
    stat_row = lax.broadcasted_iota(jnp.int32, (rows, HEAD_WIDTH), 0)
    for p in range(PAIRS):
        mix = mix_ref[p * 128 : p * 128 + 128] * table[:, p : p + 1] + got_ref[
            p * 128 : p * 128 + 128
        ].astype(jnp.float32) * table[:, PAIRS + p : PAIRS + p + 1]
        stats = jnp.where(
            stat_row == 0,
            peak[p : p + 1],
            jnp.where(
                stat_row == 1,
                high[p : p + 1],
                jnp.where(stat_row == 2, (total - high)[p : p + 1], 0.0),
            ),
        )
        for t in range(2 * per_lane):
            j = 2 * p + t // per_lane
            out_ref = packet_ref.at[2 * p * per_lane + t]
            out_ref[:mix_rows] = mix[t * mix_rows : (t + 1) * mix_rows].astype(jnp.bfloat16)
            shifted = stats if t == 0 else pltpu.roll(stats, HEAD_WIDTH - t * mix_rows, 1)
            own = slice(j * rows, (j + 1) * rows)
            out_ref[mix_rows:] = jnp.concatenate(
                [keys_high[own], keys_low[own], values[own], shifted], axis=0
            ).astype(jnp.bfloat16)


def merge_kernel(devices, requests, tokens, packed_ref, cos_ref, sin_ref, got_ref, out_ref):
    got_refs = [got_ref.at[s] for s in range(got_ref.shape[0])]
    rows = requests * tokens
    heads = QUERY_HEADS // devices
    mix_rows = heads * rows
    sources = len(got_refs)
    tails = [ref[mix_rows:].astype(jnp.float32) for ref in got_refs]
    sums = functools.reduce(jnp.add, [tail[: 3 * rows] for tail in tails])
    keys = sums[:rows] + sums[rows : 2 * rows]
    values = sums[2 * rows :].astype(jnp.bfloat16)
    turned = pltpu.roll(keys, HEAD_WIDTH // 2, 1)
    keys = (keys * cos_ref[...] + turned * sin_ref[...]).astype(jnp.bfloat16)
    query = jnp.concatenate([packed_ref[0, h] for h in range(heads)], axis=0)
    if mix_rows < 128:
        query = jnp.concatenate(
            [query, jnp.zeros((128 - mix_rows, HEAD_WIDTH), jnp.bfloat16)], axis=0
        )
    fresh = dot(keys, query, ((1,), (1,))) * SCALE
    source = lax.broadcasted_iota(jnp.int32, fresh.shape, 0)
    column = lax.broadcasted_iota(jnp.int32, fresh.shape, 1) % rows
    allowed = (source // tokens == column // tokens) & (source % tokens <= column % tokens)
    fresh_peak = jnp.max(jnp.where(allowed, fresh, NEG_FILL), axis=0, keepdims=True)
    stats = [tail[3 * rows :] for tail in tails]
    peak = functools.reduce(jnp.maximum, [stat[0:1] for stat in stats], fresh_peak)
    weights = jnp.where(allowed, jnp.exp(fresh - peak), 0.0)
    factors = [jnp.exp(stat[0:1] - peak) for stat in stats]
    total = functools.reduce(
        jnp.add,
        [factor * (stat[1:2] + stat[2:3]) for factor, stat in zip(factors, stats)],
        jnp.sum(weights, axis=0, keepdims=True),
    )
    inverse = 1.0 / total
    filler = jnp.zeros((128 - sources - 1, 128), jnp.float32)
    table = jnp.concatenate([factor * inverse for factor in factors] + [inverse, filler], axis=0)
    table = jnp.transpose(table)[:mix_rows]
    weights = jnp.transpose(
        jnp.concatenate([weights, jnp.zeros((128 - rows, 128), jnp.float32)], axis=0)
    )[:mix_rows].astype(jnp.bfloat16)
    values = jnp.concatenate(
        [values, jnp.zeros((128 - rows, HEAD_WIDTH), jnp.bfloat16)], axis=0
    )
    mix = dot(weights, values, ((1,), (0,))) * table[:, sources : sources + 1]
    for s, ref in enumerate(got_refs):
        mix += ref[:mix_rows].astype(jnp.float32) * table[:, s : s + 1]
    for h in range(heads):
        tile = mix[h * rows : (h + 1) * rows]
        for b in range(requests):
            out_ref[b, :, h * HEAD_WIDTH : (h + 1) * HEAD_WIDTH] = tile[
                b * tokens : (b + 1) * tokens
            ].astype(jnp.bfloat16)


def rotation(lengths, tokens):
    half = HEAD_WIDTH // 2
    places = (lengths[:, None] + jnp.arange(tokens, dtype=jnp.int32)[None, :]).astype(jnp.float32)
    inverse_freq = jnp.exp(
        jnp.arange(half, dtype=jnp.float32) * (-2.0 * math.log(ROPE_BASE) / HEAD_WIDTH)
    )
    angles = places.reshape(-1, 1) * inverse_freq[None, :]
    cosine, sine = jnp.cos(angles), jnp.sin(angles)
    return jnp.concatenate([cosine, cosine], axis=1), jnp.concatenate([-sine, sine], axis=1)


def vmem():
    return pl.BlockSpec(memory_space=pltpu.VMEM)


def smem():
    return pl.BlockSpec(memory_space=pltpu.SMEM)


def hbm():
    return pl.BlockSpec(memory_space=pltpu.HBM)


def cost(flops, moved):
    return pl.CostEstimate(flops=int(flops), bytes_accessed=int(moved), transcendentals=0)


def swap(x, devices, bit):
    return lax.ppermute(x, "tensor", [(d, d ^ bit) for d in range(devices)])


def per_device(
    hidden,
    queries,
    key_value_weight,
    adapter_down_weight,
    adapter_up_weight,
    cached_key_rows,
    cached_value_rows,
    request_adapter,
    adapter_rank_list,
    adapter_pool_row,
    lengths,
):
    requests, tokens, width = hidden.shape
    rows = requests * tokens
    devices = lax.axis_size("tensor")
    here = lax.axis_index("tensor")
    heads = QUERY_HEADS // devices
    chunks = width // HEAD_WIDTH
    lanes = devices // 2
    tiles = heads + chunks
    mix_rows = heads * rows

    lane_groups = [list(range(core, devices, 2)) for core in range(2)]

    def exchange(x):
        return lax.all_to_all(x, "tensor", 0, 0, axis_index_groups=lane_groups, tiled=True)

    packed = pl.pallas_call(
        functools.partial(pack_kernel, requests),
        out_shape=jax.ShapeDtypeStruct((lanes, tiles, rows, HEAD_WIDTH), jnp.bfloat16),
        in_specs=[vmem()] * 2,
        out_specs=vmem(),
        compiler_params=pltpu.CompilerParams(vmem_limit_bytes=8 * MIB),
        cost_estimate=cost(10**10, 0),
        name="pack",
    )(queries, hidden)
    lane = exchange(packed)

    base = pl.pallas_call(
        functools.partial(base_kernel, heads),
        out_shape=jax.ShapeDtypeStruct((rows, key_value_weight.shape[1]), jnp.float32),
        in_specs=[vmem()] * 2,
        out_specs=vmem(),
        compiler_params=pltpu.CompilerParams(vmem_limit_bytes=16 * MIB),
        cost_estimate=cost(2 * rows * key_value_weight.size, 2 * key_value_weight.size),
        name="base",
    )(packed, key_value_weight)
    lane, base = lax.optimization_barrier((lane, base))
    other = swap(lane, devices, 1)

    flat = requests * cached_key_rows.shape[1]
    mix_total = KEY_HEADS * 64
    send_rows = mix_total + 3 * KEY_HEADS * rows + STAT_ROWS
    send, mix, stats, proj = pl.pallas_call(
        functools.partial(partial_kernel, devices, requests, tokens),
        out_shape=(
            jax.ShapeDtypeStruct((send_rows, HEAD_WIDTH), jnp.bfloat16),
            jax.ShapeDtypeStruct((mix_total, HEAD_WIDTH), jnp.float32),
            jax.ShapeDtypeStruct((STAT_ROWS, HEAD_WIDTH), jnp.float32),
            jax.ShapeDtypeStruct((2, KEY_HEADS, rows, HEAD_WIDTH), jnp.float32),
        ),
        in_specs=[smem()] * 5 + [vmem()] * 7,
        out_specs=(vmem(),) * 4,
        compiler_params=pltpu.CompilerParams(vmem_limit_bytes=16 * MIB),
        name="partial_states",
    )(
        here.reshape(1).astype(jnp.int32),
        request_adapter,
        adapter_rank_list,
        adapter_pool_row,
        lengths,
        lane,
        other,
        base,
        adapter_down_weight[0],
        adapter_up_weight[0],
        cached_key_rows.reshape(flat, -1),
        cached_value_rows.reshape(flat, -1),
    )
    got = swap(send, devices, 1)
    packets = pl.pallas_call(
        functools.partial(join_kernel, devices, requests, tokens),
        out_shape=jax.ShapeDtypeStruct((lanes, mix_rows + 4 * rows, HEAD_WIDTH), jnp.bfloat16),
        in_specs=[vmem()] * 4,
        out_specs=vmem(),
        compiler_params=pltpu.CompilerParams(vmem_limit_bytes=8 * MIB),
        name="join",
    )(mix, stats, proj, got)
    packets = exchange(packets)
    cosine, sine = rotation(lengths, tokens)
    return pl.pallas_call(
        functools.partial(merge_kernel, devices, requests, tokens),
        out_shape=jax.ShapeDtypeStruct((requests, tokens, heads * HEAD_WIDTH), jnp.bfloat16),
        in_specs=[vmem()] * 4,
        out_specs=vmem(),
        compiler_params=pltpu.CompilerParams(vmem_limit_bytes=8 * MIB),
        name="merge_states",
    )(packed, cosine, sine, packets)


def solution(mesh):
    in_specs = (
        P("groups", None, "tensor"),
        P("groups", None, "tensor"),
        P("tensor", None),
        P("tensor", None, None),
        P("tensor", None, None),
        P("groups", "tensor", None),
        P("groups", "tensor", None),
        P("groups"),
        P(),
        P(),
        P("groups"),
    )
    out_specs = P("groups", None, "tensor")
    return jax.shard_map(
        per_device, mesh=mesh, in_specs=in_specs, out_specs=out_specs, check_vma=False
    )
```

```python
import functools
import math

import jax
import jax.numpy as jnp
from jax import lax
from jax.experimental import pallas as pl
from jax.experimental.pallas import tpu as pltpu
from jax.sharding import PartitionSpec as P

QUERY_HEADS = 128
KEY_HEADS = 8
HEAD_WIDTH = 128
ROPE_BASE = 500000.0
NEG_FILL = -1e30
SCALE = 1.0 / math.sqrt(HEAD_WIDTH)
PAIRS = KEY_HEADS // 2
STAT_ROWS = 16
MIB = 2**20


def dot(a, b, dims):
    return lax.dot_general(a, b, (dims, ((), ())), preferred_element_type=jnp.float32)


def round_bf16(x):
    return x.astype(jnp.bfloat16).astype(jnp.float32)


def pack_kernel(requests, heads, query_ref, hidden_ref, copies_ref, own_ref, query_buf, hidden_buf, sems):
    loads = [
        pltpu.make_async_copy(query_ref, query_buf, sems.at[0]),
        pltpu.make_async_copy(hidden_ref, hidden_buf, sems.at[1]),
    ]
    for load in loads:
        load.start()
    at = 0
    for load, ref in zip(loads, (query_buf, hidden_buf)):
        load.wait()
        rows = jnp.concatenate([ref[b].astype(jnp.float32) for b in range(requests)], axis=0)
        for c in range(rows.shape[1] // HEAD_WIDTH):
            tile = rows[:, c * HEAD_WIDTH : (c + 1) * HEAD_WIDTH].astype(jnp.bfloat16)
            own_ref[at] = tile
            for copy in range(copies_ref.shape[0]):
                copies_ref[copy, at] = tile
            at += 1


def base_kernel(heads, own_ref, weight_ref, *refs):
    count = (len(refs) - 3) // 2
    sources, base_ref, held = refs[:count], refs[count], refs[count + 1 : -2]
    buffer, sems = refs[-2:]
    parts, depth = buffer.shape[:2]
    loads = [
        pltpu.make_async_copy(weight_ref.at[pl.ds(p * depth, depth)], buffer.at[p], sems.at[p])
        for p in range(parts)
    ]
    others = [
        pltpu.make_async_copy(source, place, sems.at[parts + i])
        for i, (source, place) in enumerate(zip(sources, held))
    ]
    for load in loads + others:
        load.start()
    tiles = depth // HEAD_WIDTH
    total = jnp.zeros(base_ref.shape, jnp.float32)
    for p in range(parts):
        hidden = jnp.concatenate([own_ref[heads + p * tiles + c] for c in range(tiles)], axis=1)
        loads[p].wait()
        total += dot(hidden, buffer[p], ((1,), (0,)))
    base_ref[...] = total
    for load in others:
        load.wait()


def lower(side, heads, index_ref, gathered_ref, down_ref):
    lanes = gathered_ref.shape[0]
    depth = down_ref.shape[0] // lanes // 2
    total = None
    for m in range(lanes):
        hidden = jnp.concatenate(
            [gathered_ref[m, heads + c] for c in range(depth // HEAD_WIDTH)], axis=1
        )
        source = 2 * m + (index_ref[0] % 2 ^ side)
        factor = down_ref[pl.ds(pl.multiple_of(source * depth, depth), depth), :]
        term = dot(hidden, factor, ((1,), (0,)))
        total = term if total is None else total + term
    return total


def attend(requests, tokens, heads, index_ref, length_ref, query_ref, key_ref, value_ref, put):
    here = index_ref[0]
    per_lane = query_ref.shape[0] // KEY_HEADS
    positions = key_ref.shape[0] // requests
    place = lax.broadcasted_iota(jnp.int32, (requests * positions, HEAD_WIDTH), 0)
    column = lax.broadcasted_iota(jnp.int32, (requests * positions, HEAD_WIDTH), 1)
    place_request = place // positions
    limit = jnp.zeros_like(place)
    for b in range(requests):
        limit = jnp.where(place_request == b, length_ref[b], limit)
    allowed = (here * positions + place % positions < limit) & (
        place_request == (column // tokens) % requests
    )
    first = column < 64
    peaks, totals = [], []
    for p in range(PAIRS):
        spots = [2 * p * HEAD_WIDTH, (2 * p + 1) * HEAD_WIDTH]
        query = jnp.concatenate(
            [query_ref[2 * p * per_lane + t, h] for t in range(2 * per_lane) for h in range(heads)],
            axis=0,
        )
        scores = [dot(key_ref[:, at : at + HEAD_WIDTH], query, ((1,), (1,))) for at in spots]
        scores = jnp.where(first, scores[0], scores[1]) * SCALE
        peak = jnp.max(jnp.where(allowed, scores, NEG_FILL), axis=0, keepdims=True)
        peak = round_bf16(peak)
        weights = jnp.where(allowed, jnp.exp(scores - peak), 0.0)
        peaks.append(peak)
        totals.append(jnp.sum(weights, axis=0, keepdims=True))
        weights = jnp.transpose(weights.astype(jnp.bfloat16))
        for i, at in enumerate(spots):
            mix = dot(weights[64 * i : 64 * i + 64], value_ref[:, at : at + HEAD_WIDTH], ((1,), (0,)))
            put(p, i, mix)
    return peaks, totals


def rows_of(items, count):
    row = lax.broadcasted_iota(jnp.int32, (count, HEAD_WIDTH), 0)
    out = jnp.zeros((count, HEAD_WIDTH), jnp.float32)
    for i, item in enumerate(items):
        out = jnp.where(row == i, item, out)
    return out


def lower_kernel(heads, index_ref, lane_ref, down_ref, out_ref):
    out_ref[...] = lower(0, heads, index_ref, lane_ref, down_ref)


def other_kernel(requests, tokens, heads, *refs):
    (index_ref, adapter_ref, rank_ref, pool_ref, length_ref) = refs[:5]
    (other_ref, lowered_ref, base_ref, down_ref, up_ref, key_ref, value_ref) = refs[5:12]
    (send_ref, proj_ref) = refs[12:]
    rows = requests * tokens
    lowered = lowered_ref[...] + lower(1, heads, index_ref, other_ref, down_ref)
    row_request = lax.broadcasted_iota(jnp.int32, (rows, 1), 0) // tokens
    ranks = jnp.zeros((rows, 1), jnp.int32)
    owners = jnp.zeros((rows, 1), jnp.int32)
    for b in range(requests):
        adapter = adapter_ref[b]
        ranks = jnp.where(row_request == b, rank_ref[adapter], ranks)
        owners = jnp.where(row_request == b, pool_ref[adapter], owners)
    column = lax.broadcasted_iota(jnp.int32, lowered.shape, 1)
    lowered = jnp.where(column < ranks, lowered, 0.0).astype(jnp.bfloat16)
    lifted = dot(lowered, up_ref[...], ((1,), (0,)))
    projected = base_ref[...] + jnp.where(owners == index_ref[0], lifted, 0.0)
    split = KEY_HEADS * HEAD_WIDTH
    for j in range(KEY_HEADS):
        at = j * HEAD_WIDTH
        proj_ref[0, j] = projected[:, at : at + HEAD_WIDTH]
        proj_ref[1, j] = projected[:, split + at : split + at + HEAD_WIDTH]
    mix_total = KEY_HEADS * 64
    step = KEY_HEADS * rows
    keys = proj_ref[0].reshape(step, HEAD_WIDTH)
    high = keys.astype(jnp.bfloat16)
    send_ref[mix_total : mix_total + step] = high
    send_ref[mix_total + step : mix_total + 2 * step] = (keys - high.astype(jnp.float32)).astype(
        jnp.bfloat16
    )
    send_ref[mix_total + 2 * step : mix_total + 3 * step] = (
        proj_ref[1].reshape(step, HEAD_WIDTH).astype(jnp.bfloat16)
    )

    def put(p, i, mix):
        at = p * 128 + i * 64
        send_ref[at : at + 64] = mix.astype(jnp.bfloat16)

    peaks, totals = attend(
        requests, tokens, heads, index_ref, length_ref, other_ref, key_ref, value_ref, put
    )
    highs = [round_bf16(total) for total in totals]
    lows = [total - high for total, high in zip(totals, highs)]
    send_ref[mix_total + 3 * step :] = rows_of(peaks + highs + lows, STAT_ROWS).astype(jnp.bfloat16)


def own_kernel(
    requests, tokens, heads, index_ref, length_ref, lane_ref, key_ref, value_ref, mix_ref, stat_ref
):
    def put(p, i, mix):
        at = p * 128 + i * 64
        mix_ref[at : at + 64] = mix

    peaks, totals = attend(
        requests, tokens, heads, index_ref, length_ref, lane_ref, key_ref, value_ref, put
    )
    stat_ref[...] = rows_of(peaks + totals, STAT_ROWS)


def join_kernel(devices, requests, tokens, mix_ref, stat_ref, proj_ref, got_ref, packet_ref):
    rows = requests * tokens
    heads = QUERY_HEADS // devices
    mix_rows = heads * rows
    per_lane = devices // KEY_HEADS // 2
    mix_total = KEY_HEADS * 64
    step = KEY_HEADS * rows
    got = got_ref[mix_total + 3 * step :, :].astype(jnp.float32)
    own = stat_ref[...]
    own_peak, got_peak = own[:PAIRS], got[:PAIRS]
    peak = jnp.maximum(own_peak, got_peak)
    own_factor = jnp.exp(own_peak - peak)
    got_factor = jnp.exp(got_peak - peak)
    total = own_factor * own[PAIRS : 2 * PAIRS] + got_factor * (
        got[PAIRS : 2 * PAIRS] + got[2 * PAIRS : 3 * PAIRS]
    )
    high = round_bf16(total)
    filler = jnp.zeros((128 - 2 * PAIRS, 128), jnp.float32)
    table = jnp.transpose(jnp.concatenate([own_factor, got_factor, filler], axis=0))
    keys = got_ref[mix_total : mix_total + step].astype(jnp.float32) + got_ref[
        mix_total + step : mix_total + 2 * step
    ].astype(jnp.float32)
    keys += proj_ref[0].reshape(step, HEAD_WIDTH)
    values = got_ref[mix_total + 2 * step : mix_total + 3 * step].astype(jnp.float32)
    values += proj_ref[1].reshape(step, HEAD_WIDTH)
    keys_high = round_bf16(keys)
    keys_low = keys - keys_high
    stat_row = lax.broadcasted_iota(jnp.int32, (rows, HEAD_WIDTH), 0)
    for p in range(PAIRS):
        mix = mix_ref[p * 128 : p * 128 + 128] * table[:, p : p + 1] + got_ref[
            p * 128 : p * 128 + 128
        ].astype(jnp.float32) * table[:, PAIRS + p : PAIRS + p + 1]
        stats = jnp.where(
            stat_row == 0,
            peak[p : p + 1],
            jnp.where(
                stat_row == 1,
                high[p : p + 1],
                jnp.where(stat_row == 2, (total - high)[p : p + 1], 0.0),
            ),
        )
        for t in range(2 * per_lane):
            j = 2 * p + t // per_lane
            out_ref = packet_ref.at[2 * p * per_lane + t]
            out_ref[:mix_rows] = mix[t * mix_rows : (t + 1) * mix_rows].astype(jnp.bfloat16)
            shifted = stats if t == 0 else pltpu.roll(stats, HEAD_WIDTH - t * mix_rows, 1)
            own = slice(j * rows, (j + 1) * rows)
            out_ref[mix_rows:] = jnp.concatenate(
                [keys_high[own], keys_low[own], values[own], shifted], axis=0
            ).astype(jnp.bfloat16)


def merge_kernel(devices, requests, tokens, own_ref, cos_ref, sin_ref, got_ref, out_ref):
    got_refs = [got_ref.at[s] for s in range(got_ref.shape[0])]
    rows = requests * tokens
    heads = QUERY_HEADS // devices
    mix_rows = heads * rows
    sources = len(got_refs)
    tails = [ref[mix_rows:].astype(jnp.float32) for ref in got_refs]
    sums = functools.reduce(jnp.add, [tail[: 3 * rows] for tail in tails])
    keys = sums[:rows] + sums[rows : 2 * rows]
    values = sums[2 * rows :].astype(jnp.bfloat16)
    turned = pltpu.roll(keys, HEAD_WIDTH // 2, 1)
    keys = (keys * cos_ref[...] + turned * sin_ref[...]).astype(jnp.bfloat16)
    query = jnp.concatenate([own_ref[h] for h in range(heads)], axis=0)
    if mix_rows < 128:
        query = jnp.concatenate(
            [query, jnp.zeros((128 - mix_rows, HEAD_WIDTH), jnp.bfloat16)], axis=0
        )
    fresh = dot(keys, query, ((1,), (1,))) * SCALE
    source = lax.broadcasted_iota(jnp.int32, fresh.shape, 0)
    column = lax.broadcasted_iota(jnp.int32, fresh.shape, 1) % rows
    allowed = (source // tokens == column // tokens) & (source % tokens <= column % tokens)
    fresh_peak = jnp.max(jnp.where(allowed, fresh, NEG_FILL), axis=0, keepdims=True)
    stats = [tail[3 * rows :] for tail in tails]
    peak = functools.reduce(jnp.maximum, [stat[0:1] for stat in stats], fresh_peak)
    weights = jnp.where(allowed, jnp.exp(fresh - peak), 0.0)
    factors = [jnp.exp(stat[0:1] - peak) for stat in stats]
    total = functools.reduce(
        jnp.add,
        [factor * (stat[1:2] + stat[2:3]) for factor, stat in zip(factors, stats)],
        jnp.sum(weights, axis=0, keepdims=True),
    )
    inverse = 1.0 / total
    filler = jnp.zeros((128 - sources - 1, 128), jnp.float32)
    table = jnp.concatenate([factor * inverse for factor in factors] + [inverse, filler], axis=0)
    table = jnp.transpose(table)[:mix_rows]
    weights = jnp.transpose(
        jnp.concatenate([weights, jnp.zeros((128 - rows, 128), jnp.float32)], axis=0)
    )[:mix_rows].astype(jnp.bfloat16)
    values = jnp.concatenate(
        [values, jnp.zeros((128 - rows, HEAD_WIDTH), jnp.bfloat16)], axis=0
    )
    mix = dot(weights, values, ((1,), (0,))) * table[:, sources : sources + 1]
    for s, ref in enumerate(got_refs):
        mix += ref[:mix_rows].astype(jnp.float32) * table[:, s : s + 1]
    for h in range(heads):
        tile = mix[h * rows : (h + 1) * rows]
        for b in range(requests):
            out_ref[b, :, h * HEAD_WIDTH : (h + 1) * HEAD_WIDTH] = tile[
                b * tokens : (b + 1) * tokens
            ].astype(jnp.bfloat16)


def rotation(lengths, tokens):
    half = HEAD_WIDTH // 2
    places = (lengths[:, None] + jnp.arange(tokens, dtype=jnp.int32)[None, :]).astype(jnp.float32)
    inverse_freq = jnp.exp(
        jnp.arange(half, dtype=jnp.float32) * (-2.0 * math.log(ROPE_BASE) / HEAD_WIDTH)
    )
    angles = places.reshape(-1, 1) * inverse_freq[None, :]
    cosine, sine = jnp.cos(angles), jnp.sin(angles)
    return jnp.concatenate([cosine, cosine], axis=1), jnp.concatenate([-sine, sine], axis=1)


def vmem():
    return pl.BlockSpec(memory_space=pltpu.VMEM)


def smem():
    return pl.BlockSpec(memory_space=pltpu.SMEM)


def hbm():
    return pl.BlockSpec(memory_space=pltpu.HBM)


def pinned(x):
    return pltpu.with_memory_space_constraint(x, pltpu.HBM)


def cost(flops, moved):
    return pl.CostEstimate(flops=int(flops), bytes_accessed=int(moved), transcendentals=0)


def swap(x, devices, bit):
    return lax.ppermute(x, "tensor", [(d, d ^ bit) for d in range(devices)])


def per_device(
    hidden,
    queries,
    key_value_weight,
    adapter_down_weight,
    adapter_up_weight,
    cached_key_rows,
    cached_value_rows,
    request_adapter,
    adapter_rank_list,
    adapter_pool_row,
    lengths,
):
    requests, tokens, width = hidden.shape
    rows = requests * tokens
    devices = lax.axis_size("tensor")
    here = lax.axis_index("tensor")
    heads = QUERY_HEADS // devices
    chunks = width // HEAD_WIDTH
    lanes = devices // 2
    tiles = heads + chunks
    mix_rows = heads * rows

    lane_groups = [list(range(core, devices, 2)) for core in range(2)]

    def exchange(x):
        return lax.all_to_all(x, "tensor", 0, 0, axis_index_groups=lane_groups, tiled=True)

    tile_shape = (tiles, rows, HEAD_WIDTH)
    copies, own = pl.pallas_call(
        functools.partial(pack_kernel, requests, heads),
        out_shape=(
            jax.ShapeDtypeStruct((lanes,) + tile_shape, jnp.bfloat16),
            pltpu.VMEM(tile_shape, jnp.bfloat16),
        ),
        in_specs=[hbm()] * 2,
        out_specs=(vmem(),) * 2,
        scratch_shapes=[
            pltpu.VMEM(queries.shape, jnp.bfloat16),
            pltpu.VMEM(hidden.shape, jnp.bfloat16),
            pltpu.SemaphoreType.DMA((2,)),
        ],
        compiler_params=pltpu.CompilerParams(vmem_limit_bytes=4 * MIB),
        name="pack",
    )(pinned(queries), pinned(hidden))
    lane = exchange(copies)

    flat = requests * cached_key_rows.shape[1]
    big = (
        adapter_down_weight[0],
        cached_key_rows.reshape(flat, -1),
        cached_value_rows.reshape(flat, -1),
        adapter_up_weight[0],
    )
    out_width = key_value_weight.shape[1]
    parts = 4 if width % (4 * HEAD_WIDTH) == 0 else 1
    base, down, keys, values, up = pl.pallas_call(
        functools.partial(base_kernel, heads),
        out_shape=(pltpu.VMEM((rows, out_width), jnp.float32),)
        + tuple(pltpu.VMEM(x.shape, x.dtype) for x in big),
        in_specs=[vmem()] + [hbm()] * 5,
        out_specs=(vmem(),) * 5,
        scratch_shapes=[
            pltpu.VMEM((parts, width // parts, out_width), jnp.bfloat16),
            pltpu.SemaphoreType.DMA((parts + 4,)),
        ],
        compiler_params=pltpu.CompilerParams(vmem_limit_bytes=12 * MIB),
        cost_estimate=cost(10**9, 0),
        name="base",
    )(own, pinned(key_value_weight), *[pinned(x) for x in big])
    lane, base = lax.optimization_barrier((lane, base))
    other = swap(lane, devices, 1)

    index = here.reshape(1).astype(jnp.int32)
    lowered = pl.pallas_call(
        functools.partial(lower_kernel, heads),
        out_shape=pltpu.VMEM((rows, down.shape[1]), jnp.float32),
        in_specs=[smem()] + [vmem()] * 2,
        out_specs=vmem(),
        compiler_params=pltpu.CompilerParams(vmem_limit_bytes=12 * MIB),
        cost_estimate=cost(10**9, 0),
        name="lower",
    )(index, lane, down)
    mix_total = KEY_HEADS * 64
    send_rows = mix_total + 3 * KEY_HEADS * rows + STAT_ROWS
    send, proj = pl.pallas_call(
        functools.partial(other_kernel, requests, tokens, heads),
        out_shape=(
            pltpu.VMEM((send_rows, HEAD_WIDTH), jnp.bfloat16),
            pltpu.VMEM((2, KEY_HEADS, rows, HEAD_WIDTH), jnp.float32),
        ),
        in_specs=[smem()] * 5 + [vmem()] * 7,
        out_specs=(vmem(),) * 2,
        compiler_params=pltpu.CompilerParams(vmem_limit_bytes=12 * MIB),
        name="other_lane",
    )(
        index,
        request_adapter,
        adapter_rank_list,
        adapter_pool_row,
        lengths,
        other,
        lowered,
        base,
        down,
        up,
        keys,
        values,
    )
    got = swap(send, devices, 1)
    mix, stats = pl.pallas_call(
        functools.partial(own_kernel, requests, tokens, heads),
        out_shape=(
            pltpu.VMEM((mix_total, HEAD_WIDTH), jnp.float32),
            pltpu.VMEM((STAT_ROWS, HEAD_WIDTH), jnp.float32),
        ),
        in_specs=[smem()] * 2 + [vmem()] * 3,
        out_specs=(vmem(),) * 2,
        compiler_params=pltpu.CompilerParams(vmem_limit_bytes=8 * MIB),
        cost_estimate=cost(10**9, 0),
        name="own_lane",
    )(index, lengths, lane, keys, values)
    packets = pl.pallas_call(
        functools.partial(join_kernel, devices, requests, tokens),
        out_shape=jax.ShapeDtypeStruct((lanes, mix_rows + 4 * rows, HEAD_WIDTH), jnp.bfloat16),
        in_specs=[vmem()] * 4,
        out_specs=vmem(),
        compiler_params=pltpu.CompilerParams(vmem_limit_bytes=8 * MIB),
        name="join",
    )(mix, stats, proj, got)
    packets = exchange(packets)
    cosine, sine = rotation(lengths, tokens)
    return pl.pallas_call(
        functools.partial(merge_kernel, devices, requests, tokens),
        out_shape=jax.ShapeDtypeStruct((requests, tokens, heads * HEAD_WIDTH), jnp.bfloat16),
        in_specs=[vmem()] * 4,
        out_specs=vmem(),
        compiler_params=pltpu.CompilerParams(vmem_limit_bytes=8 * MIB),
        name="merge_states",
    )(own, cosine, sine, packets)


def solution(mesh):
    in_specs = (
        P("groups", None, "tensor"),
        P("groups", None, "tensor"),
        P("tensor", None),
        P("tensor", None, None),
        P("tensor", None, None),
        P("groups", "tensor", None),
        P("groups", "tensor", None),
        P("groups"),
        P(),
        P(),
        P("groups"),
    )
    out_specs = P("groups", None, "tensor")
    return jax.shard_map(
        per_device, mesh=mesh, in_specs=in_specs, out_specs=out_specs, check_vma=False
    )
```

```python
import functools
import math

import jax
import jax.numpy as jnp
from jax import lax
from jax.experimental import pallas as pl
from jax.experimental.pallas import tpu as pltpu
from jax.sharding import PartitionSpec as P

QUERY_HEADS = 128
KEY_HEADS = 8
HEAD_WIDTH = 128
ROPE_BASE = 500000.0
NEG_FILL = -1e30
SCALE = 1.0 / math.sqrt(HEAD_WIDTH)
PAIRS = KEY_HEADS // 2
STAT_ROWS = 16
MIB = 2**20


def dot(a, b, dims):
    return lax.dot_general(a, b, (dims, ((), ())), preferred_element_type=jnp.float32)


def round_bf16(x):
    return x.astype(jnp.bfloat16).astype(jnp.float32)


def pack_kernel(requests, query_ref, hidden_ref, own_ref, query_buf, hidden_buf, sems):
    loads = [
        pltpu.make_async_copy(query_ref, query_buf, sems.at[0]),
        pltpu.make_async_copy(hidden_ref, hidden_buf, sems.at[1]),
    ]
    for load in loads:
        load.start()
    at = 0
    for load, ref in zip(loads, (query_buf, hidden_buf)):
        load.wait()
        rows = jnp.concatenate([ref[b].astype(jnp.float32) for b in range(requests)], axis=0)
        for c in range(rows.shape[1] // HEAD_WIDTH):
            tile = rows[:, c * HEAD_WIDTH : (c + 1) * HEAD_WIDTH].astype(jnp.bfloat16)
            own_ref[at] = tile
            at += 1


def base_kernel(heads, own_ref, weight_ref, *refs):
    count = (len(refs) - 3) // 2
    sources, base_ref, held = refs[:count], refs[count], refs[count + 1 : -2]
    buffer, sems = refs[-2:]
    parts, depth = buffer.shape[:2]
    loads = [
        pltpu.make_async_copy(weight_ref.at[pl.ds(p * depth, depth)], buffer.at[p], sems.at[p])
        for p in range(parts)
    ]
    others = [
        pltpu.make_async_copy(source, place, sems.at[parts + i])
        for i, (source, place) in enumerate(zip(sources, held))
    ]
    for load in loads + others:
        load.start()
    tiles = depth // HEAD_WIDTH
    total = jnp.zeros(base_ref.shape, jnp.float32)
    for p in range(parts):
        hidden = jnp.concatenate([own_ref[heads + p * tiles + c] for c in range(tiles)], axis=1)
        loads[p].wait()
        total += dot(hidden, buffer[p], ((1,), (0,)))
    base_ref[...] = total
    for load in others:
        load.wait()


def stream(side, masks, index_ref, down_ref, buffer, sems, at):
    depth = buffer.shape[1]
    copies = []
    for i, mask in enumerate(masks):
        source = index_ref[0] ^ (2 * mask + side)
        rows = pl.ds(pl.multiple_of(source * depth, depth), depth)
        copies.append(pltpu.make_async_copy(down_ref.at[rows], buffer.at[at + i], sems.at[at + i]))
    for copy in copies:
        copy.start()
    return copies


def lower(heads, gathered_ref, copies, buffer, at):
    total = None
    for i, copy in enumerate(copies):
        hidden = jnp.concatenate(
            [gathered_ref[i, heads + c] for c in range(buffer.shape[1] // HEAD_WIDTH)], axis=1
        )
        copy.wait()
        term = dot(hidden, buffer[at + i], ((1,), (0,)))
        total = term if total is None else total + term
    return total


def chunks_of(masks, slots):
    order = sorted(masks)
    return [order[at : at + slots] for at in range(0, len(order), slots)]


def attend(requests, tokens, devices, masks, index_ref, length_ref, query_ref, key_ref, value_ref, put):
    here = index_ref[0]
    heads = QUERY_HEADS // devices
    tile = requests * tokens
    slot_rows = heads * tile
    per_lane = devices // 2 // KEY_HEADS
    positions = key_ref.shape[0] // requests
    place = lax.broadcasted_iota(jnp.int32, (requests * positions, HEAD_WIDTH), 0)
    column = lax.broadcasted_iota(jnp.int32, (requests * positions, HEAD_WIDTH), 1)
    place_request = place // positions
    limit = jnp.zeros_like(place)
    for b in range(requests):
        limit = jnp.where(place_request == b, length_ref[b], limit)
    allowed = (here * positions + place % positions < limit) & (
        place_request == (column // tokens) % requests
    )
    peaks, totals = [], []
    for number, chunk in enumerate(chunks_of(masks, HEAD_WIDTH // slot_rows)):
        query = jnp.concatenate(
            [query_ref[masks.index(mask), h] for mask in chunk for h in range(heads)], axis=0
        )
        key_heads = sorted({mask // per_lane for mask in chunk})
        spots = [
            pl.multiple_of(((here // 2 // per_lane) ^ head) * HEAD_WIDTH, HEAD_WIDTH)
            for head in key_heads
        ]
        share = HEAD_WIDTH // len(key_heads)
        scores = None
        for i, at in enumerate(spots):
            part = dot(key_ref[:, pl.ds(at, HEAD_WIDTH)], query, ((1,), (1,)))
            scores = part if scores is None else jnp.where(column < i * share, scores, part)
        scores = scores * SCALE
        peak = jnp.max(jnp.where(allowed, scores, NEG_FILL), axis=0, keepdims=True)
        peak = round_bf16(peak)
        weights = jnp.where(allowed, jnp.exp(scores - peak), 0.0)
        peaks.append(peak)
        totals.append(jnp.sum(weights, axis=0, keepdims=True))
        weights = jnp.transpose(weights.astype(jnp.bfloat16))
        for i, at in enumerate(spots):
            value = value_ref[:, pl.ds(at, HEAD_WIDTH)]
            put(number, i * share, dot(weights[i * share : (i + 1) * share], value, ((1,), (0,))))
    return peaks, totals


def rows_of(items, count):
    row = lax.broadcasted_iota(jnp.int32, (count, HEAD_WIDTH), 0)
    out = jnp.zeros((count, HEAD_WIDTH), jnp.float32)
    for i, item in enumerate(items):
        out = jnp.where(row == i, item, out)
    return out


def own_kernel(
    sizes, masks, with_lora, index_ref, length_ref, lane_ref, key_ref, value_ref, *refs
):
    requests, tokens, devices = sizes
    if with_lora:
        down_ref, mix_ref, stat_ref, lowered_ref, buffer, sems = refs
        copies = stream(0, masks, index_ref, down_ref, buffer, sems, 0)
    else:
        mix_ref, stat_ref = refs

    def put(chunk, row, mix):
        at = chunk * 128 + row
        mix_ref[at : at + mix.shape[0]] = mix

    peaks, totals = attend(
        requests, tokens, devices, masks, index_ref, length_ref, lane_ref, key_ref, value_ref, put
    )
    stat_ref[...] = rows_of(peaks + totals, 8)
    if with_lora:
        lowered_ref[...] = lower(QUERY_HEADS // devices, lane_ref, copies, buffer, 0)


def early_kernel(sizes, masks, *refs):
    (index_ref, length_ref, lane_ref, other_ref, key_ref, value_ref, down_ref) = refs[:7]
    (send_ref, stat_ref, lowered_ref, buffer, sems) = refs[7:]
    requests, tokens, devices = sizes
    heads = QUERY_HEADS // devices
    count = len(masks)
    lane_copies = stream(0, masks, index_ref, down_ref, buffer, sems, 0)
    other_copies = stream(1, masks, index_ref, down_ref, buffer, sems, count)

    def put(chunk, row, mix):
        at = chunk * 128 + row
        send_ref[at : at + mix.shape[0]] = mix.astype(jnp.bfloat16)

    peaks, totals = attend(
        requests, tokens, devices, masks, index_ref, length_ref, other_ref, key_ref, value_ref, put
    )
    stat_ref[...] = rows_of(peaks + totals, 8)
    lowered_ref[...] = lower(heads, lane_ref, lane_copies, buffer, 0) + lower(
        heads, other_ref, other_copies, buffer, count
    )


def late_kernel(sizes, masks, *refs):
    (index_ref, adapter_ref, rank_ref, pool_ref, length_ref) = refs[:5]
    (other_ref, key_ref, value_ref, down_ref, base_ref, up_ref) = refs[5:11]
    (early_ref, early_stat_ref, early_lowered_ref, own_lowered_ref) = refs[11:15]
    (send_ref, proj_ref, buffer, sems) = refs[15:]
    requests, tokens, devices = sizes
    rows = requests * tokens
    copies = stream(1, masks, index_ref, down_ref, buffer, sems, 0)
    mix_total = KEY_HEADS * 64
    half = mix_total // 2
    step = KEY_HEADS * rows
    send_ref[:half] = early_ref[...]

    def put(chunk, row, mix):
        at = half + chunk * 128 + row
        send_ref[at : at + mix.shape[0]] = mix.astype(jnp.bfloat16)

    peaks, totals = attend(
        requests, tokens, devices, masks, index_ref, length_ref, other_ref, key_ref, value_ref, put
    )
    early = early_stat_ref[...]
    count = PAIRS // 2
    peaks = [early[i : i + 1] for i in range(count)] + peaks
    totals = [early[count + i : count + i + 1] for i in range(count)] + totals
    highs = [round_bf16(total) for total in totals]
    lows = [total - high for total, high in zip(totals, highs)]
    send_ref[mix_total + 3 * step :] = rows_of(peaks + highs + lows, STAT_ROWS).astype(jnp.bfloat16)

    lowered = early_lowered_ref[...] + own_lowered_ref[...]
    lowered += lower(QUERY_HEADS // devices, other_ref, copies, buffer, 0)
    row_request = lax.broadcasted_iota(jnp.int32, (rows, 1), 0) // tokens
    ranks = jnp.zeros((rows, 1), jnp.int32)
    owners = jnp.zeros((rows, 1), jnp.int32)
    for b in range(requests):
        adapter = adapter_ref[b]
        ranks = jnp.where(row_request == b, rank_ref[adapter], ranks)
        owners = jnp.where(row_request == b, pool_ref[adapter], owners)
    column = lax.broadcasted_iota(jnp.int32, lowered.shape, 1)
    lowered = jnp.where(column < ranks, lowered, 0.0).astype(jnp.bfloat16)
    lifted = dot(lowered, up_ref[...], ((1,), (0,)))
    projected = base_ref[...] + jnp.where(owners == index_ref[0], lifted, 0.0)
    split = KEY_HEADS * HEAD_WIDTH
    for j in range(KEY_HEADS):
        at = j * HEAD_WIDTH
        proj_ref[0, j] = projected[:, at : at + HEAD_WIDTH]
        proj_ref[1, j] = projected[:, split + at : split + at + HEAD_WIDTH]
    keys = proj_ref[0].reshape(step, HEAD_WIDTH)
    high = keys.astype(jnp.bfloat16)
    send_ref[mix_total : mix_total + step] = high
    send_ref[mix_total + step : mix_total + 2 * step] = (keys - high.astype(jnp.float32)).astype(
        jnp.bfloat16
    )
    send_ref[mix_total + 2 * step : mix_total + 3 * step] = (
        proj_ref[1].reshape(step, HEAD_WIDTH).astype(jnp.bfloat16)
    )


def join_kernel(sizes, chunks, index_ref, *refs):
    (first_ref, second_ref, first_stat_ref, second_stat_ref, proj_ref, got_ref) = refs[:6]
    packet_ref, tail_ref = refs[6:]
    requests, tokens, devices = sizes
    chip = index_ref[0] // 2
    rows = requests * tokens
    heads = QUERY_HEADS // devices
    mix_rows = heads * rows
    per_lane = devices // 2 // KEY_HEADS
    mix_total = KEY_HEADS * 64
    step = KEY_HEADS * rows
    count = PAIRS // 2
    got = got_ref[mix_total + 3 * step :, :].astype(jnp.float32)
    first, second = first_stat_ref[...], second_stat_ref[...]
    own_peak = jnp.concatenate([first[:count], second[:count]], axis=0)
    own_total = jnp.concatenate([first[count:PAIRS], second[count:PAIRS]], axis=0)
    got_peak = got[:PAIRS]
    peak = jnp.maximum(own_peak, got_peak)
    own_factor = jnp.exp(own_peak - peak)
    got_factor = jnp.exp(got_peak - peak)
    total = own_factor * own_total + got_factor * (got[PAIRS : 2 * PAIRS] + got[2 * PAIRS : 3 * PAIRS])
    high = round_bf16(total)
    low = total - high
    filler = jnp.zeros((128 - 2 * PAIRS, 128), jnp.float32)
    table = jnp.transpose(jnp.concatenate([own_factor, got_factor, filler], axis=0))
    keys = got_ref[mix_total : mix_total + step].astype(jnp.float32) + got_ref[
        mix_total + step : mix_total + 2 * step
    ].astype(jnp.float32)
    keys += proj_ref[0].reshape(step, HEAD_WIDTH)
    values = got_ref[mix_total + 2 * step : mix_total + 3 * step].astype(jnp.float32)
    values += proj_ref[1].reshape(step, HEAD_WIDTH)
    keys_high = round_bf16(keys)
    for j in range(KEY_HEADS):
        own = slice(j * rows, (j + 1) * rows)
        tail_ref[j, :rows] = keys_high[own]
        tail_ref[j, rows : 2 * rows] = (keys - keys_high)[own]
        tail_ref[j, 2 * rows :] = values[own]
    stat_row = lax.broadcasted_iota(jnp.int32, (rows, HEAD_WIDTH), 0)
    for c, chunk in enumerate(chunks):
        own_ref, at = (first_ref, c * 128) if c < count else (second_ref, (c - count) * 128)
        mix = own_ref[at : at + 128] * table[:, c : c + 1] + got_ref[
            c * 128 : c * 128 + 128
        ].astype(jnp.float32) * table[:, PAIRS + c : PAIRS + c + 1]
        stats = jnp.where(
            stat_row == 0,
            peak[c : c + 1],
            jnp.where(
                stat_row == 1, high[c : c + 1], jnp.where(stat_row == 2, low[c : c + 1], 0.0)
            ),
        )
        for t, mask in enumerate(chunk):
            to = chip ^ mask
            shifted = stats if t == 0 else pltpu.roll(stats, HEAD_WIDTH - t * mix_rows, 1)
            tail = jnp.concatenate([tail_ref[to // per_lane], shifted], axis=0)
            packet_ref[to, :mix_rows] = mix[t * mix_rows : (t + 1) * mix_rows].astype(jnp.bfloat16)
            packet_ref[to, mix_rows:] = tail.astype(jnp.bfloat16)


def merge_kernel(devices, requests, tokens, own_ref, cos_ref, sin_ref, got_ref, out_ref):
    got_refs = [got_ref.at[s] for s in range(got_ref.shape[0])]
    rows = requests * tokens
    heads = QUERY_HEADS // devices
    mix_rows = heads * rows
    sources = len(got_refs)
    tails = [ref[mix_rows:].astype(jnp.float32) for ref in got_refs]
    sums = functools.reduce(jnp.add, [tail[: 3 * rows] for tail in tails])
    keys = sums[:rows] + sums[rows : 2 * rows]
    values = sums[2 * rows :].astype(jnp.bfloat16)
    turned = pltpu.roll(keys, HEAD_WIDTH // 2, 1)
    keys = (keys * cos_ref[...] + turned * sin_ref[...]).astype(jnp.bfloat16)
    query = jnp.concatenate([own_ref[h] for h in range(heads)], axis=0)
    if mix_rows < 128:
        query = jnp.concatenate(
            [query, jnp.zeros((128 - mix_rows, HEAD_WIDTH), jnp.bfloat16)], axis=0
        )
    fresh = dot(keys, query, ((1,), (1,))) * SCALE
    source = lax.broadcasted_iota(jnp.int32, fresh.shape, 0)
    column = lax.broadcasted_iota(jnp.int32, fresh.shape, 1) % rows
    allowed = (source // tokens == column // tokens) & (source % tokens <= column % tokens)
    fresh_peak = jnp.max(jnp.where(allowed, fresh, NEG_FILL), axis=0, keepdims=True)
    stats = [tail[3 * rows :] for tail in tails]
    peak = functools.reduce(jnp.maximum, [stat[0:1] for stat in stats], fresh_peak)
    weights = jnp.where(allowed, jnp.exp(fresh - peak), 0.0)
    factors = [jnp.exp(stat[0:1] - peak) for stat in stats]
    total = functools.reduce(
        jnp.add,
        [factor * (stat[1:2] + stat[2:3]) for factor, stat in zip(factors, stats)],
        jnp.sum(weights, axis=0, keepdims=True),
    )
    inverse = 1.0 / total
    filler = jnp.zeros((128 - sources - 1, 128), jnp.float32)
    table = jnp.concatenate([factor * inverse for factor in factors] + [inverse, filler], axis=0)
    table = jnp.transpose(table)[:mix_rows]
    weights = jnp.transpose(
        jnp.concatenate([weights, jnp.zeros((128 - rows, 128), jnp.float32)], axis=0)
    )[:mix_rows].astype(jnp.bfloat16)
    values = jnp.concatenate(
        [values, jnp.zeros((128 - rows, HEAD_WIDTH), jnp.bfloat16)], axis=0
    )
    mix = dot(weights, values, ((1,), (0,))) * table[:, sources : sources + 1]
    for s, ref in enumerate(got_refs):
        mix += ref[:mix_rows].astype(jnp.float32) * table[:, s : s + 1]
    for h in range(heads):
        tile = mix[h * rows : (h + 1) * rows]
        for b in range(requests):
            out_ref[b, :, h * HEAD_WIDTH : (h + 1) * HEAD_WIDTH] = tile[
                b * tokens : (b + 1) * tokens
            ].astype(jnp.bfloat16)


def rotation(lengths, tokens):
    half = HEAD_WIDTH // 2
    places = (lengths[:, None] + jnp.arange(tokens, dtype=jnp.int32)[None, :]).astype(jnp.float32)
    inverse_freq = jnp.exp(
        jnp.arange(half, dtype=jnp.float32) * (-2.0 * math.log(ROPE_BASE) / HEAD_WIDTH)
    )
    angles = places.reshape(-1, 1) * inverse_freq[None, :]
    cosine, sine = jnp.cos(angles), jnp.sin(angles)
    return jnp.concatenate([cosine, cosine], axis=1), jnp.concatenate([-sine, sine], axis=1)


def vmem():
    return pl.BlockSpec(memory_space=pltpu.VMEM)


def smem():
    return pl.BlockSpec(memory_space=pltpu.SMEM)


def hbm():
    return pl.BlockSpec(memory_space=pltpu.HBM)


def pinned(x):
    return pltpu.with_memory_space_constraint(x, pltpu.HBM)


def cost(flops, moved):
    return pl.CostEstimate(flops=int(flops), bytes_accessed=int(moved), transcendentals=0)


def swap(x, devices, bit):
    return lax.ppermute(x, "tensor", [(d, d ^ bit) for d in range(devices)])


def per_device(
    hidden,
    queries,
    key_value_weight,
    adapter_down_weight,
    adapter_up_weight,
    cached_key_rows,
    cached_value_rows,
    request_adapter,
    adapter_rank_list,
    adapter_pool_row,
    lengths,
):
    requests, tokens, width = hidden.shape
    rows = requests * tokens
    devices = lax.axis_size("tensor")
    here = lax.axis_index("tensor")
    heads = QUERY_HEADS // devices
    chunks = width // HEAD_WIDTH
    lanes = devices // 2
    tiles = heads + chunks
    mix_rows = heads * rows

    lane_groups = [list(range(core, devices, 2)) for core in range(2)]

    def exchange(x):
        return lax.all_to_all(x, "tensor", 0, 0, axis_index_groups=lane_groups, tiled=True)

    tile_shape = (tiles, rows, HEAD_WIDTH)
    own = pl.pallas_call(
        functools.partial(pack_kernel, requests),
        out_shape=jax.ShapeDtypeStruct(tile_shape, jnp.bfloat16),
        in_specs=[hbm()] * 2,
        out_specs=vmem(),
        scratch_shapes=[
            pltpu.VMEM(queries.shape, jnp.bfloat16),
            pltpu.VMEM(hidden.shape, jnp.bfloat16),
            pltpu.SemaphoreType.DMA((2,)),
        ],
        compiler_params=pltpu.CompilerParams(vmem_limit_bytes=4 * MIB),
        name="pack",
    )(pinned(queries), pinned(hidden))
    flat = requests * cached_key_rows.shape[1]
    big = (
        cached_key_rows.reshape(flat, -1),
        cached_value_rows.reshape(flat, -1),
        adapter_up_weight[0],
    )
    out_width = key_value_weight.shape[1]
    parts = 4 if width % (4 * HEAD_WIDTH) == 0 else 1
    base, keys, values, up = pl.pallas_call(
        functools.partial(base_kernel, heads),
        out_shape=(pltpu.VMEM((rows, out_width), jnp.float32),)
        + tuple(pltpu.VMEM(x.shape, x.dtype) for x in big),
        in_specs=[vmem()] + [hbm()] * 4,
        out_specs=(vmem(),) * 4,
        scratch_shapes=[
            pltpu.VMEM((parts, width // parts, out_width), jnp.bfloat16),
            pltpu.SemaphoreType.DMA((parts + 3,)),
        ],
        compiler_params=pltpu.CompilerParams(vmem_limit_bytes=12 * MIB),
        cost_estimate=cost(10**9, 0),
        name="base",
    )(own, pinned(key_value_weight), *[pinned(x) for x in big])
    down = pinned(adapter_down_weight[0])
    sizes = (requests, tokens, devices)
    index = here.reshape(1).astype(jnp.int32)
    rank = adapter_down_weight.shape[2]
    mix_total = KEY_HEADS * 64

    masks, lane = [0], own[None]
    bit = lanes // 2
    while bit > 1:
        masks += [mask ^ bit for mask in masks]
        lane = jnp.concatenate([lane, swap(lane, devices, 2 * bit)], axis=0)
        bit //= 2
    late_masks = [mask ^ 1 for mask in masks]
    lane, base = lax.optimization_barrier((lane, base))
    late_lane = swap(lane, devices, 2)
    other = swap(lane, devices, 1)
    slot_count = HEAD_WIDTH // mix_rows
    chunks = chunks_of(masks, slot_count) + chunks_of(late_masks, slot_count)

    def streamed(count):
        return [pltpu.VMEM((count, width, rank), jnp.bfloat16), pltpu.SemaphoreType.DMA((count,))]

    def call(kernel, operands, in_specs, out_shape, scratch, name):
        return pl.pallas_call(
            kernel,
            out_shape=tuple(out_shape),
            in_specs=in_specs,
            out_specs=(vmem(),) * len(out_shape),
            scratch_shapes=scratch,
            compiler_params=pltpu.CompilerParams(vmem_limit_bytes=12 * MIB),
            cost_estimate=cost(10**9, 0),
            name=name,
        )(*operands)

    half_mix = pltpu.VMEM((mix_total // 2, HEAD_WIDTH), jnp.float32)
    half_send = pltpu.VMEM((mix_total // 2, HEAD_WIDTH), jnp.bfloat16)
    half_stat = pltpu.VMEM((8, HEAD_WIDTH), jnp.float32)
    lowered = pltpu.VMEM((rows, rank), jnp.float32)
    first_mix, first_stats = call(
        functools.partial(own_kernel, sizes, masks, False),
        (index, lengths, lane, keys, values),
        [smem()] * 2 + [vmem()] * 3,
        [half_mix, half_stat],
        [],
        "own_first",
    )
    early_send, early_stats, early_lowered = call(
        functools.partial(early_kernel, sizes, masks),
        (index, lengths, lane, other, keys, values, down),
        [smem()] * 2 + [vmem()] * 4 + [hbm()],
        [half_send, half_stat, lowered],
        streamed(2 * len(masks)),
        "other_first",
    )
    late_lane, early_send = lax.optimization_barrier((late_lane, early_send))
    late_other = swap(late_lane, devices, 1)
    second_mix, second_stats, own_lowered = call(
        functools.partial(own_kernel, sizes, late_masks, True),
        (index, lengths, late_lane, keys, values, down),
        [smem()] * 2 + [vmem()] * 3 + [hbm()],
        [half_mix, half_stat, lowered],
        streamed(len(masks)),
        "own_second",
    )
    send_rows = mix_total + 3 * KEY_HEADS * rows + STAT_ROWS
    send, proj = call(
        functools.partial(late_kernel, sizes, late_masks),
        (
            index,
            request_adapter,
            adapter_rank_list,
            adapter_pool_row,
            lengths,
            late_other,
            keys,
            values,
            down,
            base,
            up,
            early_send,
            early_stats,
            early_lowered,
            own_lowered,
        ),
        [smem()] * 5 + [vmem()] * 3 + [hbm()] + [vmem()] * 6,
        [
            pltpu.VMEM((send_rows, HEAD_WIDTH), jnp.bfloat16),
            pltpu.VMEM((2, KEY_HEADS, rows, HEAD_WIDTH), jnp.float32),
        ],
        streamed(len(masks)),
        "other_second",
    )
    got = swap(send, devices, 1)
    packets = pl.pallas_call(
        functools.partial(join_kernel, sizes, chunks),
        out_shape=jax.ShapeDtypeStruct((lanes, mix_rows + 4 * rows, HEAD_WIDTH), jnp.bfloat16),
        in_specs=[smem()] + [vmem()] * 6,
        out_specs=vmem(),
        scratch_shapes=[pltpu.VMEM((KEY_HEADS, 3 * rows, HEAD_WIDTH), jnp.float32)],
        compiler_params=pltpu.CompilerParams(vmem_limit_bytes=8 * MIB),
        name="join",
    )(index, first_mix, second_mix, first_stats, second_stats, proj, got)
    packets = exchange(packets)
    cosine, sine = rotation(lengths, tokens)
    return pl.pallas_call(
        functools.partial(merge_kernel, devices, requests, tokens),
        out_shape=jax.ShapeDtypeStruct((requests, tokens, heads * HEAD_WIDTH), jnp.bfloat16),
        in_specs=[vmem()] * 4,
        out_specs=vmem(),
        compiler_params=pltpu.CompilerParams(vmem_limit_bytes=8 * MIB),
        name="merge_states",
    )(own, cosine, sine, packets)


def solution(mesh):
    in_specs = (
        P("groups", None, "tensor"),
        P("groups", None, "tensor"),
        P("tensor", None),
        P("tensor", None, None),
        P("tensor", None, None),
        P("groups", "tensor", None),
        P("groups", "tensor", None),
        P("groups"),
        P(),
        P(),
        P("groups"),
    )
    out_specs = P("groups", None, "tensor")
    return jax.shard_map(
        per_device, mesh=mesh, in_specs=in_specs, out_specs=out_specs, check_vma=False
    )
```

```python
import functools
import math

import jax
import jax.numpy as jnp
from jax import lax
from jax.experimental import pallas as pl
from jax.experimental.pallas import tpu as pltpu
from jax.sharding import PartitionSpec as P

QUERY_HEADS = 128
KEY_HEADS = 8
HEAD_WIDTH = 128
ROPE_BASE = 500000.0
NEG_FILL = -1e30
SCALE = 1.0 / math.sqrt(HEAD_WIDTH)
GROUPED = KEY_HEADS // 2
CHUNKS = GROUPED // 2
MIX_ROWS = GROUPED * 64
STAT_ROWS = 16
MIB = 2**20


def dot(a, b, dims):
    return lax.dot_general(a, b, (dims, ((), ())), preferred_element_type=jnp.float32)


def round_bf16(x):
    return x.astype(jnp.bfloat16).astype(jnp.float32)


def lane_of(index_ref, devices):
    here = index_ref[0]
    chip = here // 2
    per_head = devices // 2 // KEY_HEADS
    return here, chip, per_head, (chip // per_head) % 2


def head_columns(head):
    return pl.ds(pl.multiple_of(head * HEAD_WIDTH, HEAD_WIDTH), HEAD_WIDTH)


def cache_copies(key_ref, value_ref, out_ref, parity, sems):
    copies = []
    for i, ref in enumerate((key_ref, value_ref)):
        for g in range(GROUPED):
            place = out_ref.at[i, :, g * HEAD_WIDTH : (g + 1) * HEAD_WIDTH]
            source = ref.at[:, head_columns(2 * g + parity)]
            copies.append(pltpu.make_async_copy(source, place, sems.at[i * GROUPED + g]))
    return copies


def pack_kernel(sizes, index_ref, query_ref, hidden_ref, key_ref, value_ref, *refs):
    own_query_ref, own_hidden_ref, cache_ref, query_buf, hidden_buf, sems = refs
    requests, tokens, devices = sizes
    _, _, _, parity = lane_of(index_ref, devices)
    loads = [
        pltpu.make_async_copy(query_ref, query_buf, sems.at[2 * GROUPED]),
        pltpu.make_async_copy(hidden_ref, hidden_buf, sems.at[2 * GROUPED + 1]),
    ]
    caches = cache_copies(key_ref, value_ref, cache_ref, 1 - parity, sems)
    for load in loads + caches:
        load.start()
    for load, ref, out_ref in zip(
        loads, (query_buf, hidden_buf), (own_query_ref, own_hidden_ref)
    ):
        load.wait()
        rows = jnp.concatenate([ref[b].astype(jnp.float32) for b in range(requests)], axis=0)
        for c in range(rows.shape[1] // HEAD_WIDTH):
            tile = rows[:, c * HEAD_WIDTH : (c + 1) * HEAD_WIDTH]
            out_ref[c] = tile.astype(jnp.bfloat16)
    for load in caches:
        load.wait()


def base_kernel(sizes, index_ref, own_ref, weight_ref, key_ref, value_ref, *refs):
    up_ref, base_ref, cache_ref, held_up_ref, buffer, sems = refs
    requests, tokens, devices = sizes
    _, _, _, parity = lane_of(index_ref, devices)
    parts, depth = buffer.shape[:2]
    loads = [
        pltpu.make_async_copy(
            weight_ref.at[pl.ds(p * depth, depth)], buffer.at[p], sems.at[2 * GROUPED + p]
        )
        for p in range(parts)
    ]
    others = cache_copies(key_ref, value_ref, cache_ref, parity, sems)
    others.append(pltpu.make_async_copy(up_ref, held_up_ref, sems.at[2 * GROUPED + parts]))
    for load in loads + others:
        load.start()
    tiles = depth // HEAD_WIDTH
    total = jnp.zeros(base_ref.shape, jnp.float32)
    for p in range(parts):
        hidden = jnp.concatenate([own_ref[p * tiles + c] for c in range(tiles)], axis=1)
        loads[p].wait()
        total += dot(hidden, buffer[p], ((1,), (0,)))
    base_ref[...] = total
    for load in others:
        load.wait()


def lower(sizes, masks, index_ref, lane_refs, down_ref, buffer, sems):
    requests, tokens, devices = sizes
    here, _, per_head, _ = lane_of(index_ref, devices)
    heads = QUERY_HEADS // devices
    depth = buffer.shape[1]
    chunks = depth // HEAD_WIDTH
    work = []
    for side, ref in enumerate(lane_refs):
        for i, mask in enumerate(masks):
            for hop in range(2):
                source = here ^ (2 * (mask ^ hop * per_head) + side)
                rows = pl.ds(pl.multiple_of(source * depth, depth), depth)
                at = len(work)
                copy = pltpu.make_async_copy(down_ref.at[rows], buffer.at[at], sems.at[at])
                copy.start()
                work.append((copy, ref, i, heads + hop * chunks))
    total = None
    for at, (copy, ref, i, first) in enumerate(work):
        hidden = jnp.concatenate([ref[i, first + c] for c in range(chunks)], axis=1)
        copy.wait()
        term = dot(hidden, buffer[at], ((1,), (0,)))
        total = term if total is None else total + term
    return total


def early_kernel(sizes, masks, index_ref, lane_ref, other_ref, down_ref, out_ref, buffer, sems):
    out_ref[...] = lower(sizes, masks, index_ref, (lane_ref, other_ref), down_ref, buffer, sems)


def project_kernel(sizes, masks, *refs):
    (index_ref, adapter_ref, rank_ref, pool_ref) = refs[:4]
    (lane_ref, other_ref, early_ref, base_ref, down_ref, up_ref) = refs[4:10]
    (own_ref, own_parts_ref, parts_ref, all_ref, buffer, sems) = refs[10:]
    requests, tokens, devices = sizes
    rows = requests * tokens
    here, _, _, parity = lane_of(index_ref, devices)
    lowered = early_ref[...]
    lowered += lower(sizes, masks, index_ref, (lane_ref, other_ref), down_ref, buffer, sems)
    row_request = lax.broadcasted_iota(jnp.int32, (rows, 1), 0) // tokens
    ranks = jnp.zeros((rows, 1), jnp.int32)
    owners = jnp.zeros((rows, 1), jnp.int32)
    for b in range(requests):
        adapter = adapter_ref[b]
        ranks = jnp.where(row_request == b, rank_ref[adapter], ranks)
        owners = jnp.where(row_request == b, pool_ref[adapter], owners)
    column = lax.broadcasted_iota(jnp.int32, lowered.shape, 1)
    lowered = jnp.where(column < ranks, lowered, 0.0).astype(jnp.bfloat16)
    lifted = dot(lowered, up_ref[...], ((1,), (0,)))
    all_ref[...] = base_ref[...] + jnp.where(owners == here, lifted, 0.0)
    step = GROUPED * rows
    for which, out_ref in ((parity, own_parts_ref), (1 - parity, parts_ref)):
        keys = [all_ref[:, head_columns(2 * g + which)] for g in range(GROUPED)]
        values = [all_ref[:, head_columns(KEY_HEADS + 2 * g + which)] for g in range(GROUPED)]
        keys = jnp.concatenate(keys, axis=0)
        values = jnp.concatenate(values, axis=0)
        if out_ref is own_parts_ref:
            own_ref[0] = keys
            own_ref[1] = values
        high = keys.astype(jnp.bfloat16)
        out_ref[:step] = high
        out_ref[step : 2 * step] = (keys - high.astype(jnp.float32)).astype(jnp.bfloat16)
        out_ref[2 * step :] = values.astype(jnp.bfloat16)


def chunks_of(masks, slots):
    order = sorted(masks)
    return [order[at : at + slots] for at in range(0, len(order), slots)]


def attend(sizes, masks, index_ref, length_ref, first_ref, second_ref, cache_ref, far_ref, put):
    requests, tokens, devices = sizes
    here, chip, per_head, _ = lane_of(index_ref, devices)
    heads = QUERY_HEADS // devices
    slot_rows = heads * requests * tokens
    positions = cache_ref.shape[1] // requests
    half = len(masks) // 2
    place = lax.broadcasted_iota(jnp.int32, (requests * positions, HEAD_WIDTH), 0)
    column = lax.broadcasted_iota(jnp.int32, (requests * positions, HEAD_WIDTH), 1)
    place_request = place // positions
    limit = jnp.zeros_like(place)
    for b in range(requests):
        limit = jnp.where(place_request == b, length_ref[b], limit)
    same = place_request == (column // tokens) % requests
    caches = (cache_ref, far_ref)
    allowed = [
        (device * positions + place % positions < limit) & same
        for device in (here, here ^ (2 * per_head))
    ]
    peaks, totals = [], []
    for number, chunk in enumerate(chunks_of(masks, HEAD_WIDTH // slot_rows)):
        query = jnp.concatenate(
            [
                (first_ref if masks.index(mask) < half else second_ref)[masks.index(mask) % half, h]
                for mask in chunk
                for h in range(heads)
            ],
            axis=0,
        )
        key_heads = sorted({mask // per_head for mask in chunk})
        spots = [head_columns(((chip // per_head) ^ head) // 2) for head in key_heads]
        share = HEAD_WIDTH // len(key_heads)
        scores = []
        for ref, valid in zip(caches, allowed):
            score = None
            for i, spot in enumerate(spots):
                part = dot(ref[0, :, spot], query, ((1,), (1,)))
                score = part if score is None else jnp.where(column < i * share, score, part)
            scores.append(jnp.where(valid, score * SCALE, NEG_FILL))
        peak = jnp.maximum(
            jnp.max(scores[0], axis=0, keepdims=True), jnp.max(scores[1], axis=0, keepdims=True)
        )
        peak = round_bf16(peak)
        total, weights = jnp.zeros_like(peak), []
        for score, valid in zip(scores, allowed):
            weight = jnp.where(valid, jnp.exp(score - peak), 0.0)
            total += jnp.sum(weight, axis=0, keepdims=True)
            weights.append(jnp.transpose(weight.astype(jnp.bfloat16)))
        peaks.append(peak)
        totals.append(total)
        for i, spot in enumerate(spots):
            own = slice(i * share, (i + 1) * share)
            mix = dot(weights[0][own], cache_ref[1, :, spot], ((1,), (0,)))
            mix += dot(weights[1][own], far_ref[1, :, spot], ((1,), (0,)))
            put(number, i * share, mix)
    return peaks, totals


def rows_of(items, count):
    row = lax.broadcasted_iota(jnp.int32, (count, HEAD_WIDTH), 0)
    out = jnp.zeros((count, HEAD_WIDTH), jnp.float32)
    for i, item in enumerate(items):
        out = jnp.where(row == i, item, out)
    return out


def other_kernel(sizes, masks, *refs):
    (index_ref, length_ref, first_ref, second_ref, cache_ref, far_ref, parts_ref, send_ref) = refs
    proj_rows = parts_ref.shape[0]

    def put(chunk, row, mix):
        at = chunk * 128 + row
        send_ref[at : at + mix.shape[0]] = mix.astype(jnp.bfloat16)

    peaks, totals = attend(
        sizes, masks, index_ref, length_ref, first_ref, second_ref, cache_ref, far_ref, put
    )
    highs = [round_bf16(total) for total in totals]
    lows = [total - high for total, high in zip(totals, highs)]
    send_ref[MIX_ROWS : MIX_ROWS + proj_rows] = parts_ref[...]
    send_ref[MIX_ROWS + proj_rows :] = rows_of(peaks + highs + lows, STAT_ROWS).astype(jnp.bfloat16)


def own_kernel(sizes, masks, *refs):
    (index_ref, length_ref, first_ref, second_ref, cache_ref, far_ref, mix_ref, stat_ref) = refs

    def put(chunk, row, mix):
        at = chunk * 128 + row
        mix_ref[at : at + mix.shape[0]] = mix

    peaks, totals = attend(
        sizes, masks, index_ref, length_ref, first_ref, second_ref, cache_ref, far_ref, put
    )
    stat_ref[...] = rows_of(peaks + totals, 8)


def join_kernel(sizes, masks, index_ref, mix_ref, stat_ref, proj_ref, far_ref, got_ref, got_far_ref, *refs):
    packet_refs, tail_ref = refs[:-1], refs[-1]
    requests, tokens, devices = sizes
    _, chip, per_head, _ = lane_of(index_ref, devices)
    rows = requests * tokens
    heads = QUERY_HEADS // devices
    slot_rows = heads * rows
    step = GROUPED * rows
    got = got_ref[MIX_ROWS + 3 * step :].astype(jnp.float32)
    own = stat_ref[...]
    own_peak, got_peak = own[:CHUNKS], got[:CHUNKS]
    peak = jnp.maximum(own_peak, got_peak)
    own_factor = jnp.exp(own_peak - peak)
    got_factor = jnp.exp(got_peak - peak)
    total = own_factor * own[CHUNKS : 2 * CHUNKS] + got_factor * (
        got[CHUNKS : 2 * CHUNKS] + got[2 * CHUNKS : 3 * CHUNKS]
    )
    high = round_bf16(total)
    low = total - high
    filler = jnp.zeros((128 - 2 * CHUNKS, 128), jnp.float32)
    table = jnp.transpose(jnp.concatenate([own_factor, got_factor, filler], axis=0))
    keys, values = proj_ref[0], proj_ref[1]
    for ref, at in ((far_ref, 0), (got_ref, MIX_ROWS), (got_far_ref, 0)):
        keys += ref[at : at + step].astype(jnp.float32)
        keys += ref[at + step : at + 2 * step].astype(jnp.float32)
        values += ref[at + 2 * step : at + 3 * step].astype(jnp.float32)
    keys_high = round_bf16(keys)
    for g in range(GROUPED):
        part = slice(g * rows, (g + 1) * rows)
        tail_ref[g, :rows] = keys_high[part]
        tail_ref[g, rows : 2 * rows] = (keys - keys_high)[part]
        tail_ref[g, 2 * rows :] = values[part]
    stat_row = lax.broadcasted_iota(jnp.int32, (rows, HEAD_WIDTH), 0)
    for c, chunk in enumerate(chunks_of(masks, HEAD_WIDTH // slot_rows)):
        span = slice(c * 128, c * 128 + 128)
        mix = mix_ref[span] * table[:, c : c + 1]
        mix += got_ref[span].astype(jnp.float32) * table[:, CHUNKS + c : CHUNKS + c + 1]
        stats = jnp.where(
            stat_row == 0,
            peak[c : c + 1],
            jnp.where(
                stat_row == 1, high[c : c + 1], jnp.where(stat_row == 2, low[c : c + 1], 0.0)
            ),
        )
        for t, mask in enumerate(chunk):
            packet_ref = packet_refs[masks.index(mask)]
            shifted = stats if t == 0 else pltpu.roll(stats, HEAD_WIDTH - t * slot_rows, 1)
            group = ((chip // per_head) ^ (mask // per_head)) // 2
            tail = jnp.concatenate([tail_ref[group], shifted], axis=0)
            packet_ref[:slot_rows] = mix[t * slot_rows : (t + 1) * slot_rows].astype(jnp.bfloat16)
            packet_ref[slot_rows:] = tail.astype(jnp.bfloat16)


def merge_kernel(devices, requests, tokens, own_ref, cos_ref, sin_ref, *refs):
    got_refs, out_ref = refs[:-1], refs[-1]
    rows = requests * tokens
    heads = QUERY_HEADS // devices
    mix_rows = heads * rows
    sources = len(got_refs)
    tails = [ref[mix_rows:].astype(jnp.float32) for ref in got_refs]
    sums = functools.reduce(jnp.add, [tail[: 3 * rows] for tail in tails])
    keys = sums[:rows] + sums[rows : 2 * rows]
    values = sums[2 * rows :].astype(jnp.bfloat16)
    turned = pltpu.roll(keys, HEAD_WIDTH // 2, 1)
    keys = (keys * cos_ref[...] + turned * sin_ref[...]).astype(jnp.bfloat16)
    query = jnp.concatenate([own_ref[h] for h in range(heads)], axis=0)
    if mix_rows < 128:
        query = jnp.concatenate(
            [query, jnp.zeros((128 - mix_rows, HEAD_WIDTH), jnp.bfloat16)], axis=0
        )
    fresh = dot(keys, query, ((1,), (1,))) * SCALE
    source = lax.broadcasted_iota(jnp.int32, fresh.shape, 0)
    column = lax.broadcasted_iota(jnp.int32, fresh.shape, 1) % rows
    allowed = (source // tokens == column // tokens) & (source % tokens <= column % tokens)
    fresh_peak = jnp.max(jnp.where(allowed, fresh, NEG_FILL), axis=0, keepdims=True)
    stats = [tail[3 * rows :] for tail in tails]
    peak = functools.reduce(jnp.maximum, [stat[0:1] for stat in stats], fresh_peak)
    weights = jnp.where(allowed, jnp.exp(fresh - peak), 0.0)
    factors = [jnp.exp(stat[0:1] - peak) for stat in stats]
    total = functools.reduce(
        jnp.add,
        [factor * (stat[1:2] + stat[2:3]) for factor, stat in zip(factors, stats)],
        jnp.sum(weights, axis=0, keepdims=True),
    )
    inverse = 1.0 / total
    filler = jnp.zeros((128 - sources - 1, 128), jnp.float32)
    table = jnp.concatenate([factor * inverse for factor in factors] + [inverse, filler], axis=0)
    table = jnp.transpose(table)[:mix_rows]
    weights = jnp.transpose(
        jnp.concatenate([weights, jnp.zeros((128 - rows, 128), jnp.float32)], axis=0)
    )[:mix_rows].astype(jnp.bfloat16)
    values = jnp.concatenate(
        [values, jnp.zeros((128 - rows, HEAD_WIDTH), jnp.bfloat16)], axis=0
    )
    mix = dot(weights, values, ((1,), (0,))) * table[:, sources : sources + 1]
    for s, ref in enumerate(got_refs):
        mix += ref[:mix_rows].astype(jnp.float32) * table[:, s : s + 1]
    for h in range(heads):
        tile = mix[h * rows : (h + 1) * rows]
        for b in range(requests):
            out_ref[b, :, h * HEAD_WIDTH : (h + 1) * HEAD_WIDTH] = tile[
                b * tokens : (b + 1) * tokens
            ].astype(jnp.bfloat16)


def rotation(lengths, tokens):
    half = HEAD_WIDTH // 2
    places = (lengths[:, None] + jnp.arange(tokens, dtype=jnp.int32)[None, :]).astype(jnp.float32)
    inverse_freq = jnp.exp(
        jnp.arange(half, dtype=jnp.float32) * (-2.0 * math.log(ROPE_BASE) / HEAD_WIDTH)
    )
    angles = places.reshape(-1, 1) * inverse_freq[None, :]
    cosine, sine = jnp.cos(angles), jnp.sin(angles)
    return jnp.concatenate([cosine, cosine], axis=1), jnp.concatenate([-sine, sine], axis=1)


def vmem():
    return pl.BlockSpec(memory_space=pltpu.VMEM)


def smem():
    return pl.BlockSpec(memory_space=pltpu.SMEM)


def hbm():
    return pl.BlockSpec(memory_space=pltpu.HBM)


def pinned(x):
    return pltpu.with_memory_space_constraint(x, pltpu.HBM)


def cost(flops, moved):
    return pl.CostEstimate(flops=int(flops), bytes_accessed=int(moved), transcendentals=0)


def swap(x, devices, bit):
    return lax.ppermute(x, "tensor", [(d, d ^ bit) for d in range(devices)])


def per_device(
    hidden,
    queries,
    key_value_weight,
    adapter_down_weight,
    adapter_up_weight,
    cached_key_rows,
    cached_value_rows,
    request_adapter,
    adapter_rank_list,
    adapter_pool_row,
    lengths,
):
    requests, tokens, width = hidden.shape
    rows = requests * tokens
    devices = lax.axis_size("tensor")
    sizes = (requests, tokens, devices)
    heads = QUERY_HEADS // devices
    chunks = width // HEAD_WIDTH
    lanes = devices // 2
    partner = lanes // KEY_HEADS
    slot_rows = heads * rows
    index = lax.axis_index("tensor").reshape(1).astype(jnp.int32)
    flat = requests * cached_key_rows.shape[1]
    cached_keys = pinned(cached_key_rows.reshape(flat, -1))
    cached_values = pinned(cached_value_rows.reshape(flat, -1))
    cache = pltpu.VMEM((2, flat, GROUPED * HEAD_WIDTH), jnp.bfloat16)
    cache_sems = 2 * GROUPED

    def call(kernel, operands, in_specs, out_shape, scratch, name):
        return pl.pallas_call(
            kernel,
            out_shape=tuple(out_shape),
            in_specs=in_specs,
            out_specs=(vmem(),) * len(out_shape),
            scratch_shapes=scratch,
            compiler_params=pltpu.CompilerParams(vmem_limit_bytes=12 * MIB),
            cost_estimate=cost(10**9 if name == "base" else 10**6, 0),
            name=name,
        )(*operands)

    own_queries, own_hidden, far_send = call(
        functools.partial(pack_kernel, sizes),
        (index, pinned(queries), pinned(hidden), cached_keys, cached_values),
        [smem()] + [hbm()] * 4,
        [
            pltpu.VMEM((heads, rows, HEAD_WIDTH), jnp.bfloat16),
            pltpu.VMEM((chunks, rows, HEAD_WIDTH), jnp.bfloat16),
            cache,
        ],
        [
            pltpu.VMEM(queries.shape, jnp.bfloat16),
            pltpu.VMEM(hidden.shape, jnp.bfloat16),
            pltpu.SemaphoreType.DMA((cache_sems + 2,)),
        ],
        "pack",
    )
    far_hidden = swap(own_hidden, devices, 2 * partner)
    far_cache = swap(far_send, devices, 2 * partner)

    out_width = key_value_weight.shape[1]
    parts = 4 if width % (4 * HEAD_WIDTH) == 0 else 1
    up = adapter_up_weight[0]
    base, own_cache, up = call(
        functools.partial(base_kernel, sizes),
        (index, own_hidden, pinned(key_value_weight), cached_keys, cached_values, pinned(up)),
        [smem(), vmem()] + [hbm()] * 4,
        [
            pltpu.VMEM((rows, out_width), jnp.float32),
            cache,
            pltpu.VMEM(up.shape, up.dtype),
        ],
        [
            pltpu.VMEM((parts, width // parts, out_width), jnp.bfloat16),
            pltpu.SemaphoreType.DMA((cache_sems + parts + 1,)),
        ],
        "base",
    )
    far_hidden, base = lax.optimization_barrier((far_hidden, base))

    masks, lane = [0], jnp.concatenate([own_queries, own_hidden, far_hidden], axis=0)[None]
    bits = [1 << i for i in reversed(range(lanes.bit_length() - 1)) if 1 << i != partner]
    for bit in bits[:-1]:
        masks += [mask ^ bit for mask in masks]
        lane = jnp.concatenate([lane, swap(lane, devices, 2 * bit)], axis=0)
    other = swap(lane, devices, 1)
    late_lane = swap(lane, devices, 2 * bits[-1])
    late_masks = [mask ^ bits[-1] for mask in masks]

    down = pinned(adapter_down_weight[0])
    rank = down.shape[1]
    sources = 4 * len(masks)
    streamed = [
        pltpu.VMEM((sources, width, rank), jnp.bfloat16),
        pltpu.SemaphoreType.DMA((sources,)),
    ]
    (early,) = call(
        functools.partial(early_kernel, sizes, masks),
        (index, lane, other, down),
        [smem()] + [vmem()] * 2 + [hbm()],
        [pltpu.VMEM((rows, rank), jnp.float32)],
        streamed,
        "lora_first",
    )
    late_lane, early = lax.optimization_barrier((late_lane, early))
    late_other = swap(late_lane, devices, 1)
    late_other, far_cache = lax.optimization_barrier((late_other, far_cache))
    step = GROUPED * rows
    proj, own_parts, parts = call(
        functools.partial(project_kernel, sizes, late_masks),
        (
            index,
            request_adapter,
            adapter_rank_list,
            adapter_pool_row,
            late_lane,
            late_other,
            early,
            base,
            down,
            up,
        ),
        [smem()] * 4 + [vmem()] * 4 + [hbm(), vmem()],
        [
            pltpu.VMEM((2, step, HEAD_WIDTH), jnp.float32),
            pltpu.VMEM((3 * step, HEAD_WIDTH), jnp.bfloat16),
            pltpu.VMEM((3 * step, HEAD_WIDTH), jnp.bfloat16),
        ],
        [pltpu.VMEM((rows, out_width), jnp.float32)] + streamed,
        "project",
    )
    far_parts = swap(parts, devices, 2 * partner)
    all_masks = masks + late_masks
    (send,) = call(
        functools.partial(other_kernel, sizes, all_masks),
        (index, lengths, other, late_other, own_cache, far_cache, own_parts),
        [smem()] * 2 + [vmem()] * 5,
        [pltpu.VMEM((MIX_ROWS + 3 * step + STAT_ROWS, HEAD_WIDTH), jnp.bfloat16)],
        [],
        "other_lane",
    )
    got = swap(send, devices, 1)
    got_far_parts = swap(far_parts, devices, 1)
    mix, stats = call(
        functools.partial(own_kernel, sizes, all_masks),
        (index, lengths, lane, late_lane, own_cache, far_cache),
        [smem()] * 2 + [vmem()] * 4,
        [
            pltpu.VMEM((MIX_ROWS, HEAD_WIDTH), jnp.float32),
            pltpu.VMEM((8, HEAD_WIDTH), jnp.float32),
        ],
        [],
        "own_lane",
    )
    packet = pltpu.VMEM((slot_rows + 4 * rows, HEAD_WIDTH), jnp.bfloat16)
    packets = call(
        functools.partial(join_kernel, sizes, all_masks),
        (index, mix, stats, proj, far_parts, got, got_far_parts),
        [smem()] + [vmem()] * 6,
        [packet] * len(all_masks),
        [pltpu.VMEM((GROUPED, 3 * rows, HEAD_WIDTH), jnp.float32)],
        "join",
    )
    packets = [
        x if mask == 0 else swap(x, devices, 2 * mask) for x, mask in zip(packets, all_masks)
    ]
    cosine, sine = rotation(lengths, tokens)
    return pl.pallas_call(
        functools.partial(merge_kernel, devices, requests, tokens),
        out_shape=jax.ShapeDtypeStruct((requests, tokens, heads * HEAD_WIDTH), jnp.bfloat16),
        in_specs=[vmem()] * (3 + len(packets)),
        out_specs=vmem(),
        compiler_params=pltpu.CompilerParams(vmem_limit_bytes=8 * MIB),
        name="merge_states",
    )(own_queries, cosine, sine, *packets)


def solution(mesh):
    in_specs = (
        P("groups", None, "tensor"),
        P("groups", None, "tensor"),
        P("tensor", None),
        P("tensor", None, None),
        P("tensor", None, None),
        P("groups", "tensor", None),
        P("groups", "tensor", None),
        P("groups"),
        P(),
        P(),
        P("groups"),
    )
    out_specs = P("groups", None, "tensor")
    return jax.shard_map(
        per_device, mesh=mesh, in_specs=in_specs, out_specs=out_specs, check_vma=False
    )
```

```python
import functools
import math

import jax
import jax.numpy as jnp
from jax import lax
from jax.experimental import pallas as pl
from jax.experimental.pallas import tpu as pltpu
from jax.sharding import PartitionSpec as P

QUERY_HEADS = 128
KEY_HEADS = 8
HEAD_WIDTH = 128
ROPE_BASE = 500000.0
NEG_FILL = -1e30
SCALE = 1.0 / math.sqrt(HEAD_WIDTH)
GROUPED = KEY_HEADS // 2
CHUNKS = GROUPED // 2
MIX_ROWS = GROUPED * 64
STAT_ROWS = 16
MIB = 2**20


def dot(a, b, dims):
    return lax.dot_general(a, b, (dims, ((), ())), preferred_element_type=jnp.float32)


def round_bf16(x):
    return x.astype(jnp.bfloat16).astype(jnp.float32)


def lane_of(index_ref, devices):
    here = index_ref[0]
    chip = here // 2
    per_head = devices // 2 // KEY_HEADS
    return here, chip, per_head, (chip // per_head) % 2


def head_columns(head):
    return pl.ds(pl.multiple_of(head * HEAD_WIDTH, HEAD_WIDTH), HEAD_WIDTH)


def cache_copies(key_ref, value_ref, out_ref, parity, sems):
    copies = []
    for i, ref in enumerate((key_ref, value_ref)):
        for g in range(GROUPED):
            place = out_ref.at[i, :, g * HEAD_WIDTH : (g + 1) * HEAD_WIDTH]
            source = ref.at[:, head_columns(2 * g + parity)]
            copies.append(pltpu.make_async_copy(source, place, sems.at[i * GROUPED + g]))
    return copies


def pack_kernel(sizes, index_ref, query_ref, hidden_ref, key_ref, value_ref, *refs):
    own_query_ref, own_hidden_ref, cache_ref, query_buf, hidden_buf, sems = refs
    requests, tokens, devices = sizes
    _, _, _, parity = lane_of(index_ref, devices)
    loads = [
        pltpu.make_async_copy(query_ref, query_buf, sems.at[2 * GROUPED]),
        pltpu.make_async_copy(hidden_ref, hidden_buf, sems.at[2 * GROUPED + 1]),
    ]
    caches = cache_copies(key_ref, value_ref, cache_ref, 1 - parity, sems)
    for load in loads + caches:
        load.start()
    for load, ref, out_ref in zip(
        loads, (query_buf, hidden_buf), (own_query_ref, own_hidden_ref)
    ):
        load.wait()
        rows = jnp.concatenate([ref[b].astype(jnp.float32) for b in range(requests)], axis=0)
        for c in range(rows.shape[1] // HEAD_WIDTH):
            tile = rows[:, c * HEAD_WIDTH : (c + 1) * HEAD_WIDTH]
            out_ref[c] = tile.astype(jnp.bfloat16)
    for load in caches:
        load.wait()


def base_kernel(sizes, index_ref, own_ref, weight_ref, key_ref, value_ref, *refs):
    up_ref, base_ref, cache_ref, held_up_ref, buffer, sems = refs
    requests, tokens, devices = sizes
    _, _, _, parity = lane_of(index_ref, devices)
    parts, depth = buffer.shape[:2]
    loads = [
        pltpu.make_async_copy(
            weight_ref.at[pl.ds(p * depth, depth)], buffer.at[p], sems.at[2 * GROUPED + p]
        )
        for p in range(parts)
    ]
    others = cache_copies(key_ref, value_ref, cache_ref, parity, sems)
    others.append(pltpu.make_async_copy(up_ref, held_up_ref, sems.at[2 * GROUPED + parts]))
    for load in loads + others:
        load.start()
    tiles = depth // HEAD_WIDTH
    total = jnp.zeros(base_ref.shape, jnp.float32)
    for p in range(parts):
        hidden = jnp.concatenate([own_ref[p * tiles + c] for c in range(tiles)], axis=1)
        loads[p].wait()
        total += dot(hidden, buffer[p], ((1,), (0,)))
    base_ref[...] = total
    for load in others:
        load.wait()


def places_of(sizes, masks, chunks):
    requests, tokens, devices = sizes
    heads = QUERY_HEADS // devices
    per_head = devices // 2 // KEY_HEADS
    return [
        (side, i, heads + hop * chunks, 2 * (mask ^ hop * per_head) + side)
        for side in range(2)
        for i, mask in enumerate(masks)
        for hop in range(2)
    ]


def streams(sizes, masks, index_ref, down_ref, buffer, sems):
    depth = buffer.shape[1]
    copies = []
    for at, (_, _, _, mask) in enumerate(places_of(sizes, masks, depth // HEAD_WIDTH)):
        rows = pl.ds(pl.multiple_of((index_ref[0] ^ mask) * depth, depth), depth)
        copies.append(pltpu.make_async_copy(down_ref.at[rows], buffer.at[at], sems.at[at]))
    return copies


def lower(sizes, masks, lane_refs, buffer, copies):
    total = None
    chunks = buffer.shape[1] // HEAD_WIDTH
    for at, (side, i, first, _) in enumerate(places_of(sizes, masks, chunks)):
        tiles = range(first, first + chunks)
        hidden = jnp.concatenate([lane_refs[side][i, c] for c in tiles], axis=1)
        if copies:
            copies[at].wait()
        term = dot(hidden, buffer[at], ((1,), (0,)))
        total = term if total is None else total + term
    return total


def early_kernel(sizes, masks, late_masks, *refs):
    (index_ref, lane_ref, other_ref, down_ref, out_ref, held_ref, buffer, sems, late_sems) = refs
    copies = streams(sizes, masks, index_ref, down_ref, buffer, sems)
    late = streams(sizes, late_masks, index_ref, down_ref, held_ref, late_sems)
    for copy in copies + late:
        copy.start()
    out_ref[...] = lower(sizes, masks, (lane_ref, other_ref), buffer, copies)
    for copy in late:
        copy.wait()


def project_kernel(sizes, masks, *refs):
    (index_ref, adapter_ref, rank_ref, pool_ref) = refs[:4]
    (lane_ref, other_ref, early_ref, base_ref, down_ref, up_ref) = refs[4:10]
    (own_ref, own_parts_ref, parts_ref, all_ref) = refs[10:]
    requests, tokens, devices = sizes
    rows = requests * tokens
    here, _, _, parity = lane_of(index_ref, devices)
    lowered = early_ref[...] + lower(sizes, masks, (lane_ref, other_ref), down_ref, [])
    row_request = lax.broadcasted_iota(jnp.int32, (rows, 1), 0) // tokens
    ranks = jnp.zeros((rows, 1), jnp.int32)
    owners = jnp.zeros((rows, 1), jnp.int32)
    for b in range(requests):
        adapter = adapter_ref[b]
        ranks = jnp.where(row_request == b, rank_ref[adapter], ranks)
        owners = jnp.where(row_request == b, pool_ref[adapter], owners)
    column = lax.broadcasted_iota(jnp.int32, lowered.shape, 1)
    lowered = jnp.where(column < ranks, lowered, 0.0).astype(jnp.bfloat16)
    lifted = dot(lowered, up_ref[...], ((1,), (0,)))
    all_ref[...] = base_ref[...] + jnp.where(owners == here, lifted, 0.0)
    step = GROUPED * rows
    for which, out_ref in ((parity, own_parts_ref), (1 - parity, parts_ref)):
        keys = [all_ref[:, head_columns(2 * g + which)] for g in range(GROUPED)]
        values = [all_ref[:, head_columns(KEY_HEADS + 2 * g + which)] for g in range(GROUPED)]
        keys = jnp.concatenate(keys, axis=0)
        values = jnp.concatenate(values, axis=0)
        if out_ref is own_parts_ref:
            own_ref[0] = keys
            own_ref[1] = values
        high = keys.astype(jnp.bfloat16)
        out_ref[:step] = high
        out_ref[step : 2 * step] = (keys - high.astype(jnp.float32)).astype(jnp.bfloat16)
        out_ref[2 * step :] = values.astype(jnp.bfloat16)


def chunks_of(masks, slots):
    order = sorted(masks)
    return [order[at : at + slots] for at in range(0, len(order), slots)]


def attend(sizes, masks, index_ref, length_ref, first_ref, second_ref, cache_ref, far_ref, put):
    requests, tokens, devices = sizes
    here, chip, per_head, _ = lane_of(index_ref, devices)
    heads = QUERY_HEADS // devices
    slot_rows = heads * requests * tokens
    positions = cache_ref.shape[1] // requests
    half = len(masks) // 2
    place = lax.broadcasted_iota(jnp.int32, (requests * positions, HEAD_WIDTH), 0)
    column = lax.broadcasted_iota(jnp.int32, (requests * positions, HEAD_WIDTH), 1)
    place_request = place // positions
    limit = jnp.zeros_like(place)
    for b in range(requests):
        limit = jnp.where(place_request == b, length_ref[b], limit)
    same = place_request == (column // tokens) % requests
    caches = (cache_ref, far_ref)
    allowed = [
        (device * positions + place % positions < limit) & same
        for device in (here, here ^ (2 * per_head))
    ]
    peaks, totals = [], []
    for number, chunk in enumerate(chunks_of(masks, HEAD_WIDTH // slot_rows)):
        query = jnp.concatenate(
            [
                (first_ref if masks.index(mask) < half else second_ref)[masks.index(mask) % half, h]
                for mask in chunk
                for h in range(heads)
            ],
            axis=0,
        )
        key_heads = sorted({mask // per_head for mask in chunk})
        spots = [head_columns(((chip // per_head) ^ head) // 2) for head in key_heads]
        share = HEAD_WIDTH // len(key_heads)
        scores = []
        for ref, valid in zip(caches, allowed):
            score = None
            for i, spot in enumerate(spots):
                part = dot(ref[0, :, spot], query, ((1,), (1,)))
                score = part if score is None else jnp.where(column < i * share, score, part)
            scores.append(jnp.where(valid, score * SCALE, NEG_FILL))
        peak = jnp.maximum(
            jnp.max(scores[0], axis=0, keepdims=True), jnp.max(scores[1], axis=0, keepdims=True)
        )
        peak = round_bf16(peak)
        total, weights = jnp.zeros_like(peak), []
        for score, valid in zip(scores, allowed):
            weight = jnp.where(valid, jnp.exp(score - peak), 0.0)
            total += jnp.sum(weight, axis=0, keepdims=True)
            weights.append(jnp.transpose(weight.astype(jnp.bfloat16)))
        peaks.append(peak)
        totals.append(total)
        for i, spot in enumerate(spots):
            own = slice(i * share, (i + 1) * share)
            mix = dot(weights[0][own], cache_ref[1, :, spot], ((1,), (0,)))
            mix += dot(weights[1][own], far_ref[1, :, spot], ((1,), (0,)))
            put(number, i * share, mix)
    return peaks, totals


def rows_of(items, count):
    row = lax.broadcasted_iota(jnp.int32, (count, HEAD_WIDTH), 0)
    out = jnp.zeros((count, HEAD_WIDTH), jnp.float32)
    for i, item in enumerate(items):
        out = jnp.where(row == i, item, out)
    return out


def other_kernel(sizes, masks, *refs):
    (index_ref, length_ref, first_ref, second_ref, cache_ref, far_ref, parts_ref, send_ref) = refs
    proj_rows = parts_ref.shape[0]

    def put(chunk, row, mix):
        at = chunk * 128 + row
        send_ref[at : at + mix.shape[0]] = mix.astype(jnp.bfloat16)

    peaks, totals = attend(
        sizes, masks, index_ref, length_ref, first_ref, second_ref, cache_ref, far_ref, put
    )
    highs = [round_bf16(total) for total in totals]
    lows = [total - high for total, high in zip(totals, highs)]
    send_ref[MIX_ROWS : MIX_ROWS + proj_rows] = parts_ref[...]
    send_ref[MIX_ROWS + proj_rows :] = rows_of(peaks + highs + lows, STAT_ROWS).astype(jnp.bfloat16)


def own_kernel(sizes, masks, *refs):
    (index_ref, length_ref, first_ref, second_ref, cache_ref, far_ref, mix_ref, stat_ref) = refs

    def put(chunk, row, mix):
        at = chunk * 128 + row
        mix_ref[at : at + mix.shape[0]] = mix

    peaks, totals = attend(
        sizes, masks, index_ref, length_ref, first_ref, second_ref, cache_ref, far_ref, put
    )
    stat_ref[...] = rows_of(peaks + totals, 8)


def join_kernel(sizes, masks, index_ref, mix_ref, stat_ref, proj_ref, far_ref, got_ref, got_far_ref, *refs):
    packet_refs, tail_ref = refs[:-1], refs[-1]
    requests, tokens, devices = sizes
    _, chip, per_head, _ = lane_of(index_ref, devices)
    rows = requests * tokens
    heads = QUERY_HEADS // devices
    slot_rows = heads * rows
    step = GROUPED * rows
    got = got_ref[MIX_ROWS + 3 * step :].astype(jnp.float32)
    own = stat_ref[...]
    own_peak, got_peak = own[:CHUNKS], got[:CHUNKS]
    peak = jnp.maximum(own_peak, got_peak)
    own_factor = jnp.exp(own_peak - peak)
    got_factor = jnp.exp(got_peak - peak)
    total = own_factor * own[CHUNKS : 2 * CHUNKS] + got_factor * (
        got[CHUNKS : 2 * CHUNKS] + got[2 * CHUNKS : 3 * CHUNKS]
    )
    high = round_bf16(total)
    low = total - high
    filler = jnp.zeros((128 - 2 * CHUNKS, 128), jnp.float32)
    table = jnp.transpose(jnp.concatenate([own_factor, got_factor, filler], axis=0))
    keys, values = proj_ref[0], proj_ref[1]
    for ref, at in ((far_ref, 0), (got_ref, MIX_ROWS), (got_far_ref, 0)):
        keys += ref[at : at + step].astype(jnp.float32)
        keys += ref[at + step : at + 2 * step].astype(jnp.float32)
        values += ref[at + 2 * step : at + 3 * step].astype(jnp.float32)
    keys_high = round_bf16(keys)
    for g in range(GROUPED):
        part = slice(g * rows, (g + 1) * rows)
        tail_ref[g, :rows] = keys_high[part]
        tail_ref[g, rows : 2 * rows] = (keys - keys_high)[part]
        tail_ref[g, 2 * rows :] = values[part]
    stat_row = lax.broadcasted_iota(jnp.int32, (rows, HEAD_WIDTH), 0)
    for c, chunk in enumerate(chunks_of(masks, HEAD_WIDTH // slot_rows)):
        span = slice(c * 128, c * 128 + 128)
        mix = mix_ref[span] * table[:, c : c + 1]
        mix += got_ref[span].astype(jnp.float32) * table[:, CHUNKS + c : CHUNKS + c + 1]
        stats = jnp.where(
            stat_row == 0,
            peak[c : c + 1],
            jnp.where(
                stat_row == 1, high[c : c + 1], jnp.where(stat_row == 2, low[c : c + 1], 0.0)
            ),
        )
        for t, mask in enumerate(chunk):
            packet_ref = packet_refs[masks.index(mask)]
            shifted = stats if t == 0 else pltpu.roll(stats, HEAD_WIDTH - t * slot_rows, 1)
            group = ((chip // per_head) ^ (mask // per_head)) // 2
            tail = jnp.concatenate([tail_ref[group], shifted], axis=0)
            packet_ref[:slot_rows] = mix[t * slot_rows : (t + 1) * slot_rows].astype(jnp.bfloat16)
            packet_ref[slot_rows:] = tail.astype(jnp.bfloat16)


def merge_kernel(devices, requests, tokens, own_ref, cos_ref, sin_ref, *refs):
    got_refs, out_ref = refs[:-1], refs[-1]
    rows = requests * tokens
    heads = QUERY_HEADS // devices
    mix_rows = heads * rows
    sources = len(got_refs)
    tails = [ref[mix_rows:].astype(jnp.float32) for ref in got_refs]
    sums = functools.reduce(jnp.add, [tail[: 3 * rows] for tail in tails])
    keys = sums[:rows] + sums[rows : 2 * rows]
    values = sums[2 * rows :].astype(jnp.bfloat16)
    turned = pltpu.roll(keys, HEAD_WIDTH // 2, 1)
    keys = (keys * cos_ref[...] + turned * sin_ref[...]).astype(jnp.bfloat16)
    query = jnp.concatenate([own_ref[h] for h in range(heads)], axis=0)
    if mix_rows < 128:
        query = jnp.concatenate(
            [query, jnp.zeros((128 - mix_rows, HEAD_WIDTH), jnp.bfloat16)], axis=0
        )
    fresh = dot(keys, query, ((1,), (1,))) * SCALE
    source = lax.broadcasted_iota(jnp.int32, fresh.shape, 0)
    column = lax.broadcasted_iota(jnp.int32, fresh.shape, 1) % rows
    allowed = (source // tokens == column // tokens) & (source % tokens <= column % tokens)
    fresh_peak = jnp.max(jnp.where(allowed, fresh, NEG_FILL), axis=0, keepdims=True)
    stats = [tail[3 * rows :] for tail in tails]
    peak = functools.reduce(jnp.maximum, [stat[0:1] for stat in stats], fresh_peak)
    weights = jnp.where(allowed, jnp.exp(fresh - peak), 0.0)
    factors = [jnp.exp(stat[0:1] - peak) for stat in stats]
    total = functools.reduce(
        jnp.add,
        [factor * (stat[1:2] + stat[2:3]) for factor, stat in zip(factors, stats)],
        jnp.sum(weights, axis=0, keepdims=True),
    )
    inverse = 1.0 / total
    filler = jnp.zeros((128 - sources - 1, 128), jnp.float32)
    table = jnp.concatenate([factor * inverse for factor in factors] + [inverse, filler], axis=0)
    table = jnp.transpose(table)[:mix_rows]
    weights = jnp.transpose(
        jnp.concatenate([weights, jnp.zeros((128 - rows, 128), jnp.float32)], axis=0)
    )[:mix_rows].astype(jnp.bfloat16)
    values = jnp.concatenate(
        [values, jnp.zeros((128 - rows, HEAD_WIDTH), jnp.bfloat16)], axis=0
    )
    mix = dot(weights, values, ((1,), (0,))) * table[:, sources : sources + 1]
    for s, ref in enumerate(got_refs):
        mix += ref[:mix_rows].astype(jnp.float32) * table[:, s : s + 1]
    for h in range(heads):
        tile = mix[h * rows : (h + 1) * rows]
        for b in range(requests):
            out_ref[b, :, h * HEAD_WIDTH : (h + 1) * HEAD_WIDTH] = tile[
                b * tokens : (b + 1) * tokens
            ].astype(jnp.bfloat16)


def rotation(lengths, tokens):
    half = HEAD_WIDTH // 2
    places = (lengths[:, None] + jnp.arange(tokens, dtype=jnp.int32)[None, :]).astype(jnp.float32)
    inverse_freq = jnp.exp(
        jnp.arange(half, dtype=jnp.float32) * (-2.0 * math.log(ROPE_BASE) / HEAD_WIDTH)
    )
    angles = places.reshape(-1, 1) * inverse_freq[None, :]
    cosine, sine = jnp.cos(angles), jnp.sin(angles)
    return jnp.concatenate([cosine, cosine], axis=1), jnp.concatenate([-sine, sine], axis=1)


def vmem():
    return pl.BlockSpec(memory_space=pltpu.VMEM)


def smem():
    return pl.BlockSpec(memory_space=pltpu.SMEM)


def hbm():
    return pl.BlockSpec(memory_space=pltpu.HBM)


def pinned(x):
    return pltpu.with_memory_space_constraint(x, pltpu.HBM)


def cost(flops, moved):
    return pl.CostEstimate(flops=int(flops), bytes_accessed=int(moved), transcendentals=0)


def swap(x, devices, bit):
    return lax.ppermute(x, "tensor", [(d, d ^ bit) for d in range(devices)])


def per_device(
    hidden,
    queries,
    key_value_weight,
    adapter_down_weight,
    adapter_up_weight,
    cached_key_rows,
    cached_value_rows,
    request_adapter,
    adapter_rank_list,
    adapter_pool_row,
    lengths,
):
    requests, tokens, width = hidden.shape
    rows = requests * tokens
    devices = lax.axis_size("tensor")
    sizes = (requests, tokens, devices)
    heads = QUERY_HEADS // devices
    chunks = width // HEAD_WIDTH
    lanes = devices // 2
    partner = lanes // KEY_HEADS
    slot_rows = heads * rows
    index = lax.axis_index("tensor").reshape(1).astype(jnp.int32)
    flat = requests * cached_key_rows.shape[1]
    cached_keys = pinned(cached_key_rows.reshape(flat, -1))
    cached_values = pinned(cached_value_rows.reshape(flat, -1))
    cache = pltpu.VMEM((2, flat, GROUPED * HEAD_WIDTH), jnp.bfloat16)
    cache_sems = 2 * GROUPED

    def call(kernel, operands, in_specs, out_shape, scratch, name):
        return pl.pallas_call(
            kernel,
            out_shape=tuple(out_shape),
            in_specs=in_specs,
            out_specs=(vmem(),) * len(out_shape),
            scratch_shapes=scratch,
            compiler_params=pltpu.CompilerParams(vmem_limit_bytes=12 * MIB),
            cost_estimate=cost(10**9 if name == "base" else 10**6, 0),
            name=name,
        )(*operands)

    own_queries, own_hidden, far_send = call(
        functools.partial(pack_kernel, sizes),
        (index, pinned(queries), pinned(hidden), cached_keys, cached_values),
        [smem()] + [hbm()] * 4,
        [
            pltpu.VMEM((heads, rows, HEAD_WIDTH), jnp.bfloat16),
            pltpu.VMEM((chunks, rows, HEAD_WIDTH), jnp.bfloat16),
            cache,
        ],
        [
            pltpu.VMEM(queries.shape, jnp.bfloat16),
            pltpu.VMEM(hidden.shape, jnp.bfloat16),
            pltpu.SemaphoreType.DMA((cache_sems + 2,)),
        ],
        "pack",
    )
    far_cache = swap(far_send, devices, 2 * partner)
    bits = [1 << i for i in reversed(range(lanes.bit_length() - 1)) if 1 << i != partner]
    own_slot = jnp.concatenate([own_queries, own_hidden], axis=0)
    first_slot = swap(own_slot, devices, 2 * bits[0])
    far_hidden = swap(own_hidden, devices, 2 * partner)
    first_far_hidden = swap(own_hidden, devices, 2 * (partner ^ bits[0]))

    out_width = key_value_weight.shape[1]
    parts = 4 if width % (4 * HEAD_WIDTH) == 0 else 1
    up = adapter_up_weight[0]
    base, own_cache, up = call(
        functools.partial(base_kernel, sizes),
        (index, own_hidden, pinned(key_value_weight), cached_keys, cached_values, pinned(up)),
        [smem(), vmem()] + [hbm()] * 4,
        [
            pltpu.VMEM((rows, out_width), jnp.float32),
            cache,
            pltpu.VMEM(up.shape, up.dtype),
        ],
        [
            pltpu.VMEM((parts, width // parts, out_width), jnp.bfloat16),
            pltpu.SemaphoreType.DMA((cache_sems + parts + 1,)),
        ],
        "base",
    )
    first_far_hidden, base = lax.optimization_barrier((first_far_hidden, base))

    masks = [0, bits[0]]
    slots = [own_slot, far_hidden, first_slot, first_far_hidden]
    lane = jnp.concatenate(slots, axis=0).reshape(2, -1, rows, HEAD_WIDTH)
    for bit in bits[1:-1]:
        masks += [mask ^ bit for mask in masks]
        lane = jnp.concatenate([lane, swap(lane, devices, 2 * bit)], axis=0)
    other = swap(lane, devices, 1)
    late_lane = swap(lane, devices, 2 * bits[-1])
    late_masks = [mask ^ bits[-1] for mask in masks]

    down = pinned(adapter_down_weight[0])
    rank = down.shape[1]
    sources = 4 * len(masks)
    half = pltpu.VMEM((sources, width, rank), jnp.bfloat16)
    (early, late_down) = call(
        functools.partial(early_kernel, sizes, masks, late_masks),
        (index, lane, other, down),
        [smem()] + [vmem()] * 2 + [hbm()],
        [pltpu.VMEM((rows, rank), jnp.float32), half],
        [half, pltpu.SemaphoreType.DMA((sources,)), pltpu.SemaphoreType.DMA((sources,))],
        "lora_first",
    )
    late_lane, early = lax.optimization_barrier((late_lane, early))
    late_other = swap(late_lane, devices, 1)
    late_other, far_cache = lax.optimization_barrier((late_other, far_cache))
    step = GROUPED * rows
    proj, own_parts, parts = call(
        functools.partial(project_kernel, sizes, late_masks),
        (
            index,
            request_adapter,
            adapter_rank_list,
            adapter_pool_row,
            late_lane,
            late_other,
            early,
            base,
            late_down,
            up,
        ),
        [smem()] * 4 + [vmem()] * 6,
        [
            pltpu.VMEM((2, step, HEAD_WIDTH), jnp.float32),
            pltpu.VMEM((3 * step, HEAD_WIDTH), jnp.bfloat16),
            pltpu.VMEM((3 * step, HEAD_WIDTH), jnp.bfloat16),
        ],
        [pltpu.VMEM((rows, out_width), jnp.float32)],
        "project",
    )
    far_parts = swap(parts, devices, 2 * partner)
    all_masks = masks + late_masks
    (send,) = call(
        functools.partial(other_kernel, sizes, all_masks),
        (index, lengths, other, late_other, own_cache, far_cache, own_parts),
        [smem()] * 2 + [vmem()] * 5,
        [pltpu.VMEM((MIX_ROWS + 3 * step + STAT_ROWS, HEAD_WIDTH), jnp.bfloat16)],
        [],
        "other_lane",
    )
    got = swap(send, devices, 1)
    got_far_parts = swap(far_parts, devices, 1)
    mix, stats = call(
        functools.partial(own_kernel, sizes, all_masks),
        (index, lengths, lane, late_lane, own_cache, far_cache),
        [smem()] * 2 + [vmem()] * 4,
        [
            pltpu.VMEM((MIX_ROWS, HEAD_WIDTH), jnp.float32),
            pltpu.VMEM((8, HEAD_WIDTH), jnp.float32),
        ],
        [],
        "own_lane",
    )
    packet = pltpu.VMEM((slot_rows + 4 * rows, HEAD_WIDTH), jnp.bfloat16)
    packets = call(
        functools.partial(join_kernel, sizes, all_masks),
        (index, mix, stats, proj, far_parts, got, got_far_parts),
        [smem()] + [vmem()] * 6,
        [packet] * len(all_masks),
        [pltpu.VMEM((GROUPED, 3 * rows, HEAD_WIDTH), jnp.float32)],
        "join",
    )
    order = sorted(range(len(all_masks)), key=lambda i: -all_masks[i])
    order = [i for i in order if all_masks[i] not in (0, bits[0])] + [1]
    packets = [packets[0]] + [swap(packets[i], devices, 2 * all_masks[i]) for i in order]
    cosine, sine = rotation(lengths, tokens)
    return pl.pallas_call(
        functools.partial(merge_kernel, devices, requests, tokens),
        out_shape=jax.ShapeDtypeStruct((requests, tokens, heads * HEAD_WIDTH), jnp.bfloat16),
        in_specs=[vmem()] * (3 + len(packets)),
        out_specs=vmem(),
        compiler_params=pltpu.CompilerParams(vmem_limit_bytes=8 * MIB),
        name="merge_states",
    )(own_queries, cosine, sine, *packets)


def solution(mesh):
    in_specs = (
        P("groups", None, "tensor"),
        P("groups", None, "tensor"),
        P("tensor", None),
        P("tensor", None, None),
        P("tensor", None, None),
        P("groups", "tensor", None),
        P("groups", "tensor", None),
        P("groups"),
        P(),
        P(),
        P("groups"),
    )
    out_specs = P("groups", None, "tensor")
    return jax.shard_map(
        per_device, mesh=mesh, in_specs=in_specs, out_specs=out_specs, check_vma=False
    )
```

```python
import functools
import math

import jax
import jax.numpy as jnp
from jax import lax
from jax.experimental import pallas as pl
from jax.experimental.pallas import tpu as pltpu
from jax.sharding import PartitionSpec as P

QUERY_HEADS = 128
KEY_HEADS = 8
HEAD_WIDTH = 128
ROPE_BASE = 500000.0
NEG_FILL = -1e30
SCALE = 1.0 / math.sqrt(HEAD_WIDTH)
GROUPED = KEY_HEADS // 2
CHUNKS = GROUPED // 2
MIX_ROWS = GROUPED * 64
STAT_ROWS = 16
MIB = 2**20


def dot(a, b, dims):
    return lax.dot_general(a, b, (dims, ((), ())), preferred_element_type=jnp.float32)


def round_bf16(x):
    return x.astype(jnp.bfloat16).astype(jnp.float32)


class Plan:
    def __init__(self, devices, width):
        lanes = devices // 2
        per_head = lanes // KEY_HEADS
        self.devices, self.per_head, self.partner = devices, per_head, per_head
        self.heads, self.chunks = QUERY_HEADS // devices, width // HEAD_WIDTH
        near = [m for m in range(1, lanes) if not m & self.partner]
        far = [m for m in range(lanes) if m & self.partner]
        if per_head > 1:
            self.single = 1
            self.near_pairs = [(m, m ^ 1) for m in near if m % 2 == 0]
        else:
            self.single = near[-1]
            self.near_pairs = list(zip(near[:-1:2], near[1:-1:2]))
        self.far_pairs = list(zip(far[::2], far[1::2]))
        size = self.heads + self.chunks
        slots = [((0, 0), ((0, 0), (1, 0))), ((self.single,) * 2, ((2, 0), (3, 0)))]
        for k, (a, b) in enumerate(self.near_pairs):
            at = size + 2 * size * k
            slots.append(((a, b), ((2, at), (2, at + size))))
            slots.append(((b, a), ((3, at + size), (3, at))))
        self.slots = sorted(slots, key=self.head_masks)
        self.far_slots = []
        for k, (a, b) in enumerate(self.far_pairs):
            at = 2 * self.chunks * k
            self.far_slots.append(((a, b), ((0, at), (0, at + self.chunks))))
            self.far_slots.append(((b, a), ((1, at + self.chunks), (1, at))))

    def head_masks(self, slot):
        return tuple(mask // self.per_head for mask in slot[0])

    def attention_chunks(self, slot_rows, side=0):
        count = HEAD_WIDTH // slot_rows
        by_masks = {slot[0]: slot for slot in self.slots}
        slots = [by_masks[slot[0][::-1]] if side else slot for slot in self.slots]
        chunks = []
        for at in range(0, len(slots), count):
            runs = []
            for slot in slots[at : at + count]:
                if runs and self.head_masks(runs[-1][0]) == self.head_masks(slot):
                    runs[-1].append(slot)
                else:
                    runs.append([slot])
            chunks.append(runs)
        return chunks


def here_mask(masks, here):
    return masks[0] if masks[0] == masks[1] else jnp.where(here % 2 == 0, masks[0], masks[1])


def sources_of(slots, skip):
    return [
        (array, tile + skip, masks, side)
        for masks, places in slots
        for side, (array, tile) in enumerate(places)
    ]


def streams(sources, index_ref, down_ref, buffer, sems):
    depth = buffer.shape[1]
    here = index_ref[0]
    copies = []
    for at, (_, _, masks, side) in enumerate(sources):
        source = here ^ (2 * here_mask(masks, here) + side)
        rows = pl.ds(pl.multiple_of(source * depth, depth), depth)
        copies.append(pltpu.make_async_copy(down_ref.at[rows], buffer.at[at], sems.at[at]))
    return copies


def lower(sources, arrays, buffer, copies):
    total = None
    chunks = buffer.shape[1] // HEAD_WIDTH
    for at, (array, first, _, _) in enumerate(sources):
        hidden = jnp.concatenate([arrays[array][first + c] for c in range(chunks)], axis=1)
        if copies:
            copies[at].wait()
        term = dot(hidden, buffer[at], ((1,), (0,)))
        total = term if total is None else total + term
    return total


def early_kernel(plan, *refs):
    (index_ref, *arrays, down_ref, out_ref, held_ref, buffer, sems, late_sems) = refs
    sources = sources_of(plan.slots, plan.heads)
    copies = streams(sources, index_ref, down_ref, buffer, sems)
    late = streams(sources_of(plan.far_slots, 0), index_ref, down_ref, held_ref, late_sems)
    for copy in copies + late:
        copy.start()
    out_ref[...] = lower(sources, arrays, buffer, copies)
    for copy in late:
        copy.wait()


def lane_of(index_ref, devices):
    here = index_ref[0]
    chip = here // 2
    per_head = devices // 2 // KEY_HEADS
    return here, chip, per_head, (chip // per_head) % 2


def head_columns(head):
    return pl.ds(pl.multiple_of(head * HEAD_WIDTH, HEAD_WIDTH), HEAD_WIDTH)


def cache_copies(key_ref, value_ref, out_ref, parity, sems):
    copies = []
    for i, ref in enumerate((key_ref, value_ref)):
        for g in range(GROUPED):
            place = out_ref.at[i, :, g * HEAD_WIDTH : (g + 1) * HEAD_WIDTH]
            source = ref.at[:, head_columns(2 * g + parity)]
            copies.append(pltpu.make_async_copy(source, place, sems.at[i * GROUPED + g]))
    return copies


def pack_kernel(sizes, index_ref, query_ref, hidden_ref, key_ref, value_ref, *refs):
    own_ref, cache_ref, query_buf, hidden_buf, sems = refs
    requests, tokens, devices = sizes
    _, _, _, parity = lane_of(index_ref, devices)
    loads = [
        pltpu.make_async_copy(query_ref, query_buf, sems.at[2 * GROUPED]),
        pltpu.make_async_copy(hidden_ref, hidden_buf, sems.at[2 * GROUPED + 1]),
    ]
    caches = cache_copies(key_ref, value_ref, cache_ref, 1 - parity, sems)
    for load in loads + caches:
        load.start()
    at = 0
    for load, ref in zip(loads, (query_buf, hidden_buf)):
        load.wait()
        rows = jnp.concatenate([ref[b].astype(jnp.float32) for b in range(requests)], axis=0)
        for c in range(rows.shape[1] // HEAD_WIDTH):
            tile = rows[:, c * HEAD_WIDTH : (c + 1) * HEAD_WIDTH]
            own_ref[at] = tile.astype(jnp.bfloat16)
            at += 1
    for load in caches:
        load.wait()


def base_kernel(sizes, index_ref, own_ref, weight_ref, key_ref, value_ref, *refs):
    up_ref, base_ref, cache_ref, held_up_ref, buffer, sems = refs
    requests, tokens, devices = sizes
    _, _, _, parity = lane_of(index_ref, devices)
    parts, depth = buffer.shape[:2]
    loads = [
        pltpu.make_async_copy(
            weight_ref.at[pl.ds(p * depth, depth)], buffer.at[p], sems.at[2 * GROUPED + p]
        )
        for p in range(parts)
    ]
    others = cache_copies(key_ref, value_ref, cache_ref, parity, sems)
    others.append(pltpu.make_async_copy(up_ref, held_up_ref, sems.at[2 * GROUPED + parts]))
    for load in loads + others:
        load.start()
    tiles = depth // HEAD_WIDTH
    first = QUERY_HEADS // devices
    total = jnp.zeros(base_ref.shape, jnp.float32)
    for p in range(parts):
        hidden = jnp.concatenate([own_ref[first + p * tiles + c] for c in range(tiles)], axis=1)
        loads[p].wait()
        total += dot(hidden, buffer[p], ((1,), (0,)))
    base_ref[...] = total
    for load in others:
        load.wait()


def project_kernel(sizes, plan, *refs):
    (index_ref, adapter_ref, rank_ref, pool_ref) = refs[:4]
    (far_ref, other_far_ref, early_ref, base_ref, down_ref, up_ref) = refs[4:10]
    (own_ref, own_parts_ref, parts_ref, all_ref) = refs[10:]
    requests, tokens, devices = sizes
    rows = requests * tokens
    here, _, _, parity = lane_of(index_ref, devices)
    sources = sources_of(plan.far_slots, 0)
    lowered = early_ref[...] + lower(sources, (far_ref, other_far_ref), down_ref, [])
    row_request = lax.broadcasted_iota(jnp.int32, (rows, 1), 0) // tokens
    ranks = jnp.zeros((rows, 1), jnp.int32)
    owners = jnp.zeros((rows, 1), jnp.int32)
    for b in range(requests):
        adapter = adapter_ref[b]
        ranks = jnp.where(row_request == b, rank_ref[adapter], ranks)
        owners = jnp.where(row_request == b, pool_ref[adapter], owners)
    column = lax.broadcasted_iota(jnp.int32, lowered.shape, 1)
    lowered = jnp.where(column < ranks, lowered, 0.0).astype(jnp.bfloat16)
    lifted = dot(lowered, up_ref[...], ((1,), (0,)))
    all_ref[...] = base_ref[...] + jnp.where(owners == here, lifted, 0.0)
    step = GROUPED * rows
    for which, out_ref in ((parity, own_parts_ref), (1 - parity, parts_ref)):
        keys = [all_ref[:, head_columns(2 * g + which)] for g in range(GROUPED)]
        values = [all_ref[:, head_columns(KEY_HEADS + 2 * g + which)] for g in range(GROUPED)]
        keys = jnp.concatenate(keys, axis=0)
        values = jnp.concatenate(values, axis=0)
        if out_ref is own_parts_ref:
            own_ref[0] = keys
            own_ref[1] = values
        high = keys.astype(jnp.bfloat16)
        out_ref[:step] = high
        out_ref[step : 2 * step] = (keys - high.astype(jnp.float32)).astype(jnp.bfloat16)
        out_ref[2 * step :] = values.astype(jnp.bfloat16)


def attend(sizes, plan, side, index_ref, length_ref, arrays, cache_ref, far_ref, put):
    requests, tokens, devices = sizes
    here, chip, per_head, _ = lane_of(index_ref, devices)
    heads = plan.heads
    slot_rows = heads * requests * tokens
    positions = cache_ref.shape[1] // requests
    place = lax.broadcasted_iota(jnp.int32, (requests * positions, HEAD_WIDTH), 0)
    column = lax.broadcasted_iota(jnp.int32, (requests * positions, HEAD_WIDTH), 1)
    place_request = place // positions
    limit = jnp.zeros_like(place)
    for b in range(requests):
        limit = jnp.where(place_request == b, length_ref[b], limit)
    same = place_request == (column // tokens) % requests
    caches = (cache_ref, far_ref)
    allowed = [
        (device * positions + place % positions < limit) & same
        for device in (here, here ^ (2 * per_head))
    ]
    peaks, totals = [], []
    for number, runs in enumerate(plan.attention_chunks(slot_rows, side)):
        places = [places[side] for run in runs for _, places in run]
        query = jnp.concatenate(
            [arrays[array][tile + h] for array, tile in places for h in range(heads)], axis=0
        )
        spots = [
            head_columns(((chip // per_head) ^ (here_mask(run[0][0], here) // per_head)) // 2)
            for run in runs
        ]
        share = HEAD_WIDTH // len(runs)
        scores = []
        for ref, valid in zip(caches, allowed):
            score = None
            for i, spot in enumerate(spots):
                part = dot(ref[0, :, spot], query, ((1,), (1,)))
                score = part if score is None else jnp.where(column < i * share, score, part)
            scores.append(jnp.where(valid, score * SCALE, NEG_FILL))
        peak = jnp.maximum(
            jnp.max(scores[0], axis=0, keepdims=True), jnp.max(scores[1], axis=0, keepdims=True)
        )
        peak = round_bf16(peak)
        total, weights = jnp.zeros_like(peak), []
        for score, valid in zip(scores, allowed):
            weight = jnp.where(valid, jnp.exp(score - peak), 0.0)
            total += jnp.sum(weight, axis=0, keepdims=True)
            weights.append(jnp.transpose(weight.astype(jnp.bfloat16)))
        peaks.append(peak)
        totals.append(total)
        for i, spot in enumerate(spots):
            own = slice(i * share, (i + 1) * share)
            mix = dot(weights[0][own], cache_ref[1, :, spot], ((1,), (0,)))
            mix += dot(weights[1][own], far_ref[1, :, spot], ((1,), (0,)))
            put(number, i * share, mix)
    return peaks, totals


def rows_of(items, count):
    row = lax.broadcasted_iota(jnp.int32, (count, HEAD_WIDTH), 0)
    out = jnp.zeros((count, HEAD_WIDTH), jnp.float32)
    for i, item in enumerate(items):
        out = jnp.where(row == i, item, out)
    return out


def other_kernel(sizes, plan, *refs):
    (index_ref, length_ref, *arrays, cache_ref, far_ref, parts_ref, send_ref) = refs
    proj_rows = parts_ref.shape[0]

    def put(chunk, row, mix):
        at = chunk * 128 + row
        send_ref[at : at + mix.shape[0]] = mix.astype(jnp.bfloat16)

    peaks, totals = attend(
        sizes, plan, 1, index_ref, length_ref, arrays, cache_ref, far_ref, put
    )
    highs = [round_bf16(total) for total in totals]
    lows = [total - high for total, high in zip(totals, highs)]
    send_ref[MIX_ROWS : MIX_ROWS + proj_rows] = parts_ref[...]
    send_ref[MIX_ROWS + proj_rows :] = rows_of(peaks + highs + lows, STAT_ROWS).astype(jnp.bfloat16)


def own_kernel(sizes, plan, *refs):
    (index_ref, length_ref, *arrays, cache_ref, far_ref, mix_ref, stat_ref) = refs

    def put(chunk, row, mix):
        at = chunk * 128 + row
        mix_ref[at : at + mix.shape[0]] = mix

    peaks, totals = attend(
        sizes, plan, 0, index_ref, length_ref, arrays, cache_ref, far_ref, put
    )
    stat_ref[...] = rows_of(peaks + totals, 8)


def join_kernel(sizes, plan, index_ref, mix_ref, stat_ref, proj_ref, far_ref, got_ref, got_far_ref, *refs):
    packet_refs, tail_ref = refs[:-1], refs[-1]
    requests, tokens, devices = sizes
    here, chip, per_head, _ = lane_of(index_ref, devices)
    rows = requests * tokens
    heads = QUERY_HEADS // devices
    slot_rows = heads * rows
    step = GROUPED * rows
    got = got_ref[MIX_ROWS + 3 * step :].astype(jnp.float32)
    own = stat_ref[...]
    own_peak, got_peak = own[:CHUNKS], got[:CHUNKS]
    peak = jnp.maximum(own_peak, got_peak)
    own_factor = jnp.exp(own_peak - peak)
    got_factor = jnp.exp(got_peak - peak)
    total = own_factor * own[CHUNKS : 2 * CHUNKS] + got_factor * (
        got[CHUNKS : 2 * CHUNKS] + got[2 * CHUNKS : 3 * CHUNKS]
    )
    high = round_bf16(total)
    low = total - high
    filler = jnp.zeros((128 - 2 * CHUNKS, 128), jnp.float32)
    table = jnp.transpose(jnp.concatenate([own_factor, got_factor, filler], axis=0))
    keys, values = proj_ref[0], proj_ref[1]
    for ref, at in ((far_ref, 0), (got_ref, MIX_ROWS), (got_far_ref, 0)):
        keys += ref[at : at + step].astype(jnp.float32)
        keys += ref[at + step : at + 2 * step].astype(jnp.float32)
        values += ref[at + 2 * step : at + 3 * step].astype(jnp.float32)
    keys_high = round_bf16(keys)
    for g in range(GROUPED):
        part = slice(g * rows, (g + 1) * rows)
        tail_ref[g, :rows] = keys_high[part]
        tail_ref[g, rows : 2 * rows] = (keys - keys_high)[part]
        tail_ref[g, 2 * rows :] = values[part]
    stat_row = lax.broadcasted_iota(jnp.int32, (rows, HEAD_WIDTH), 0)
    for c, runs in enumerate(plan.attention_chunks(slot_rows)):
        span = slice(c * 128, c * 128 + 128)
        mix = mix_ref[span] * table[:, c : c + 1]
        mix += got_ref[span].astype(jnp.float32) * table[:, CHUNKS + c : CHUNKS + c + 1]
        stats = jnp.where(
            stat_row == 0,
            peak[c : c + 1],
            jnp.where(
                stat_row == 1, high[c : c + 1], jnp.where(stat_row == 2, low[c : c + 1], 0.0)
            ),
        )
        chunk = [masks for run in runs for masks, _ in run]
        for t, masks in enumerate(chunk):
            packet_ref = packet_refs[c * len(chunk) + t]
            shifted = stats if t == 0 else pltpu.roll(stats, HEAD_WIDTH - t * slot_rows, 1)
            group = ((chip // per_head) ^ (here_mask(masks, here) // per_head)) // 2
            tail = jnp.concatenate([tail_ref[group], shifted], axis=0)
            packet_ref[:slot_rows] = mix[t * slot_rows : (t + 1) * slot_rows].astype(jnp.bfloat16)
            packet_ref[slot_rows:] = tail.astype(jnp.bfloat16)


def merge_kernel(devices, requests, tokens, own_ref, cos_ref, sin_ref, *refs):
    got_refs, out_ref = refs[:-1], refs[-1]
    rows = requests * tokens
    heads = QUERY_HEADS // devices
    mix_rows = heads * rows
    sources = len(got_refs)
    tails = [ref[mix_rows:].astype(jnp.float32) for ref in got_refs]
    sums = functools.reduce(jnp.add, [tail[: 3 * rows] for tail in tails])
    keys = sums[:rows] + sums[rows : 2 * rows]
    values = sums[2 * rows :].astype(jnp.bfloat16)
    turned = pltpu.roll(keys, HEAD_WIDTH // 2, 1)
    keys = (keys * cos_ref[...] + turned * sin_ref[...]).astype(jnp.bfloat16)
    query = jnp.concatenate([own_ref[h] for h in range(heads)], axis=0)
    if mix_rows < 128:
        query = jnp.concatenate(
            [query, jnp.zeros((128 - mix_rows, HEAD_WIDTH), jnp.bfloat16)], axis=0
        )
    fresh = dot(keys, query, ((1,), (1,))) * SCALE
    source = lax.broadcasted_iota(jnp.int32, fresh.shape, 0)
    column = lax.broadcasted_iota(jnp.int32, fresh.shape, 1) % rows
    allowed = (source // tokens == column // tokens) & (source % tokens <= column % tokens)
    fresh_peak = jnp.max(jnp.where(allowed, fresh, NEG_FILL), axis=0, keepdims=True)
    stats = [tail[3 * rows :] for tail in tails]
    peak = functools.reduce(jnp.maximum, [stat[0:1] for stat in stats], fresh_peak)
    weights = jnp.where(allowed, jnp.exp(fresh - peak), 0.0)
    factors = [jnp.exp(stat[0:1] - peak) for stat in stats]
    total = functools.reduce(
        jnp.add,
        [factor * (stat[1:2] + stat[2:3]) for factor, stat in zip(factors, stats)],
        jnp.sum(weights, axis=0, keepdims=True),
    )
    inverse = 1.0 / total
    filler = jnp.zeros((128 - sources - 1, 128), jnp.float32)
    table = jnp.concatenate([factor * inverse for factor in factors] + [inverse, filler], axis=0)
    table = jnp.transpose(table)[:mix_rows]
    weights = jnp.transpose(
        jnp.concatenate([weights, jnp.zeros((128 - rows, 128), jnp.float32)], axis=0)
    )[:mix_rows].astype(jnp.bfloat16)
    values = jnp.concatenate(
        [values, jnp.zeros((128 - rows, HEAD_WIDTH), jnp.bfloat16)], axis=0
    )
    mix = dot(weights, values, ((1,), (0,))) * table[:, sources : sources + 1]
    for s, ref in enumerate(got_refs):
        mix += ref[:mix_rows].astype(jnp.float32) * table[:, s : s + 1]
    for h in range(heads):
        tile = mix[h * rows : (h + 1) * rows]
        for b in range(requests):
            out_ref[b, :, h * HEAD_WIDTH : (h + 1) * HEAD_WIDTH] = tile[
                b * tokens : (b + 1) * tokens
            ].astype(jnp.bfloat16)


def rotation(lengths, tokens):
    half = HEAD_WIDTH // 2
    places = (lengths[:, None] + jnp.arange(tokens, dtype=jnp.int32)[None, :]).astype(jnp.float32)
    inverse_freq = jnp.exp(
        jnp.arange(half, dtype=jnp.float32) * (-2.0 * math.log(ROPE_BASE) / HEAD_WIDTH)
    )
    angles = places.reshape(-1, 1) * inverse_freq[None, :]
    cosine, sine = jnp.cos(angles), jnp.sin(angles)
    return jnp.concatenate([cosine, cosine], axis=1), jnp.concatenate([-sine, sine], axis=1)


def vmem():
    return pl.BlockSpec(memory_space=pltpu.VMEM)


def smem():
    return pl.BlockSpec(memory_space=pltpu.SMEM)


def hbm():
    return pl.BlockSpec(memory_space=pltpu.HBM)


def pinned(x):
    return pltpu.with_memory_space_constraint(x, pltpu.HBM)


def cost(flops, moved):
    return pl.CostEstimate(flops=int(flops), bytes_accessed=int(moved), transcendentals=0)


def trade(x, devices, even, odd, core=0):
    pairs = [(d, d ^ (2 * (odd if d % 2 else even) + core)) for d in range(devices)]
    return lax.ppermute(x, "tensor", pairs)


def per_device(
    hidden,
    queries,
    key_value_weight,
    adapter_down_weight,
    adapter_up_weight,
    cached_key_rows,
    cached_value_rows,
    request_adapter,
    adapter_rank_list,
    adapter_pool_row,
    lengths,
):
    requests, tokens, width = hidden.shape
    rows = requests * tokens
    devices = lax.axis_size("tensor")
    sizes = (requests, tokens, devices)
    plan = Plan(devices, width)
    heads, chunks, partner = plan.heads, plan.chunks, plan.partner
    slot_rows = heads * rows
    index = lax.axis_index("tensor").reshape(1).astype(jnp.int32)
    flat = requests * cached_key_rows.shape[1]
    cached_keys = pinned(cached_key_rows.reshape(flat, -1))
    cached_values = pinned(cached_value_rows.reshape(flat, -1))
    cache = pltpu.VMEM((2, flat, GROUPED * HEAD_WIDTH), jnp.bfloat16)
    cache_sems = 2 * GROUPED

    def call(kernel, operands, in_specs, out_shape, scratch, name):
        return pl.pallas_call(
            kernel,
            out_shape=tuple(out_shape),
            in_specs=in_specs,
            out_specs=(vmem(),) * len(out_shape),
            scratch_shapes=scratch,
            compiler_params=pltpu.CompilerParams(vmem_limit_bytes=12 * MIB),
            cost_estimate=cost(10**9 if name == "base" else 10**6, 0),
            name=name,
        )(*operands)

    def core_swap(x):
        return trade(x, devices, 0, 0, core=1)

    own, far_send = call(
        functools.partial(pack_kernel, sizes),
        (index, pinned(queries), pinned(hidden), cached_keys, cached_values),
        [smem()] + [hbm()] * 4,
        [pltpu.VMEM((heads + chunks, rows, HEAD_WIDTH), jnp.bfloat16), cache],
        [
            pltpu.VMEM(queries.shape, jnp.bfloat16),
            pltpu.VMEM(hidden.shape, jnp.bfloat16),
            pltpu.SemaphoreType.DMA((cache_sems + 2,)),
        ],
        "pack",
    )
    far_cache = trade(far_send, devices, partner, partner)
    own, other = lax.optimization_barrier((own, core_swap(own)))
    near = [trade(own, devices, plan.single, plan.single)]
    both = jnp.concatenate([own, other], axis=0)
    both_hidden = jnp.concatenate([own[heads:], other[heads:]], axis=0)
    near += [trade(both, devices, a, b) for a, b in plan.near_pairs]
    far = [trade(both_hidden, devices, a, b) for a, b in plan.far_pairs]

    out_width = key_value_weight.shape[1]
    parts = 4 if width % (4 * HEAD_WIDTH) == 0 else 1
    up = adapter_up_weight[0]
    base, own_cache, up = call(
        functools.partial(base_kernel, sizes),
        (index, own, pinned(key_value_weight), cached_keys, cached_values, pinned(up)),
        [smem(), vmem()] + [hbm()] * 4,
        [
            pltpu.VMEM((rows, out_width), jnp.float32),
            cache,
            pltpu.VMEM(up.shape, up.dtype),
        ],
        [
            pltpu.VMEM((parts, width // parts, out_width), jnp.bfloat16),
            pltpu.SemaphoreType.DMA((cache_sems + parts + 1,)),
        ],
        "base",
    )
    near = jnp.concatenate(near, axis=0)
    other_near = core_swap(near)
    far = jnp.concatenate(far, axis=0)
    far, base = lax.optimization_barrier((far, base))
    other_far, far_cache = lax.optimization_barrier((core_swap(far), far_cache))

    down = pinned(adapter_down_weight[0])
    rank = down.shape[1]
    half = pltpu.VMEM((devices // 2, width, rank), jnp.bfloat16)
    half_sems = pltpu.SemaphoreType.DMA((devices // 2,))
    arrays = (own, other, near, other_near)
    (early, far_down) = call(
        functools.partial(early_kernel, plan),
        (index,) + arrays + (down,),
        [smem()] + [vmem()] * 4 + [hbm()],
        [pltpu.VMEM((rows, rank), jnp.float32), half],
        [half, half_sems, half_sems],
        "lora_near",
    )
    step = GROUPED * rows
    proj, own_parts, parts = call(
        functools.partial(project_kernel, sizes, plan),
        (
            index,
            request_adapter,
            adapter_rank_list,
            adapter_pool_row,
            far,
            other_far,
            early,
            base,
            far_down,
            up,
        ),
        [smem()] * 4 + [vmem()] * 6,
        [
            pltpu.VMEM((2, step, HEAD_WIDTH), jnp.float32),
            pltpu.VMEM((3 * step, HEAD_WIDTH), jnp.bfloat16),
            pltpu.VMEM((3 * step, HEAD_WIDTH), jnp.bfloat16),
        ],
        [pltpu.VMEM((rows, out_width), jnp.float32)],
        "project",
    )
    far_parts = trade(parts, devices, partner, partner)
    (send,) = call(
        functools.partial(other_kernel, sizes, plan),
        (index, lengths) + arrays + (own_cache, far_cache, own_parts),
        [smem()] * 2 + [vmem()] * 7,
        [pltpu.VMEM((MIX_ROWS + 3 * step + STAT_ROWS, HEAD_WIDTH), jnp.bfloat16)],
        [],
        "other_lane",
    )
    got = core_swap(send)
    got_far_parts = core_swap(far_parts)
    mix, stats = call(
        functools.partial(own_kernel, sizes, plan),
        (index, lengths) + arrays + (own_cache, far_cache),
        [smem()] * 2 + [vmem()] * 6,
        [
            pltpu.VMEM((MIX_ROWS, HEAD_WIDTH), jnp.float32),
            pltpu.VMEM((8, HEAD_WIDTH), jnp.float32),
        ],
        [],
        "own_lane",
    )
    packet = pltpu.VMEM((slot_rows + 4 * rows, HEAD_WIDTH), jnp.bfloat16)
    packets = call(
        functools.partial(join_kernel, sizes, plan),
        (index, mix, stats, proj, far_parts, got, got_far_parts),
        [smem()] + [vmem()] * 6,
        [packet] * len(plan.slots),
        [pltpu.VMEM((GROUPED, 3 * rows, HEAD_WIDTH), jnp.float32)],
        "join",
    )
    packets = [
        trade(x, devices, *masks) if masks != (0, 0) else x
        for x, (masks, _) in zip(packets, plan.slots)
    ]
    cosine, sine = rotation(lengths, tokens)
    return pl.pallas_call(
        functools.partial(merge_kernel, devices, requests, tokens),
        out_shape=jax.ShapeDtypeStruct((requests, tokens, heads * HEAD_WIDTH), jnp.bfloat16),
        in_specs=[vmem()] * (3 + len(packets)),
        out_specs=vmem(),
        compiler_params=pltpu.CompilerParams(vmem_limit_bytes=8 * MIB),
        name="merge_states",
    )(own, cosine, sine, *packets)


def solution(mesh):
    in_specs = (
        P("groups", None, "tensor"),
        P("groups", None, "tensor"),
        P("tensor", None),
        P("tensor", None, None),
        P("tensor", None, None),
        P("groups", "tensor", None),
        P("groups", "tensor", None),
        P("groups"),
        P(),
        P(),
        P("groups"),
    )
    out_specs = P("groups", None, "tensor")
    return jax.shard_map(
        per_device, mesh=mesh, in_specs=in_specs, out_specs=out_specs, check_vma=False
    )
```

```python
import functools
import math

import jax
import jax.numpy as jnp
from jax import lax
from jax.experimental import pallas as pl
from jax.experimental.pallas import tpu as pltpu
from jax.sharding import PartitionSpec as P

QUERY_HEADS = 128
KEY_HEADS = 8
HEAD_WIDTH = 128
ROPE_BASE = 500000.0
NEG_FILL = -1e30
SCALE = 1.0 / math.sqrt(HEAD_WIDTH)
GROUPED = KEY_HEADS // 2
CHUNKS = GROUPED // 2
MIX_ROWS = GROUPED * 64
STAT_ROWS = 16
MIB = 2**20


def dot(a, b, dims):
    return lax.dot_general(a, b, (dims, ((), ())), preferred_element_type=jnp.float32)


def round_bf16(x):
    return x.astype(jnp.bfloat16).astype(jnp.float32)


class Plan:
    def __init__(self, devices, width):
        lanes = devices // 2
        per_head = lanes // KEY_HEADS
        self.devices, self.per_head, self.partner = devices, per_head, per_head
        self.heads, self.chunks = QUERY_HEADS // devices, width // HEAD_WIDTH
        near = [m for m in range(1, lanes) if not m & self.partner]
        if per_head > 1:
            self.single = 1
            self.near_pairs = [(m, m ^ 1) for m in near if m % 2 == 0]
        else:
            self.single = near[-1]
            self.near_pairs = list(zip(near[:-1:2], near[1:-1:2]))
        size = self.heads + 2 * self.chunks
        slots = [((self.single,) * 2, ((0, 0), (1, 0)))]
        for k, (a, b) in enumerate(self.near_pairs):
            at = size + 2 * size * k
            slots.append(((a, b), ((0, at), (0, at + size))))
            slots.append(((b, a), ((1, at + size), (1, at))))
        self.near_slots = slots
        shifted = [(masks, tuple((i + 2, at) for i, at in places)) for masks, places in slots]
        self.slots = sorted([((0, 0), ((0, 0), (1, 0)))] + shifted, key=self.head_masks)

    def head_masks(self, slot):
        return tuple(mask // self.per_head for mask in slot[0])

    def attention_chunks(self, slot_rows, side=0):
        count = HEAD_WIDTH // slot_rows
        by_masks = {slot[0]: slot for slot in self.slots}
        slots = [by_masks[slot[0][::-1]] if side else slot for slot in self.slots]
        chunks = []
        for at in range(0, len(slots), count):
            runs = []
            for slot in slots[at : at + count]:
                if runs and self.head_masks(runs[-1][0]) == self.head_masks(slot):
                    runs[-1].append(slot)
                else:
                    runs.append([slot])
            chunks.append(runs)
        return chunks


def here_mask(masks, here):
    return masks[0] if masks[0] == masks[1] else jnp.where(here % 2 == 0, masks[0], masks[1])


def sources_of(plan, slots):
    return [
        (array, tile + plan.heads + hop * plan.chunks, tuple(m ^ hop * plan.partner for m in masks), side)
        for masks, places in slots
        for side, (array, tile) in enumerate(places)
        for hop in range(2)
    ]


def streams(sources, index_ref, down_ref, buffer, sems):
    depth = buffer.shape[1]
    here = index_ref[0]
    copies = []
    for at, (_, _, masks, side) in enumerate(sources):
        source = here ^ (2 * here_mask(masks, here) + side)
        rows = pl.ds(pl.multiple_of(source * depth, depth), depth)
        copies.append(pltpu.make_async_copy(down_ref.at[rows], buffer.at[at], sems.at[at]))
    return copies


def lower(sources, arrays, buffer, copies):
    total = None
    chunks = buffer.shape[1] // HEAD_WIDTH
    for at, (array, first, _, _) in enumerate(sources):
        hidden = jnp.concatenate([arrays[array][first + c] for c in range(chunks)], axis=1)
        if copies:
            copies[at].wait()
        term = dot(hidden, buffer[at], ((1,), (0,)))
        total = term if total is None else total + term
    return total


def early_kernel(plan, *refs):
    (index_ref, *arrays, down_ref, out_ref, held_ref, buffer, sems, late_sems) = refs
    sources = sources_of(plan, [((0, 0), ((0, 0), (1, 0)))])
    copies = streams(sources, index_ref, down_ref, buffer, sems)
    late = streams(sources_of(plan, plan.near_slots), index_ref, down_ref, held_ref, late_sems)
    for copy in copies + late:
        copy.start()
    out_ref[...] = lower(sources, arrays, buffer, copies)
    for copy in late:
        copy.wait()


def lane_of(index_ref, devices):
    here = index_ref[0]
    chip = here // 2
    per_head = devices // 2 // KEY_HEADS
    return here, chip, per_head, (chip // per_head) % 2


def head_columns(head):
    return pl.ds(pl.multiple_of(head * HEAD_WIDTH, HEAD_WIDTH), HEAD_WIDTH)


def cache_copies(key_ref, value_ref, out_ref, parity, sems):
    copies = []
    for i, ref in enumerate((key_ref, value_ref)):
        for g in range(GROUPED):
            place = out_ref.at[i, :, g * HEAD_WIDTH : (g + 1) * HEAD_WIDTH]
            source = ref.at[:, head_columns(2 * g + parity)]
            copies.append(pltpu.make_async_copy(source, place, sems.at[i * GROUPED + g]))
    return copies


def pack_kernel(sizes, index_ref, query_ref, hidden_ref, key_ref, value_ref, *refs):
    own_query_ref, own_hidden_ref, cache_ref, query_buf, hidden_buf, sems = refs
    requests, tokens, devices = sizes
    _, _, _, parity = lane_of(index_ref, devices)
    loads = [
        pltpu.make_async_copy(query_ref, query_buf, sems.at[2 * GROUPED]),
        pltpu.make_async_copy(hidden_ref, hidden_buf, sems.at[2 * GROUPED + 1]),
    ]
    caches = cache_copies(key_ref, value_ref, cache_ref, 1 - parity, sems)
    for load in loads + caches:
        load.start()
    for load, ref, out_ref in zip(loads, (query_buf, hidden_buf), (own_query_ref, own_hidden_ref)):
        load.wait()
        rows = jnp.concatenate([ref[b].astype(jnp.float32) for b in range(requests)], axis=0)
        for c in range(rows.shape[1] // HEAD_WIDTH):
            tile = rows[:, c * HEAD_WIDTH : (c + 1) * HEAD_WIDTH]
            out_ref[c] = tile.astype(jnp.bfloat16)
    for load in caches:
        load.wait()


def base_kernel(sizes, index_ref, own_ref, weight_ref, key_ref, value_ref, *refs):
    up_ref, base_ref, cache_ref, held_up_ref, buffer, sems = refs
    requests, tokens, devices = sizes
    _, _, _, parity = lane_of(index_ref, devices)
    parts, depth = buffer.shape[:2]
    loads = [
        pltpu.make_async_copy(
            weight_ref.at[pl.ds(p * depth, depth)], buffer.at[p], sems.at[2 * GROUPED + p]
        )
        for p in range(parts)
    ]
    others = cache_copies(key_ref, value_ref, cache_ref, parity, sems)
    others.append(pltpu.make_async_copy(up_ref, held_up_ref, sems.at[2 * GROUPED + parts]))
    for load in loads + others:
        load.start()
    tiles = depth // HEAD_WIDTH
    total = jnp.zeros(base_ref.shape, jnp.float32)
    for p in range(parts):
        hidden = jnp.concatenate([own_ref[p * tiles + c] for c in range(tiles)], axis=1)
        loads[p].wait()
        total += dot(hidden, buffer[p], ((1,), (0,)))
    base_ref[...] = total
    for load in others:
        load.wait()


def project_kernel(sizes, plan, *refs):
    (index_ref, adapter_ref, rank_ref, pool_ref) = refs[:4]
    (near_ref, other_near_ref, early_ref, base_ref, down_ref, up_ref) = refs[4:10]
    (own_ref, own_parts_ref, parts_ref, all_ref) = refs[10:]
    requests, tokens, devices = sizes
    rows = requests * tokens
    here, _, _, parity = lane_of(index_ref, devices)
    sources = sources_of(plan, plan.near_slots)
    lowered = early_ref[...] + lower(sources, (near_ref, other_near_ref), down_ref, [])
    row_request = lax.broadcasted_iota(jnp.int32, (rows, 1), 0) // tokens
    ranks = jnp.zeros((rows, 1), jnp.int32)
    owners = jnp.zeros((rows, 1), jnp.int32)
    for b in range(requests):
        adapter = adapter_ref[b]
        ranks = jnp.where(row_request == b, rank_ref[adapter], ranks)
        owners = jnp.where(row_request == b, pool_ref[adapter], owners)
    column = lax.broadcasted_iota(jnp.int32, lowered.shape, 1)
    lowered = jnp.where(column < ranks, lowered, 0.0).astype(jnp.bfloat16)
    lifted = dot(lowered, up_ref[...], ((1,), (0,)))
    all_ref[...] = base_ref[...] + jnp.where(owners == here, lifted, 0.0)
    step = GROUPED * rows
    for which, out_ref in ((parity, own_parts_ref), (1 - parity, parts_ref)):
        keys = [all_ref[:, head_columns(2 * g + which)] for g in range(GROUPED)]
        values = [all_ref[:, head_columns(KEY_HEADS + 2 * g + which)] for g in range(GROUPED)]
        keys = jnp.concatenate(keys, axis=0)
        values = jnp.concatenate(values, axis=0)
        if out_ref is own_parts_ref:
            own_ref[0] = keys
            own_ref[1] = values
        high = keys.astype(jnp.bfloat16)
        out_ref[:step] = high
        out_ref[step : 2 * step] = (keys - high.astype(jnp.float32)).astype(jnp.bfloat16)
        out_ref[2 * step :] = values.astype(jnp.bfloat16)


def attend(sizes, plan, side, index_ref, length_ref, arrays, cache_ref, far_ref, put):
    requests, tokens, devices = sizes
    here, chip, per_head, _ = lane_of(index_ref, devices)
    heads = plan.heads
    slot_rows = heads * requests * tokens
    positions = cache_ref.shape[1] // requests
    place = lax.broadcasted_iota(jnp.int32, (requests * positions, HEAD_WIDTH), 0)
    column = lax.broadcasted_iota(jnp.int32, (requests * positions, HEAD_WIDTH), 1)
    place_request = place // positions
    limit = jnp.zeros_like(place)
    for b in range(requests):
        limit = jnp.where(place_request == b, length_ref[b], limit)
    same = place_request == (column // tokens) % requests
    caches = (cache_ref, far_ref)
    allowed = [
        (device * positions + place % positions < limit) & same
        for device in (here, here ^ (2 * per_head))
    ]
    peaks, totals = [], []
    for number, runs in enumerate(plan.attention_chunks(slot_rows, side)):
        places = [places[side] for run in runs for _, places in run]
        query = jnp.concatenate(
            [arrays[array][tile + h] for array, tile in places for h in range(heads)], axis=0
        )
        spots = [
            head_columns(((chip // per_head) ^ (here_mask(run[0][0], here) // per_head)) // 2)
            for run in runs
        ]
        share = HEAD_WIDTH // len(runs)
        scores = []
        for ref, valid in zip(caches, allowed):
            score = None
            for i, spot in enumerate(spots):
                part = dot(ref[0, :, spot], query, ((1,), (1,)))
                score = part if score is None else jnp.where(column < i * share, score, part)
            scores.append(jnp.where(valid, score * SCALE, NEG_FILL))
        peak = jnp.maximum(
            jnp.max(scores[0], axis=0, keepdims=True), jnp.max(scores[1], axis=0, keepdims=True)
        )
        peak = round_bf16(peak)
        total, weights = jnp.zeros_like(peak), []
        for score, valid in zip(scores, allowed):
            weight = jnp.where(valid, jnp.exp(score - peak), 0.0)
            total += jnp.sum(weight, axis=0, keepdims=True)
            weights.append(jnp.transpose(weight.astype(jnp.bfloat16)))
        peaks.append(peak)
        totals.append(total)
        for i, spot in enumerate(spots):
            own = slice(i * share, (i + 1) * share)
            mix = dot(weights[0][own], cache_ref[1, :, spot], ((1,), (0,)))
            mix += dot(weights[1][own], far_ref[1, :, spot], ((1,), (0,)))
            put(number, i * share, mix)
    return peaks, totals


def rows_of(items, count):
    row = lax.broadcasted_iota(jnp.int32, (count, HEAD_WIDTH), 0)
    out = jnp.zeros((count, HEAD_WIDTH), jnp.float32)
    for i, item in enumerate(items):
        out = jnp.where(row == i, item, out)
    return out


def other_kernel(sizes, plan, *refs):
    (index_ref, length_ref, *arrays, cache_ref, far_ref, parts_ref, send_ref) = refs
    proj_rows = parts_ref.shape[0]

    def put(chunk, row, mix):
        at = chunk * 128 + row
        send_ref[at : at + mix.shape[0]] = mix.astype(jnp.bfloat16)

    peaks, totals = attend(
        sizes, plan, 1, index_ref, length_ref, arrays, cache_ref, far_ref, put
    )
    highs = [round_bf16(total) for total in totals]
    lows = [total - high for total, high in zip(totals, highs)]
    send_ref[MIX_ROWS : MIX_ROWS + proj_rows] = parts_ref[...]
    send_ref[MIX_ROWS + proj_rows :] = rows_of(peaks + highs + lows, STAT_ROWS).astype(jnp.bfloat16)


def own_kernel(sizes, plan, *refs):
    (index_ref, length_ref, *arrays, cache_ref, far_ref, mix_ref, stat_ref) = refs

    def put(chunk, row, mix):
        at = chunk * 128 + row
        mix_ref[at : at + mix.shape[0]] = mix

    peaks, totals = attend(
        sizes, plan, 0, index_ref, length_ref, arrays, cache_ref, far_ref, put
    )
    stat_ref[...] = rows_of(peaks + totals, 8)


def join_kernel(sizes, plan, index_ref, mix_ref, stat_ref, proj_ref, far_ref, got_ref, got_far_ref, *refs):
    packet_refs, tail_ref = refs[:-1], refs[-1]
    requests, tokens, devices = sizes
    here, chip, per_head, _ = lane_of(index_ref, devices)
    rows = requests * tokens
    heads = QUERY_HEADS // devices
    slot_rows = heads * rows
    step = GROUPED * rows
    got = got_ref[MIX_ROWS + 3 * step :].astype(jnp.float32)
    own = stat_ref[...]
    own_peak, got_peak = own[:CHUNKS], got[:CHUNKS]
    peak = jnp.maximum(own_peak, got_peak)
    own_factor = jnp.exp(own_peak - peak)
    got_factor = jnp.exp(got_peak - peak)
    total = own_factor * own[CHUNKS : 2 * CHUNKS] + got_factor * (
        got[CHUNKS : 2 * CHUNKS] + got[2 * CHUNKS : 3 * CHUNKS]
    )
    high = round_bf16(total)
    low = total - high
    filler = jnp.zeros((128 - 2 * CHUNKS, 128), jnp.float32)
    table = jnp.transpose(jnp.concatenate([own_factor, got_factor, filler], axis=0))
    keys, values = proj_ref[0], proj_ref[1]
    for ref, at in ((far_ref, 0), (got_ref, MIX_ROWS), (got_far_ref, 0)):
        keys += ref[at : at + step].astype(jnp.float32)
        keys += ref[at + step : at + 2 * step].astype(jnp.float32)
        values += ref[at + 2 * step : at + 3 * step].astype(jnp.float32)
    keys_high = round_bf16(keys)
    for g in range(GROUPED):
        part = slice(g * rows, (g + 1) * rows)
        tail_ref[g, :rows] = keys_high[part]
        tail_ref[g, rows : 2 * rows] = (keys - keys_high)[part]
        tail_ref[g, 2 * rows :] = values[part]
    stat_row = lax.broadcasted_iota(jnp.int32, (rows, HEAD_WIDTH), 0)
    for c, runs in enumerate(plan.attention_chunks(slot_rows)):
        span = slice(c * 128, c * 128 + 128)
        mix = mix_ref[span] * table[:, c : c + 1]
        mix += got_ref[span].astype(jnp.float32) * table[:, CHUNKS + c : CHUNKS + c + 1]
        stats = jnp.where(
            stat_row == 0,
            peak[c : c + 1],
            jnp.where(
                stat_row == 1, high[c : c + 1], jnp.where(stat_row == 2, low[c : c + 1], 0.0)
            ),
        )
        chunk = [masks for run in runs for masks, _ in run]
        for t, masks in enumerate(chunk):
            packet_ref = packet_refs[c * len(chunk) + t]
            shifted = stats if t == 0 else pltpu.roll(stats, HEAD_WIDTH - t * slot_rows, 1)
            group = ((chip // per_head) ^ (here_mask(masks, here) // per_head)) // 2
            tail = jnp.concatenate([tail_ref[group], shifted], axis=0)
            packet_ref[:slot_rows] = mix[t * slot_rows : (t + 1) * slot_rows].astype(jnp.bfloat16)
            packet_ref[slot_rows:] = tail.astype(jnp.bfloat16)


def merge_kernel(devices, requests, tokens, own_ref, cos_ref, sin_ref, *refs):
    got_refs, out_ref = refs[:-1], refs[-1]
    rows = requests * tokens
    heads = QUERY_HEADS // devices
    mix_rows = heads * rows
    sources = len(got_refs)
    tails = [ref[mix_rows:].astype(jnp.float32) for ref in got_refs]
    sums = functools.reduce(jnp.add, [tail[: 3 * rows] for tail in tails])
    keys = sums[:rows] + sums[rows : 2 * rows]
    values = sums[2 * rows :].astype(jnp.bfloat16)
    turned = pltpu.roll(keys, HEAD_WIDTH // 2, 1)
    keys = (keys * cos_ref[...] + turned * sin_ref[...]).astype(jnp.bfloat16)
    query = jnp.concatenate([own_ref[h] for h in range(heads)], axis=0)
    if mix_rows < 128:
        query = jnp.concatenate(
            [query, jnp.zeros((128 - mix_rows, HEAD_WIDTH), jnp.bfloat16)], axis=0
        )
    fresh = dot(keys, query, ((1,), (1,))) * SCALE
    source = lax.broadcasted_iota(jnp.int32, fresh.shape, 0)
    column = lax.broadcasted_iota(jnp.int32, fresh.shape, 1) % rows
    allowed = (source // tokens == column // tokens) & (source % tokens <= column % tokens)
    fresh_peak = jnp.max(jnp.where(allowed, fresh, NEG_FILL), axis=0, keepdims=True)
    stats = [tail[3 * rows :] for tail in tails]
    peak = functools.reduce(jnp.maximum, [stat[0:1] for stat in stats], fresh_peak)
    weights = jnp.where(allowed, jnp.exp(fresh - peak), 0.0)
    factors = [jnp.exp(stat[0:1] - peak) for stat in stats]
    total = functools.reduce(
        jnp.add,
        [factor * (stat[1:2] + stat[2:3]) for factor, stat in zip(factors, stats)],
        jnp.sum(weights, axis=0, keepdims=True),
    )
    inverse = 1.0 / total
    filler = jnp.zeros((128 - sources - 1, 128), jnp.float32)
    table = jnp.concatenate([factor * inverse for factor in factors] + [inverse, filler], axis=0)
    table = jnp.transpose(table)[:mix_rows]
    weights = jnp.transpose(
        jnp.concatenate([weights, jnp.zeros((128 - rows, 128), jnp.float32)], axis=0)
    )[:mix_rows].astype(jnp.bfloat16)
    values = jnp.concatenate(
        [values, jnp.zeros((128 - rows, HEAD_WIDTH), jnp.bfloat16)], axis=0
    )
    mix = dot(weights, values, ((1,), (0,))) * table[:, sources : sources + 1]
    for s, ref in enumerate(got_refs):
        mix += ref[:mix_rows].astype(jnp.float32) * table[:, s : s + 1]
    for h in range(heads):
        tile = mix[h * rows : (h + 1) * rows]
        for b in range(requests):
            out_ref[b, :, h * HEAD_WIDTH : (h + 1) * HEAD_WIDTH] = tile[
                b * tokens : (b + 1) * tokens
            ].astype(jnp.bfloat16)


def rotation(lengths, tokens):
    half = HEAD_WIDTH // 2
    places = (lengths[:, None] + jnp.arange(tokens, dtype=jnp.int32)[None, :]).astype(jnp.float32)
    inverse_freq = jnp.exp(
        jnp.arange(half, dtype=jnp.float32) * (-2.0 * math.log(ROPE_BASE) / HEAD_WIDTH)
    )
    angles = places.reshape(-1, 1) * inverse_freq[None, :]
    cosine, sine = jnp.cos(angles), jnp.sin(angles)
    return jnp.concatenate([cosine, cosine], axis=1), jnp.concatenate([-sine, sine], axis=1)


def vmem():
    return pl.BlockSpec(memory_space=pltpu.VMEM)


def smem():
    return pl.BlockSpec(memory_space=pltpu.SMEM)


def hbm():
    return pl.BlockSpec(memory_space=pltpu.HBM)


def pinned(x):
    return pltpu.with_memory_space_constraint(x, pltpu.HBM)


def cost(flops, moved):
    return pl.CostEstimate(flops=int(flops), bytes_accessed=int(moved), transcendentals=0)


def trade(x, devices, even, odd, core=0):
    pairs = [(d, d ^ (2 * (odd if d % 2 else even) + core)) for d in range(devices)]
    return lax.ppermute(x, "tensor", pairs)


def per_device(
    hidden,
    queries,
    key_value_weight,
    adapter_down_weight,
    adapter_up_weight,
    cached_key_rows,
    cached_value_rows,
    request_adapter,
    adapter_rank_list,
    adapter_pool_row,
    lengths,
):
    requests, tokens, width = hidden.shape
    rows = requests * tokens
    devices = lax.axis_size("tensor")
    sizes = (requests, tokens, devices)
    plan = Plan(devices, width)
    heads, chunks, partner = plan.heads, plan.chunks, plan.partner
    slot_rows = heads * rows
    index = lax.axis_index("tensor").reshape(1).astype(jnp.int32)
    flat = requests * cached_key_rows.shape[1]
    cached_keys = pinned(cached_key_rows.reshape(flat, -1))
    cached_values = pinned(cached_value_rows.reshape(flat, -1))
    cache = pltpu.VMEM((2, flat, GROUPED * HEAD_WIDTH), jnp.bfloat16)
    cache_sems = 2 * GROUPED

    def call(kernel, operands, in_specs, out_shape, scratch, name):
        return pl.pallas_call(
            kernel,
            out_shape=tuple(out_shape),
            in_specs=in_specs,
            out_specs=(vmem(),) * len(out_shape),
            scratch_shapes=scratch,
            compiler_params=pltpu.CompilerParams(vmem_limit_bytes=12 * MIB),
            cost_estimate=cost(10**6, 0),
            name=name,
        )(*operands)

    def core_swap(x):
        return trade(x, devices, 0, 0, core=1)

    own_queries, own_hidden, far_send = call(
        functools.partial(pack_kernel, sizes),
        (index, pinned(queries), pinned(hidden), cached_keys, cached_values),
        [smem()] + [hbm()] * 4,
        [
            pltpu.VMEM((heads, rows, HEAD_WIDTH), jnp.bfloat16),
            pltpu.VMEM((chunks, rows, HEAD_WIDTH), jnp.bfloat16),
            cache,
        ],
        [
            pltpu.VMEM(queries.shape, jnp.bfloat16),
            pltpu.VMEM(hidden.shape, jnp.bfloat16),
            pltpu.SemaphoreType.DMA((cache_sems + 2,)),
        ],
        "pack",
    )
    far_hidden = trade(own_hidden, devices, partner, partner)
    far_cache = trade(far_send, devices, partner, partner)
    out_width = key_value_weight.shape[1]
    parts = 4 if width % (4 * HEAD_WIDTH) == 0 else 1
    up = adapter_up_weight[0]
    base, own_cache, up = call(
        functools.partial(base_kernel, sizes),
        (index, own_hidden, pinned(key_value_weight), cached_keys, cached_values, pinned(up)),
        [smem(), vmem()] + [hbm()] * 4,
        [
            pltpu.VMEM((rows, out_width), jnp.float32),
            cache,
            pltpu.VMEM(up.shape, up.dtype),
        ],
        [
            pltpu.VMEM((parts, width // parts, out_width), jnp.bfloat16),
            pltpu.SemaphoreType.DMA((cache_sems + parts + 1,)),
        ],
        "base",
    )
    far_hidden, base = lax.optimization_barrier((far_hidden, base))
    own = jnp.concatenate([own_queries, own_hidden, far_hidden], axis=0)
    other = core_swap(own)
    both = jnp.concatenate([own, other], axis=0)
    near = [trade(own, devices, plan.single, plan.single)]
    near += [trade(both, devices, a, b) for a, b in plan.near_pairs]
    near = jnp.concatenate(near, axis=0)

    down = pinned(adapter_down_weight[0])
    rank = down.shape[1]
    (early, near_down) = call(
        functools.partial(early_kernel, plan),
        (index, own, other, down),
        [smem()] + [vmem()] * 2 + [hbm()],
        [
            pltpu.VMEM((rows, rank), jnp.float32),
            pltpu.VMEM((devices - 4, width, rank), jnp.bfloat16),
        ],
        [
            pltpu.VMEM((4, width, rank), jnp.bfloat16),
            pltpu.SemaphoreType.DMA((4,)),
            pltpu.SemaphoreType.DMA((devices - 4,)),
        ],
        "lora_own",
    )
    near, early, far_cache = lax.optimization_barrier((near, early, far_cache))
    other_near = core_swap(near)
    arrays = (own, other, near, other_near)
    step = GROUPED * rows
    proj, own_parts, parts = call(
        functools.partial(project_kernel, sizes, plan),
        (
            index,
            request_adapter,
            adapter_rank_list,
            adapter_pool_row,
            near,
            other_near,
            early,
            base,
            near_down,
            up,
        ),
        [smem()] * 4 + [vmem()] * 6,
        [
            pltpu.VMEM((2, step, HEAD_WIDTH), jnp.float32),
            pltpu.VMEM((3 * step, HEAD_WIDTH), jnp.bfloat16),
            pltpu.VMEM((3 * step, HEAD_WIDTH), jnp.bfloat16),
        ],
        [pltpu.VMEM((rows, out_width), jnp.float32)],
        "project",
    )
    far_parts = trade(parts, devices, partner, partner)
    (send,) = call(
        functools.partial(other_kernel, sizes, plan),
        (index, lengths) + arrays + (own_cache, far_cache, own_parts),
        [smem()] * 2 + [vmem()] * 7,
        [pltpu.VMEM((MIX_ROWS + 3 * step + STAT_ROWS, HEAD_WIDTH), jnp.bfloat16)],
        [],
        "other_lane",
    )
    got = core_swap(send)
    got_far_parts = core_swap(far_parts)
    mix, stats = call(
        functools.partial(own_kernel, sizes, plan),
        (index, lengths) + arrays + (own_cache, far_cache),
        [smem()] * 2 + [vmem()] * 6,
        [
            pltpu.VMEM((MIX_ROWS, HEAD_WIDTH), jnp.float32),
            pltpu.VMEM((8, HEAD_WIDTH), jnp.float32),
        ],
        [],
        "own_lane",
    )
    packet = pltpu.VMEM((slot_rows + 4 * rows, HEAD_WIDTH), jnp.bfloat16)
    packets = call(
        functools.partial(join_kernel, sizes, plan),
        (index, mix, stats, proj, far_parts, got, got_far_parts),
        [smem()] + [vmem()] * 6,
        [packet] * len(plan.slots),
        [pltpu.VMEM((GROUPED, 3 * rows, HEAD_WIDTH), jnp.float32)],
        "join",
    )
    packets = [
        trade(x, devices, *masks) if masks != (0, 0) else x
        for x, (masks, _) in zip(packets, plan.slots)
    ]
    cosine, sine = rotation(lengths, tokens)
    return pl.pallas_call(
        functools.partial(merge_kernel, devices, requests, tokens),
        out_shape=jax.ShapeDtypeStruct((requests, tokens, heads * HEAD_WIDTH), jnp.bfloat16),
        in_specs=[vmem()] * (3 + len(packets)),
        out_specs=vmem(),
        compiler_params=pltpu.CompilerParams(vmem_limit_bytes=8 * MIB),
        name="merge_states",
    )(own_queries, cosine, sine, *packets)


def solution(mesh):
    in_specs = (
        P("groups", None, "tensor"),
        P("groups", None, "tensor"),
        P("tensor", None),
        P("tensor", None, None),
        P("tensor", None, None),
        P("groups", "tensor", None),
        P("groups", "tensor", None),
        P("groups"),
        P(),
        P(),
        P("groups"),
    )
    out_specs = P("groups", None, "tensor")
    return jax.shard_map(
        per_device, mesh=mesh, in_specs=in_specs, out_specs=out_specs, check_vma=False
    )
```

```python
import functools
import math

import jax
import jax.numpy as jnp
from jax import lax
from jax.experimental import pallas as pl
from jax.experimental.pallas import tpu as pltpu
from jax.sharding import PartitionSpec as P

QUERY_HEADS = 128
KEY_HEADS = 8
HEAD_WIDTH = 128
ROPE_BASE = 500000.0
NEG_FILL = -1e30
SCALE = 1.0 / math.sqrt(HEAD_WIDTH)
CHUNKS = KEY_HEADS // 2
MIX_ROWS = CHUNKS * 128
STAT_ROWS = 16
MIB = 2**20


def dot(a, b, dims):
    return lax.dot_general(a, b, (dims, ((), ())), preferred_element_type=jnp.float32)


def round_bf16(x):
    return x.astype(jnp.bfloat16).astype(jnp.float32)


class Plan:
    def __init__(self, devices, width):
        lanes = devices // 2
        self.per_head = per_head = lanes // KEY_HEADS
        self.heads, self.chunks = QUERY_HEADS // devices, width // HEAD_WIDTH
        if per_head > 1:
            self.single = 1
            self.pairs = [(m, m ^ 1) for m in range(lanes - 2, 0, -2)]
        else:
            self.single = lanes - 1
            self.pairs = [(m, m + 1) for m in range(lanes - 3, 0, -2)]
        size = self.heads + self.chunks
        self.own = ((0, 0), ((0, 0), (1, 0)))
        self.one = ((self.single,) * 2, ((2, 0), (3, 0)))
        self.mine, self.theirs = [], []
        for k, (a, b) in enumerate(self.pairs):
            self.mine.append(((a, b), ((4 + 2 * k, 0), (4 + 2 * k, size))))
            self.theirs.append(((b, a), ((5 + 2 * k, size), (5 + 2 * k, 0))))

    def head_masks(self, unit):
        return tuple(mask // self.per_head for mask in unit[0][0])

    def units(self, keep):
        if keep:
            units = [(self.own, 0), (self.one, 0)]
            units += [(slot, side) for slot in self.mine for side in (0, 1)]
        else:
            units = [(self.own, 1), (self.one, 1)]
            units += [(slot, side) for slot in self.theirs for side in (1, 0)]
        if self.per_head > 1:
            units.sort(key=self.head_masks)
        return units

    def attention_chunks(self, slot_rows, keep):
        units = self.units(keep)
        count = HEAD_WIDTH // slot_rows
        chunks = []
        for at in range(0, len(units), count):
            runs = []
            for unit in units[at : at + count]:
                if runs and self.head_masks(runs[-1][0]) == self.head_masks(unit):
                    runs[-1].append(unit)
                else:
                    runs.append([unit])
            chunks.append(runs)
        return chunks

    def slots(self):
        return [self.own, self.one] + self.mine + self.theirs


def here_mask(masks, here):
    return masks[0] if masks[0] == masks[1] else jnp.where(here % 2 == 0, masks[0], masks[1])


def head_columns(head):
    return pl.ds(pl.multiple_of(head * HEAD_WIDTH, HEAD_WIDTH), HEAD_WIDTH)


def sources_of(plan):
    return [
        (array, tile + plan.heads, masks, side)
        for masks, places in plan.slots()
        for side, (array, tile) in enumerate(places)
    ]


def streams(sources, index_ref, down_ref, halves, sems):
    count, depth = halves[0].shape[:2]
    here = index_ref[0]
    copies = []
    for at, (_, _, masks, side) in enumerate(sources):
        source = here ^ (2 * here_mask(masks, here) + side)
        rows = pl.ds(pl.multiple_of(source * depth, depth), depth)
        place = halves[at // count].at[at % count]
        copies.append(pltpu.make_async_copy(down_ref.at[rows], place, sems.at[at]))
    return copies


def lower(sources, arrays, halves):
    total = None
    count, depth = halves[0].shape[:2]
    for at, (array, first, _, _) in enumerate(sources):
        tiles = range(first, first + depth // HEAD_WIDTH)
        hidden = jnp.concatenate([arrays[array][c] for c in tiles], axis=1)
        term = dot(hidden, halves[at // count][at % count], ((1,), (0,)))
        total = term if total is None else total + term
    return total


def pack_kernel(requests, query_ref, hidden_ref, own_ref, query_buf, hidden_buf, sems):
    loads = [
        pltpu.make_async_copy(query_ref, query_buf, sems.at[0]),
        pltpu.make_async_copy(hidden_ref, hidden_buf, sems.at[1]),
    ]
    for load in loads:
        load.start()
    at = 0
    for load, ref in zip(loads, (query_buf, hidden_buf)):
        load.wait()
        rows = jnp.concatenate([ref[b].astype(jnp.float32) for b in range(requests)], axis=0)
        for c in range(rows.shape[1] // HEAD_WIDTH):
            tile = rows[:, c * HEAD_WIDTH : (c + 1) * HEAD_WIDTH]
            own_ref[at] = tile.astype(jnp.bfloat16)
            at += 1


def base_kernel(plan, index_ref, own_ref, weight_ref, *refs):
    down_ref, *sources = refs[:4]
    base_ref, *held = refs[4:8]
    halves, (buffer, sems, down_sems) = refs[8:10], refs[10:]
    parts, depth = buffer.shape[:2]
    loads = [
        pltpu.make_async_copy(weight_ref.at[pl.ds(p * depth, depth)], buffer.at[p], sems.at[p])
        for p in range(parts)
    ]
    others = [
        pltpu.make_async_copy(source, place, sems.at[parts + i])
        for i, (source, place) in enumerate(zip(sources, held))
    ]
    others += streams(sources_of(plan), index_ref, down_ref, halves, down_sems)
    for load in loads + others:
        load.start()
    tiles = depth // HEAD_WIDTH
    total = jnp.zeros(base_ref.shape, jnp.float32)
    for p in range(parts):
        first = plan.heads + p * tiles
        hidden = jnp.concatenate([own_ref[first + c] for c in range(tiles)], axis=1)
        loads[p].wait()
        total += dot(hidden, buffer[p], ((1,), (0,)))
    base_ref[...] = total
    for load in others:
        load.wait()


def project_kernel(sizes, plan, *refs):
    (index_ref, adapter_ref, rank_ref, pool_ref, *arrays) = refs[:-6]
    (base_ref, up_ref, *halves, own_ref, parts_ref) = refs[-6:]
    requests, tokens, devices = sizes
    rows = requests * tokens
    lowered = lower(sources_of(plan), arrays, halves)
    row_request = lax.broadcasted_iota(jnp.int32, (rows, 1), 0) // tokens
    ranks = jnp.zeros((rows, 1), jnp.int32)
    owners = jnp.zeros((rows, 1), jnp.int32)
    for b in range(requests):
        adapter = adapter_ref[b]
        ranks = jnp.where(row_request == b, rank_ref[adapter], ranks)
        owners = jnp.where(row_request == b, pool_ref[adapter], owners)
    column = lax.broadcasted_iota(jnp.int32, lowered.shape, 1)
    lowered = jnp.where(column < ranks, lowered, 0.0).astype(jnp.bfloat16)
    lifted = dot(lowered, up_ref[...], ((1,), (0,)))
    projected = base_ref[...] + jnp.where(owners == index_ref[0], lifted, 0.0)
    split = KEY_HEADS * HEAD_WIDTH
    step = KEY_HEADS * rows
    keys, values = [
        jnp.concatenate(
            [projected[:, at + j * HEAD_WIDTH : at + (j + 1) * HEAD_WIDTH] for j in range(KEY_HEADS)],
            axis=0,
        )
        for at in (0, split)
    ]
    own_ref[0] = keys
    own_ref[1] = values
    high = keys.astype(jnp.bfloat16)
    parts_ref[:step] = high
    parts_ref[step : 2 * step] = (keys - high.astype(jnp.float32)).astype(jnp.bfloat16)
    parts_ref[2 * step :] = values.astype(jnp.bfloat16)


def attend(sizes, plan, keep, index_ref, length_ref, arrays, key_ref, value_ref, put):
    requests, tokens, devices = sizes
    here = index_ref[0]
    chip = here // 2
    per_head = plan.per_head
    slot_rows = plan.heads * requests * tokens
    positions = key_ref.shape[0] // requests
    place = lax.broadcasted_iota(jnp.int32, (requests * positions, HEAD_WIDTH), 0)
    column = lax.broadcasted_iota(jnp.int32, (requests * positions, HEAD_WIDTH), 1)
    place_request = place // positions
    limit = jnp.zeros_like(place)
    for b in range(requests):
        limit = jnp.where(place_request == b, length_ref[b], limit)
    allowed = (here * positions + place % positions < limit) & (
        place_request == (column // tokens) % requests
    )
    peaks, totals = [], []
    for number, runs in enumerate(plan.attention_chunks(slot_rows, keep)):
        places = [slot[1][side] for run in runs for slot, side in run]
        query = jnp.concatenate(
            [arrays[array][tile + h] for array, tile in places for h in range(plan.heads)], axis=0
        )
        spots = [
            head_columns((chip // per_head) ^ (here_mask(run[0][0][0], here) // per_head))
            for run in runs
        ]
        share = HEAD_WIDTH // len(runs)
        scores = None
        for i, spot in enumerate(spots):
            part = dot(key_ref[:, spot], query, ((1,), (1,)))
            scores = part if scores is None else jnp.where(column < i * share, scores, part)
        scores = scores * SCALE
        peak = jnp.max(jnp.where(allowed, scores, NEG_FILL), axis=0, keepdims=True)
        peak = round_bf16(peak)
        weights = jnp.where(allowed, jnp.exp(scores - peak), 0.0)
        peaks.append(peak)
        totals.append(jnp.sum(weights, axis=0, keepdims=True))
        weights = jnp.transpose(weights.astype(jnp.bfloat16))
        for i, spot in enumerate(spots):
            own = slice(i * share, (i + 1) * share)
            put(number, i * share, dot(weights[own], value_ref[:, spot], ((1,), (0,))))
    return peaks, totals


def rows_of(items, count):
    row = lax.broadcasted_iota(jnp.int32, (count, HEAD_WIDTH), 0)
    out = jnp.zeros((count, HEAD_WIDTH), jnp.float32)
    for i, item in enumerate(items):
        out = jnp.where(row == i, item, out)
    return out


def send_kernel(sizes, plan, *refs):
    (index_ref, length_ref, *arrays, key_ref, value_ref, send_ref) = refs

    def put(chunk, row, mix):
        at = chunk * 128 + row
        send_ref[at : at + mix.shape[0]] = mix.astype(jnp.bfloat16)

    peaks, totals = attend(
        sizes, plan, False, index_ref, length_ref, arrays, key_ref, value_ref, put
    )
    highs = [round_bf16(total) for total in totals]
    lows = [total - high for total, high in zip(totals, highs)]
    send_ref[MIX_ROWS:] = rows_of(peaks + highs + lows, STAT_ROWS).astype(jnp.bfloat16)


def keep_kernel(sizes, plan, *refs):
    (index_ref, length_ref, *arrays, key_ref, value_ref, mix_ref, stat_ref) = refs

    def put(chunk, row, mix):
        at = chunk * 128 + row
        mix_ref[at : at + mix.shape[0]] = mix

    peaks, totals = attend(
        sizes, plan, True, index_ref, length_ref, arrays, key_ref, value_ref, put
    )
    stat_ref[...] = rows_of(peaks + totals, 8)


def join_kernel(sizes, plan, index_ref, mix_ref, stat_ref, proj_ref, got_parts_ref, got_ref, *refs):
    packet_refs, tail_ref = refs[:-1], refs[-1]
    requests, tokens, devices = sizes
    here = index_ref[0]
    chip = here // 2
    per_head = plan.per_head
    rows = requests * tokens
    slot_rows = plan.heads * rows
    step = KEY_HEADS * rows
    got = got_ref[MIX_ROWS:].astype(jnp.float32)
    own = stat_ref[...]
    own_peak, got_peak = own[:CHUNKS], got[:CHUNKS]
    peak = jnp.maximum(own_peak, got_peak)
    own_factor = jnp.exp(own_peak - peak)
    got_factor = jnp.exp(got_peak - peak)
    total = own_factor * own[CHUNKS : 2 * CHUNKS] + got_factor * (
        got[CHUNKS : 2 * CHUNKS] + got[2 * CHUNKS : 3 * CHUNKS]
    )
    high = round_bf16(total)
    low = total - high
    filler = jnp.zeros((128 - 2 * CHUNKS, 128), jnp.float32)
    table = jnp.transpose(jnp.concatenate([own_factor, got_factor, filler], axis=0))
    keys = proj_ref[0] + got_parts_ref[:step].astype(jnp.float32)
    keys += got_parts_ref[step : 2 * step].astype(jnp.float32)
    values = proj_ref[1] + got_parts_ref[2 * step :].astype(jnp.float32)
    keys_high = round_bf16(keys)
    for j in range(KEY_HEADS):
        part = slice(j * rows, (j + 1) * rows)
        tail_ref[j, :rows] = keys_high[part]
        tail_ref[j, rows : 2 * rows] = (keys - keys_high)[part]
        tail_ref[j, 2 * rows :] = values[part]
    stat_row = lax.broadcasted_iota(jnp.int32, (rows, HEAD_WIDTH), 0)
    packet = {id(slot): ref for slot, ref in zip([plan.own, plan.one] + plan.mine, packet_refs)}
    for c, runs in enumerate(plan.attention_chunks(slot_rows, True)):
        span = slice(c * 128, c * 128 + 128)
        mix = mix_ref[span] * table[:, c : c + 1]
        mix += got_ref[span].astype(jnp.float32) * table[:, CHUNKS + c : CHUNKS + c + 1]
        stats = jnp.where(
            stat_row == 0,
            peak[c : c + 1],
            jnp.where(
                stat_row == 1, high[c : c + 1], jnp.where(stat_row == 2, low[c : c + 1], 0.0)
            ),
        )
        for t, (slot, side) in enumerate(unit for run in runs for unit in run):
            packet_ref = packet[id(slot)]
            at = side * slot_rows
            packet_ref[at : at + slot_rows] = mix[t * slot_rows : (t + 1) * slot_rows].astype(
                jnp.bfloat16
            )
            if side == 0:
                shifted = stats if t == 0 else pltpu.roll(stats, HEAD_WIDTH - t * slot_rows, 1)
                head = (chip // per_head) ^ (here_mask(slot[0], here) // per_head)
                tail = jnp.concatenate([tail_ref[head], shifted], axis=0)
                packet_ref[packet_ref.shape[0] - 4 * rows :] = tail.astype(jnp.bfloat16)


def merge_kernel(devices, requests, tokens, swapped, own_ref, cos_ref, sin_ref, *refs):
    got_refs, out_ref = refs[:-1], refs[-1]
    rows = requests * tokens
    heads = QUERY_HEADS // devices
    mix_rows = heads * rows
    sources = len(got_refs)
    tails = [ref[ref.shape[0] - 4 * rows :].astype(jnp.float32) for ref in got_refs]
    sums = functools.reduce(jnp.add, [tail[: 3 * rows] for tail in tails])
    keys = sums[:rows] + sums[rows : 2 * rows]
    values = sums[2 * rows :].astype(jnp.bfloat16)
    turned = pltpu.roll(keys, HEAD_WIDTH // 2, 1)
    keys = (keys * cos_ref[...] + turned * sin_ref[...]).astype(jnp.bfloat16)
    query = jnp.concatenate([own_ref[h] for h in range(heads)], axis=0)
    if mix_rows < 128:
        query = jnp.concatenate(
            [query, jnp.zeros((128 - mix_rows, HEAD_WIDTH), jnp.bfloat16)], axis=0
        )
    fresh = dot(keys, query, ((1,), (1,))) * SCALE
    source = lax.broadcasted_iota(jnp.int32, fresh.shape, 0)
    column = lax.broadcasted_iota(jnp.int32, fresh.shape, 1) % rows
    allowed = (source // tokens == column // tokens) & (source % tokens <= column % tokens)
    fresh_peak = jnp.max(jnp.where(allowed, fresh, NEG_FILL), axis=0, keepdims=True)
    stats = [tail[3 * rows :] for tail in tails]
    for s in range(swapped, sources):
        stats[s] = pltpu.roll(stats[s], HEAD_WIDTH - mix_rows, 1)
    peak = functools.reduce(jnp.maximum, [stat[0:1] for stat in stats], fresh_peak)
    weights = jnp.where(allowed, jnp.exp(fresh - peak), 0.0)
    factors = [jnp.exp(stat[0:1] - peak) for stat in stats]
    total = functools.reduce(
        jnp.add,
        [factor * (stat[1:2] + stat[2:3]) for factor, stat in zip(factors, stats)],
        jnp.sum(weights, axis=0, keepdims=True),
    )
    inverse = 1.0 / total
    filler = jnp.zeros((128 - sources - 1, 128), jnp.float32)
    table = jnp.concatenate([factor * inverse for factor in factors] + [inverse, filler], axis=0)
    table = jnp.transpose(table)[:mix_rows]
    weights = jnp.transpose(
        jnp.concatenate([weights, jnp.zeros((128 - rows, 128), jnp.float32)], axis=0)
    )[:mix_rows].astype(jnp.bfloat16)
    values = jnp.concatenate(
        [values, jnp.zeros((128 - rows, HEAD_WIDTH), jnp.bfloat16)], axis=0
    )
    mix = dot(weights, values, ((1,), (0,))) * table[:, sources : sources + 1]
    for s, ref in enumerate(got_refs):
        mix += ref[:mix_rows].astype(jnp.float32) * table[:, s : s + 1]
    for h in range(heads):
        tile = mix[h * rows : (h + 1) * rows]
        for b in range(requests):
            out_ref[b, :, h * HEAD_WIDTH : (h + 1) * HEAD_WIDTH] = tile[
                b * tokens : (b + 1) * tokens
            ].astype(jnp.bfloat16)


def rotation(lengths, tokens):
    half = HEAD_WIDTH // 2
    places = (lengths[:, None] + jnp.arange(tokens, dtype=jnp.int32)[None, :]).astype(jnp.float32)
    inverse_freq = jnp.exp(
        jnp.arange(half, dtype=jnp.float32) * (-2.0 * math.log(ROPE_BASE) / HEAD_WIDTH)
    )
    angles = places.reshape(-1, 1) * inverse_freq[None, :]
    cosine, sine = jnp.cos(angles), jnp.sin(angles)
    return jnp.concatenate([cosine, cosine], axis=1), jnp.concatenate([-sine, sine], axis=1)


def vmem():
    return pl.BlockSpec(memory_space=pltpu.VMEM)


def smem():
    return pl.BlockSpec(memory_space=pltpu.SMEM)


def hbm():
    return pl.BlockSpec(memory_space=pltpu.HBM)


def pinned(x):
    return pltpu.with_memory_space_constraint(x, pltpu.HBM)


def cost(flops, moved):
    return pl.CostEstimate(flops=int(flops), bytes_accessed=int(moved), transcendentals=0)


def trade(x, devices, even, odd, core=0):
    pairs = [(d, d ^ (2 * (odd if d % 2 else even) + core)) for d in range(devices)]
    return lax.ppermute(x, "tensor", pairs)


def per_device(
    hidden,
    queries,
    key_value_weight,
    adapter_down_weight,
    adapter_up_weight,
    cached_key_rows,
    cached_value_rows,
    request_adapter,
    adapter_rank_list,
    adapter_pool_row,
    lengths,
):
    requests, tokens, width = hidden.shape
    rows = requests * tokens
    devices = lax.axis_size("tensor")
    sizes = (requests, tokens, devices)
    plan = Plan(devices, width)
    heads, chunks = plan.heads, plan.chunks
    slot_rows = heads * rows
    index = lax.axis_index("tensor").reshape(1).astype(jnp.int32)

    def call(kernel, operands, in_specs, out_shape, scratch, name):
        return pl.pallas_call(
            kernel,
            out_shape=tuple(out_shape),
            in_specs=in_specs,
            out_specs=(vmem(),) * len(out_shape),
            scratch_shapes=scratch,
            compiler_params=pltpu.CompilerParams(vmem_limit_bytes=12 * MIB),
            cost_estimate=cost(10**6, 0),
            name=name,
        )(*operands)

    def core_swap(x):
        return trade(x, devices, 0, 0, core=1)

    (own,) = call(
        functools.partial(pack_kernel, requests),
        (pinned(queries), pinned(hidden)),
        [hbm()] * 2,
        [pltpu.VMEM((heads + chunks, rows, HEAD_WIDTH), jnp.bfloat16)],
        [
            pltpu.VMEM(queries.shape, jnp.bfloat16),
            pltpu.VMEM(hidden.shape, jnp.bfloat16),
            pltpu.SemaphoreType.DMA((2,)),
        ],
        "pack",
    )
    other = core_swap(own)
    one = trade(own, devices, plan.single, plan.single)
    both = jnp.concatenate([own, other], axis=0)
    mine = [trade(both, devices, a, b) for a, b in plan.pairs]

    flat = requests * cached_key_rows.shape[1]
    big = (
        cached_key_rows.reshape(flat, -1),
        cached_value_rows.reshape(flat, -1),
        adapter_up_weight[0],
    )
    out_width = key_value_weight.shape[1]
    parts = 4 if width % (4 * HEAD_WIDTH) == 0 else 1
    down = adapter_down_weight[0]
    half = pltpu.VMEM((devices // 2, width, down.shape[1]), jnp.bfloat16)
    base, keys, values, up, *halves = call(
        functools.partial(base_kernel, plan),
        (index, own, pinned(key_value_weight), pinned(down)) + tuple(pinned(x) for x in big),
        [smem(), vmem()] + [hbm()] * 5,
        [pltpu.VMEM((rows, out_width), jnp.float32)]
        + [pltpu.VMEM(x.shape, x.dtype) for x in big]
        + [half, half],
        [
            pltpu.VMEM((parts, width // parts, out_width), jnp.bfloat16),
            pltpu.SemaphoreType.DMA((parts + 3,)),
            pltpu.SemaphoreType.DMA((devices,)),
        ],
        "base",
    )
    one, mine[0], base = lax.optimization_barrier((one, mine[0], base))
    arrays = [own, other, one, core_swap(one)]
    for x in mine:
        arrays += [x, core_swap(x)]
    arrays = tuple(arrays)
    step = KEY_HEADS * rows
    proj, proj_parts = call(
        functools.partial(project_kernel, sizes, plan),
        (index, request_adapter, adapter_rank_list, adapter_pool_row)
        + arrays
        + (base, up, *halves),
        [smem()] * 4 + [vmem()] * (len(arrays) + 4),
        [
            pltpu.VMEM((2, step, HEAD_WIDTH), jnp.float32),
            pltpu.VMEM((3 * step, HEAD_WIDTH), jnp.bfloat16),
        ],
        [],
        "project",
    )
    got_parts = core_swap(proj_parts)
    (send,) = call(
        functools.partial(send_kernel, sizes, plan),
        (index, lengths) + arrays + (keys, values),
        [smem()] * 2 + [vmem()] * (len(arrays) + 2),
        [pltpu.VMEM((MIX_ROWS + STAT_ROWS, HEAD_WIDTH), jnp.bfloat16)],
        [],
        "send_states",
    )
    got = core_swap(send)
    mix, stats = call(
        functools.partial(keep_kernel, sizes, plan),
        (index, lengths) + arrays + (keys, values),
        [smem()] * 2 + [vmem()] * (len(arrays) + 2),
        [
            pltpu.VMEM((MIX_ROWS, HEAD_WIDTH), jnp.float32),
            pltpu.VMEM((8, HEAD_WIDTH), jnp.float32),
        ],
        [],
        "keep_states",
    )
    packets = call(
        functools.partial(join_kernel, sizes, plan),
        (index, mix, stats, proj, got_parts, got),
        [smem()] + [vmem()] * 5,
        [pltpu.VMEM((slot_rows + 4 * rows, HEAD_WIDTH), jnp.bfloat16)] * 2
        + [pltpu.VMEM((2 * slot_rows + 4 * rows, HEAD_WIDTH), jnp.bfloat16)] * len(plan.pairs),
        [pltpu.VMEM((KEY_HEADS, 3 * rows, HEAD_WIDTH), jnp.float32)],
        "join",
    )
    heard = [packets[0], trade(packets[1], devices, plan.single, plan.single)]
    heard += [trade(x, devices, a, b) for x, (a, b) in zip(packets[2:], plan.pairs)]
    heard[1], heard[2] = lax.optimization_barrier((heard[1], heard[2]))
    heard += [core_swap(x[slot_rows:]) for x in heard[2:]]
    cosine, sine = rotation(lengths, tokens)
    return pl.pallas_call(
        functools.partial(merge_kernel, devices, requests, tokens, 2 + len(plan.pairs)),
        out_shape=jax.ShapeDtypeStruct((requests, tokens, heads * HEAD_WIDTH), jnp.bfloat16),
        in_specs=[vmem()] * (3 + len(heard)),
        out_specs=vmem(),
        compiler_params=pltpu.CompilerParams(vmem_limit_bytes=8 * MIB),
        name="merge_states",
    )(own, cosine, sine, *heard)


def solution(mesh):
    in_specs = (
        P("groups", None, "tensor"),
        P("groups", None, "tensor"),
        P("tensor", None),
        P("tensor", None, None),
        P("tensor", None, None),
        P("groups", "tensor", None),
        P("groups", "tensor", None),
        P("groups"),
        P(),
        P(),
        P("groups"),
    )
    out_specs = P("groups", None, "tensor")
    return jax.shard_map(
        per_device, mesh=mesh, in_specs=in_specs, out_specs=out_specs, check_vma=False
    )
```

```python
import functools
import math

import jax
import jax.numpy as jnp
from jax import lax
from jax.experimental import pallas as pl
from jax.experimental.pallas import tpu as pltpu
from jax.sharding import PartitionSpec as P

QUERY_HEADS = 128
KEY_HEADS = 8
HEAD_WIDTH = 128
ROPE_BASE = 500000.0
NEG_FILL = -1e30
SCALE = 1.0 / math.sqrt(HEAD_WIDTH)
CHUNKS = KEY_HEADS // 2
MIX_ROWS = CHUNKS * 128
STAT_ROWS = 16
MIB = 2**20


def dot(a, b, dims):
    return lax.dot_general(a, b, (dims, ((), ())), preferred_element_type=jnp.float32)


def round_bf16(x):
    return x.astype(jnp.bfloat16).astype(jnp.float32)


class Plan:
    def __init__(self, devices, width):
        lanes = devices // 2
        self.per_head = per_head = lanes // KEY_HEADS
        self.heads, self.chunks = QUERY_HEADS // devices, width // HEAD_WIDTH
        self.single = 1
        self.pairs = [(m, m + 1) for m in range(lanes - 2, 0, -2)]
        size = self.heads + self.chunks
        self.own = ((0, 0), ((0, 0), (1, 0)))
        self.one = ((self.single,) * 2, ((2, 0), (3, 0)))
        self.mine, self.theirs = [], []
        for k, (a, b) in enumerate(self.pairs):
            at = 2 * size * k
            self.mine.append(((a, b), ((4, at), (4, at + size))))
            self.theirs.append(((b, a), ((5, at + size), (5, at))))

    def head_masks(self, unit):
        return tuple(mask // self.per_head for mask in unit[0][0])

    def units(self, keep):
        if keep:
            units = [(self.own, 0), (self.one, 0)]
            units += [(slot, side) for slot in self.mine for side in (0, 1)]
        else:
            units = [(self.own, 1), (self.one, 1)]
            units += [(slot, side) for slot in self.theirs for side in (1, 0)]
        if self.per_head > 1:
            units.sort(key=self.head_masks)
        return units

    def attention_chunks(self, slot_rows, keep):
        units = self.units(keep)
        count = HEAD_WIDTH // slot_rows
        chunks = []
        for at in range(0, len(units), count):
            runs = []
            for unit in units[at : at + count]:
                if runs and self.head_masks(runs[-1][0]) == self.head_masks(unit):
                    runs[-1].append(unit)
                else:
                    runs.append([unit])
            chunks.append(runs)
        return chunks

    def slots(self):
        return [self.own, self.one] + self.mine + self.theirs


def here_mask(masks, here):
    return masks[0] if masks[0] == masks[1] else jnp.where(here % 2 == 0, masks[0], masks[1])


def head_columns(head):
    return pl.ds(pl.multiple_of(head * HEAD_WIDTH, HEAD_WIDTH), HEAD_WIDTH)


def sources_of(plan):
    return [
        (array, tile + plan.heads, masks, side)
        for masks, places in plan.slots()
        for side, (array, tile) in enumerate(places)
    ]


def streams(sources, index_ref, down_ref, half_ref, sems):
    depth = half_ref.shape[1]
    here = index_ref[0]
    copies = []
    for at, (_, _, masks, side) in enumerate(sources):
        source = here ^ (2 * here_mask(masks, here) + side)
        rows = pl.ds(pl.multiple_of(source * depth, depth), depth)
        copies.append(pltpu.make_async_copy(down_ref.at[rows], half_ref.at[at], sems.at[at]))
    return copies


def lower(sources, arrays, halves):
    total = None
    count, depth = halves[0].shape[:2]
    for at, (array, first, _, _) in enumerate(sources):
        tiles = range(first, first + depth // HEAD_WIDTH)
        hidden = jnp.concatenate([arrays[array][c] for c in tiles], axis=1)
        term = dot(hidden, halves[at // count][at % count], ((1,), (0,)))
        total = term if total is None else total + term
    return total


def pack_kernel(requests, query_ref, hidden_ref, own_ref, query_buf, hidden_buf, sems):
    loads = [
        pltpu.make_async_copy(query_ref, query_buf, sems.at[0]),
        pltpu.make_async_copy(hidden_ref, hidden_buf, sems.at[1]),
    ]
    for load in loads:
        load.start()
    at = 0
    for load, ref in zip(loads, (query_buf, hidden_buf)):
        load.wait()
        rows = jnp.concatenate([ref[b].astype(jnp.float32) for b in range(requests)], axis=0)
        for c in range(rows.shape[1] // HEAD_WIDTH):
            tile = rows[:, c * HEAD_WIDTH : (c + 1) * HEAD_WIDTH]
            own_ref[at] = tile.astype(jnp.bfloat16)
            at += 1


def base_kernel(heads, own_ref, weight_ref, *refs):
    sources, base_ref, held = refs[:3], refs[3], refs[4:7]
    buffer, sems = refs[7:]
    parts, depth = buffer.shape[:2]
    loads = [
        pltpu.make_async_copy(weight_ref.at[pl.ds(p * depth, depth)], buffer.at[p], sems.at[p])
        for p in range(parts)
    ]
    others = [
        pltpu.make_async_copy(source, place, sems.at[parts + i])
        for i, (source, place) in enumerate(zip(sources, held))
    ]
    for load in loads + others:
        load.start()
    tiles = depth // HEAD_WIDTH
    total = jnp.zeros(base_ref.shape, jnp.float32)
    for p in range(parts):
        hidden = jnp.concatenate([own_ref[heads + p * tiles + c] for c in range(tiles)], axis=1)
        loads[p].wait()
        total += dot(hidden, buffer[p], ((1,), (0,)))
    base_ref[...] = total
    for load in others:
        load.wait()


def fetch_kernel(sources, index_ref, down_ref, half_ref, sems):
    copies = streams(sources, index_ref, down_ref, half_ref, sems)
    for copy in copies:
        copy.start()
    for copy in copies:
        copy.wait()


def attend(sizes, plan, keep, index_ref, length_ref, arrays, key_ref, value_ref, put):
    requests, tokens, devices = sizes
    here = index_ref[0]
    chip = here // 2
    per_head = plan.per_head
    slot_rows = plan.heads * requests * tokens
    positions = key_ref.shape[0] // requests
    place = lax.broadcasted_iota(jnp.int32, (requests * positions, HEAD_WIDTH), 0)
    column = lax.broadcasted_iota(jnp.int32, (requests * positions, HEAD_WIDTH), 1)
    place_request = place // positions
    limit = jnp.zeros_like(place)
    for b in range(requests):
        limit = jnp.where(place_request == b, length_ref[b], limit)
    allowed = (here * positions + place % positions < limit) & (
        place_request == (column // tokens) % requests
    )
    peaks, totals = [], []
    for number, runs in enumerate(plan.attention_chunks(slot_rows, keep)):
        places = [slot[1][side] for run in runs for slot, side in run]
        query = jnp.concatenate(
            [arrays[array][tile + h] for array, tile in places for h in range(plan.heads)], axis=0
        )
        spots = [
            head_columns((chip // per_head) ^ (here_mask(run[0][0][0], here) // per_head))
            for run in runs
        ]
        share = HEAD_WIDTH // len(runs)
        scores = None
        for i, spot in enumerate(spots):
            part = dot(key_ref[:, spot], query, ((1,), (1,)))
            scores = part if scores is None else jnp.where(column < i * share, scores, part)
        scores = scores * SCALE
        peak = jnp.max(jnp.where(allowed, scores, NEG_FILL), axis=0, keepdims=True)
        peak = round_bf16(peak)
        weights = jnp.where(allowed, jnp.exp(scores - peak), 0.0)
        peaks.append(peak)
        totals.append(jnp.sum(weights, axis=0, keepdims=True))
        weights = jnp.transpose(weights.astype(jnp.bfloat16))
        for i, spot in enumerate(spots):
            own = slice(i * share, (i + 1) * share)
            put(number, i * share, dot(weights[own], value_ref[:, spot], ((1,), (0,))))
    return peaks, totals


def rows_of(items, count):
    row = lax.broadcasted_iota(jnp.int32, (count, HEAD_WIDTH), 0)
    out = jnp.zeros((count, HEAD_WIDTH), jnp.float32)
    for i, item in enumerate(items):
        out = jnp.where(row == i, item, out)
    return out


def send_kernel(sizes, plan, *refs):
    (index_ref, length_ref, adapter_ref, rank_ref, pool_ref, *arrays) = refs[:-9]
    (key_ref, value_ref, base_ref, up_ref, *halves, send_ref, own_ref, parts_ref) = refs[-9:]
    requests, tokens, devices = sizes

    def put(chunk, row, mix):
        at = chunk * 128 + row
        send_ref[at : at + mix.shape[0]] = mix.astype(jnp.bfloat16)

    peaks, totals = attend(
        sizes, plan, False, index_ref, length_ref, arrays, key_ref, value_ref, put
    )
    highs = [round_bf16(total) for total in totals]
    lows = [total - high for total, high in zip(totals, highs)]
    send_ref[MIX_ROWS:] = rows_of(peaks + highs + lows, STAT_ROWS).astype(jnp.bfloat16)

    rows = requests * tokens
    lowered = lower(sources_of(plan), arrays, halves)
    row_request = lax.broadcasted_iota(jnp.int32, (rows, 1), 0) // tokens
    ranks = jnp.zeros((rows, 1), jnp.int32)
    owners = jnp.zeros((rows, 1), jnp.int32)
    for b in range(requests):
        adapter = adapter_ref[b]
        ranks = jnp.where(row_request == b, rank_ref[adapter], ranks)
        owners = jnp.where(row_request == b, pool_ref[adapter], owners)
    column = lax.broadcasted_iota(jnp.int32, lowered.shape, 1)
    lowered = jnp.where(column < ranks, lowered, 0.0).astype(jnp.bfloat16)
    lifted = dot(lowered, up_ref[...], ((1,), (0,)))
    projected = base_ref[...] + jnp.where(owners == index_ref[0], lifted, 0.0)
    split = KEY_HEADS * HEAD_WIDTH
    step = KEY_HEADS * rows
    keys, values = [
        jnp.concatenate(
            [projected[:, at + j * HEAD_WIDTH : at + (j + 1) * HEAD_WIDTH] for j in range(KEY_HEADS)],
            axis=0,
        )
        for at in (0, split)
    ]
    own_ref[0] = keys
    own_ref[1] = values
    high = keys.astype(jnp.bfloat16)
    parts_ref[:step] = high
    parts_ref[step : 2 * step] = (keys - high.astype(jnp.float32)).astype(jnp.bfloat16)
    parts_ref[2 * step :] = values.astype(jnp.bfloat16)


def keep_kernel(sizes, plan, *refs):
    (index_ref, length_ref, *arrays, key_ref, value_ref, mix_ref, stat_ref) = refs

    def put(chunk, row, mix):
        at = chunk * 128 + row
        mix_ref[at : at + mix.shape[0]] = mix

    peaks, totals = attend(
        sizes, plan, True, index_ref, length_ref, arrays, key_ref, value_ref, put
    )
    stat_ref[...] = rows_of(peaks + totals, 8)


def join_kernel(sizes, plan, index_ref, mix_ref, stat_ref, proj_ref, got_parts_ref, got_ref, *refs):
    packet_refs, tail_ref = refs[:-1], refs[-1]
    requests, tokens, devices = sizes
    here = index_ref[0]
    chip = here // 2
    per_head = plan.per_head
    rows = requests * tokens
    slot_rows = plan.heads * rows
    step = KEY_HEADS * rows
    got = got_ref[MIX_ROWS:].astype(jnp.float32)
    own = stat_ref[...]
    own_peak, got_peak = own[:CHUNKS], got[:CHUNKS]
    peak = jnp.maximum(own_peak, got_peak)
    own_factor = jnp.exp(own_peak - peak)
    got_factor = jnp.exp(got_peak - peak)
    total = own_factor * own[CHUNKS : 2 * CHUNKS] + got_factor * (
        got[CHUNKS : 2 * CHUNKS] + got[2 * CHUNKS : 3 * CHUNKS]
    )
    high = round_bf16(total)
    low = total - high
    filler = jnp.zeros((128 - 2 * CHUNKS, 128), jnp.float32)
    table = jnp.transpose(jnp.concatenate([own_factor, got_factor, filler], axis=0))
    keys = proj_ref[0] + got_parts_ref[:step].astype(jnp.float32)
    keys += got_parts_ref[step : 2 * step].astype(jnp.float32)
    values = proj_ref[1] + got_parts_ref[2 * step :].astype(jnp.float32)
    keys_high = round_bf16(keys)
    for j in range(KEY_HEADS):
        part = slice(j * rows, (j + 1) * rows)
        tail_ref[j, :rows] = keys_high[part]
        tail_ref[j, rows : 2 * rows] = (keys - keys_high)[part]
        tail_ref[j, 2 * rows :] = values[part]
    stat_row = lax.broadcasted_iota(jnp.int32, (rows, HEAD_WIDTH), 0)
    packet = {id(slot): ref for slot, ref in zip([plan.own, plan.one] + plan.mine, packet_refs)}
    for c, runs in enumerate(plan.attention_chunks(slot_rows, True)):
        span = slice(c * 128, c * 128 + 128)
        mix = mix_ref[span] * table[:, c : c + 1]
        mix += got_ref[span].astype(jnp.float32) * table[:, CHUNKS + c : CHUNKS + c + 1]
        stats = jnp.where(
            stat_row == 0,
            peak[c : c + 1],
            jnp.where(
                stat_row == 1, high[c : c + 1], jnp.where(stat_row == 2, low[c : c + 1], 0.0)
            ),
        )
        for t, (slot, side) in enumerate(unit for run in runs for unit in run):
            packet_ref = packet[id(slot)]
            at = side * slot_rows
            packet_ref[at : at + slot_rows] = mix[t * slot_rows : (t + 1) * slot_rows].astype(
                jnp.bfloat16
            )
            if side == 0:
                shifted = stats if t == 0 else pltpu.roll(stats, HEAD_WIDTH - t * slot_rows, 1)
                head = (chip // per_head) ^ (here_mask(slot[0], here) // per_head)
                tail = jnp.concatenate([tail_ref[head], shifted], axis=0)
                packet_ref[packet_ref.shape[0] - 4 * rows :] = tail.astype(jnp.bfloat16)


def merge_kernel(devices, requests, tokens, swapped, own_ref, cos_ref, sin_ref, *refs):
    got_refs, out_ref = refs[:-1], refs[-1]
    rows = requests * tokens
    heads = QUERY_HEADS // devices
    mix_rows = heads * rows
    sources = len(got_refs)
    tails = [ref[ref.shape[0] - 4 * rows :].astype(jnp.float32) for ref in got_refs]
    sums = functools.reduce(jnp.add, [tail[: 3 * rows] for tail in tails])
    keys = sums[:rows] + sums[rows : 2 * rows]
    values = sums[2 * rows :].astype(jnp.bfloat16)
    turned = pltpu.roll(keys, HEAD_WIDTH // 2, 1)
    keys = (keys * cos_ref[...] + turned * sin_ref[...]).astype(jnp.bfloat16)
    query = jnp.concatenate([own_ref[h] for h in range(heads)], axis=0)
    if mix_rows < 128:
        query = jnp.concatenate(
            [query, jnp.zeros((128 - mix_rows, HEAD_WIDTH), jnp.bfloat16)], axis=0
        )
    fresh = dot(keys, query, ((1,), (1,))) * SCALE
    source = lax.broadcasted_iota(jnp.int32, fresh.shape, 0)
    column = lax.broadcasted_iota(jnp.int32, fresh.shape, 1) % rows
    allowed = (source // tokens == column // tokens) & (source % tokens <= column % tokens)
    fresh_peak = jnp.max(jnp.where(allowed, fresh, NEG_FILL), axis=0, keepdims=True)
    stats = [tail[3 * rows :] for tail in tails]
    for s in range(swapped, sources):
        stats[s] = pltpu.roll(stats[s], HEAD_WIDTH - mix_rows, 1)
    peak = functools.reduce(jnp.maximum, [stat[0:1] for stat in stats], fresh_peak)
    weights = jnp.where(allowed, jnp.exp(fresh - peak), 0.0)
    factors = [jnp.exp(stat[0:1] - peak) for stat in stats]
    total = functools.reduce(
        jnp.add,
        [factor * (stat[1:2] + stat[2:3]) for factor, stat in zip(factors, stats)],
        jnp.sum(weights, axis=0, keepdims=True),
    )
    inverse = 1.0 / total
    filler = jnp.zeros((128 - sources - 1, 128), jnp.float32)
    table = jnp.concatenate([factor * inverse for factor in factors] + [inverse, filler], axis=0)
    table = jnp.transpose(table)[:mix_rows]
    weights = jnp.transpose(
        jnp.concatenate([weights, jnp.zeros((128 - rows, 128), jnp.float32)], axis=0)
    )[:mix_rows].astype(jnp.bfloat16)
    values = jnp.concatenate(
        [values, jnp.zeros((128 - rows, HEAD_WIDTH), jnp.bfloat16)], axis=0
    )
    mix = dot(weights, values, ((1,), (0,))) * table[:, sources : sources + 1]
    for s, ref in enumerate(got_refs):
        mix += ref[:mix_rows].astype(jnp.float32) * table[:, s : s + 1]
    for h in range(heads):
        tile = mix[h * rows : (h + 1) * rows]
        for b in range(requests):
            out_ref[b, :, h * HEAD_WIDTH : (h + 1) * HEAD_WIDTH] = tile[
                b * tokens : (b + 1) * tokens
            ].astype(jnp.bfloat16)


def rotation(lengths, tokens):
    half = HEAD_WIDTH // 2
    places = (lengths[:, None] + jnp.arange(tokens, dtype=jnp.int32)[None, :]).astype(jnp.float32)
    inverse_freq = jnp.exp(
        jnp.arange(half, dtype=jnp.float32) * (-2.0 * math.log(ROPE_BASE) / HEAD_WIDTH)
    )
    angles = places.reshape(-1, 1) * inverse_freq[None, :]
    cosine, sine = jnp.cos(angles), jnp.sin(angles)
    return jnp.concatenate([cosine, cosine], axis=1), jnp.concatenate([-sine, sine], axis=1)


def vmem():
    return pl.BlockSpec(memory_space=pltpu.VMEM)


def smem():
    return pl.BlockSpec(memory_space=pltpu.SMEM)


def hbm():
    return pl.BlockSpec(memory_space=pltpu.HBM)


def pinned(x):
    return pltpu.with_memory_space_constraint(x, pltpu.HBM)


def cost(flops, moved):
    return pl.CostEstimate(flops=int(flops), bytes_accessed=int(moved), transcendentals=0)


def trade(x, devices, even, odd, core=0):
    pairs = [(d, d ^ (2 * (odd if d % 2 else even) + core)) for d in range(devices)]
    return lax.ppermute(x, "tensor", pairs)


def per_device(
    hidden,
    queries,
    key_value_weight,
    adapter_down_weight,
    adapter_up_weight,
    cached_key_rows,
    cached_value_rows,
    request_adapter,
    adapter_rank_list,
    adapter_pool_row,
    lengths,
):
    requests, tokens, width = hidden.shape
    rows = requests * tokens
    devices = lax.axis_size("tensor")
    sizes = (requests, tokens, devices)
    plan = Plan(devices, width)
    heads, chunks = plan.heads, plan.chunks
    slot_rows = heads * rows
    index = lax.axis_index("tensor").reshape(1).astype(jnp.int32)

    def call(kernel, operands, in_specs, out_shape, scratch, name):
        return pl.pallas_call(
            kernel,
            out_shape=tuple(out_shape),
            in_specs=in_specs,
            out_specs=(vmem(),) * len(out_shape),
            scratch_shapes=scratch,
            compiler_params=pltpu.CompilerParams(vmem_limit_bytes=12 * MIB),
            cost_estimate=cost(10**6, 0),
            name=name,
        )(*operands)

    def core_swap(x):
        return trade(x, devices, 0, 0, core=1)

    (own,) = call(
        functools.partial(pack_kernel, requests),
        (pinned(queries), pinned(hidden)),
        [hbm()] * 2,
        [pltpu.VMEM((heads + chunks, rows, HEAD_WIDTH), jnp.bfloat16)],
        [
            pltpu.VMEM(queries.shape, jnp.bfloat16),
            pltpu.VMEM(hidden.shape, jnp.bfloat16),
            pltpu.SemaphoreType.DMA((2,)),
        ],
        "pack",
    )
    other = core_swap(own)
    one = trade(own, devices, plan.single, plan.single)
    both = jnp.concatenate([own, other], axis=0)
    mine = [trade(both, devices, a, b) for a, b in plan.pairs]

    flat = requests * cached_key_rows.shape[1]
    big = (
        cached_key_rows.reshape(flat, -1),
        cached_value_rows.reshape(flat, -1),
        adapter_up_weight[0],
    )
    out_width = key_value_weight.shape[1]
    parts = 4 if width % (4 * HEAD_WIDTH) == 0 else 1
    base, keys, values, up = call(
        functools.partial(base_kernel, heads),
        (own, pinned(key_value_weight)) + tuple(pinned(x) for x in big),
        [vmem()] + [hbm()] * 4,
        [pltpu.VMEM((rows, out_width), jnp.float32)] + [pltpu.VMEM(x.shape, x.dtype) for x in big],
        [
            pltpu.VMEM((parts, width // parts, out_width), jnp.bfloat16),
            pltpu.SemaphoreType.DMA((parts + 3,)),
        ],
        "base",
    )
    down = adapter_down_weight[0]
    count = devices // 2
    first, second = [
        call(
            functools.partial(fetch_kernel, sources_of(plan)[at : at + count]),
            (index, pinned(down)),
            [smem(), hbm()],
            [pltpu.VMEM((count, width, down.shape[1]), jnp.bfloat16)],
            [pltpu.SemaphoreType.DMA((count,))],
            "fetch",
        )[0]
        for at in (0, count)
    ]
    one, base, first = lax.optimization_barrier((one, base, first))
    other_one = core_swap(one)
    mine = jnp.concatenate(mine, axis=0)
    mine, other_one = lax.optimization_barrier((mine, other_one))
    other_mine, second = lax.optimization_barrier((core_swap(mine), second))
    arrays = (own, other, one, other_one, mine, other_mine)
    halves = (first, second)
    step = KEY_HEADS * rows
    send, proj, proj_parts = call(
        functools.partial(send_kernel, sizes, plan),
        (index, lengths, request_adapter, adapter_rank_list, adapter_pool_row)
        + arrays
        + (keys, values, base, up, *halves),
        [smem()] * 5 + [vmem()] * (len(arrays) + 6),
        [
            pltpu.VMEM((MIX_ROWS + STAT_ROWS, HEAD_WIDTH), jnp.bfloat16),
            pltpu.VMEM((2, step, HEAD_WIDTH), jnp.float32),
            pltpu.VMEM((3 * step, HEAD_WIDTH), jnp.bfloat16),
        ],
        [],
        "send_states",
    )
    got_parts = core_swap(proj_parts)
    got = core_swap(send)
    mix, stats = call(
        functools.partial(keep_kernel, sizes, plan),
        (index, lengths) + arrays + (keys, values),
        [smem()] * 2 + [vmem()] * (len(arrays) + 2),
        [
            pltpu.VMEM((MIX_ROWS, HEAD_WIDTH), jnp.float32),
            pltpu.VMEM((8, HEAD_WIDTH), jnp.float32),
        ],
        [],
        "keep_states",
    )
    packets = call(
        functools.partial(join_kernel, sizes, plan),
        (index, mix, stats, proj, got_parts, got),
        [smem()] + [vmem()] * 5,
        [pltpu.VMEM((slot_rows + 4 * rows, HEAD_WIDTH), jnp.bfloat16)] * 2
        + [pltpu.VMEM((2 * slot_rows + 4 * rows, HEAD_WIDTH), jnp.bfloat16)] * len(plan.pairs),
        [pltpu.VMEM((KEY_HEADS, 3 * rows, HEAD_WIDTH), jnp.float32)],
        "join",
    )
    heard = [packets[0], trade(packets[1], devices, plan.single, plan.single)]
    heard += [trade(x, devices, a, b) for x, (a, b) in zip(packets[2:], plan.pairs)]
    heard += [core_swap(x[slot_rows:]) for x in heard[2:]]
    cosine, sine = rotation(lengths, tokens)
    return pl.pallas_call(
        functools.partial(merge_kernel, devices, requests, tokens, 2 + len(plan.pairs)),
        out_shape=jax.ShapeDtypeStruct((requests, tokens, heads * HEAD_WIDTH), jnp.bfloat16),
        in_specs=[vmem()] * (3 + len(heard)),
        out_specs=vmem(),
        compiler_params=pltpu.CompilerParams(vmem_limit_bytes=8 * MIB),
        name="merge_states",
    )(own, cosine, sine, *heard)


def solution(mesh):
    in_specs = (
        P("groups", None, "tensor"),
        P("groups", None, "tensor"),
        P("tensor", None),
        P("tensor", None, None),
        P("tensor", None, None),
        P("groups", "tensor", None),
        P("groups", "tensor", None),
        P("groups"),
        P(),
        P(),
        P("groups"),
    )
    out_specs = P("groups", None, "tensor")
    return jax.shard_map(
        per_device, mesh=mesh, in_specs=in_specs, out_specs=out_specs, check_vma=False
    )
```

```python
import functools
import math

import jax
import jax.numpy as jnp
from jax import lax
from jax.experimental import pallas as pl
from jax.experimental.pallas import tpu as pltpu
from jax.sharding import PartitionSpec as P

QUERY_HEADS = 128
KEY_HEADS = 8
HEAD_WIDTH = 128
ROPE_BASE = 500000.0
NEG_FILL = -1e30
SCALE = 1.0 / math.sqrt(HEAD_WIDTH)
CHUNKS = KEY_HEADS // 2
MIX_ROWS = CHUNKS * 128
STAT_ROWS = 16
MIB = 2**20


def dot(a, b, dims):
    return lax.dot_general(a, b, (dims, ((), ())), preferred_element_type=jnp.float32)


def round_bf16(x):
    return x.astype(jnp.bfloat16).astype(jnp.float32)


class Plan:
    def __init__(self, devices, width):
        lanes = devices // 2
        self.per_head = per_head = lanes // KEY_HEADS
        self.heads, self.chunks = QUERY_HEADS // devices, width // HEAD_WIDTH
        self.single = 1
        self.pairs = [(m, m + 1) for m in range(lanes - 2, 0, -2)]
        self.pairs[:2] = self.pairs[1::-1]
        size = self.heads + self.chunks
        self.own = ((0, 0), ((0, 0), (1, 0)))
        self.one = ((self.single,) * 2, ((2, 0), (3, 0)))
        self.mine, self.theirs = [], []
        for k, (a, b) in enumerate(self.pairs):
            at = 2 * size * k
            self.mine.append(((a, b), ((4, at), (4, at + size))))
            self.theirs.append(((b, a), ((5, at + size), (5, at))))

    def head_masks(self, unit):
        return tuple(mask // self.per_head for mask in unit[0][0])

    def units(self, keep):
        if keep:
            units = [(self.own, 0), (self.one, 0)]
            units += [(slot, side) for slot in self.mine for side in (0, 1)]
        else:
            units = [(self.own, 1), (self.one, 1)]
            units += [(slot, side) for slot in self.theirs for side in (1, 0)]
        if self.per_head > 1:
            units.sort(key=self.head_masks)
        return units

    def attention_chunks(self, slot_rows, keep):
        units = self.units(keep)
        count = HEAD_WIDTH // slot_rows
        chunks = []
        for at in range(0, len(units), count):
            runs = []
            for unit in units[at : at + count]:
                if runs and self.head_masks(runs[-1][0]) == self.head_masks(unit):
                    runs[-1].append(unit)
                else:
                    runs.append([unit])
            chunks.append(runs)
        return chunks

    def slots(self):
        return [self.own, self.one] + self.mine + self.theirs


def here_mask(masks, here):
    return masks[0] if masks[0] == masks[1] else jnp.where(here % 2 == 0, masks[0], masks[1])


def head_columns(head):
    return pl.ds(pl.multiple_of(head * HEAD_WIDTH, HEAD_WIDTH), HEAD_WIDTH)


def sources_of(plan):
    return [
        (array, tile + plan.heads, masks, side)
        for masks, places in plan.slots()
        for side, (array, tile) in enumerate(places)
    ]


def streams(sources, index_ref, down_ref, rows_ref, sems):
    depth = rows_ref.shape[1]
    here = index_ref[0]
    copies = []
    for at, (_, _, masks, side) in enumerate(sources):
        source = here ^ (2 * here_mask(masks, here) + side)
        rows = pl.ds(pl.multiple_of(source * depth, depth), depth)
        copies.append(pltpu.make_async_copy(down_ref.at[rows], rows_ref.at[at], sems.at[at]))
    return copies


def lower(sources, arrays, factors):
    total = None
    count, depth = factors[0].shape[:2]
    for at, (array, first, _, _) in enumerate(sources):
        tiles = range(first, first + depth // HEAD_WIDTH)
        hidden = jnp.concatenate([arrays[array][c] for c in tiles], axis=1)
        factor = factors[0][at] if at < count else factors[1][at - count]
        term = dot(hidden, factor, ((1,), (0,)))
        total = term if total is None else total + term
    return total


def pack_kernel(requests, query_ref, hidden_ref, own_ref, query_buf, hidden_buf, sems):
    loads = [
        pltpu.make_async_copy(query_ref, query_buf, sems.at[0]),
        pltpu.make_async_copy(hidden_ref, hidden_buf, sems.at[1]),
    ]
    for load in loads:
        load.start()
    at = 0
    for load, ref in zip(loads, (query_buf, hidden_buf)):
        load.wait()
        rows = jnp.concatenate([ref[b].astype(jnp.float32) for b in range(requests)], axis=0)
        for c in range(rows.shape[1] // HEAD_WIDTH):
            tile = rows[:, c * HEAD_WIDTH : (c + 1) * HEAD_WIDTH]
            own_ref[at] = tile.astype(jnp.bfloat16)
            at += 1


def load_kernel(*refs):
    count = len(refs) // 2
    sems = refs[-1]
    copies = [
        pltpu.make_async_copy(refs[i], refs[count + i], sems.at[i]) for i in range(count)
    ]
    for copy in copies:
        copy.start()
    for copy in copies:
        copy.wait()


def base_kernel(heads, sources, index_ref, own_ref, weight_ref, down_ref, base_ref, rows_ref, *scratch):
    buffer, sems, row_sems = scratch
    parts, depth = buffer.shape[:2]
    loads = [
        pltpu.make_async_copy(weight_ref.at[pl.ds(p * depth, depth)], buffer.at[p], sems.at[p])
        for p in range(parts)
    ]
    others = streams(sources, index_ref, down_ref, rows_ref, row_sems)
    for load in loads + others:
        load.start()
    tiles = depth // HEAD_WIDTH
    total = jnp.zeros(base_ref.shape, jnp.float32)
    for p in range(parts):
        hidden = jnp.concatenate([own_ref[heads + p * tiles + c] for c in range(tiles)], axis=1)
        loads[p].wait()
        total += dot(hidden, buffer[p], ((1,), (0,)))
    base_ref[...] = total
    for load in others:
        load.wait()


def fetch_kernel(sources, index_ref, down_ref, rows_ref, sems):
    copies = streams(sources, index_ref, down_ref, rows_ref, sems)
    for copy in copies:
        copy.start()
    for copy in copies:
        copy.wait()


def attend(sizes, plan, keep, index_ref, length_ref, arrays, key_ref, value_ref, put):
    requests, tokens, devices = sizes
    here = index_ref[0]
    chip = here // 2
    per_head = plan.per_head
    slot_rows = plan.heads * requests * tokens
    positions = key_ref.shape[0] // requests
    place = lax.broadcasted_iota(jnp.int32, (requests * positions, HEAD_WIDTH), 0)
    column = lax.broadcasted_iota(jnp.int32, (requests * positions, HEAD_WIDTH), 1)
    place_request = place // positions
    limit = jnp.zeros_like(place)
    for b in range(requests):
        limit = jnp.where(place_request == b, length_ref[b], limit)
    allowed = (here * positions + place % positions < limit) & (
        place_request == (column // tokens) % requests
    )
    peaks, totals = [], []
    for number, runs in enumerate(plan.attention_chunks(slot_rows, keep)):
        places = [slot[1][side] for run in runs for slot, side in run]
        query = jnp.concatenate(
            [arrays[array][tile + h] for array, tile in places for h in range(plan.heads)], axis=0
        )
        spots = [
            head_columns((chip // per_head) ^ (here_mask(run[0][0][0], here) // per_head))
            for run in runs
        ]
        share = HEAD_WIDTH // len(runs)
        scores = None
        for i, spot in enumerate(spots):
            part = dot(key_ref[:, spot], query, ((1,), (1,)))
            scores = part if scores is None else jnp.where(column < i * share, scores, part)
        scores = scores * SCALE
        peak = jnp.max(jnp.where(allowed, scores, NEG_FILL), axis=0, keepdims=True)
        peak = round_bf16(peak)
        weights = jnp.where(allowed, jnp.exp(scores - peak), 0.0)
        peaks.append(peak)
        totals.append(jnp.sum(weights, axis=0, keepdims=True))
        weights = jnp.transpose(weights.astype(jnp.bfloat16))
        for i, spot in enumerate(spots):
            own = slice(i * share, (i + 1) * share)
            put(number, i * share, dot(weights[own], value_ref[:, spot], ((1,), (0,))))
    return peaks, totals


def rows_of(items, count):
    row = lax.broadcasted_iota(jnp.int32, (count, HEAD_WIDTH), 0)
    out = jnp.zeros((count, HEAD_WIDTH), jnp.float32)
    for i, item in enumerate(items):
        out = jnp.where(row == i, item, out)
    return out


def send_kernel(sizes, plan, *refs):
    (index_ref, length_ref, adapter_ref, rank_ref, pool_ref, *arrays) = refs[:-9]
    (key_ref, value_ref, base_ref, up_ref, *factors, send_ref, own_ref, parts_ref) = refs[-9:]
    requests, tokens, devices = sizes

    def put(chunk, row, mix):
        at = chunk * 128 + row
        send_ref[at : at + mix.shape[0]] = mix.astype(jnp.bfloat16)

    peaks, totals = attend(
        sizes, plan, False, index_ref, length_ref, arrays, key_ref, value_ref, put
    )
    highs = [round_bf16(total) for total in totals]
    lows = [total - high for total, high in zip(totals, highs)]
    send_ref[MIX_ROWS:] = rows_of(peaks + highs + lows, STAT_ROWS).astype(jnp.bfloat16)

    rows = requests * tokens
    lowered = lower(sources_of(plan), arrays, factors)
    row_request = lax.broadcasted_iota(jnp.int32, (rows, 1), 0) // tokens
    ranks = jnp.zeros((rows, 1), jnp.int32)
    owners = jnp.zeros((rows, 1), jnp.int32)
    for b in range(requests):
        adapter = adapter_ref[b]
        ranks = jnp.where(row_request == b, rank_ref[adapter], ranks)
        owners = jnp.where(row_request == b, pool_ref[adapter], owners)
    column = lax.broadcasted_iota(jnp.int32, lowered.shape, 1)
    lowered = jnp.where(column < ranks, lowered, 0.0).astype(jnp.bfloat16)
    lifted = dot(lowered, up_ref[...], ((1,), (0,)))
    projected = base_ref[...] + jnp.where(owners == index_ref[0], lifted, 0.0)
    split = KEY_HEADS * HEAD_WIDTH
    step = KEY_HEADS * rows
    keys, values = [
        jnp.concatenate(
            [projected[:, at + j * HEAD_WIDTH : at + (j + 1) * HEAD_WIDTH] for j in range(KEY_HEADS)],
            axis=0,
        )
        for at in (0, split)
    ]
    own_ref[0] = keys
    own_ref[1] = values
    high = keys.astype(jnp.bfloat16)
    parts_ref[:step] = high
    parts_ref[step : 2 * step] = (keys - high.astype(jnp.float32)).astype(jnp.bfloat16)
    parts_ref[2 * step :] = values.astype(jnp.bfloat16)


def keep_kernel(sizes, plan, *refs):
    (index_ref, length_ref, *arrays, key_ref, value_ref, mix_ref, stat_ref) = refs

    def put(chunk, row, mix):
        at = chunk * 128 + row
        mix_ref[at : at + mix.shape[0]] = mix

    peaks, totals = attend(
        sizes, plan, True, index_ref, length_ref, arrays, key_ref, value_ref, put
    )
    stat_ref[...] = rows_of(peaks + totals, 8)


def join_kernel(sizes, plan, index_ref, mix_ref, stat_ref, proj_ref, got_parts_ref, got_ref, *refs):
    packet_refs, tail_ref = refs[:-1], refs[-1]
    requests, tokens, devices = sizes
    here = index_ref[0]
    chip = here // 2
    per_head = plan.per_head
    rows = requests * tokens
    slot_rows = plan.heads * rows
    step = KEY_HEADS * rows
    got = got_ref[MIX_ROWS:].astype(jnp.float32)
    own = stat_ref[...]
    own_peak, got_peak = own[:CHUNKS], got[:CHUNKS]
    peak = jnp.maximum(own_peak, got_peak)
    own_factor = jnp.exp(own_peak - peak)
    got_factor = jnp.exp(got_peak - peak)
    total = own_factor * own[CHUNKS : 2 * CHUNKS] + got_factor * (
        got[CHUNKS : 2 * CHUNKS] + got[2 * CHUNKS : 3 * CHUNKS]
    )
    high = round_bf16(total)
    low = total - high
    filler = jnp.zeros((128 - 2 * CHUNKS, 128), jnp.float32)
    table = jnp.transpose(jnp.concatenate([own_factor, got_factor, filler], axis=0))
    keys = proj_ref[0] + got_parts_ref[:step].astype(jnp.float32)
    keys += got_parts_ref[step : 2 * step].astype(jnp.float32)
    values = proj_ref[1] + got_parts_ref[2 * step :].astype(jnp.float32)
    keys_high = round_bf16(keys)
    for j in range(KEY_HEADS):
        part = slice(j * rows, (j + 1) * rows)
        tail_ref[j, :rows] = keys_high[part]
        tail_ref[j, rows : 2 * rows] = (keys - keys_high)[part]
        tail_ref[j, 2 * rows :] = values[part]
    stat_row = lax.broadcasted_iota(jnp.int32, (rows, HEAD_WIDTH), 0)
    packet = {id(slot): ref for slot, ref in zip([plan.own, plan.one] + plan.mine, packet_refs)}
    for c, runs in enumerate(plan.attention_chunks(slot_rows, True)):
        span = slice(c * 128, c * 128 + 128)
        mix = mix_ref[span] * table[:, c : c + 1]
        mix += got_ref[span].astype(jnp.float32) * table[:, CHUNKS + c : CHUNKS + c + 1]
        stats = jnp.where(
            stat_row == 0,
            peak[c : c + 1],
            jnp.where(
                stat_row == 1, high[c : c + 1], jnp.where(stat_row == 2, low[c : c + 1], 0.0)
            ),
        )
        for t, (slot, side) in enumerate(unit for run in runs for unit in run):
            packet_ref = packet[id(slot)]
            at = side * slot_rows
            packet_ref[at : at + slot_rows] = mix[t * slot_rows : (t + 1) * slot_rows].astype(
                jnp.bfloat16
            )
            if side == 0:
                shifted = stats if t == 0 else pltpu.roll(stats, HEAD_WIDTH - t * slot_rows, 1)
                head = (chip // per_head) ^ (here_mask(slot[0], here) // per_head)
                tail = jnp.concatenate([tail_ref[head], shifted], axis=0)
                packet_ref[packet_ref.shape[0] - 4 * rows :] = tail.astype(jnp.bfloat16)


def merge_kernel(devices, requests, tokens, swapped, own_ref, cos_ref, sin_ref, *refs):
    got_refs, out_ref = refs[:-1], refs[-1]
    rows = requests * tokens
    heads = QUERY_HEADS // devices
    mix_rows = heads * rows
    sources = len(got_refs)
    tails = [ref[ref.shape[0] - 4 * rows :].astype(jnp.float32) for ref in got_refs]
    sums = functools.reduce(jnp.add, [tail[: 3 * rows] for tail in tails])
    keys = sums[:rows] + sums[rows : 2 * rows]
    values = sums[2 * rows :].astype(jnp.bfloat16)
    turned = pltpu.roll(keys, HEAD_WIDTH // 2, 1)
    keys = (keys * cos_ref[...] + turned * sin_ref[...]).astype(jnp.bfloat16)
    query = jnp.concatenate([own_ref[h] for h in range(heads)], axis=0)
    if mix_rows < 128:
        query = jnp.concatenate(
            [query, jnp.zeros((128 - mix_rows, HEAD_WIDTH), jnp.bfloat16)], axis=0
        )
    fresh = dot(keys, query, ((1,), (1,))) * SCALE
    source = lax.broadcasted_iota(jnp.int32, fresh.shape, 0)
    column = lax.broadcasted_iota(jnp.int32, fresh.shape, 1) % rows
    allowed = (source // tokens == column // tokens) & (source % tokens <= column % tokens)
    fresh_peak = jnp.max(jnp.where(allowed, fresh, NEG_FILL), axis=0, keepdims=True)
    stats = [tail[3 * rows :] for tail in tails]
    for s in range(swapped, sources):
        stats[s] = pltpu.roll(stats[s], HEAD_WIDTH - mix_rows, 1)
    peak = functools.reduce(jnp.maximum, [stat[0:1] for stat in stats], fresh_peak)
    weights = jnp.where(allowed, jnp.exp(fresh - peak), 0.0)
    factors = [jnp.exp(stat[0:1] - peak) for stat in stats]
    total = functools.reduce(
        jnp.add,
        [factor * (stat[1:2] + stat[2:3]) for factor, stat in zip(factors, stats)],
        jnp.sum(weights, axis=0, keepdims=True),
    )
    inverse = 1.0 / total
    filler = jnp.zeros((128 - sources - 1, 128), jnp.float32)
    table = jnp.concatenate([factor * inverse for factor in factors] + [inverse, filler], axis=0)
    table = jnp.transpose(table)[:mix_rows]
    weights = jnp.transpose(
        jnp.concatenate([weights, jnp.zeros((128 - rows, 128), jnp.float32)], axis=0)
    )[:mix_rows].astype(jnp.bfloat16)
    values = jnp.concatenate(
        [values, jnp.zeros((128 - rows, HEAD_WIDTH), jnp.bfloat16)], axis=0
    )
    mix = dot(weights, values, ((1,), (0,))) * table[:, sources : sources + 1]
    for s, ref in enumerate(got_refs):
        mix += ref[:mix_rows].astype(jnp.float32) * table[:, s : s + 1]
    for h in range(heads):
        tile = mix[h * rows : (h + 1) * rows]
        for b in range(requests):
            out_ref[b, :, h * HEAD_WIDTH : (h + 1) * HEAD_WIDTH] = tile[
                b * tokens : (b + 1) * tokens
            ].astype(jnp.bfloat16)


def rotation(lengths, tokens):
    half = HEAD_WIDTH // 2
    places = (lengths[:, None] + jnp.arange(tokens, dtype=jnp.int32)[None, :]).astype(jnp.float32)
    inverse_freq = jnp.exp(
        jnp.arange(half, dtype=jnp.float32) * (-2.0 * math.log(ROPE_BASE) / HEAD_WIDTH)
    )
    angles = places.reshape(-1, 1) * inverse_freq[None, :]
    cosine, sine = jnp.cos(angles), jnp.sin(angles)
    return jnp.concatenate([cosine, cosine], axis=1), jnp.concatenate([-sine, sine], axis=1)


def vmem():
    return pl.BlockSpec(memory_space=pltpu.VMEM)


def smem():
    return pl.BlockSpec(memory_space=pltpu.SMEM)


def hbm():
    return pl.BlockSpec(memory_space=pltpu.HBM)


def pinned(x):
    return pltpu.with_memory_space_constraint(x, pltpu.HBM)


def cost(flops, moved):
    return pl.CostEstimate(flops=int(flops), bytes_accessed=int(moved), transcendentals=0)


def trade(x, devices, even, odd, core=0):
    pairs = [(d, d ^ (2 * (odd if d % 2 else even) + core)) for d in range(devices)]
    return lax.ppermute(x, "tensor", pairs)


def per_device(
    hidden,
    queries,
    key_value_weight,
    adapter_down_weight,
    adapter_up_weight,
    cached_key_rows,
    cached_value_rows,
    request_adapter,
    adapter_rank_list,
    adapter_pool_row,
    lengths,
):
    requests, tokens, width = hidden.shape
    rows = requests * tokens
    devices = lax.axis_size("tensor")
    sizes = (requests, tokens, devices)
    plan = Plan(devices, width)
    heads, chunks = plan.heads, plan.chunks
    slot_rows = heads * rows
    index = lax.axis_index("tensor").reshape(1).astype(jnp.int32)

    def call(kernel, operands, in_specs, out_shape, scratch, name):
        return pl.pallas_call(
            kernel,
            out_shape=tuple(out_shape),
            in_specs=in_specs,
            out_specs=(vmem(),) * len(out_shape),
            scratch_shapes=scratch,
            compiler_params=pltpu.CompilerParams(vmem_limit_bytes=12 * MIB),
            cost_estimate=cost(10**6, 0),
            name=name,
        )(*operands)

    def core_swap(x):
        return trade(x, devices, 0, 0, core=1)

    (own,) = call(
        functools.partial(pack_kernel, requests),
        (pinned(queries), pinned(hidden)),
        [hbm()] * 2,
        [pltpu.VMEM((heads + chunks, rows, HEAD_WIDTH), jnp.bfloat16)],
        [
            pltpu.VMEM(queries.shape, jnp.bfloat16),
            pltpu.VMEM(hidden.shape, jnp.bfloat16),
            pltpu.SemaphoreType.DMA((2,)),
        ],
        "pack",
    )
    flat = requests * cached_key_rows.shape[1]
    big = (
        cached_key_rows.reshape(flat, -1),
        cached_value_rows.reshape(flat, -1),
        adapter_up_weight[0],
    )
    keys, values, up = call(
        load_kernel,
        tuple(pinned(x) for x in big),
        [hbm()] * 3,
        [pltpu.VMEM(x.shape, x.dtype) for x in big],
        [pltpu.SemaphoreType.DMA((3,))],
        "load",
    )
    other, keys = lax.optimization_barrier((core_swap(own), keys))
    one = trade(own, devices, plan.single, plan.single)
    both = jnp.concatenate([own, other], axis=0)
    mine = [trade(both, devices, a, b) for a, b in plan.pairs]

    out_width = key_value_weight.shape[1]
    parts = 4 if width % (4 * HEAD_WIDTH) == 0 else 1
    down = pinned(adapter_down_weight[0])
    rank = down.shape[1]
    sources = sources_of(plan)
    count = 5 * devices // 8
    base, first = call(
        functools.partial(base_kernel, heads, sources[:count]),
        (index, own, pinned(key_value_weight), down),
        [smem(), vmem()] + [hbm()] * 2,
        [
            pltpu.VMEM((rows, out_width), jnp.float32),
            pltpu.VMEM((count, width, rank), jnp.bfloat16),
        ],
        [
            pltpu.VMEM((parts, width // parts, out_width), jnp.bfloat16),
            pltpu.SemaphoreType.DMA((parts,)),
            pltpu.SemaphoreType.DMA((count,)),
        ],
        "base",
    )
    mine, one, base = lax.optimization_barrier((jnp.concatenate(mine, axis=0), one, base))
    other_one, other_mine = core_swap(one), core_swap(mine)
    (second,) = call(
        functools.partial(fetch_kernel, sources[count:]),
        (index, down),
        [smem(), hbm()],
        [pltpu.VMEM((devices - count, width, rank), jnp.bfloat16)],
        [pltpu.SemaphoreType.DMA((devices - count,))],
        "fetch",
    )
    other_mine, second = lax.optimization_barrier((other_mine, second))
    arrays = (own, other, one, other_one, mine, other_mine)
    step = KEY_HEADS * rows
    send, proj, proj_parts = call(
        functools.partial(send_kernel, sizes, plan),
        (index, lengths, request_adapter, adapter_rank_list, adapter_pool_row)
        + arrays
        + (keys, values, base, up, first, second),
        [smem()] * 5 + [vmem()] * (len(arrays) + 6),
        [
            pltpu.VMEM((MIX_ROWS + STAT_ROWS, HEAD_WIDTH), jnp.bfloat16),
            pltpu.VMEM((2, step, HEAD_WIDTH), jnp.float32),
            pltpu.VMEM((3 * step, HEAD_WIDTH), jnp.bfloat16),
        ],
        [],
        "send_states",
    )
    got_parts = core_swap(proj_parts)
    got = core_swap(send)
    mix, stats = call(
        functools.partial(keep_kernel, sizes, plan),
        (index, lengths) + arrays + (keys, values),
        [smem()] * 2 + [vmem()] * (len(arrays) + 2),
        [
            pltpu.VMEM((MIX_ROWS, HEAD_WIDTH), jnp.float32),
            pltpu.VMEM((8, HEAD_WIDTH), jnp.float32),
        ],
        [],
        "keep_states",
    )
    packets = call(
        functools.partial(join_kernel, sizes, plan),
        (index, mix, stats, proj, got_parts, got),
        [smem()] + [vmem()] * 5,
        [pltpu.VMEM((slot_rows + 4 * rows, HEAD_WIDTH), jnp.bfloat16)] * 2
        + [pltpu.VMEM((2 * slot_rows + 4 * rows, HEAD_WIDTH), jnp.bfloat16)] * len(plan.pairs),
        [pltpu.VMEM((KEY_HEADS, 3 * rows, HEAD_WIDTH), jnp.float32)],
        "join",
    )
    heard = [packets[0], trade(packets[1], devices, plan.single, plan.single)]
    heard += [trade(x, devices, a, b) for x, (a, b) in zip(packets[2:], plan.pairs)]
    heard += [core_swap(x[slot_rows:]) for x in heard[2:]]
    cosine, sine = rotation(lengths, tokens)
    return pl.pallas_call(
        functools.partial(merge_kernel, devices, requests, tokens, 2 + len(plan.pairs)),
        out_shape=jax.ShapeDtypeStruct((requests, tokens, heads * HEAD_WIDTH), jnp.bfloat16),
        in_specs=[vmem()] * (3 + len(heard)),
        out_specs=vmem(),
        compiler_params=pltpu.CompilerParams(vmem_limit_bytes=8 * MIB),
        name="merge_states",
    )(own, cosine, sine, *heard)


def solution(mesh):
    in_specs = (
        P("groups", None, "tensor"),
        P("groups", None, "tensor"),
        P("tensor", None),
        P("tensor", None, None),
        P("tensor", None, None),
        P("groups", "tensor", None),
        P("groups", "tensor", None),
        P("groups"),
        P(),
        P(),
        P("groups"),
    )
    out_specs = P("groups", None, "tensor")
    return jax.shard_map(
        per_device, mesh=mesh, in_specs=in_specs, out_specs=out_specs, check_vma=False
    )
```

```python
import functools
import math

import jax
import jax.numpy as jnp
from jax import lax
from jax.experimental import pallas as pl
from jax.experimental.pallas import tpu as pltpu
from jax.sharding import PartitionSpec as P

QUERY_HEADS = 128
KEY_HEADS = 8
HEAD_WIDTH = 128
ROPE_BASE = 500000.0
NEG_FILL = -(2.0**100)
SCALE = 1.0 / math.sqrt(HEAD_WIDTH)
CHUNKS = KEY_HEADS // 2
MIX_ROWS = CHUNKS * 128
STAT_ROWS = 16
MIB = 2**20


def dot(a, b, dims):
    return lax.dot_general(a, b, (dims, ((), ())), preferred_element_type=jnp.float32)


def round_bf16(x):
    return x.astype(jnp.bfloat16).astype(jnp.float32)


class Plan:
    def __init__(self, devices, width):
        lanes = devices // 2
        self.per_head = per_head = lanes // KEY_HEADS
        self.heads, self.chunks = QUERY_HEADS // devices, width // HEAD_WIDTH
        self.single = 1
        self.pairs = [(m, m + 1) for m in range(2, lanes, 2)]
        self.pairs[-2:] = self.pairs[:-3:-1]
        size = self.heads + self.chunks
        self.own = ((0, 0), ((0, 0), (1, 0)))
        self.one = ((self.single,) * 2, ((2, 0), (3, 0)))
        self.mine, self.theirs = [], []
        for k, (a, b) in enumerate(self.pairs):
            at = 2 * size * k
            self.mine.append(((a, b), ((4, at), (4, at + size))))
            self.theirs.append(((b, a), ((5, at + size), (5, at))))

    def head_masks(self, unit):
        return tuple(mask // self.per_head for mask in unit[0][0])

    def units(self, keep):
        if keep:
            units = [(self.own, 0), (self.one, 0)]
            units += [(slot, side) for slot in self.mine for side in (0, 1)]
        else:
            units = [(self.own, 1), (self.one, 1)]
            units += [(slot, side) for slot in self.theirs for side in (1, 0)]
        if self.per_head > 1:
            units.sort(key=self.head_masks)
        return units

    def attention_chunks(self, slot_rows, keep):
        units = self.units(keep)
        count = HEAD_WIDTH // slot_rows
        chunks = []
        for at in range(0, len(units), count):
            runs = []
            for unit in units[at : at + count]:
                if runs and self.head_masks(runs[-1][0]) == self.head_masks(unit):
                    runs[-1].append(unit)
                else:
                    runs.append([unit])
            chunks.append(runs)
        return chunks

    def slots(self):
        return [self.own, self.one] + self.mine + self.theirs


def here_mask(masks, here):
    return masks[0] if masks[0] == masks[1] else jnp.where(here % 2 == 0, masks[0], masks[1])


def head_columns(head):
    return pl.ds(pl.multiple_of(head * HEAD_WIDTH, HEAD_WIDTH), HEAD_WIDTH)


def sources_of(plan):
    return [
        (array, tile + plan.heads, masks, side)
        for masks, places in plan.slots()
        for side, (array, tile) in enumerate(places)
    ]


def streams(sources, index_ref, down_ref, halves, sems):
    count, depth = halves[0].shape[:2]
    here = index_ref[0]
    copies = []
    for at, (_, _, masks, side) in enumerate(sources):
        source = here ^ (2 * here_mask(masks, here) + side)
        rows = pl.ds(pl.multiple_of(source * depth, depth), depth)
        place = halves[at // count].at[at % count]
        copies.append(pltpu.make_async_copy(down_ref.at[rows], place, sems.at[at]))
    return copies


def lower(sources, arrays, halves):
    total = None
    count, depth = halves[0].shape[:2]
    for at, (array, first, _, _) in enumerate(sources):
        tiles = range(first, first + depth // HEAD_WIDTH)
        hidden = jnp.concatenate([arrays[array][c] for c in tiles], axis=1)
        term = dot(hidden, halves[at // count][at % count], ((1,), (0,)))
        total = term if total is None else total + term
    return total


def pack_kernel(requests, query_ref, hidden_ref, own_ref, query_buf, hidden_buf, sems):
    loads = [
        pltpu.make_async_copy(query_ref, query_buf, sems.at[0]),
        pltpu.make_async_copy(hidden_ref, hidden_buf, sems.at[1]),
    ]
    for load in loads:
        load.start()
    at = 0
    for load, ref in zip(loads, (query_buf, hidden_buf)):
        load.wait()
        rows = jnp.concatenate([ref[b].astype(jnp.float32) for b in range(requests)], axis=0)
        for c in range(rows.shape[1] // HEAD_WIDTH):
            tile = rows[:, c * HEAD_WIDTH : (c + 1) * HEAD_WIDTH]
            own_ref[at] = tile.astype(jnp.bfloat16)
            at += 1


def base_kernel(heads, sources, index_ref, own_ref, weight_ref, down_ref, *refs):
    others, (base_ref, *held) = refs[:3], refs[3:7]
    *halves, buffer, sems, row_sems = refs[7:]
    parts, depth = buffer.shape[:2]
    loads = [
        pltpu.make_async_copy(weight_ref.at[pl.ds(p * depth, depth)], buffer.at[p], sems.at[p])
        for p in range(parts)
    ]
    others = [
        pltpu.make_async_copy(source, place, sems.at[parts + i])
        for i, (source, place) in enumerate(zip(others, held))
    ]
    others += streams(sources, index_ref, down_ref, halves, row_sems)
    for load in loads + others:
        load.start()
    tiles = depth // HEAD_WIDTH
    total = jnp.zeros(base_ref.shape, jnp.float32)
    for p in range(parts):
        hidden = jnp.concatenate([own_ref[heads + p * tiles + c] for c in range(tiles)], axis=1)
        loads[p].wait()
        total += dot(hidden, buffer[p], ((1,), (0,)))
    base_ref[...] = total
    for load in others:
        load.wait()


def attend(sizes, plan, keep, index_ref, length_ref, arrays, key_ref, value_ref, put):
    requests, tokens, devices = sizes
    here = index_ref[0]
    chip = here // 2
    per_head = plan.per_head
    slot_rows = plan.heads * requests * tokens
    positions = key_ref.shape[0] // requests
    place = lax.broadcasted_iota(jnp.int32, (requests * positions, HEAD_WIDTH), 0)
    column = lax.broadcasted_iota(jnp.int32, (requests * positions, HEAD_WIDTH), 1)
    place_request = place // positions
    limit = jnp.zeros_like(place)
    for b in range(requests):
        limit = jnp.where(place_request == b, length_ref[b], limit)
    allowed = (here * positions + place % positions < limit) & (
        place_request == (column // tokens) % requests
    )
    peaks, totals = [], []
    for number, runs in enumerate(plan.attention_chunks(slot_rows, keep)):
        places = [slot[1][side] for run in runs for slot, side in run]
        query = jnp.concatenate(
            [arrays[array][tile + h] for array, tile in places for h in range(plan.heads)], axis=0
        )
        spots = [
            head_columns((chip // per_head) ^ (here_mask(run[0][0][0], here) // per_head))
            for run in runs
        ]
        share = HEAD_WIDTH // len(runs)
        scores = None
        for i, spot in enumerate(spots):
            part = dot(key_ref[:, spot], query, ((1,), (1,)))
            scores = part if scores is None else jnp.where(column < i * share, scores, part)
        scores = jnp.where(allowed, scores * SCALE, NEG_FILL)
        peak = round_bf16(jnp.max(scores, axis=0, keepdims=True))
        weights = jnp.exp(scores - peak)
        peaks.append(peak)
        totals.append(jnp.sum(weights, axis=0, keepdims=True))
        weights = jnp.transpose(weights.astype(jnp.bfloat16))
        for i, spot in enumerate(spots):
            own = slice(i * share, (i + 1) * share)
            put(number, i * share, dot(weights[own], value_ref[:, spot], ((1,), (0,))))
    return peaks, totals


def rows_of(items, count):
    row = lax.broadcasted_iota(jnp.int32, (count, HEAD_WIDTH), 0)
    out = jnp.zeros((count, HEAD_WIDTH), jnp.float32)
    for i, item in enumerate(items):
        out = jnp.where(row == i, item, out)
    return out


def send_kernel(sizes, plan, *refs):
    (index_ref, length_ref, adapter_ref, rank_ref, pool_ref, *arrays) = refs[:-9]
    (key_ref, value_ref, base_ref, up_ref, *halves, send_ref, own_ref, parts_ref) = refs[-9:]
    requests, tokens, devices = sizes

    def put(chunk, row, mix):
        at = chunk * 128 + row
        send_ref[at : at + mix.shape[0]] = mix.astype(jnp.bfloat16)

    peaks, totals = attend(
        sizes, plan, False, index_ref, length_ref, arrays, key_ref, value_ref, put
    )
    highs = [round_bf16(total) for total in totals]
    lows = [total - high for total, high in zip(totals, highs)]
    send_ref[MIX_ROWS:] = rows_of(peaks + highs + lows, STAT_ROWS).astype(jnp.bfloat16)

    rows = requests * tokens
    lowered = lower(sources_of(plan), arrays, halves)
    row_request = lax.broadcasted_iota(jnp.int32, (rows, 1), 0) // tokens
    ranks = jnp.zeros((rows, 1), jnp.int32)
    owners = jnp.zeros((rows, 1), jnp.int32)
    for b in range(requests):
        adapter = adapter_ref[b]
        ranks = jnp.where(row_request == b, rank_ref[adapter], ranks)
        owners = jnp.where(row_request == b, pool_ref[adapter], owners)
    column = lax.broadcasted_iota(jnp.int32, lowered.shape, 1)
    lowered = jnp.where(column < ranks, lowered, 0.0).astype(jnp.bfloat16)
    lifted = dot(lowered, up_ref[...], ((1,), (0,)))
    projected = base_ref[...] + jnp.where(owners == index_ref[0], lifted, 0.0)
    split = KEY_HEADS * HEAD_WIDTH
    step = KEY_HEADS * rows
    keys, values = [
        jnp.concatenate(
            [projected[:, at + j * HEAD_WIDTH : at + (j + 1) * HEAD_WIDTH] for j in range(KEY_HEADS)],
            axis=0,
        )
        for at in (0, split)
    ]
    own_ref[0] = keys
    own_ref[1] = values
    high = keys.astype(jnp.bfloat16)
    parts_ref[:step] = high
    parts_ref[step : 2 * step] = (keys - high.astype(jnp.float32)).astype(jnp.bfloat16)
    parts_ref[2 * step :] = values.astype(jnp.bfloat16)


def keep_kernel(sizes, plan, *refs):
    (index_ref, length_ref, own_ref, one_ref, pairs_ref) = refs[:5]
    (key_ref, value_ref, mix_ref, stat_ref) = refs[5:]
    arrays = {0: own_ref, 2: one_ref, 4: pairs_ref}

    def put(chunk, row, mix):
        at = chunk * 128 + row
        mix_ref[at : at + mix.shape[0]] = mix

    peaks, totals = attend(
        sizes, plan, True, index_ref, length_ref, arrays, key_ref, value_ref, put
    )
    stat_ref[...] = rows_of(peaks + totals, 8)


def join_kernel(sizes, plan, index_ref, mix_ref, stat_ref, proj_ref, got_parts_ref, got_ref, *refs):
    packet_refs, tail_ref = refs[:-1], refs[-1]
    requests, tokens, devices = sizes
    here = index_ref[0]
    chip = here // 2
    per_head = plan.per_head
    rows = requests * tokens
    slot_rows = plan.heads * rows
    step = KEY_HEADS * rows
    got = got_ref[MIX_ROWS:].astype(jnp.float32)
    own = stat_ref[...]
    own_peak, got_peak = own[:CHUNKS], got[:CHUNKS]
    peak = jnp.maximum(own_peak, got_peak)
    own_factor = jnp.exp(own_peak - peak)
    got_factor = jnp.exp(got_peak - peak)
    total = own_factor * own[CHUNKS : 2 * CHUNKS] + got_factor * (
        got[CHUNKS : 2 * CHUNKS] + got[2 * CHUNKS : 3 * CHUNKS]
    )
    high = round_bf16(total)
    low = total - high
    filler = jnp.zeros((128 - 2 * CHUNKS, 128), jnp.float32)
    table = jnp.transpose(jnp.concatenate([own_factor, got_factor, filler], axis=0))
    keys = proj_ref[0] + got_parts_ref[:step].astype(jnp.float32)
    keys += got_parts_ref[step : 2 * step].astype(jnp.float32)
    values = proj_ref[1] + got_parts_ref[2 * step :].astype(jnp.float32)
    keys_high = round_bf16(keys)
    for j in range(KEY_HEADS):
        part = slice(j * rows, (j + 1) * rows)
        tail_ref[j, :rows] = keys_high[part]
        tail_ref[j, rows : 2 * rows] = (keys - keys_high)[part]
        tail_ref[j, 2 * rows :] = values[part]
    stat_row = lax.broadcasted_iota(jnp.int32, (rows, HEAD_WIDTH), 0)
    packet = {id(slot): ref for slot, ref in zip([plan.own, plan.one] + plan.mine, packet_refs)}
    for c, runs in enumerate(plan.attention_chunks(slot_rows, True)):
        span = slice(c * 128, c * 128 + 128)
        mix = mix_ref[span] * table[:, c : c + 1]
        mix += got_ref[span].astype(jnp.float32) * table[:, CHUNKS + c : CHUNKS + c + 1]
        stats = jnp.where(
            stat_row == 0,
            peak[c : c + 1],
            jnp.where(
                stat_row == 1, high[c : c + 1], jnp.where(stat_row == 2, low[c : c + 1], 0.0)
            ),
        )
        for t, (slot, side) in enumerate(unit for run in runs for unit in run):
            packet_ref = packet[id(slot)]
            at = side * slot_rows
            packet_ref[at : at + slot_rows] = mix[t * slot_rows : (t + 1) * slot_rows].astype(
                jnp.bfloat16
            )
            if side == 0:
                shifted = stats if t == 0 else pltpu.roll(stats, HEAD_WIDTH - t * slot_rows, 1)
                head = (chip // per_head) ^ (here_mask(slot[0], here) // per_head)
                tail = jnp.concatenate([tail_ref[head], shifted], axis=0)
                packet_ref[packet_ref.shape[0] - 4 * rows :] = tail.astype(jnp.bfloat16)


def merge_kernel(devices, requests, tokens, swapped, own_ref, cos_ref, sin_ref, *refs):
    got_refs, out_ref = refs[:-1], refs[-1]
    rows = requests * tokens
    heads = QUERY_HEADS // devices
    mix_rows = heads * rows
    sources = len(got_refs)
    tails = [ref[ref.shape[0] - 4 * rows :].astype(jnp.float32) for ref in got_refs]
    sums = functools.reduce(jnp.add, [tail[: 3 * rows] for tail in tails])
    keys = sums[:rows] + sums[rows : 2 * rows]
    values = sums[2 * rows :].astype(jnp.bfloat16)
    turned = pltpu.roll(keys, HEAD_WIDTH // 2, 1)
    keys = (keys * cos_ref[...] + turned * sin_ref[...]).astype(jnp.bfloat16)
    query = jnp.concatenate([own_ref[h] for h in range(heads)], axis=0)
    if mix_rows < 128:
        query = jnp.concatenate(
            [query, jnp.zeros((128 - mix_rows, HEAD_WIDTH), jnp.bfloat16)], axis=0
        )
    fresh = dot(keys, query, ((1,), (1,))) * SCALE
    source = lax.broadcasted_iota(jnp.int32, fresh.shape, 0)
    column = lax.broadcasted_iota(jnp.int32, fresh.shape, 1) % rows
    allowed = (source // tokens == column // tokens) & (source % tokens <= column % tokens)
    fresh_peak = jnp.max(jnp.where(allowed, fresh, NEG_FILL), axis=0, keepdims=True)
    stats = [tail[3 * rows :] for tail in tails]
    for s in range(swapped, sources):
        stats[s] = pltpu.roll(stats[s], HEAD_WIDTH - mix_rows, 1)
    peak = functools.reduce(jnp.maximum, [stat[0:1] for stat in stats], fresh_peak)
    weights = jnp.where(allowed, jnp.exp(fresh - peak), 0.0)
    factors = [jnp.exp(stat[0:1] - peak) for stat in stats]
    total = functools.reduce(
        jnp.add,
        [factor * (stat[1:2] + stat[2:3]) for factor, stat in zip(factors, stats)],
        jnp.sum(weights, axis=0, keepdims=True),
    )
    inverse = 1.0 / total
    start = -(-(sources + 1) // rows) * rows
    table = jnp.concatenate(
        [factor * inverse for factor in factors]
        + [inverse, jnp.zeros((start - sources - 1, 128), jnp.float32), weights]
        + [jnp.zeros((128 - start - rows, 128), jnp.float32)],
        axis=0,
    )
    table = jnp.transpose(table)[:mix_rows]
    lane = lax.broadcasted_iota(jnp.int32, table.shape, 1)
    weights = jnp.where((lane >= start) & (lane < start + rows), table, 0.0).astype(jnp.bfloat16)
    values = jnp.concatenate(
        [
            jnp.zeros((start, HEAD_WIDTH), jnp.bfloat16),
            values,
            jnp.zeros((128 - start - rows, HEAD_WIDTH), jnp.bfloat16),
        ],
        axis=0,
    )
    mix = dot(weights, values, ((1,), (0,))) * table[:, sources : sources + 1]
    for s, ref in enumerate(got_refs):
        mix += ref[:mix_rows].astype(jnp.float32) * table[:, s : s + 1]
    for h in range(heads):
        tile = mix[h * rows : (h + 1) * rows]
        for b in range(requests):
            out_ref[b, :, h * HEAD_WIDTH : (h + 1) * HEAD_WIDTH] = tile[
                b * tokens : (b + 1) * tokens
            ].astype(jnp.bfloat16)


def rotation(lengths, tokens):
    half = HEAD_WIDTH // 2
    places = (lengths[:, None] + jnp.arange(tokens, dtype=jnp.int32)[None, :]).astype(jnp.float32)
    inverse_freq = jnp.exp(
        jnp.arange(half, dtype=jnp.float32) * (-2.0 * math.log(ROPE_BASE) / HEAD_WIDTH)
    )
    angles = places.reshape(-1, 1) * inverse_freq[None, :]
    cosine, sine = jnp.cos(angles), jnp.sin(angles)
    return jnp.concatenate([cosine, cosine], axis=1), jnp.concatenate([-sine, sine], axis=1)


def vmem():
    return pl.BlockSpec(memory_space=pltpu.VMEM)


def smem():
    return pl.BlockSpec(memory_space=pltpu.SMEM)


def hbm():
    return pl.BlockSpec(memory_space=pltpu.HBM)


def pinned(x):
    return pltpu.with_memory_space_constraint(x, pltpu.HBM)


def cost(flops, moved):
    return pl.CostEstimate(flops=int(flops), bytes_accessed=int(moved), transcendentals=0)


def trade(x, devices, even, odd, core=0):
    pairs = [(d, d ^ (2 * (odd if d % 2 else even) + core)) for d in range(devices)]
    return lax.ppermute(x, "tensor", pairs)


def per_device(
    hidden,
    queries,
    key_value_weight,
    adapter_down_weight,
    adapter_up_weight,
    cached_key_rows,
    cached_value_rows,
    request_adapter,
    adapter_rank_list,
    adapter_pool_row,
    lengths,
):
    requests, tokens, width = hidden.shape
    rows = requests * tokens
    devices = lax.axis_size("tensor")
    sizes = (requests, tokens, devices)
    plan = Plan(devices, width)
    heads, chunks = plan.heads, plan.chunks
    slot_rows = heads * rows
    index = lax.axis_index("tensor").reshape(1).astype(jnp.int32)

    def call(kernel, operands, in_specs, out_shape, scratch, name):
        return pl.pallas_call(
            kernel,
            out_shape=tuple(out_shape),
            in_specs=in_specs,
            out_specs=(vmem(),) * len(out_shape),
            scratch_shapes=scratch,
            compiler_params=pltpu.CompilerParams(vmem_limit_bytes=12 * MIB),
            cost_estimate=cost(10**6, 0),
            name=name,
        )(*operands)

    def core_swap(x):
        return trade(x, devices, 0, 0, core=1)

    (own,) = call(
        functools.partial(pack_kernel, requests),
        (pinned(queries), pinned(hidden)),
        [hbm()] * 2,
        [pltpu.VMEM((heads + chunks, rows, HEAD_WIDTH), jnp.bfloat16)],
        [
            pltpu.VMEM(queries.shape, jnp.bfloat16),
            pltpu.VMEM(hidden.shape, jnp.bfloat16),
            pltpu.SemaphoreType.DMA((2,)),
        ],
        "pack",
    )
    flat = requests * cached_key_rows.shape[1]
    one = trade(own, devices, plan.single, plan.single)
    other, late_own, late_lengths = lax.optimization_barrier((core_swap(own), own, lengths))
    both = jnp.concatenate([own, other], axis=0)
    mine = [trade(both, devices, a, b) for a, b in plan.pairs]

    out_width = key_value_weight.shape[1]
    parts = 4 if width % (4 * HEAD_WIDTH) == 0 else 1
    down = pinned(adapter_down_weight[0])
    rank = down.shape[1]
    big = (
        cached_key_rows.reshape(flat, -1),
        cached_value_rows.reshape(flat, -1),
        adapter_up_weight[0],
    )
    base, keys, values, up, *halves = call(
        functools.partial(base_kernel, heads, sources_of(plan)),
        (index, late_own, pinned(key_value_weight), down) + tuple(pinned(x) for x in big),
        [smem(), vmem()] + [hbm()] * 5,
        [pltpu.VMEM((rows, out_width), jnp.float32)]
        + [pltpu.VMEM(x.shape, x.dtype) for x in big]
        + [pltpu.VMEM((devices // 2, width, rank), jnp.bfloat16)] * 2,
        [
            pltpu.VMEM((parts, width // parts, out_width), jnp.bfloat16),
            pltpu.SemaphoreType.DMA((parts + 3,)),
            pltpu.SemaphoreType.DMA((devices,)),
        ],
        "base",
    )
    cosine, sine = rotation(late_lengths, tokens)
    mine = jnp.concatenate(mine, axis=0)
    mine, one, base, cosine, sine = lax.optimization_barrier((mine, one, base, cosine, sine))
    other_one, other_mine = core_swap(one), core_swap(mine)
    mix, stats = call(
        functools.partial(keep_kernel, sizes, plan),
        (index, lengths, own, one, mine, keys, values),
        [smem()] * 2 + [vmem()] * 5,
        [
            pltpu.VMEM((MIX_ROWS, HEAD_WIDTH), jnp.float32),
            pltpu.VMEM((8, HEAD_WIDTH), jnp.float32),
        ],
        [],
        "keep_states",
    )
    other_mine, mix = lax.optimization_barrier((other_mine, mix))
    arrays = (own, other, one, other_one, mine, other_mine)
    step = KEY_HEADS * rows
    send, proj, proj_parts = call(
        functools.partial(send_kernel, sizes, plan),
        (index, lengths, request_adapter, adapter_rank_list, adapter_pool_row)
        + arrays
        + (keys, values, base, up, *halves),
        [smem()] * 5 + [vmem()] * (len(arrays) + 6),
        [
            pltpu.VMEM((MIX_ROWS + STAT_ROWS, HEAD_WIDTH), jnp.bfloat16),
            pltpu.VMEM((2, step, HEAD_WIDTH), jnp.float32),
            pltpu.VMEM((3 * step, HEAD_WIDTH), jnp.bfloat16),
        ],
        [],
        "send_states",
    )
    got_parts = core_swap(proj_parts)
    got = core_swap(send)
    packets = call(
        functools.partial(join_kernel, sizes, plan),
        (index, mix, stats, proj, got_parts, got),
        [smem()] + [vmem()] * 5,
        [pltpu.VMEM((slot_rows + 4 * rows, HEAD_WIDTH), jnp.bfloat16)] * 2
        + [pltpu.VMEM((2 * slot_rows + 4 * rows, HEAD_WIDTH), jnp.bfloat16)] * len(plan.pairs),
        [pltpu.VMEM((KEY_HEADS, 3 * rows, HEAD_WIDTH), jnp.float32)],
        "join",
    )
    heard = [packets[0], trade(packets[1], devices, plan.single, plan.single)]
    heard += [trade(x, devices, a, b) for x, (a, b) in zip(packets[:1:-1], plan.pairs[::-1])]
    heard += [core_swap(x[slot_rows:]) for x in heard[2:]]
    return pl.pallas_call(
        functools.partial(merge_kernel, devices, requests, tokens, 2 + len(plan.pairs)),
        out_shape=jax.ShapeDtypeStruct((requests, tokens, heads * HEAD_WIDTH), jnp.bfloat16),
        in_specs=[vmem()] * (3 + len(heard)),
        out_specs=vmem(),
        compiler_params=pltpu.CompilerParams(vmem_limit_bytes=8 * MIB),
        name="merge_states",
    )(own, cosine, sine, *heard)


def solution(mesh):
    in_specs = (
        P("groups", None, "tensor"),
        P("groups", None, "tensor"),
        P("tensor", None),
        P("tensor", None, None),
        P("tensor", None, None),
        P("groups", "tensor", None),
        P("groups", "tensor", None),
        P("groups"),
        P(),
        P(),
        P("groups"),
    )
    out_specs = P("groups", None, "tensor")
    return jax.shard_map(
        per_device, mesh=mesh, in_specs=in_specs, out_specs=out_specs, check_vma=False
    )
```

```python
import functools
import math

import jax
import jax.numpy as jnp
from jax import lax
from jax.experimental import pallas as pl
from jax.experimental.pallas import tpu as pltpu
from jax.sharding import PartitionSpec as P

QUERY_HEADS = 128
KEY_HEADS = 8
HEAD_WIDTH = 128
ROPE_BASE = 500000.0
NEG_FILL = -(2.0**100)
SCALE = 1.0 / math.sqrt(HEAD_WIDTH)
CHUNKS = KEY_HEADS // 2
MIX_ROWS = CHUNKS * 128
STAT_ROWS = 16
MIB = 2**20


def dot(a, b, dims):
    return lax.dot_general(a, b, (dims, ((), ())), preferred_element_type=jnp.float32)


def round_bf16(x):
    return x.astype(jnp.bfloat16).astype(jnp.float32)


class Plan:
    def __init__(self, devices, width):
        lanes = devices // 2
        self.per_head = per_head = lanes // KEY_HEADS
        self.heads, self.chunks = QUERY_HEADS // devices, width // HEAD_WIDTH
        self.single = 1
        self.pairs = [(m, m + 1) for m in range(lanes - 2, 0, -2)]
        self.pairs[:2] = self.pairs[1::-1]
        size = self.heads + self.chunks
        self.own = ((0, 0), ((0, 0), (1, 0)))
        self.one = ((self.single,) * 2, ((2, 0), (3, 0)))
        self.mine, self.theirs = [], []
        for k, (a, b) in enumerate(self.pairs):
            at = size + 2 * size * k
            self.mine.append(((a, b), ((2, at), (2, at + size))))
            self.theirs.append(((b, a), ((3, at + size), (3, at))))

    def head_masks(self, unit):
        return tuple(mask // self.per_head for mask in unit[0][0])

    def units(self, keep):
        if keep:
            units = [(self.own, 0), (self.one, 0)]
            units += [(slot, side) for slot in self.mine for side in (0, 1)]
        else:
            units = [(self.own, 1), (self.one, 1)]
            units += [(slot, side) for slot in self.theirs for side in (1, 0)]
        if self.per_head > 1:
            units.sort(key=self.head_masks)
        return units

    def attention_chunks(self, slot_rows, keep):
        units = self.units(keep)
        count = HEAD_WIDTH // slot_rows
        chunks = []
        for at in range(0, len(units), count):
            runs = []
            for unit in units[at : at + count]:
                if runs and self.head_masks(runs[-1][0]) == self.head_masks(unit):
                    runs[-1].append(unit)
                else:
                    runs.append([unit])
            chunks.append(runs)
        return chunks

    def slots(self):
        return [self.own, self.one] + self.mine + self.theirs


def here_mask(masks, here):
    return masks[0] if masks[0] == masks[1] else jnp.where(here % 2 == 0, masks[0], masks[1])


def head_columns(head):
    return pl.ds(pl.multiple_of(head * HEAD_WIDTH, HEAD_WIDTH), HEAD_WIDTH)


def sources_of(plan):
    return [
        (array, tile + plan.heads, masks, side)
        for masks, places in plan.slots()
        for side, (array, tile) in enumerate(places)
    ]


def streams(sources, index_ref, down_ref, halves, sems):
    count, depth = halves[0].shape[:2]
    here = index_ref[0]
    copies = []
    for at, (_, _, masks, side) in enumerate(sources):
        source = here ^ (2 * here_mask(masks, here) + side)
        rows = pl.ds(pl.multiple_of(source * depth, depth), depth)
        place = halves[at // count].at[at % count]
        copies.append(pltpu.make_async_copy(down_ref.at[rows], place, sems.at[at]))
    return copies


def lower(sources, arrays, halves):
    total = None
    count, depth = halves[0].shape[:2]
    for at, (array, first, _, _) in enumerate(sources):
        tiles = range(first, first + depth // HEAD_WIDTH)
        hidden = jnp.concatenate([arrays[array][c] for c in tiles], axis=1)
        term = dot(hidden, halves[at // count][at % count], ((1,), (0,)))
        total = term if total is None else total + term
    return total


def tiles_of(refs, requests, out_ref, at):
    for ref in refs:
        rows = jnp.concatenate([ref[b].astype(jnp.float32) for b in range(requests)], axis=0)
        for c in range(rows.shape[1] // HEAD_WIDTH):
            tile = rows[:, c * HEAD_WIDTH : (c + 1) * HEAD_WIDTH]
            out_ref[at] = tile.astype(jnp.bfloat16)
            at += 1


def pack_kernel(requests, query_ref, hidden_ref, own_ref, query_buf, hidden_buf, sems):
    loads = [
        pltpu.make_async_copy(query_ref, query_buf, sems.at[0]),
        pltpu.make_async_copy(hidden_ref, hidden_buf, sems.at[1]),
    ]
    for load in loads:
        load.start()
    for load in loads:
        load.wait()
    tiles_of((query_buf, hidden_buf), requests, own_ref, 0)


def pack_other_kernel(requests, own_ref, query_ref, hidden_ref, other_ref, both_ref):
    size = own_ref.shape[0]
    both_ref[:size] = own_ref[...]
    tiles_of((query_ref, hidden_ref), requests, both_ref, size)
    other_ref[...] = both_ref[size:]


def base_kernel(heads, sources, index_ref, own_ref, weight_ref, down_ref, *refs):
    others, (base_ref, *held) = refs[:3], refs[3:7]
    *halves, buffer, sems, row_sems = refs[7:]
    parts, depth = buffer.shape[:2]
    loads = [
        pltpu.make_async_copy(weight_ref.at[pl.ds(p * depth, depth)], buffer.at[p], sems.at[p])
        for p in range(parts)
    ]
    others = [
        pltpu.make_async_copy(source, place, sems.at[parts + i])
        for i, (source, place) in enumerate(zip(others, held))
    ]
    others += streams(sources, index_ref, down_ref, halves, row_sems)
    for load in loads + others:
        load.start()
    tiles = depth // HEAD_WIDTH
    total = jnp.zeros(base_ref.shape, jnp.float32)
    for p in range(parts):
        hidden = jnp.concatenate([own_ref[heads + p * tiles + c] for c in range(tiles)], axis=1)
        loads[p].wait()
        total += dot(hidden, buffer[p], ((1,), (0,)))
    base_ref[...] = total
    for load in others:
        load.wait()


def attend(sizes, plan, keep, numbers, index_ref, length_ref, arrays, key_ref, value_ref, put):
    requests, tokens, devices = sizes
    here = index_ref[0]
    chip = here // 2
    per_head = plan.per_head
    slot_rows = plan.heads * requests * tokens
    positions = key_ref.shape[0] // requests
    place = lax.broadcasted_iota(jnp.int32, (requests * positions, HEAD_WIDTH), 0)
    column = lax.broadcasted_iota(jnp.int32, (requests * positions, HEAD_WIDTH), 1)
    place_request = place // positions
    limit = jnp.zeros_like(place)
    for b in range(requests):
        limit = jnp.where(place_request == b, length_ref[b], limit)
    allowed = (here * positions + place % positions < limit) & (
        place_request == (column // tokens) % requests
    )
    peaks, totals = [], []
    chunks = plan.attention_chunks(slot_rows, keep)
    for number, runs in enumerate(chunks[i] for i in numbers):
        places = [slot[1][side] for run in runs for slot, side in run]
        query = jnp.concatenate(
            [arrays[array][tile + h] for array, tile in places for h in range(plan.heads)], axis=0
        )
        spots = [
            head_columns((chip // per_head) ^ (here_mask(run[0][0][0], here) // per_head))
            for run in runs
        ]
        share = HEAD_WIDTH // len(runs)
        scores = None
        for i, spot in enumerate(spots):
            part = dot(key_ref[:, spot], query, ((1,), (1,)))
            scores = part if scores is None else jnp.where(column < i * share, scores, part)
        scores = jnp.where(allowed, scores * SCALE, NEG_FILL)
        peak = round_bf16(jnp.max(scores, axis=0, keepdims=True))
        weights = jnp.exp(scores - peak)
        peaks.append(peak)
        totals.append(jnp.sum(weights, axis=0, keepdims=True))
        weights = jnp.transpose(weights.astype(jnp.bfloat16))
        for i, spot in enumerate(spots):
            own = slice(i * share, (i + 1) * share)
            put(number, i * share, dot(weights[own], value_ref[:, spot], ((1,), (0,))))
    return peaks, totals


def rows_of(items, count):
    row = lax.broadcasted_iota(jnp.int32, (count, HEAD_WIDTH), 0)
    out = jnp.zeros((count, HEAD_WIDTH), jnp.float32)
    for i, item in enumerate(items):
        out = jnp.where(row == i, item, out)
    return out


def send_kernel(sizes, plan, *refs):
    (index_ref, length_ref, adapter_ref, rank_ref, pool_ref, *arrays) = refs[:-8]
    (key_ref, value_ref, base_ref, up_ref, *halves, send_ref, own_ref) = refs[-8:]
    requests, tokens, devices = sizes

    def put(chunk, row, mix):
        at = chunk * 128 + row
        send_ref[at : at + mix.shape[0]] = mix.astype(jnp.bfloat16)

    peaks, totals = attend(
        sizes, plan, False, range(CHUNKS), index_ref, length_ref, arrays, key_ref, value_ref, put
    )
    highs = [round_bf16(total) for total in totals]
    lows = [total - high for total, high in zip(totals, highs)]
    send_ref[-STAT_ROWS:] = rows_of(peaks + highs + lows, STAT_ROWS).astype(jnp.bfloat16)

    rows = requests * tokens
    lowered = lower(sources_of(plan), arrays, halves)
    row_request = lax.broadcasted_iota(jnp.int32, (rows, 1), 0) // tokens
    ranks = jnp.zeros((rows, 1), jnp.int32)
    owners = jnp.zeros((rows, 1), jnp.int32)
    for b in range(requests):
        adapter = adapter_ref[b]
        ranks = jnp.where(row_request == b, rank_ref[adapter], ranks)
        owners = jnp.where(row_request == b, pool_ref[adapter], owners)
    column = lax.broadcasted_iota(jnp.int32, lowered.shape, 1)
    lowered = jnp.where(column < ranks, lowered, 0.0).astype(jnp.bfloat16)
    lifted = dot(lowered, up_ref[...], ((1,), (0,)))
    projected = base_ref[...] + jnp.where(owners == index_ref[0], lifted, 0.0)
    split = KEY_HEADS * HEAD_WIDTH
    step = KEY_HEADS * rows
    keys, values = [
        jnp.concatenate(
            [projected[:, at + j * HEAD_WIDTH : at + (j + 1) * HEAD_WIDTH] for j in range(KEY_HEADS)],
            axis=0,
        )
        for at in (0, split)
    ]
    own_ref[0] = keys
    own_ref[1] = values
    high = keys.astype(jnp.bfloat16)
    send_ref[MIX_ROWS : MIX_ROWS + step] = high
    send_ref[MIX_ROWS + step : MIX_ROWS + 2 * step] = (keys - high.astype(jnp.float32)).astype(
        jnp.bfloat16
    )
    send_ref[MIX_ROWS + 2 * step : MIX_ROWS + 3 * step] = values.astype(jnp.bfloat16)


def keep_kernel(sizes, plan, numbers, *refs):
    (index_ref, length_ref, own_ref, near_ref, key_ref, value_ref, mix_ref, stat_ref) = refs
    arrays = {0: own_ref, 2: near_ref}

    def put(chunk, row, mix):
        at = chunk * 128 + row
        mix_ref[at : at + mix.shape[0]] = mix

    peaks, totals = attend(
        sizes, plan, True, numbers, index_ref, length_ref, arrays, key_ref, value_ref, put
    )
    stat_ref[...] = rows_of(peaks + totals, 8)


def join_kernel(sizes, plan, index_ref, *refs):
    mix_refs, stat_refs, (proj_ref, got_ref) = refs[:2], refs[2:4], refs[4:6]
    packet_refs, tail_ref = refs[6:-1], refs[-1]
    requests, tokens, devices = sizes
    here = index_ref[0]
    chip = here // 2
    per_head = plan.per_head
    rows = requests * tokens
    slot_rows = plan.heads * rows
    step = KEY_HEADS * rows
    got = got_ref[MIX_ROWS + 3 * step :].astype(jnp.float32)
    half = CHUNKS // 2
    own_peak = jnp.concatenate([ref[:half] for ref in stat_refs], axis=0)
    own_total = jnp.concatenate([ref[half : 2 * half] for ref in stat_refs], axis=0)
    got_peak = got[:CHUNKS]
    peak = jnp.maximum(own_peak, got_peak)
    own_factor = jnp.exp(own_peak - peak)
    got_factor = jnp.exp(got_peak - peak)
    total = own_factor * own_total + got_factor * (
        got[CHUNKS : 2 * CHUNKS] + got[2 * CHUNKS : 3 * CHUNKS]
    )
    high = round_bf16(total)
    low = total - high
    filler = jnp.zeros((128 - 2 * CHUNKS, 128), jnp.float32)
    table = jnp.transpose(jnp.concatenate([own_factor, got_factor, filler], axis=0))
    parts = got_ref[MIX_ROWS : MIX_ROWS + 3 * step].astype(jnp.float32)
    keys = proj_ref[0] + parts[:step] + parts[step : 2 * step]
    values = proj_ref[1] + parts[2 * step :]
    keys_high = round_bf16(keys)
    for j in range(KEY_HEADS):
        part = slice(j * rows, (j + 1) * rows)
        tail_ref[j, :rows] = keys_high[part]
        tail_ref[j, rows : 2 * rows] = (keys - keys_high)[part]
        tail_ref[j, 2 * rows :] = values[part]
    stat_row = lax.broadcasted_iota(jnp.int32, (rows, HEAD_WIDTH), 0)
    packet = {id(slot): ref for slot, ref in zip([plan.own, plan.one] + plan.mine, packet_refs)}
    for c, runs in enumerate(plan.attention_chunks(slot_rows, True)):
        span = slice(c * 128, c * 128 + 128)
        at = c % half * 128
        mix = mix_refs[c // half][at : at + 128] * table[:, c : c + 1]
        mix += got_ref[span].astype(jnp.float32) * table[:, CHUNKS + c : CHUNKS + c + 1]
        stats = jnp.where(
            stat_row == 0,
            peak[c : c + 1],
            jnp.where(
                stat_row == 1, high[c : c + 1], jnp.where(stat_row == 2, low[c : c + 1], 0.0)
            ),
        )
        for t, (slot, side) in enumerate(unit for run in runs for unit in run):
            packet_ref = packet[id(slot)]
            at = side * slot_rows
            packet_ref[at : at + slot_rows] = mix[t * slot_rows : (t + 1) * slot_rows].astype(
                jnp.bfloat16
            )
            if side == 0:
                shifted = stats if t == 0 else pltpu.roll(stats, HEAD_WIDTH - t * slot_rows, 1)
                head = (chip // per_head) ^ (here_mask(slot[0], here) // per_head)
                tail = jnp.concatenate([tail_ref[head], shifted], axis=0)
                packet_ref[packet_ref.shape[0] - 4 * rows :] = tail.astype(jnp.bfloat16)


def merge_kernel(devices, requests, tokens, swapped, own_ref, cos_ref, sin_ref, *refs):
    got_refs, out_ref = refs[:-1], refs[-1]
    rows = requests * tokens
    heads = QUERY_HEADS // devices
    mix_rows = heads * rows
    sources = len(got_refs)
    tails = [ref[ref.shape[0] - 4 * rows :].astype(jnp.float32) for ref in got_refs]
    sums = functools.reduce(jnp.add, [tail[: 3 * rows] for tail in tails])
    keys = sums[:rows] + sums[rows : 2 * rows]
    values = sums[2 * rows :].astype(jnp.bfloat16)
    turned = pltpu.roll(keys, HEAD_WIDTH // 2, 1)
    keys = (keys * cos_ref[...] + turned * sin_ref[...]).astype(jnp.bfloat16)
    query = jnp.concatenate([own_ref[h] for h in range(heads)], axis=0)
    if mix_rows < 128:
        query = jnp.concatenate(
            [query, jnp.zeros((128 - mix_rows, HEAD_WIDTH), jnp.bfloat16)], axis=0
        )
    fresh = dot(keys, query, ((1,), (1,))) * SCALE
    source = lax.broadcasted_iota(jnp.int32, fresh.shape, 0)
    column = lax.broadcasted_iota(jnp.int32, fresh.shape, 1) % rows
    allowed = (source // tokens == column // tokens) & (source % tokens <= column % tokens)
    fresh_peak = jnp.max(jnp.where(allowed, fresh, NEG_FILL), axis=0, keepdims=True)
    stats = [tail[3 * rows :] for tail in tails]
    for s in range(swapped, sources):
        stats[s] = pltpu.roll(stats[s], HEAD_WIDTH - mix_rows, 1)
    peak = functools.reduce(jnp.maximum, [stat[0:1] for stat in stats], fresh_peak)
    weights = jnp.where(allowed, jnp.exp(fresh - peak), 0.0)
    factors = [jnp.exp(stat[0:1] - peak) for stat in stats]
    total = functools.reduce(
        jnp.add,
        [factor * (stat[1:2] + stat[2:3]) for factor, stat in zip(factors, stats)],
        jnp.sum(weights, axis=0, keepdims=True),
    )
    inverse = 1.0 / total
    start = -(-(sources + 1) // rows) * rows
    table = jnp.concatenate(
        [factor * inverse for factor in factors]
        + [inverse, jnp.zeros((start - sources - 1, 128), jnp.float32), weights]
        + [jnp.zeros((128 - start - rows, 128), jnp.float32)],
        axis=0,
    )
    table = jnp.transpose(table)[:mix_rows]
    lane = lax.broadcasted_iota(jnp.int32, table.shape, 1)
    weights = jnp.where((lane >= start) & (lane < start + rows), table, 0.0).astype(jnp.bfloat16)
    values = jnp.concatenate(
        [
            jnp.zeros((start, HEAD_WIDTH), jnp.bfloat16),
            values,
            jnp.zeros((128 - start - rows, HEAD_WIDTH), jnp.bfloat16),
        ],
        axis=0,
    )
    mix = dot(weights, values, ((1,), (0,))) * table[:, sources : sources + 1]
    for s, ref in enumerate(got_refs):
        mix += ref[:mix_rows].astype(jnp.float32) * table[:, s : s + 1]
    for h in range(heads):
        tile = mix[h * rows : (h + 1) * rows]
        for b in range(requests):
            out_ref[b, :, h * HEAD_WIDTH : (h + 1) * HEAD_WIDTH] = tile[
                b * tokens : (b + 1) * tokens
            ].astype(jnp.bfloat16)


def rotation(lengths, tokens):
    half = HEAD_WIDTH // 2
    places = (lengths[:, None] + jnp.arange(tokens, dtype=jnp.int32)[None, :]).astype(jnp.float32)
    inverse_freq = jnp.exp(
        jnp.arange(half, dtype=jnp.float32) * (-2.0 * math.log(ROPE_BASE) / HEAD_WIDTH)
    )
    angles = places.reshape(-1, 1) * inverse_freq[None, :]
    cosine, sine = jnp.cos(angles), jnp.sin(angles)
    return jnp.concatenate([cosine, cosine], axis=1), jnp.concatenate([-sine, sine], axis=1)


def vmem():
    return pl.BlockSpec(memory_space=pltpu.VMEM)


def smem():
    return pl.BlockSpec(memory_space=pltpu.SMEM)


def hbm():
    return pl.BlockSpec(memory_space=pltpu.HBM)


def pinned(x):
    return pltpu.with_memory_space_constraint(x, pltpu.HBM)


def cost(flops, moved):
    return pl.CostEstimate(flops=int(flops), bytes_accessed=int(moved), transcendentals=0)


def trade(x, devices, even, odd, core=0):
    pairs = [(d, d ^ (2 * (odd if d % 2 else even) + core)) for d in range(devices)]
    return lax.ppermute(x, "tensor", pairs)


def per_device(
    hidden,
    queries,
    key_value_weight,
    adapter_down_weight,
    adapter_up_weight,
    cached_key_rows,
    cached_value_rows,
    request_adapter,
    adapter_rank_list,
    adapter_pool_row,
    lengths,
):
    requests, tokens, width = hidden.shape
    rows = requests * tokens
    devices = lax.axis_size("tensor")
    sizes = (requests, tokens, devices)
    plan = Plan(devices, width)
    heads, chunks = plan.heads, plan.chunks
    slot_rows = heads * rows
    index = lax.axis_index("tensor").reshape(1).astype(jnp.int32)

    def call(kernel, operands, in_specs, out_shape, scratch, name):
        return pl.pallas_call(
            kernel,
            out_shape=tuple(out_shape),
            in_specs=in_specs,
            out_specs=(vmem(),) * len(out_shape),
            scratch_shapes=scratch,
            compiler_params=pltpu.CompilerParams(vmem_limit_bytes=12 * MIB),
            cost_estimate=cost(10**6, 0),
            name=name,
        )(*operands)

    def core_swap(x):
        return trade(x, devices, 0, 0, core=1)

    (own,) = call(
        functools.partial(pack_kernel, requests),
        (pinned(queries), pinned(hidden)),
        [hbm()] * 2,
        [pltpu.VMEM((heads + chunks, rows, HEAD_WIDTH), jnp.bfloat16)],
        [
            pltpu.VMEM(queries.shape, jnp.bfloat16),
            pltpu.VMEM(hidden.shape, jnp.bfloat16),
            pltpu.SemaphoreType.DMA((2,)),
        ],
        "pack",
    )
    flat = requests * cached_key_rows.shape[1]
    other_queries, other_hidden = core_swap(queries), core_swap(hidden)
    other_queries, late_own, late_lengths = lax.optimization_barrier((other_queries, own, lengths))
    shape = (heads + chunks, rows, HEAD_WIDTH)
    other, both = call(
        functools.partial(pack_other_kernel, requests),
        (late_own, other_queries, other_hidden),
        [vmem()] * 3,
        [pltpu.VMEM(shape, jnp.bfloat16), pltpu.VMEM((2 * shape[0],) + shape[1:], jnp.bfloat16)],
        [],
        "pack_other",
    )
    both, late_own = lax.optimization_barrier((both, late_own))
    one = trade(late_own, devices, plan.single, plan.single)
    mine = [trade(both, devices, a, b) for a, b in plan.pairs]
    flat = requests * cached_key_rows.shape[1]

    out_width = key_value_weight.shape[1]
    parts = 4 if width % (4 * HEAD_WIDTH) == 0 else 1
    down = pinned(adapter_down_weight[0])
    rank = down.shape[1]
    big = (
        cached_key_rows.reshape(flat, -1),
        cached_value_rows.reshape(flat, -1),
        adapter_up_weight[0],
    )
    base, keys, values, up, *halves = call(
        functools.partial(base_kernel, heads, sources_of(plan)),
        (index, late_own, pinned(key_value_weight), down) + tuple(pinned(x) for x in big),
        [smem(), vmem()] + [hbm()] * 5,
        [pltpu.VMEM((rows, out_width), jnp.float32)]
        + [pltpu.VMEM(x.shape, x.dtype) for x in big]
        + [pltpu.VMEM((devices // 2, width, rank), jnp.bfloat16)] * 2,
        [
            pltpu.VMEM((parts, width // parts, out_width), jnp.bfloat16),
            pltpu.SemaphoreType.DMA((parts + 3,)),
            pltpu.SemaphoreType.DMA((devices,)),
        ],
        "base",
    )
    cosine, sine = rotation(late_lengths, tokens)
    near = jnp.concatenate([one] + mine, axis=0)
    near, base, cosine, sine = lax.optimization_barrier((near, base, cosine, sine))
    other_near = core_swap(near)

    def keep(numbers):
        return call(
            functools.partial(keep_kernel, sizes, plan, numbers),
            (index, lengths, own, near, keys, values),
            [smem()] * 2 + [vmem()] * 4,
            [
                pltpu.VMEM((MIX_ROWS // 2, HEAD_WIDTH), jnp.float32),
                pltpu.VMEM((8, HEAD_WIDTH), jnp.float32),
            ],
            [],
            "keep_states",
        )

    first_mix, first_stats = keep(range(CHUNKS // 2))
    other_near, first_mix = lax.optimization_barrier((other_near, first_mix))
    arrays = (own, other, near, other_near)
    step = KEY_HEADS * rows
    send, proj = call(
        functools.partial(send_kernel, sizes, plan),
        (index, lengths, request_adapter, adapter_rank_list, adapter_pool_row)
        + arrays
        + (keys, values, base, up, *halves),
        [smem()] * 5 + [vmem()] * (len(arrays) + 6),
        [
            pltpu.VMEM((MIX_ROWS + 3 * step + STAT_ROWS, HEAD_WIDTH), jnp.bfloat16),
            pltpu.VMEM((2, step, HEAD_WIDTH), jnp.float32),
        ],
        [],
        "send_states",
    )
    got = core_swap(send)
    second_mix, second_stats = keep(range(CHUNKS // 2, CHUNKS))
    packets = call(
        functools.partial(join_kernel, sizes, plan),
        (index, first_mix, second_mix, first_stats, second_stats, proj, got),
        [smem()] + [vmem()] * 6,
        [pltpu.VMEM((slot_rows + 4 * rows, HEAD_WIDTH), jnp.bfloat16)] * 2
        + [pltpu.VMEM((2 * slot_rows + 4 * rows, HEAD_WIDTH), jnp.bfloat16)] * len(plan.pairs),
        [pltpu.VMEM((KEY_HEADS, 3 * rows, HEAD_WIDTH), jnp.float32)],
        "join",
    )
    heard = [packets[0], trade(packets[1], devices, plan.single, plan.single)]
    heard += [trade(x, devices, a, b) for x, (a, b) in zip(packets[2:], plan.pairs)]
    heard += [core_swap(x[slot_rows:]) for x in heard[2:]]
    return pl.pallas_call(
        functools.partial(merge_kernel, devices, requests, tokens, 2 + len(plan.pairs)),
        out_shape=jax.ShapeDtypeStruct((requests, tokens, heads * HEAD_WIDTH), jnp.bfloat16),
        in_specs=[vmem()] * (3 + len(heard)),
        out_specs=vmem(),
        compiler_params=pltpu.CompilerParams(vmem_limit_bytes=8 * MIB),
        name="merge_states",
    )(own, cosine, sine, *heard)


def solution(mesh):
    in_specs = (
        P("groups", None, "tensor"),
        P("groups", None, "tensor"),
        P("tensor", None),
        P("tensor", None, None),
        P("tensor", None, None),
        P("groups", "tensor", None),
        P("groups", "tensor", None),
        P("groups"),
        P(),
        P(),
        P("groups"),
    )
    out_specs = P("groups", None, "tensor")
    return jax.shard_map(
        per_device, mesh=mesh, in_specs=in_specs, out_specs=out_specs, check_vma=False
    )
```

```python
import functools
import math

import jax
import jax.numpy as jnp
from jax import lax
from jax.experimental import pallas as pl
from jax.experimental.pallas import tpu as pltpu
from jax.sharding import PartitionSpec as P

QUERY_HEADS = 128
KEY_HEADS = 8
HEAD_WIDTH = 128
ROPE_BASE = 500000.0
NEG_FILL = -(2.0**100)
SCALE = 1.0 / math.sqrt(HEAD_WIDTH)
CHUNKS = KEY_HEADS // 2
MIX_ROWS = CHUNKS * 128
STAT_ROWS = 16
MIB = 2**20


def dot(a, b, dims):
    return lax.dot_general(a, b, (dims, ((), ())), preferred_element_type=jnp.float32)


def round_bf16(x):
    return x.astype(jnp.bfloat16).astype(jnp.float32)


class Plan:
    def __init__(self, devices, width):
        lanes = devices // 2
        self.per_head = per_head = lanes // KEY_HEADS
        self.heads, self.chunks = QUERY_HEADS // devices, width // HEAD_WIDTH
        self.single = 1
        self.pairs = [(m, m + 1) for m in range(lanes - 2, 0, -2)]
        self.pairs[:2] = self.pairs[1::-1]
        size = self.heads + self.chunks
        self.own = ((0, 0), ((0, 0), (1, 0)))
        self.one = ((self.single,) * 2, ((2, 0), (3, 0)))
        self.mine, self.theirs = [], []
        for k, (a, b) in enumerate(self.pairs):
            at = size + 2 * size * k
            self.mine.append(((a, b), ((2, at), (2, at + size))))
            self.theirs.append(((b, a), ((3, at + size), (3, at))))

    def head_masks(self, unit):
        return tuple(mask // self.per_head for mask in unit[0][0])

    def units(self, keep):
        if keep:
            units = [(self.own, 0), (self.one, 0)]
            units += [(slot, side) for slot in self.mine for side in (0, 1)]
        else:
            units = [(self.own, 1), (self.one, 1)]
            units += [(slot, side) for slot in self.theirs for side in (1, 0)]
        if self.per_head > 1:
            units.sort(key=self.head_masks)
        return units

    def attention_chunks(self, slot_rows, keep):
        units = self.units(keep)
        count = HEAD_WIDTH // slot_rows
        chunks = []
        for at in range(0, len(units), count):
            runs = []
            for unit in units[at : at + count]:
                if runs and self.head_masks(runs[-1][0]) == self.head_masks(unit):
                    runs[-1].append(unit)
                else:
                    runs.append([unit])
            chunks.append(runs)
        return chunks

    def slots(self):
        return [self.own, self.one] + self.mine + self.theirs


def here_mask(masks, here):
    return masks[0] if masks[0] == masks[1] else jnp.where(here % 2 == 0, masks[0], masks[1])


def head_columns(head):
    return pl.ds(pl.multiple_of(head * HEAD_WIDTH, HEAD_WIDTH), HEAD_WIDTH)


def sources_of(plan):
    return [
        (array, tile + plan.heads, masks, side)
        for masks, places in plan.slots()
        for side, (array, tile) in enumerate(places)
    ]


def streams(sources, index_ref, down_ref, halves, sems):
    count, depth = halves[0].shape[:2]
    here = index_ref[0]
    copies = []
    for at, (_, _, masks, side) in enumerate(sources):
        source = here ^ (2 * here_mask(masks, here) + side)
        rows = pl.ds(pl.multiple_of(source * depth, depth), depth)
        place = halves[at // count].at[at % count]
        copies.append(pltpu.make_async_copy(down_ref.at[rows], place, sems.at[at]))
    return copies


def lower(sources, arrays, halves):
    total = None
    count, depth = halves[0].shape[:2]
    for at, (array, first, _, _) in enumerate(sources):
        tiles = range(first, first + depth // HEAD_WIDTH)
        hidden = jnp.concatenate([arrays[array][c] for c in tiles], axis=1)
        term = dot(hidden, halves[at // count][at % count], ((1,), (0,)))
        total = term if total is None else total + term
    return total


def tiles_of(refs, requests, out_ref, at):
    for ref in refs:
        rows = jnp.concatenate([ref[b].astype(jnp.float32) for b in range(requests)], axis=0)
        for c in range(rows.shape[1] // HEAD_WIDTH):
            tile = rows[:, c * HEAD_WIDTH : (c + 1) * HEAD_WIDTH]
            out_ref[at] = tile.astype(jnp.bfloat16)
            at += 1


def pack_kernel(requests, query_ref, hidden_ref, key_ref, value_ref, *refs):
    own_ref, held_key_ref, held_value_ref, query_buf, hidden_buf, sems = refs
    sources = (query_ref, hidden_ref, key_ref, value_ref)
    places = (query_buf, hidden_buf, held_key_ref, held_value_ref)
    loads = [
        pltpu.make_async_copy(source, place, sems.at[i])
        for i, (source, place) in enumerate(zip(sources, places))
    ]
    for load in loads:
        load.start()
    for load in loads[:2]:
        load.wait()
    tiles_of((query_buf, hidden_buf), requests, own_ref, 0)
    for load in loads[2:]:
        load.wait()


def pack_other_kernel(requests, own_ref, query_ref, hidden_ref, other_ref, both_ref):
    size = own_ref.shape[0]
    both_ref[:size] = own_ref[...]
    tiles_of((query_ref, hidden_ref), requests, both_ref, size)
    other_ref[...] = both_ref[size:]


def base_kernel(heads, sources, index_ref, own_ref, weight_ref, down_ref, *refs):
    up_ref, base_ref, held_up_ref, *halves, buffer, sems, row_sems = refs
    parts, depth = buffer.shape[:2]
    loads = [
        pltpu.make_async_copy(weight_ref.at[pl.ds(p * depth, depth)], buffer.at[p], sems.at[p])
        for p in range(parts)
    ]
    others = [pltpu.make_async_copy(up_ref, held_up_ref, sems.at[parts])]
    others += streams(sources, index_ref, down_ref, halves, row_sems)
    for load in loads + others:
        load.start()
    tiles = depth // HEAD_WIDTH
    total = jnp.zeros(base_ref.shape, jnp.float32)
    for p in range(parts):
        hidden = jnp.concatenate([own_ref[heads + p * tiles + c] for c in range(tiles)], axis=1)
        loads[p].wait()
        total += dot(hidden, buffer[p], ((1,), (0,)))
    base_ref[...] = total
    for load in others:
        load.wait()


def attend(sizes, plan, keep, numbers, index_ref, length_ref, arrays, key_ref, value_ref, put):
    requests, tokens, devices = sizes
    here = index_ref[0]
    chip = here // 2
    per_head = plan.per_head
    slot_rows = plan.heads * requests * tokens
    positions = key_ref.shape[0] // requests
    place = lax.broadcasted_iota(jnp.int32, (requests * positions, HEAD_WIDTH), 0)
    column = lax.broadcasted_iota(jnp.int32, (requests * positions, HEAD_WIDTH), 1)
    place_request = place // positions
    limit = jnp.zeros_like(place)
    for b in range(requests):
        limit = jnp.where(place_request == b, length_ref[b], limit)
    allowed = (here * positions + place % positions < limit) & (
        place_request == (column // tokens) % requests
    )
    peaks, totals = [], []
    chunks = plan.attention_chunks(slot_rows, keep)
    for number, runs in enumerate(chunks[i] for i in numbers):
        places = [slot[1][side] for run in runs for slot, side in run]
        query = jnp.concatenate(
            [arrays[array][tile + h] for array, tile in places for h in range(plan.heads)], axis=0
        )
        spots = [
            head_columns((chip // per_head) ^ (here_mask(run[0][0][0], here) // per_head))
            for run in runs
        ]
        share = HEAD_WIDTH // len(runs)
        scores = None
        for i, spot in enumerate(spots):
            part = dot(key_ref[:, spot], query, ((1,), (1,)))
            scores = part if scores is None else jnp.where(column < i * share, scores, part)
        scores = jnp.where(allowed, scores * SCALE, NEG_FILL)
        peak = round_bf16(jnp.max(scores, axis=0, keepdims=True))
        weights = jnp.exp(scores - peak)
        peaks.append(peak)
        totals.append(jnp.sum(weights, axis=0, keepdims=True))
        weights = jnp.transpose(weights.astype(jnp.bfloat16))
        for i, spot in enumerate(spots):
            own = slice(i * share, (i + 1) * share)
            put(number, i * share, dot(weights[own], value_ref[:, spot], ((1,), (0,))))
    return peaks, totals


def rows_of(items, count):
    row = lax.broadcasted_iota(jnp.int32, (count, HEAD_WIDTH), 0)
    out = jnp.zeros((count, HEAD_WIDTH), jnp.float32)
    for i, item in enumerate(items):
        out = jnp.where(row == i, item, out)
    return out


def send_kernel(sizes, plan, *refs):
    (index_ref, length_ref, adapter_ref, rank_ref, pool_ref, *arrays) = refs[:-8]
    (key_ref, value_ref, base_ref, up_ref, *halves, send_ref, own_ref) = refs[-8:]
    requests, tokens, devices = sizes

    def put(chunk, row, mix):
        at = chunk * 128 + row
        send_ref[at : at + mix.shape[0]] = mix.astype(jnp.bfloat16)

    peaks, totals = attend(
        sizes, plan, False, range(CHUNKS), index_ref, length_ref, arrays, key_ref, value_ref, put
    )
    highs = [round_bf16(total) for total in totals]
    lows = [total - high for total, high in zip(totals, highs)]
    send_ref[-STAT_ROWS:] = rows_of(peaks + highs + lows, STAT_ROWS).astype(jnp.bfloat16)

    rows = requests * tokens
    lowered = lower(sources_of(plan), arrays, halves)
    row_request = lax.broadcasted_iota(jnp.int32, (rows, 1), 0) // tokens
    ranks = jnp.zeros((rows, 1), jnp.int32)
    owners = jnp.zeros((rows, 1), jnp.int32)
    for b in range(requests):
        adapter = adapter_ref[b]
        ranks = jnp.where(row_request == b, rank_ref[adapter], ranks)
        owners = jnp.where(row_request == b, pool_ref[adapter], owners)
    column = lax.broadcasted_iota(jnp.int32, lowered.shape, 1)
    lowered = jnp.where(column < ranks, lowered, 0.0).astype(jnp.bfloat16)
    lifted = dot(lowered, up_ref[...], ((1,), (0,)))
    projected = base_ref[...] + jnp.where(owners == index_ref[0], lifted, 0.0)
    split = KEY_HEADS * HEAD_WIDTH
    step = KEY_HEADS * rows
    keys, values = [
        jnp.concatenate(
            [projected[:, at + j * HEAD_WIDTH : at + (j + 1) * HEAD_WIDTH] for j in range(KEY_HEADS)],
            axis=0,
        )
        for at in (0, split)
    ]
    own_ref[0] = keys
    own_ref[1] = values
    high = keys.astype(jnp.bfloat16)
    send_ref[MIX_ROWS : MIX_ROWS + step] = high
    send_ref[MIX_ROWS + step : MIX_ROWS + 2 * step] = (keys - high.astype(jnp.float32)).astype(
        jnp.bfloat16
    )
    send_ref[MIX_ROWS + 2 * step : MIX_ROWS + 3 * step] = values.astype(jnp.bfloat16)


def keep_kernel(sizes, plan, numbers, *refs):
    (index_ref, length_ref, own_ref, near_ref, key_ref, value_ref, mix_ref, stat_ref) = refs
    arrays = {0: own_ref, 2: near_ref}

    def put(chunk, row, mix):
        at = chunk * 128 + row
        mix_ref[at : at + mix.shape[0]] = mix

    peaks, totals = attend(
        sizes, plan, True, numbers, index_ref, length_ref, arrays, key_ref, value_ref, put
    )
    stat_ref[...] = rows_of(peaks + totals, 8)


def join_kernel(sizes, plan, index_ref, *refs):
    mix_refs, stat_refs, (proj_ref, got_ref) = refs[:2], refs[2:4], refs[4:6]
    packet_refs, tail_ref = refs[6:-1], refs[-1]
    requests, tokens, devices = sizes
    here = index_ref[0]
    chip = here // 2
    per_head = plan.per_head
    rows = requests * tokens
    slot_rows = plan.heads * rows
    step = KEY_HEADS * rows
    got = got_ref[MIX_ROWS + 3 * step :].astype(jnp.float32)
    half = CHUNKS // 2
    own_peak = jnp.concatenate([ref[:half] for ref in stat_refs], axis=0)
    own_total = jnp.concatenate([ref[half : 2 * half] for ref in stat_refs], axis=0)
    got_peak = got[:CHUNKS]
    peak = jnp.maximum(own_peak, got_peak)
    own_factor = jnp.exp(own_peak - peak)
    got_factor = jnp.exp(got_peak - peak)
    total = own_factor * own_total + got_factor * (
        got[CHUNKS : 2 * CHUNKS] + got[2 * CHUNKS : 3 * CHUNKS]
    )
    high = round_bf16(total)
    low = total - high
    filler = jnp.zeros((128 - 2 * CHUNKS, 128), jnp.float32)
    table = jnp.transpose(jnp.concatenate([own_factor, got_factor, filler], axis=0))
    parts = got_ref[MIX_ROWS : MIX_ROWS + 3 * step].astype(jnp.float32)
    keys = proj_ref[0] + parts[:step] + parts[step : 2 * step]
    values = proj_ref[1] + parts[2 * step :]
    keys_high = round_bf16(keys)
    for j in range(KEY_HEADS):
        part = slice(j * rows, (j + 1) * rows)
        tail_ref[j, :rows] = keys_high[part]
        tail_ref[j, rows : 2 * rows] = (keys - keys_high)[part]
        tail_ref[j, 2 * rows :] = values[part]
    stat_row = lax.broadcasted_iota(jnp.int32, (rows, HEAD_WIDTH), 0)
    packet = {id(slot): ref for slot, ref in zip([plan.own, plan.one] + plan.mine, packet_refs)}
    for c, runs in enumerate(plan.attention_chunks(slot_rows, True)):
        span = slice(c * 128, c * 128 + 128)
        at = c % half * 128
        mix = mix_refs[c // half][at : at + 128] * table[:, c : c + 1]
        mix += got_ref[span].astype(jnp.float32) * table[:, CHUNKS + c : CHUNKS + c + 1]
        stats = jnp.where(
            stat_row == 0,
            peak[c : c + 1],
            jnp.where(
                stat_row == 1, high[c : c + 1], jnp.where(stat_row == 2, low[c : c + 1], 0.0)
            ),
        )
        for t, (slot, side) in enumerate(unit for run in runs for unit in run):
            packet_ref = packet[id(slot)]
            at = side * slot_rows
            packet_ref[at : at + slot_rows] = mix[t * slot_rows : (t + 1) * slot_rows].astype(
                jnp.bfloat16
            )
            if side == 0:
                shifted = stats if t == 0 else pltpu.roll(stats, HEAD_WIDTH - t * slot_rows, 1)
                head = (chip // per_head) ^ (here_mask(slot[0], here) // per_head)
                tail = jnp.concatenate([tail_ref[head], shifted], axis=0)
                packet_ref[packet_ref.shape[0] - 4 * rows :] = tail.astype(jnp.bfloat16)


def merge_kernel(devices, requests, tokens, swapped, own_ref, cos_ref, sin_ref, *refs):
    got_refs, out_ref = refs[:-1], refs[-1]
    rows = requests * tokens
    heads = QUERY_HEADS // devices
    mix_rows = heads * rows
    sources = len(got_refs)
    tails = [ref[ref.shape[0] - 4 * rows :].astype(jnp.float32) for ref in got_refs]
    sums = functools.reduce(jnp.add, [tail[: 3 * rows] for tail in tails])
    keys = sums[:rows] + sums[rows : 2 * rows]
    values = sums[2 * rows :].astype(jnp.bfloat16)
    turned = pltpu.roll(keys, HEAD_WIDTH // 2, 1)
    keys = (keys * cos_ref[...] + turned * sin_ref[...]).astype(jnp.bfloat16)
    query = jnp.concatenate([own_ref[h] for h in range(heads)], axis=0)
    if mix_rows < 128:
        query = jnp.concatenate(
            [query, jnp.zeros((128 - mix_rows, HEAD_WIDTH), jnp.bfloat16)], axis=0
        )
    fresh = dot(keys, query, ((1,), (1,))) * SCALE
    source = lax.broadcasted_iota(jnp.int32, fresh.shape, 0)
    column = lax.broadcasted_iota(jnp.int32, fresh.shape, 1) % rows
    allowed = (source // tokens == column // tokens) & (source % tokens <= column % tokens)
    fresh_peak = jnp.max(jnp.where(allowed, fresh, NEG_FILL), axis=0, keepdims=True)
    stats = [tail[3 * rows :] for tail in tails]
    for s in range(swapped, sources):
        stats[s] = pltpu.roll(stats[s], HEAD_WIDTH - mix_rows, 1)
    peak = functools.reduce(jnp.maximum, [stat[0:1] for stat in stats], fresh_peak)
    weights = jnp.where(allowed, jnp.exp(fresh - peak), 0.0)
    factors = [jnp.exp(stat[0:1] - peak) for stat in stats]
    total = functools.reduce(
        jnp.add,
        [factor * (stat[1:2] + stat[2:3]) for factor, stat in zip(factors, stats)],
        jnp.sum(weights, axis=0, keepdims=True),
    )
    inverse = 1.0 / total
    start = -(-(sources + 1) // rows) * rows
    table = jnp.concatenate(
        [factor * inverse for factor in factors]
        + [inverse, jnp.zeros((start - sources - 1, 128), jnp.float32), weights]
        + [jnp.zeros((128 - start - rows, 128), jnp.float32)],
        axis=0,
    )
    table = jnp.transpose(table)[:mix_rows]
    lane = lax.broadcasted_iota(jnp.int32, table.shape, 1)
    weights = jnp.where((lane >= start) & (lane < start + rows), table, 0.0).astype(jnp.bfloat16)
    values = jnp.concatenate(
        [
            jnp.zeros((start, HEAD_WIDTH), jnp.bfloat16),
            values,
            jnp.zeros((128 - start - rows, HEAD_WIDTH), jnp.bfloat16),
        ],
        axis=0,
    )
    mix = dot(weights, values, ((1,), (0,))) * table[:, sources : sources + 1]
    for s, ref in enumerate(got_refs):
        mix += ref[:mix_rows].astype(jnp.float32) * table[:, s : s + 1]
    for h in range(heads):
        tile = mix[h * rows : (h + 1) * rows]
        for b in range(requests):
            out_ref[b, :, h * HEAD_WIDTH : (h + 1) * HEAD_WIDTH] = tile[
                b * tokens : (b + 1) * tokens
            ].astype(jnp.bfloat16)


def rotation(lengths, tokens):
    half = HEAD_WIDTH // 2
    places = (lengths[:, None] + jnp.arange(tokens, dtype=jnp.int32)[None, :]).astype(jnp.float32)
    inverse_freq = jnp.exp(
        jnp.arange(half, dtype=jnp.float32) * (-2.0 * math.log(ROPE_BASE) / HEAD_WIDTH)
    )
    angles = places.reshape(-1, 1) * inverse_freq[None, :]
    cosine, sine = jnp.cos(angles), jnp.sin(angles)
    return jnp.concatenate([cosine, cosine], axis=1), jnp.concatenate([-sine, sine], axis=1)


def vmem():
    return pl.BlockSpec(memory_space=pltpu.VMEM)


def smem():
    return pl.BlockSpec(memory_space=pltpu.SMEM)


def hbm():
    return pl.BlockSpec(memory_space=pltpu.HBM)


def pinned(x):
    return pltpu.with_memory_space_constraint(x, pltpu.HBM)


def cost(flops, moved):
    return pl.CostEstimate(flops=int(flops), bytes_accessed=int(moved), transcendentals=0)


def trade(x, devices, even, odd, core=0):
    pairs = [(d, d ^ (2 * (odd if d % 2 else even) + core)) for d in range(devices)]
    return lax.ppermute(x, "tensor", pairs)


def per_device(
    hidden,
    queries,
    key_value_weight,
    adapter_down_weight,
    adapter_up_weight,
    cached_key_rows,
    cached_value_rows,
    request_adapter,
    adapter_rank_list,
    adapter_pool_row,
    lengths,
):
    requests, tokens, width = hidden.shape
    rows = requests * tokens
    devices = lax.axis_size("tensor")
    sizes = (requests, tokens, devices)
    plan = Plan(devices, width)
    heads, chunks = plan.heads, plan.chunks
    slot_rows = heads * rows
    index = lax.axis_index("tensor").reshape(1).astype(jnp.int32)

    def call(kernel, operands, in_specs, out_shape, scratch, name):
        return pl.pallas_call(
            kernel,
            out_shape=tuple(out_shape),
            in_specs=in_specs,
            out_specs=(vmem(),) * len(out_shape),
            scratch_shapes=scratch,
            compiler_params=pltpu.CompilerParams(vmem_limit_bytes=12 * MIB),
            cost_estimate=cost(10**6, 0),
            name=name,
        )(*operands)

    def core_swap(x):
        return trade(x, devices, 0, 0, core=1)

    flat = requests * cached_key_rows.shape[1]
    caches = (cached_key_rows.reshape(flat, -1), cached_value_rows.reshape(flat, -1))
    own, keys, values = call(
        functools.partial(pack_kernel, requests),
        tuple(pinned(x) for x in (queries, hidden) + caches),
        [hbm()] * 4,
        [pltpu.VMEM((heads + chunks, rows, HEAD_WIDTH), jnp.bfloat16)]
        + [pltpu.VMEM(x.shape, x.dtype) for x in caches],
        [
            pltpu.VMEM(queries.shape, jnp.bfloat16),
            pltpu.VMEM(hidden.shape, jnp.bfloat16),
            pltpu.SemaphoreType.DMA((4,)),
        ],
        "pack",
    )
    other_queries, other_hidden = core_swap(queries), core_swap(hidden)
    other_queries, late_own = lax.optimization_barrier((other_queries, own))
    shape = (heads + chunks, rows, HEAD_WIDTH)
    other, both = call(
        functools.partial(pack_other_kernel, requests),
        (late_own, other_queries, other_hidden),
        [vmem()] * 3,
        [pltpu.VMEM(shape, jnp.bfloat16), pltpu.VMEM((2 * shape[0],) + shape[1:], jnp.bfloat16)],
        [],
        "pack_other",
    )
    both, late_own = lax.optimization_barrier((both, late_own))
    one = trade(late_own, devices, plan.single, plan.single)
    mine = [trade(both, devices, a, b) for a, b in plan.pairs]

    out_width = key_value_weight.shape[1]
    parts = 4 if width % (4 * HEAD_WIDTH) == 0 else 1
    down = pinned(adapter_down_weight[0])
    rank = down.shape[1]
    up = adapter_up_weight[0]
    base, up, *halves = call(
        functools.partial(base_kernel, heads, sources_of(plan)),
        (index, late_own, pinned(key_value_weight), down, pinned(up)),
        [smem(), vmem()] + [hbm()] * 3,
        [pltpu.VMEM((rows, out_width), jnp.float32), pltpu.VMEM(up.shape, up.dtype)]
        + [pltpu.VMEM((devices // 2, width, rank), jnp.bfloat16)] * 2,
        [
            pltpu.VMEM((parts, width // parts, out_width), jnp.bfloat16),
            pltpu.SemaphoreType.DMA((parts + 1,)),
            pltpu.SemaphoreType.DMA((devices,)),
        ],
        "base",
    )
    near = jnp.concatenate([one] + mine, axis=0)
    near, base = lax.optimization_barrier((near, base))
    other_near = core_swap(near)

    def keep(numbers):
        return call(
            functools.partial(keep_kernel, sizes, plan, numbers),
            (index, lengths, own, near, keys, values),
            [smem()] * 2 + [vmem()] * 4,
            [
                pltpu.VMEM((MIX_ROWS // 2, HEAD_WIDTH), jnp.float32),
                pltpu.VMEM((8, HEAD_WIDTH), jnp.float32),
            ],
            [],
            "keep_states",
        )

    first_mix, first_stats = keep(range(CHUNKS // 2))
    other_near, first_mix = lax.optimization_barrier((other_near, first_mix))
    arrays = (own, other, near, other_near)
    step = KEY_HEADS * rows
    send, proj = call(
        functools.partial(send_kernel, sizes, plan),
        (index, lengths, request_adapter, adapter_rank_list, adapter_pool_row)
        + arrays
        + (keys, values, base, up, *halves),
        [smem()] * 5 + [vmem()] * (len(arrays) + 6),
        [
            pltpu.VMEM((MIX_ROWS + 3 * step + STAT_ROWS, HEAD_WIDTH), jnp.bfloat16),
            pltpu.VMEM((2, step, HEAD_WIDTH), jnp.float32),
        ],
        [],
        "send_states",
    )
    got = core_swap(send)
    second_mix, second_stats = keep(range(CHUNKS // 2, CHUNKS))
    packets = call(
        functools.partial(join_kernel, sizes, plan),
        (index, first_mix, second_mix, first_stats, second_stats, proj, got),
        [smem()] + [vmem()] * 6,
        [pltpu.VMEM((slot_rows + 4 * rows, HEAD_WIDTH), jnp.bfloat16)] * 2
        + [pltpu.VMEM((2 * slot_rows + 4 * rows, HEAD_WIDTH), jnp.bfloat16)] * len(plan.pairs),
        [pltpu.VMEM((KEY_HEADS, 3 * rows, HEAD_WIDTH), jnp.float32)],
        "join",
    )
    sent = sorted(zip(packets[2:], plan.pairs), key=lambda item: -sum(item[1]))
    back = [trade(x, devices, a, b) for x, (a, b) in sent]
    back[0], late_lengths = lax.optimization_barrier((back[0], lengths))
    cosine, sine = rotation(late_lengths, tokens)
    heard = [packets[0], trade(packets[1], devices, plan.single, plan.single)] + back
    heard += [core_swap(x[slot_rows:]) for x in back]
    return pl.pallas_call(
        functools.partial(merge_kernel, devices, requests, tokens, 2 + len(plan.pairs)),
        out_shape=jax.ShapeDtypeStruct((requests, tokens, heads * HEAD_WIDTH), jnp.bfloat16),
        in_specs=[vmem()] * (3 + len(heard)),
        out_specs=vmem(),
        compiler_params=pltpu.CompilerParams(vmem_limit_bytes=8 * MIB),
        name="merge_states",
    )(own, cosine, sine, *heard)


def solution(mesh):
    in_specs = (
        P("groups", None, "tensor"),
        P("groups", None, "tensor"),
        P("tensor", None),
        P("tensor", None, None),
        P("tensor", None, None),
        P("groups", "tensor", None),
        P("groups", "tensor", None),
        P("groups"),
        P(),
        P(),
        P("groups"),
    )
    out_specs = P("groups", None, "tensor")
    return jax.shard_map(
        per_device, mesh=mesh, in_specs=in_specs, out_specs=out_specs, check_vma=False
    )
```

```python
import functools
import math

import jax
import jax.numpy as jnp
from jax import lax
from jax.experimental import pallas as pl
from jax.experimental.pallas import tpu as pltpu
from jax.sharding import PartitionSpec as P

QUERY_HEADS = 128
KEY_HEADS = 8
HEAD_WIDTH = 128
ROPE_BASE = 500000.0
NEG_FILL = -(2.0**100)
SCALE = 1.0 / math.sqrt(HEAD_WIDTH)
CHUNKS = KEY_HEADS // 2
MIX_ROWS = CHUNKS * 128
STAT_ROWS = 16
MIB = 2**20


def dot(a, b, dims):
    return lax.dot_general(a, b, (dims, ((), ())), preferred_element_type=jnp.float32)


def round_bf16(x):
    return x.astype(jnp.bfloat16).astype(jnp.float32)


class Plan:
    def __init__(self, devices, width):
        lanes = devices // 2
        self.per_head = per_head = lanes // KEY_HEADS
        self.heads, self.chunks = QUERY_HEADS // devices, width // HEAD_WIDTH
        self.single = 1
        self.pairs = [(m, m + 1) for m in range(lanes - 2, 0, -2)]
        self.pairs[:2] = self.pairs[1::-1]
        size = self.heads + self.chunks
        self.own = ((0, 0), ((0, 0), (1, 0)))
        self.one = ((self.single,) * 2, ((2, 0), (3, 0)))
        self.mine, self.theirs = [], []
        for k, (a, b) in enumerate(self.pairs):
            at = size + 2 * size * k
            self.mine.append(((a, b), ((2, at), (2, at + size))))
            self.theirs.append(((b, a), ((3, at + size), (3, at))))

    def head_masks(self, unit):
        return tuple(mask // self.per_head for mask in unit[0][0])

    def units(self, keep):
        if keep:
            units = [(self.own, 0), (self.one, 0)]
            units += [(slot, side) for slot in self.mine for side in (0, 1)]
        else:
            units = [(self.own, 1), (self.one, 1)]
            units += [(slot, side) for slot in self.theirs for side in (1, 0)]
        if self.per_head > 1:
            units.sort(key=self.head_masks)
        return units

    def attention_chunks(self, slot_rows, keep):
        units = self.units(keep)
        count = HEAD_WIDTH // slot_rows
        chunks = []
        for at in range(0, len(units), count):
            runs = []
            for unit in units[at : at + count]:
                if runs and self.head_masks(runs[-1][0]) == self.head_masks(unit):
                    runs[-1].append(unit)
                else:
                    runs.append([unit])
            chunks.append(runs)
        return chunks

    def slots(self):
        return [self.own, self.one] + self.mine + self.theirs


def here_mask(masks, here):
    return masks[0] if masks[0] == masks[1] else jnp.where(here % 2 == 0, masks[0], masks[1])


def head_columns(head):
    return pl.ds(pl.multiple_of(head * HEAD_WIDTH, HEAD_WIDTH), HEAD_WIDTH)


def sources_of(plan):
    return [
        (array, tile + plan.heads, masks, side)
        for masks, places in plan.slots()
        for side, (array, tile) in enumerate(places)
    ]


def streams(sources, index_ref, down_ref, halves, sems):
    count, depth = halves[0].shape[:2]
    here = index_ref[0]
    copies = []
    for at, (_, _, masks, side) in enumerate(sources):
        source = here ^ (2 * here_mask(masks, here) + side)
        rows = pl.ds(pl.multiple_of(source * depth, depth), depth)
        place = halves[at // count].at[at % count]
        copies.append(pltpu.make_async_copy(down_ref.at[rows], place, sems.at[at]))
    return copies


def lower(sources, arrays, halves):
    total = None
    count, depth = halves[0].shape[:2]
    for at, (array, first, _, _) in enumerate(sources):
        tiles = range(first, first + depth // HEAD_WIDTH)
        hidden = jnp.concatenate([arrays[array][c] for c in tiles], axis=1)
        term = dot(hidden, halves[at // count][at % count], ((1,), (0,)))
        total = term if total is None else total + term
    return total


def tiles_of(refs, requests, out_ref, at):
    for ref in refs:
        rows = jnp.concatenate([ref[b].astype(jnp.float32) for b in range(requests)], axis=0)
        for c in range(rows.shape[1] // HEAD_WIDTH):
            tile = rows[:, c * HEAD_WIDTH : (c + 1) * HEAD_WIDTH]
            out_ref[at] = tile.astype(jnp.bfloat16)
            at += 1


def pack_kernel(requests, query_ref, hidden_ref, key_ref, *refs):
    own_ref, held_key_ref, query_buf, hidden_buf, sems = refs
    sources = (query_ref, hidden_ref, key_ref)
    places = (query_buf, hidden_buf, held_key_ref)
    loads = [
        pltpu.make_async_copy(source, place, sems.at[i])
        for i, (source, place) in enumerate(zip(sources, places))
    ]
    for load in loads:
        load.start()
    for load in loads[:2]:
        load.wait()
    tiles_of((query_buf, hidden_buf), requests, own_ref, 0)
    for load in loads[2:]:
        load.wait()


def pack_other_kernel(requests, own_ref, query_ref, hidden_ref, other_ref, both_ref):
    size = own_ref.shape[0]
    both_ref[:size] = own_ref[...]
    tiles_of((query_ref, hidden_ref), requests, both_ref, size)
    other_ref[...] = both_ref[size:]


def base_kernel(heads, sources, index_ref, own_ref, weight_ref, down_ref, *refs):
    up_ref, value_ref, base_ref, held_up_ref, held_value_ref, *halves, buffer, sems, row_sems = refs
    parts, depth = buffer.shape[:2]
    loads = [
        pltpu.make_async_copy(weight_ref.at[pl.ds(p * depth, depth)], buffer.at[p], sems.at[p])
        for p in range(parts)
    ]
    others = [
        pltpu.make_async_copy(up_ref, held_up_ref, sems.at[parts]),
        pltpu.make_async_copy(value_ref, held_value_ref, sems.at[parts + 1]),
    ]
    others += streams(sources, index_ref, down_ref, halves, row_sems)
    for load in loads + others:
        load.start()
    tiles = depth // HEAD_WIDTH
    total = jnp.zeros(base_ref.shape, jnp.float32)
    for p in range(parts):
        hidden = jnp.concatenate([own_ref[heads + p * tiles + c] for c in range(tiles)], axis=1)
        loads[p].wait()
        total += dot(hidden, buffer[p], ((1,), (0,)))
    base_ref[...] = total
    for load in others:
        load.wait()


def attend(sizes, plan, keep, numbers, index_ref, length_ref, arrays, key_ref, value_ref, put):
    requests, tokens, devices = sizes
    here = index_ref[0]
    chip = here // 2
    per_head = plan.per_head
    slot_rows = plan.heads * requests * tokens
    positions = key_ref.shape[0] // requests
    place = lax.broadcasted_iota(jnp.int32, (requests * positions, HEAD_WIDTH), 0)
    column = lax.broadcasted_iota(jnp.int32, (requests * positions, HEAD_WIDTH), 1)
    place_request = place // positions
    limit = jnp.zeros_like(place)
    for b in range(requests):
        limit = jnp.where(place_request == b, length_ref[b], limit)
    allowed = (here * positions + place % positions < limit) & (
        place_request == (column // tokens) % requests
    )
    bias = jnp.where(allowed, 0.0, NEG_FILL)
    chunks = plan.attention_chunks(slot_rows, keep)
    chunks = [chunks[i] for i in numbers]
    spots, scores = [], []
    for runs in chunks:
        places = [slot[1][side] for run in runs for slot, side in run]
        query = jnp.concatenate(
            [arrays[array][tile + h] for array, tile in places for h in range(plan.heads)], axis=0
        )
        spots.append(
            [
                head_columns((chip // per_head) ^ (here_mask(run[0][0][0], here) // per_head))
                for run in runs
            ]
        )
        share = HEAD_WIDTH // len(runs)
        score = None
        for i, spot in enumerate(spots[-1]):
            part = dot(key_ref[:, spot], query, ((1,), (1,)))
            score = part if score is None else jnp.where(column < i * share, score, part)
        scores.append(score * SCALE + bias)
    peaks = [round_bf16(jnp.max(score, axis=0, keepdims=True)) for score in scores]
    weights = [jnp.exp(score - peak) for score, peak in zip(scores, peaks)]
    totals = [jnp.sum(weight, axis=0, keepdims=True) for weight in weights]
    weights = [jnp.transpose(weight.astype(jnp.bfloat16)) for weight in weights]
    for number, weight in enumerate(weights):
        share = HEAD_WIDTH // len(spots[number])
        for i, spot in enumerate(spots[number]):
            own = slice(i * share, (i + 1) * share)
            put(number, i * share, dot(weight[own], value_ref[:, spot], ((1,), (0,))))
    return peaks, totals


def rows_of(items, count):
    row = lax.broadcasted_iota(jnp.int32, (count, HEAD_WIDTH), 0)
    out = jnp.zeros((count, HEAD_WIDTH), jnp.float32)
    for i, item in enumerate(items):
        out = jnp.where(row == i, item, out)
    return out


def send_kernel(sizes, plan, *refs):
    (index_ref, length_ref, adapter_ref, rank_ref, pool_ref, *arrays) = refs[:-8]
    (key_ref, value_ref, base_ref, up_ref, *halves, send_ref, own_ref) = refs[-8:]
    requests, tokens, devices = sizes

    def put(chunk, row, mix):
        at = chunk * 128 + row
        send_ref[at : at + mix.shape[0]] = mix.astype(jnp.bfloat16)

    peaks, totals = attend(
        sizes, plan, False, range(CHUNKS), index_ref, length_ref, arrays, key_ref, value_ref, put
    )
    highs = [round_bf16(total) for total in totals]
    lows = [total - high for total, high in zip(totals, highs)]
    send_ref[-STAT_ROWS:] = rows_of(peaks + highs + lows, STAT_ROWS).astype(jnp.bfloat16)

    rows = requests * tokens
    lowered = lower(sources_of(plan), arrays, halves)
    row_request = lax.broadcasted_iota(jnp.int32, (rows, 1), 0) // tokens
    ranks = jnp.zeros((rows, 1), jnp.int32)
    owners = jnp.zeros((rows, 1), jnp.int32)
    for b in range(requests):
        adapter = adapter_ref[b]
        ranks = jnp.where(row_request == b, rank_ref[adapter], ranks)
        owners = jnp.where(row_request == b, pool_ref[adapter], owners)
    column = lax.broadcasted_iota(jnp.int32, lowered.shape, 1)
    lowered = jnp.where(column < ranks, lowered, 0.0).astype(jnp.bfloat16)
    lifted = dot(lowered, up_ref[...], ((1,), (0,)))
    projected = base_ref[...] + jnp.where(owners == index_ref[0], lifted, 0.0)
    split = KEY_HEADS * HEAD_WIDTH
    step = KEY_HEADS * rows
    keys, values = [
        jnp.concatenate(
            [projected[:, at + j * HEAD_WIDTH : at + (j + 1) * HEAD_WIDTH] for j in range(KEY_HEADS)],
            axis=0,
        )
        for at in (0, split)
    ]
    own_ref[0] = keys
    own_ref[1] = values
    high = keys.astype(jnp.bfloat16)
    send_ref[MIX_ROWS : MIX_ROWS + step] = high
    send_ref[MIX_ROWS + step : MIX_ROWS + 2 * step] = (keys - high.astype(jnp.float32)).astype(
        jnp.bfloat16
    )
    send_ref[MIX_ROWS + 2 * step : MIX_ROWS + 3 * step] = values.astype(jnp.bfloat16)


def keep_kernel(sizes, plan, numbers, *refs):
    (index_ref, length_ref, own_ref, near_ref, key_ref, value_ref, mix_ref, stat_ref) = refs
    arrays = {0: own_ref, 2: near_ref}

    def put(chunk, row, mix):
        at = chunk * 128 + row
        mix_ref[at : at + mix.shape[0]] = mix

    peaks, totals = attend(
        sizes, plan, True, numbers, index_ref, length_ref, arrays, key_ref, value_ref, put
    )
    stat_ref[...] = rows_of(peaks + totals, 8)


def join_kernel(sizes, plan, index_ref, *refs):
    mix_refs, stat_refs, (proj_ref, got_ref) = refs[:2], refs[2:4], refs[4:6]
    packet_refs, tail_ref = refs[6:-1], refs[-1]
    requests, tokens, devices = sizes
    here = index_ref[0]
    chip = here // 2
    per_head = plan.per_head
    rows = requests * tokens
    slot_rows = plan.heads * rows
    step = KEY_HEADS * rows
    got = got_ref[MIX_ROWS + 3 * step :].astype(jnp.float32)
    half = CHUNKS // 2
    own_peak = jnp.concatenate([ref[:half] for ref in stat_refs], axis=0)
    own_total = jnp.concatenate([ref[half : 2 * half] for ref in stat_refs], axis=0)
    got_peak = got[:CHUNKS]
    peak = jnp.maximum(own_peak, got_peak)
    own_factor = jnp.exp(own_peak - peak)
    got_factor = jnp.exp(got_peak - peak)
    total = own_factor * own_total + got_factor * (
        got[CHUNKS : 2 * CHUNKS] + got[2 * CHUNKS : 3 * CHUNKS]
    )
    high = round_bf16(total)
    low = total - high
    filler = jnp.zeros((128 - 2 * CHUNKS, 128), jnp.float32)
    table = jnp.transpose(jnp.concatenate([own_factor, got_factor, filler], axis=0))
    parts = got_ref[MIX_ROWS : MIX_ROWS + 3 * step].astype(jnp.float32)
    keys = proj_ref[0] + parts[:step] + parts[step : 2 * step]
    values = proj_ref[1] + parts[2 * step :]
    keys_high = round_bf16(keys)
    for j in range(KEY_HEADS):
        part = slice(j * rows, (j + 1) * rows)
        tail_ref[j, :rows] = keys_high[part]
        tail_ref[j, rows : 2 * rows] = (keys - keys_high)[part]
        tail_ref[j, 2 * rows :] = values[part]
    stat_row = lax.broadcasted_iota(jnp.int32, (rows, HEAD_WIDTH), 0)
    packet = {id(slot): ref for slot, ref in zip([plan.own, plan.one] + plan.mine, packet_refs)}
    for c, runs in enumerate(plan.attention_chunks(slot_rows, True)):
        span = slice(c * 128, c * 128 + 128)
        at = c % half * 128
        mix = mix_refs[c // half][at : at + 128] * table[:, c : c + 1]
        mix += got_ref[span].astype(jnp.float32) * table[:, CHUNKS + c : CHUNKS + c + 1]
        stats = jnp.where(
            stat_row == 0,
            peak[c : c + 1],
            jnp.where(
                stat_row == 1, high[c : c + 1], jnp.where(stat_row == 2, low[c : c + 1], 0.0)
            ),
        )
        for t, (slot, side) in enumerate(unit for run in runs for unit in run):
            packet_ref = packet[id(slot)]
            at = side * slot_rows
            packet_ref[at : at + slot_rows] = mix[t * slot_rows : (t + 1) * slot_rows].astype(
                jnp.bfloat16
            )
            if side == 0:
                shifted = stats if t == 0 else pltpu.roll(stats, HEAD_WIDTH - t * slot_rows, 1)
                head = (chip // per_head) ^ (here_mask(slot[0], here) // per_head)
                tail = jnp.concatenate([tail_ref[head], shifted], axis=0)
                packet_ref[packet_ref.shape[0] - 4 * rows :] = tail.astype(jnp.bfloat16)


def merge_kernel(devices, requests, tokens, swapped, own_ref, cos_ref, sin_ref, *refs):
    got_refs, out_ref = refs[:-1], refs[-1]
    rows = requests * tokens
    heads = QUERY_HEADS // devices
    mix_rows = heads * rows
    sources = len(got_refs)
    tails = [ref[ref.shape[0] - 4 * rows :].astype(jnp.float32) for ref in got_refs]
    sums = functools.reduce(jnp.add, [tail[: 3 * rows] for tail in tails])
    keys = sums[:rows] + sums[rows : 2 * rows]
    values = sums[2 * rows :].astype(jnp.bfloat16)
    turned = pltpu.roll(keys, HEAD_WIDTH // 2, 1)
    keys = (keys * cos_ref[...] + turned * sin_ref[...]).astype(jnp.bfloat16)
    query = jnp.concatenate([own_ref[h] for h in range(heads)], axis=0)
    if mix_rows < 128:
        query = jnp.concatenate(
            [query, jnp.zeros((128 - mix_rows, HEAD_WIDTH), jnp.bfloat16)], axis=0
        )
    fresh = dot(keys, query, ((1,), (1,))) * SCALE
    source = lax.broadcasted_iota(jnp.int32, fresh.shape, 0)
    column = lax.broadcasted_iota(jnp.int32, fresh.shape, 1) % rows
    allowed = (source // tokens == column // tokens) & (source % tokens <= column % tokens)
    fresh_peak = jnp.max(jnp.where(allowed, fresh, NEG_FILL), axis=0, keepdims=True)
    stats = [tail[3 * rows :] for tail in tails]
    for s in range(swapped, sources):
        stats[s] = pltpu.roll(stats[s], HEAD_WIDTH - mix_rows, 1)
    peak = functools.reduce(jnp.maximum, [stat[0:1] for stat in stats], fresh_peak)
    weights = jnp.where(allowed, jnp.exp(fresh - peak), 0.0)
    factors = [jnp.exp(stat[0:1] - peak) for stat in stats]
    total = functools.reduce(
        jnp.add,
        [factor * (stat[1:2] + stat[2:3]) for factor, stat in zip(factors, stats)],
        jnp.sum(weights, axis=0, keepdims=True),
    )
    inverse = 1.0 / total
    start = -(-(sources + 1) // rows) * rows
    table = jnp.concatenate(
        [factor * inverse for factor in factors]
        + [inverse, jnp.zeros((start - sources - 1, 128), jnp.float32), weights]
        + [jnp.zeros((128 - start - rows, 128), jnp.float32)],
        axis=0,
    )
    table = jnp.transpose(table)[:mix_rows]
    lane = lax.broadcasted_iota(jnp.int32, table.shape, 1)
    weights = jnp.where((lane >= start) & (lane < start + rows), table, 0.0).astype(jnp.bfloat16)
    values = jnp.concatenate(
        [
            jnp.zeros((start, HEAD_WIDTH), jnp.bfloat16),
            values,
            jnp.zeros((128 - start - rows, HEAD_WIDTH), jnp.bfloat16),
        ],
        axis=0,
    )
    mix = dot(weights, values, ((1,), (0,))) * table[:, sources : sources + 1]
    for s, ref in enumerate(got_refs):
        mix += ref[:mix_rows].astype(jnp.float32) * table[:, s : s + 1]
    for h in range(heads):
        tile = mix[h * rows : (h + 1) * rows]
        for b in range(requests):
            out_ref[b, :, h * HEAD_WIDTH : (h + 1) * HEAD_WIDTH] = tile[
                b * tokens : (b + 1) * tokens
            ].astype(jnp.bfloat16)


def rotation(lengths, tokens):
    half = HEAD_WIDTH // 2
    places = (lengths[:, None] + jnp.arange(tokens, dtype=jnp.int32)[None, :]).astype(jnp.float32)
    inverse_freq = jnp.exp(
        jnp.arange(half, dtype=jnp.float32) * (-2.0 * math.log(ROPE_BASE) / HEAD_WIDTH)
    )
    angles = places.reshape(-1, 1) * inverse_freq[None, :]
    cosine, sine = jnp.cos(angles), jnp.sin(angles)
    return jnp.concatenate([cosine, cosine], axis=1), jnp.concatenate([-sine, sine], axis=1)


def vmem():
    return pl.BlockSpec(memory_space=pltpu.VMEM)


def smem():
    return pl.BlockSpec(memory_space=pltpu.SMEM)


def hbm():
    return pl.BlockSpec(memory_space=pltpu.HBM)


def pinned(x):
    return pltpu.with_memory_space_constraint(x, pltpu.HBM)


def cost(flops, moved):
    return pl.CostEstimate(flops=int(flops), bytes_accessed=int(moved), transcendentals=0)


def trade(x, devices, even, odd, core=0):
    pairs = [(d, d ^ (2 * (odd if d % 2 else even) + core)) for d in range(devices)]
    return lax.ppermute(x, "tensor", pairs)


def per_device(
    hidden,
    queries,
    key_value_weight,
    adapter_down_weight,
    adapter_up_weight,
    cached_key_rows,
    cached_value_rows,
    request_adapter,
    adapter_rank_list,
    adapter_pool_row,
    lengths,
):
    requests, tokens, width = hidden.shape
    rows = requests * tokens
    devices = lax.axis_size("tensor")
    sizes = (requests, tokens, devices)
    plan = Plan(devices, width)
    heads, chunks = plan.heads, plan.chunks
    slot_rows = heads * rows
    index = lax.axis_index("tensor").reshape(1).astype(jnp.int32)

    def call(kernel, operands, in_specs, out_shape, scratch, name):
        return pl.pallas_call(
            kernel,
            out_shape=tuple(out_shape),
            in_specs=in_specs,
            out_specs=(vmem(),) * len(out_shape),
            scratch_shapes=scratch,
            compiler_params=pltpu.CompilerParams(vmem_limit_bytes=12 * MIB),
            cost_estimate=cost(10**6, 0),
            name=name,
        )(*operands)

    def core_swap(x):
        return trade(x, devices, 0, 0, core=1)

    flat = requests * cached_key_rows.shape[1]
    keys = cached_key_rows.reshape(flat, -1)
    values = cached_value_rows.reshape(flat, -1)
    own, keys = call(
        functools.partial(pack_kernel, requests),
        tuple(pinned(x) for x in (queries, hidden, keys)),
        [hbm()] * 3,
        [
            pltpu.VMEM((heads + chunks, rows, HEAD_WIDTH), jnp.bfloat16),
            pltpu.VMEM(keys.shape, keys.dtype),
        ],
        [
            pltpu.VMEM(queries.shape, jnp.bfloat16),
            pltpu.VMEM(hidden.shape, jnp.bfloat16),
            pltpu.SemaphoreType.DMA((3,)),
        ],
        "pack",
    )
    other_queries, other_hidden = core_swap(queries), core_swap(hidden)
    other_queries, late_own = lax.optimization_barrier((other_queries, own))
    shape = (heads + chunks, rows, HEAD_WIDTH)
    other, both = call(
        functools.partial(pack_other_kernel, requests),
        (late_own, other_queries, other_hidden),
        [vmem()] * 3,
        [pltpu.VMEM(shape, jnp.bfloat16), pltpu.VMEM((2 * shape[0],) + shape[1:], jnp.bfloat16)],
        [],
        "pack_other",
    )
    both, late_own = lax.optimization_barrier((both, late_own))
    one = trade(late_own, devices, plan.single, plan.single)
    mine = [trade(both, devices, a, b) for a, b in plan.pairs]

    out_width = key_value_weight.shape[1]
    parts = 4 if width % (4 * HEAD_WIDTH) == 0 else 1
    down = pinned(adapter_down_weight[0])
    rank = down.shape[1]
    up = adapter_up_weight[0]
    base, up, values, *halves = call(
        functools.partial(base_kernel, heads, sources_of(plan)),
        (index, late_own, pinned(key_value_weight), down, pinned(up), pinned(values)),
        [smem(), vmem()] + [hbm()] * 4,
        [
            pltpu.VMEM((rows, out_width), jnp.float32),
            pltpu.VMEM(up.shape, up.dtype),
            pltpu.VMEM(values.shape, values.dtype),
        ]
        + [pltpu.VMEM((devices // 2, width, rank), jnp.bfloat16)] * 2,
        [
            pltpu.VMEM((parts, width // parts, out_width), jnp.bfloat16),
            pltpu.SemaphoreType.DMA((parts + 2,)),
            pltpu.SemaphoreType.DMA((devices,)),
        ],
        "base",
    )
    near = jnp.concatenate([one] + mine, axis=0)
    near, base = lax.optimization_barrier((near, base))
    other_near = core_swap(near)

    def keep(numbers):
        return call(
            functools.partial(keep_kernel, sizes, plan, numbers),
            (index, lengths, own, near, keys, values),
            [smem()] * 2 + [vmem()] * 4,
            [
                pltpu.VMEM((MIX_ROWS // 2, HEAD_WIDTH), jnp.float32),
                pltpu.VMEM((8, HEAD_WIDTH), jnp.float32),
            ],
            [],
            "keep_states",
        )

    first_mix, first_stats = keep(range(CHUNKS // 2))
    other_near, first_mix = lax.optimization_barrier((other_near, first_mix))
    arrays = (own, other, near, other_near)
    step = KEY_HEADS * rows
    send, proj = call(
        functools.partial(send_kernel, sizes, plan),
        (index, lengths, request_adapter, adapter_rank_list, adapter_pool_row)
        + arrays
        + (keys, values, base, up, *halves),
        [smem()] * 5 + [vmem()] * (len(arrays) + 6),
        [
            pltpu.VMEM((MIX_ROWS + 3 * step + STAT_ROWS, HEAD_WIDTH), jnp.bfloat16),
            pltpu.VMEM((2, step, HEAD_WIDTH), jnp.float32),
        ],
        [],
        "send_states",
    )
    got = core_swap(send)
    second_mix, second_stats = keep(range(CHUNKS // 2, CHUNKS))
    packets = call(
        functools.partial(join_kernel, sizes, plan),
        (index, first_mix, second_mix, first_stats, second_stats, proj, got),
        [smem()] + [vmem()] * 6,
        [pltpu.VMEM((slot_rows + 4 * rows, HEAD_WIDTH), jnp.bfloat16)] * 2
        + [pltpu.VMEM((2 * slot_rows + 4 * rows, HEAD_WIDTH), jnp.bfloat16)] * len(plan.pairs),
        [pltpu.VMEM((KEY_HEADS, 3 * rows, HEAD_WIDTH), jnp.float32)],
        "join",
    )
    sent = sorted(zip(packets[2:], plan.pairs), key=lambda item: -sum(item[1]))
    back = [trade(x, devices, a, b) for x, (a, b) in sent]
    back[0], late_lengths = lax.optimization_barrier((back[0], lengths))
    cosine, sine = rotation(late_lengths, tokens)
    heard = [packets[0], trade(packets[1], devices, plan.single, plan.single)] + back
    heard += [core_swap(x[slot_rows:]) for x in back]
    return pl.pallas_call(
        functools.partial(merge_kernel, devices, requests, tokens, 2 + len(plan.pairs)),
        out_shape=jax.ShapeDtypeStruct((requests, tokens, heads * HEAD_WIDTH), jnp.bfloat16),
        in_specs=[vmem()] * (3 + len(heard)),
        out_specs=vmem(),
        compiler_params=pltpu.CompilerParams(vmem_limit_bytes=8 * MIB),
        name="merge_states",
    )(own, cosine, sine, *heard)


def solution(mesh):
    in_specs = (
        P("groups", None, "tensor"),
        P("groups", None, "tensor"),
        P("tensor", None),
        P("tensor", None, None),
        P("tensor", None, None),
        P("groups", "tensor", None),
        P("groups", "tensor", None),
        P("groups"),
        P(),
        P(),
        P("groups"),
    )
    out_specs = P("groups", None, "tensor")
    return jax.shard_map(
        per_device, mesh=mesh, in_specs=in_specs, out_specs=out_specs, check_vma=False
    )
```

```python
import functools
import math

import jax
import jax.numpy as jnp
from jax import lax
from jax.experimental import pallas as pl
from jax.experimental.pallas import tpu as pltpu
from jax.sharding import PartitionSpec as P

QUERY_HEADS = 128
KEY_HEADS = 8
HEAD_WIDTH = 128
ROPE_BASE = 500000.0
NEG_FILL = -(2.0**100)
SCALE = 1.0 / math.sqrt(HEAD_WIDTH)
CHUNKS = KEY_HEADS // 2
MIX_ROWS = CHUNKS * 128
STAT_ROWS = 16
MIB = 2**20


def dot(a, b, dims):
    return lax.dot_general(a, b, (dims, ((), ())), preferred_element_type=jnp.float32)


def round_bf16(x):
    return x.astype(jnp.bfloat16).astype(jnp.float32)


class Plan:
    def __init__(self, devices, width):
        lanes = devices // 2
        self.per_head = per_head = lanes // KEY_HEADS
        self.heads, self.chunks = QUERY_HEADS // devices, width // HEAD_WIDTH
        self.single = 1
        self.pairs = [(m, m + 1) for m in range(lanes - 2, 0, -2)]
        self.pairs[:2] = self.pairs[1::-1]
        size = self.heads + self.chunks
        self.own = ((0, 0), ((0, 0), (1, 0)))
        self.one = ((self.single,) * 2, ((2, 0), (3, 0)))
        self.mine, self.theirs = [], []
        for k, (a, b) in enumerate(self.pairs):
            at = size + 2 * size * k
            self.mine.append(((a, b), ((2, at), (2, at + size))))
            self.theirs.append(((b, a), ((3, at + size), (3, at))))

    def head_masks(self, unit):
        return tuple(mask // self.per_head for mask in unit[0][0])

    def units(self, keep):
        if keep:
            units = [(self.own, 0), (self.one, 0)]
            units += [(slot, side) for slot in self.mine for side in (0, 1)]
        else:
            units = [(self.own, 1), (self.one, 1)]
            units += [(slot, side) for slot in self.theirs for side in (1, 0)]
        if self.per_head > 1:
            units.sort(key=self.head_masks)
        return units

    def attention_chunks(self, slot_rows, keep):
        units = self.units(keep)
        count = HEAD_WIDTH // slot_rows
        chunks = []
        for at in range(0, len(units), count):
            runs = []
            for unit in units[at : at + count]:
                if runs and self.head_masks(runs[-1][0]) == self.head_masks(unit):
                    runs[-1].append(unit)
                else:
                    runs.append([unit])
            chunks.append(runs)
        return chunks

    def slots(self):
        return [self.own, self.one] + self.mine + self.theirs


def here_mask(masks, here):
    return masks[0] if masks[0] == masks[1] else jnp.where(here % 2 == 0, masks[0], masks[1])


def head_columns(head):
    return pl.ds(pl.multiple_of(head * HEAD_WIDTH, HEAD_WIDTH), HEAD_WIDTH)


def sources_of(plan):
    sources = [
        (array, tile + plan.heads, masks, side)
        for masks, places in plan.slots()
        for side, (array, tile) in enumerate(places)
    ]
    return sorted(sources, key=lambda source: source[0] % 2)


def streams(sources, index_ref, down_ref, halves, sems):
    count, depth = halves[0].shape[:2]
    here = index_ref[0]
    copies = []
    for at, (_, _, masks, side) in enumerate(sources):
        source = here ^ (2 * here_mask(masks, here) + side)
        rows = pl.ds(pl.multiple_of(source * depth, depth), depth)
        place = halves[at // count].at[at % count]
        copies.append(pltpu.make_async_copy(down_ref.at[rows], place, sems.at[at]))
    return copies


def lower(sources, arrays, half_ref):
    total = None
    depth = half_ref.shape[1]
    for at, (array, first, _, _) in enumerate(sources):
        tiles = range(first, first + depth // HEAD_WIDTH)
        hidden = jnp.concatenate([arrays[array][c] for c in tiles], axis=1)
        term = dot(hidden, half_ref[at], ((1,), (0,)))
        total = term if total is None else total + term
    return total


def tiles_of(refs, requests, out_ref, at):
    for ref in refs:
        rows = jnp.concatenate([ref[b].astype(jnp.float32) for b in range(requests)], axis=0)
        for c in range(rows.shape[1] // HEAD_WIDTH):
            tile = rows[:, c * HEAD_WIDTH : (c + 1) * HEAD_WIDTH]
            out_ref[at] = tile.astype(jnp.bfloat16)
            at += 1


def pack_kernel(requests, query_ref, hidden_ref, own_ref, query_buf, hidden_buf, sems):
    loads = [
        pltpu.make_async_copy(query_ref, query_buf, sems.at[0]),
        pltpu.make_async_copy(hidden_ref, hidden_buf, sems.at[1]),
    ]
    for load in loads:
        load.start()
    for load in loads:
        load.wait()
    tiles_of((query_buf, hidden_buf), requests, own_ref, 0)


def pack_other_kernel(requests, own_ref, query_ref, hidden_ref, other_ref, both_ref):
    size = own_ref.shape[0]
    both_ref[:size] = own_ref[...]
    tiles_of((query_ref, hidden_ref), requests, both_ref, size)
    other_ref[...] = both_ref[size:]


def base_kernel(sizes, plan, *refs):
    (index_ref, length_ref, adapter_ref, rank_ref, pool_ref) = refs[:5]
    (own_ref, weight_ref, down_ref, *sources) = refs[5:11]
    (base_ref, bias_ref, mask_ref, *held) = refs[11:17]
    *halves, buffer, sems, row_sems = refs[17:]
    requests, tokens, devices = sizes
    rows = requests * tokens
    here = index_ref[0]
    parts, depth = buffer.shape[:2]
    loads = [
        pltpu.make_async_copy(weight_ref.at[pl.ds(p * depth, depth)], buffer.at[p], sems.at[p])
        for p in range(parts)
    ]
    others = [
        pltpu.make_async_copy(source, place, sems.at[parts + i])
        for i, (source, place) in enumerate(zip(sources, held))
    ]
    others += streams(sources_of(plan), index_ref, down_ref, halves, row_sems)
    for load in loads + others:
        load.start()

    positions = bias_ref.shape[0] // requests
    place = lax.broadcasted_iota(jnp.int32, bias_ref.shape, 0)
    column = lax.broadcasted_iota(jnp.int32, bias_ref.shape, 1)
    place_request = place // positions
    limit = jnp.zeros_like(place)
    for b in range(requests):
        limit = jnp.where(place_request == b, length_ref[b], limit)
    allowed = (here * positions + place % positions < limit) & (
        place_request == (column // tokens) % requests
    )
    bias_ref[...] = jnp.where(allowed, 0.0, NEG_FILL)
    row_request = lax.broadcasted_iota(jnp.int32, (rows, HEAD_WIDTH), 0) // tokens
    ranks = jnp.zeros((rows, HEAD_WIDTH), jnp.int32)
    owners = jnp.zeros((rows, HEAD_WIDTH), jnp.int32)
    for b in range(requests):
        adapter = adapter_ref[b]
        ranks = jnp.where(row_request == b, rank_ref[adapter], ranks)
        owners = jnp.where(row_request == b, pool_ref[adapter], owners)
    column = lax.broadcasted_iota(jnp.int32, ranks.shape, 1)
    mask_ref[0] = jnp.where(column < ranks, 1.0, 0.0)
    mask_ref[1] = jnp.where(owners == here, 1.0, 0.0)

    tiles = depth // HEAD_WIDTH
    total = jnp.zeros(base_ref.shape, jnp.float32)
    for p in range(parts):
        first = plan.heads + p * tiles
        hidden = jnp.concatenate([own_ref[first + c] for c in range(tiles)], axis=1)
        loads[p].wait()
        total += dot(hidden, buffer[p], ((1,), (0,)))
    base_ref[...] = total
    for load in others:
        load.wait()


def attend(sizes, plan, keep, numbers, index_ref, bias_ref, arrays, key_ref, value_ref, put):
    requests, tokens, devices = sizes
    here = index_ref[0]
    chip = here // 2
    per_head = plan.per_head
    slot_rows = plan.heads * requests * tokens
    bias = bias_ref[...]
    column = lax.broadcasted_iota(jnp.int32, bias.shape, 1)
    chunks = plan.attention_chunks(slot_rows, keep)
    chunks = [chunks[i] for i in numbers]
    spots, scores = [], []
    for runs in chunks:
        places = [slot[1][side] for run in runs for slot, side in run]
        query = jnp.concatenate(
            [arrays[array][tile + h] for array, tile in places for h in range(plan.heads)], axis=0
        )
        spots.append(
            [
                head_columns((chip // per_head) ^ (here_mask(run[0][0][0], here) // per_head))
                for run in runs
            ]
        )
        share = HEAD_WIDTH // len(runs)
        score = None
        for i, spot in enumerate(spots[-1]):
            part = dot(key_ref[:, spot], query, ((1,), (1,)))
            score = part if score is None else jnp.where(column < i * share, score, part)
        scores.append(score * SCALE + bias)
    peaks = [round_bf16(jnp.max(score, axis=0, keepdims=True)) for score in scores]
    weights = [jnp.exp(score - peak) for score, peak in zip(scores, peaks)]
    totals = [jnp.sum(weight, axis=0, keepdims=True) for weight in weights]
    weights = [jnp.transpose(weight.astype(jnp.bfloat16)) for weight in weights]
    for number, weight in enumerate(weights):
        share = HEAD_WIDTH // len(spots[number])
        for i, spot in enumerate(spots[number]):
            own = slice(i * share, (i + 1) * share)
            put(number, i * share, dot(weight[own], value_ref[:, spot], ((1,), (0,))))
    return peaks, totals


def rows_of(items, count):
    row = lax.broadcasted_iota(jnp.int32, (count, HEAD_WIDTH), 0)
    out = jnp.zeros((count, HEAD_WIDTH), jnp.float32)
    for i, item in enumerate(items):
        out = jnp.where(row == i, item, out)
    return out


def send_kernel(sizes, plan, *refs):
    (index_ref, bias_ref, *arrays) = refs[:6]
    (key_ref, value_ref, base_ref, up_ref, half_ref, lowered_ref, mask_ref) = refs[6:13]
    (send_ref, own_ref) = refs[13:]
    requests, tokens, devices = sizes

    def put(chunk, row, mix):
        at = chunk * 128 + row
        send_ref[at : at + mix.shape[0]] = mix.astype(jnp.bfloat16)

    peaks, totals = attend(
        sizes, plan, False, range(CHUNKS), index_ref, bias_ref, arrays, key_ref, value_ref, put
    )
    highs = [round_bf16(total) for total in totals]
    lows = [total - high for total, high in zip(totals, highs)]
    send_ref[-STAT_ROWS:] = rows_of(peaks + highs + lows, STAT_ROWS).astype(jnp.bfloat16)

    rows = requests * tokens
    sources = sources_of(plan)
    lowered = lowered_ref[...] + lower(sources[devices // 2 :], arrays, half_ref)
    lowered = jnp.where(mask_ref[0] > 0.0, lowered, 0.0).astype(jnp.bfloat16)
    lifted = dot(lowered, up_ref[...], ((1,), (0,)))
    projected = base_ref[...] + jnp.where(mask_ref[1][:, :1] > 0.0, lifted, 0.0)
    split = KEY_HEADS * HEAD_WIDTH
    step = KEY_HEADS * rows
    keys, values = [
        jnp.concatenate(
            [projected[:, at + j * HEAD_WIDTH : at + (j + 1) * HEAD_WIDTH] for j in range(KEY_HEADS)],
            axis=0,
        )
        for at in (0, split)
    ]
    own_ref[0] = keys
    own_ref[1] = values
    high = keys.astype(jnp.bfloat16)
    send_ref[MIX_ROWS : MIX_ROWS + step] = high
    send_ref[MIX_ROWS + step : MIX_ROWS + 2 * step] = (keys - high.astype(jnp.float32)).astype(
        jnp.bfloat16
    )
    send_ref[MIX_ROWS + 2 * step : MIX_ROWS + 3 * step] = values.astype(jnp.bfloat16)


def keep_kernel(sizes, plan, numbers, *refs):
    (index_ref, bias_ref, own_ref, near_ref, key_ref, value_ref) = refs[:6]
    arrays = {0: own_ref, 2: near_ref}
    if len(refs) > 8:
        half_ref, mix_ref, stat_ref, lowered_ref = refs[6:]
        lowered_ref[...] = lower(sources_of(plan)[: half_ref.shape[0]], arrays, half_ref)
    else:
        mix_ref, stat_ref = refs[6:]

    def put(chunk, row, mix):
        at = chunk * 128 + row
        mix_ref[at : at + mix.shape[0]] = mix

    peaks, totals = attend(
        sizes, plan, True, numbers, index_ref, bias_ref, arrays, key_ref, value_ref, put
    )
    stat_ref[...] = rows_of(peaks + totals, 8)


def join_kernel(sizes, plan, index_ref, *refs):
    mix_refs, stat_refs, (proj_ref, got_ref) = refs[:2], refs[2:4], refs[4:6]
    packet_refs, tail_ref = refs[6:-1], refs[-1]
    requests, tokens, devices = sizes
    here = index_ref[0]
    chip = here // 2
    per_head = plan.per_head
    rows = requests * tokens
    slot_rows = plan.heads * rows
    step = KEY_HEADS * rows
    got = got_ref[MIX_ROWS + 3 * step :].astype(jnp.float32)
    half = CHUNKS // 2
    own_peak = jnp.concatenate([ref[:half] for ref in stat_refs], axis=0)
    own_total = jnp.concatenate([ref[half : 2 * half] for ref in stat_refs], axis=0)
    got_peak = got[:CHUNKS]
    peak = jnp.maximum(own_peak, got_peak)
    own_factor = jnp.exp(own_peak - peak)
    got_factor = jnp.exp(got_peak - peak)
    total = own_factor * own_total + got_factor * (
        got[CHUNKS : 2 * CHUNKS] + got[2 * CHUNKS : 3 * CHUNKS]
    )
    high = round_bf16(total)
    low = total - high
    filler = jnp.zeros((128 - 2 * CHUNKS, 128), jnp.float32)
    table = jnp.transpose(jnp.concatenate([own_factor, got_factor, filler], axis=0))
    parts = got_ref[MIX_ROWS : MIX_ROWS + 3 * step].astype(jnp.float32)
    keys = proj_ref[0] + parts[:step] + parts[step : 2 * step]
    values = proj_ref[1] + parts[2 * step :]
    keys_high = round_bf16(keys)
    for j in range(KEY_HEADS):
        part = slice(j * rows, (j + 1) * rows)
        tail_ref[j, :rows] = keys_high[part]
        tail_ref[j, rows : 2 * rows] = (keys - keys_high)[part]
        tail_ref[j, 2 * rows :] = values[part]
    stat_row = lax.broadcasted_iota(jnp.int32, (rows, HEAD_WIDTH), 0)
    packet = {id(slot): ref for slot, ref in zip([plan.own, plan.one] + plan.mine, packet_refs)}
    for c, runs in enumerate(plan.attention_chunks(slot_rows, True)):
        span = slice(c * 128, c * 128 + 128)
        at = c % half * 128
        mix = mix_refs[c // half][at : at + 128] * table[:, c : c + 1]
        mix += got_ref[span].astype(jnp.float32) * table[:, CHUNKS + c : CHUNKS + c + 1]
        stats = jnp.where(
            stat_row == 0,
            peak[c : c + 1],
            jnp.where(
                stat_row == 1, high[c : c + 1], jnp.where(stat_row == 2, low[c : c + 1], 0.0)
            ),
        )
        for t, (slot, side) in enumerate(unit for run in runs for unit in run):
            packet_ref = packet[id(slot)]
            at = side * slot_rows
            packet_ref[at : at + slot_rows] = mix[t * slot_rows : (t + 1) * slot_rows].astype(
                jnp.bfloat16
            )
            if side == 0:
                shifted = stats if t == 0 else pltpu.roll(stats, HEAD_WIDTH - t * slot_rows, 1)
                head = (chip // per_head) ^ (here_mask(slot[0], here) // per_head)
                tail = jnp.concatenate([tail_ref[head], shifted], axis=0)
                packet_ref[packet_ref.shape[0] - 4 * rows :] = tail.astype(jnp.bfloat16)


def merge_kernel(devices, requests, tokens, swapped, own_ref, cos_ref, sin_ref, *refs):
    got_refs, out_ref = refs[:-1], refs[-1]
    rows = requests * tokens
    heads = QUERY_HEADS // devices
    mix_rows = heads * rows
    sources = len(got_refs)
    tails = [ref[ref.shape[0] - 4 * rows :].astype(jnp.float32) for ref in got_refs]
    sums = functools.reduce(jnp.add, [tail[: 3 * rows] for tail in tails])
    keys = sums[:rows] + sums[rows : 2 * rows]
    values = sums[2 * rows :].astype(jnp.bfloat16)
    turned = pltpu.roll(keys, HEAD_WIDTH // 2, 1)
    keys = (keys * cos_ref[...] + turned * sin_ref[...]).astype(jnp.bfloat16)
    query = jnp.concatenate([own_ref[h] for h in range(heads)], axis=0)
    if mix_rows < 128:
        query = jnp.concatenate(
            [query, jnp.zeros((128 - mix_rows, HEAD_WIDTH), jnp.bfloat16)], axis=0
        )
    fresh = dot(keys, query, ((1,), (1,))) * SCALE
    source = lax.broadcasted_iota(jnp.int32, fresh.shape, 0)
    column = lax.broadcasted_iota(jnp.int32, fresh.shape, 1) % rows
    allowed = (source // tokens == column // tokens) & (source % tokens <= column % tokens)
    fresh_peak = jnp.max(jnp.where(allowed, fresh, NEG_FILL), axis=0, keepdims=True)
    stats = [tail[3 * rows :] for tail in tails]
    for s in range(swapped, sources):
        stats[s] = pltpu.roll(stats[s], HEAD_WIDTH - mix_rows, 1)
    past_peak = functools.reduce(jnp.maximum, [stat[0:1] for stat in stats])
    factors = [jnp.exp(stat[0:1] - past_peak) for stat in stats]
    past_total = functools.reduce(
        jnp.add, [factor * (stat[1:2] + stat[2:3]) for factor, stat in zip(factors, stats)]
    )
    table = jnp.concatenate(factors + [jnp.zeros((128 - sources, 128), jnp.float32)], axis=0)
    table = jnp.transpose(table)[:mix_rows]
    mix = None
    for s, ref in enumerate(got_refs):
        term = ref[:mix_rows].astype(jnp.float32) * table[:, s : s + 1]
        mix = term if mix is None else mix + term
    peak = jnp.maximum(past_peak, fresh_peak)
    scale = jnp.exp(past_peak - peak)
    weights = jnp.where(allowed, jnp.exp(fresh - peak), 0.0)
    inverse = 1.0 / (past_total * scale + jnp.sum(weights, axis=0, keepdims=True))
    table = jnp.concatenate(
        [
            scale * inverse,
            inverse,
            jnp.zeros((rows - 2, 128), jnp.float32),
            weights,
            jnp.zeros((128 - 2 * rows, 128), jnp.float32),
        ],
        axis=0,
    )
    table = jnp.transpose(table)[:mix_rows]
    lane = lax.broadcasted_iota(jnp.int32, table.shape, 1)
    weights = jnp.where((lane >= rows) & (lane < 2 * rows), table, 0.0).astype(jnp.bfloat16)
    values = jnp.concatenate(
        [
            jnp.zeros((rows, HEAD_WIDTH), jnp.bfloat16),
            values,
            jnp.zeros((128 - 2 * rows, HEAD_WIDTH), jnp.bfloat16),
        ],
        axis=0,
    )
    mix = mix * table[:, 0:1] + dot(weights, values, ((1,), (0,))) * table[:, 1:2]
    for h in range(heads):
        tile = mix[h * rows : (h + 1) * rows]
        for b in range(requests):
            out_ref[b, :, h * HEAD_WIDTH : (h + 1) * HEAD_WIDTH] = tile[
                b * tokens : (b + 1) * tokens
            ].astype(jnp.bfloat16)


def rotation(lengths, tokens):
    half = HEAD_WIDTH // 2
    places = (lengths[:, None] + jnp.arange(tokens, dtype=jnp.int32)[None, :]).astype(jnp.float32)
    inverse_freq = jnp.exp(
        jnp.arange(half, dtype=jnp.float32) * (-2.0 * math.log(ROPE_BASE) / HEAD_WIDTH)
    )
    angles = places.reshape(-1, 1) * inverse_freq[None, :]
    cosine, sine = jnp.cos(angles), jnp.sin(angles)
    return jnp.concatenate([cosine, cosine], axis=1), jnp.concatenate([-sine, sine], axis=1)


def vmem():
    return pl.BlockSpec(memory_space=pltpu.VMEM)


def smem():
    return pl.BlockSpec(memory_space=pltpu.SMEM)


def hbm():
    return pl.BlockSpec(memory_space=pltpu.HBM)


def pinned(x):
    return pltpu.with_memory_space_constraint(x, pltpu.HBM)


def cost(flops, moved):
    return pl.CostEstimate(flops=int(flops), bytes_accessed=int(moved), transcendentals=0)


def trade(x, devices, even, odd, core=0):
    pairs = [(d, d ^ (2 * (odd if d % 2 else even) + core)) for d in range(devices)]
    return lax.ppermute(x, "tensor", pairs)


def per_device(
    hidden,
    queries,
    key_value_weight,
    adapter_down_weight,
    adapter_up_weight,
    cached_key_rows,
    cached_value_rows,
    request_adapter,
    adapter_rank_list,
    adapter_pool_row,
    lengths,
):
    requests, tokens, width = hidden.shape
    rows = requests * tokens
    devices = lax.axis_size("tensor")
    sizes = (requests, tokens, devices)
    plan = Plan(devices, width)
    heads, chunks = plan.heads, plan.chunks
    slot_rows = heads * rows
    index = lax.axis_index("tensor").reshape(1).astype(jnp.int32)

    def call(kernel, operands, in_specs, out_shape, scratch, name):
        return pl.pallas_call(
            kernel,
            out_shape=tuple(out_shape),
            in_specs=in_specs,
            out_specs=(vmem(),) * len(out_shape),
            scratch_shapes=scratch,
            compiler_params=pltpu.CompilerParams(vmem_limit_bytes=12 * MIB),
            cost_estimate=cost(10**6, 0),
            name=name,
        )(*operands)

    def core_swap(x):
        return trade(x, devices, 0, 0, core=1)

    flat = requests * cached_key_rows.shape[1]
    keys = cached_key_rows.reshape(flat, -1)
    values = cached_value_rows.reshape(flat, -1)
    (own,) = call(
        functools.partial(pack_kernel, requests),
        (pinned(queries), pinned(hidden)),
        [hbm()] * 2,
        [pltpu.VMEM((heads + chunks, rows, HEAD_WIDTH), jnp.bfloat16)],
        [
            pltpu.VMEM(queries.shape, jnp.bfloat16),
            pltpu.VMEM(hidden.shape, jnp.bfloat16),
            pltpu.SemaphoreType.DMA((2,)),
        ],
        "pack",
    )
    other_queries, other_hidden = core_swap(queries), core_swap(hidden)
    other_queries, late_own = lax.optimization_barrier((other_queries, own))
    shape = (heads + chunks, rows, HEAD_WIDTH)
    other, both = call(
        functools.partial(pack_other_kernel, requests),
        (late_own, other_queries, other_hidden),
        [vmem()] * 3,
        [pltpu.VMEM(shape, jnp.bfloat16), pltpu.VMEM((2 * shape[0],) + shape[1:], jnp.bfloat16)],
        [],
        "pack_other",
    )
    both, late_own = lax.optimization_barrier((both, late_own))
    one = trade(late_own, devices, plan.single, plan.single)
    mine = [trade(both, devices, a, b) for a, b in plan.pairs]

    out_width = key_value_weight.shape[1]
    parts = 4 if width % (4 * HEAD_WIDTH) == 0 else 1
    down = pinned(adapter_down_weight[0])
    rank = down.shape[1]
    up = adapter_up_weight[0]
    big = (keys, values, up)
    base, bias, masks, keys, values, up, *halves = call(
        functools.partial(base_kernel, sizes, plan),
        (index, lengths, request_adapter, adapter_rank_list, adapter_pool_row)
        + (late_own, pinned(key_value_weight), down)
        + tuple(pinned(x) for x in big),
        [smem()] * 5 + [vmem()] + [hbm()] * 5,
        [
            pltpu.VMEM((rows, out_width), jnp.float32),
            pltpu.VMEM((flat, HEAD_WIDTH), jnp.float32),
            pltpu.VMEM((2, rows, HEAD_WIDTH), jnp.float32),
        ]
        + [pltpu.VMEM(x.shape, x.dtype) for x in big]
        + [pltpu.VMEM((devices // 2, width, rank), jnp.bfloat16)] * 2,
        [
            pltpu.VMEM((parts, width // parts, out_width), jnp.bfloat16),
            pltpu.SemaphoreType.DMA((parts + 3,)),
            pltpu.SemaphoreType.DMA((devices,)),
        ],
        "base",
    )
    near = jnp.concatenate([one] + mine, axis=0)
    near, base = lax.optimization_barrier((near, base))
    other_near = core_swap(near)

    def keep(numbers, *half):
        return call(
            functools.partial(keep_kernel, sizes, plan, numbers),
            (index, bias, own, near, keys, values) + half,
            [smem()] + [vmem()] * (5 + len(half)),
            [
                pltpu.VMEM((MIX_ROWS // 2, HEAD_WIDTH), jnp.float32),
                pltpu.VMEM((8, HEAD_WIDTH), jnp.float32),
            ]
            + [pltpu.VMEM((rows, rank), jnp.float32)] * len(half),
            [],
            "keep_states",
        )

    first_mix, first_stats, lowered = keep(range(CHUNKS // 2), halves[0])
    other_near, first_mix = lax.optimization_barrier((other_near, first_mix))
    arrays = (own, other, near, other_near)
    step = KEY_HEADS * rows
    send, proj = call(
        functools.partial(send_kernel, sizes, plan),
        (index, bias) + arrays + (keys, values, base, up, halves[1], lowered, masks),
        [smem()] + [vmem()] * 12,
        [
            pltpu.VMEM((MIX_ROWS + 3 * step + STAT_ROWS, HEAD_WIDTH), jnp.bfloat16),
            pltpu.VMEM((2, step, HEAD_WIDTH), jnp.float32),
        ],
        [],
        "send_states",
    )
    got = core_swap(send)
    second_mix, second_stats = keep(range(CHUNKS // 2, CHUNKS))
    packets = call(
        functools.partial(join_kernel, sizes, plan),
        (index, first_mix, second_mix, first_stats, second_stats, proj, got),
        [smem()] + [vmem()] * 6,
        [pltpu.VMEM((slot_rows + 4 * rows, HEAD_WIDTH), jnp.bfloat16)] * 2
        + [pltpu.VMEM((2 * slot_rows + 4 * rows, HEAD_WIDTH), jnp.bfloat16)] * len(plan.pairs),
        [pltpu.VMEM((KEY_HEADS, 3 * rows, HEAD_WIDTH), jnp.float32)],
        "join",
    )
    sent = sorted(zip(packets[2:], plan.pairs), key=lambda item: -sum(item[1]))
    back = [trade(x, devices, a, b) for x, (a, b) in sent]
    back[0], late_lengths = lax.optimization_barrier((back[0], lengths))
    cosine, sine = rotation(late_lengths, tokens)
    heard = [packets[0], trade(packets[1], devices, plan.single, plan.single)] + back
    heard += [core_swap(x[slot_rows:]) for x in back]
    return pl.pallas_call(
        functools.partial(merge_kernel, devices, requests, tokens, 2 + len(plan.pairs)),
        out_shape=jax.ShapeDtypeStruct((requests, tokens, heads * HEAD_WIDTH), jnp.bfloat16),
        in_specs=[vmem()] * (3 + len(heard)),
        out_specs=vmem(),
        compiler_params=pltpu.CompilerParams(vmem_limit_bytes=8 * MIB),
        name="merge_states",
    )(own, cosine, sine, *heard)


def solution(mesh):
    in_specs = (
        P("groups", None, "tensor"),
        P("groups", None, "tensor"),
        P("tensor", None),
        P("tensor", None, None),
        P("tensor", None, None),
        P("groups", "tensor", None),
        P("groups", "tensor", None),
        P("groups"),
        P(),
        P(),
        P("groups"),
    )
    out_specs = P("groups", None, "tensor")
    return jax.shard_map(
        per_device, mesh=mesh, in_specs=in_specs, out_specs=out_specs, check_vma=False
    )
```

```python
import functools
import math

import jax
import jax.numpy as jnp
from jax import lax
from jax.experimental import pallas as pl
from jax.experimental.pallas import tpu as pltpu
from jax.sharding import PartitionSpec as P

QUERY_HEADS = 128
KEY_HEADS = 8
HEAD_WIDTH = 128
ROPE_BASE = 500000.0
NEG_FILL = -(2.0**100)
SCALE = 1.0 / math.sqrt(HEAD_WIDTH)
CHUNKS = KEY_HEADS // 2
MIX_ROWS = CHUNKS * 128
STAT_ROWS = 16
MIB = 2**20


def dot(a, b, dims):
    return lax.dot_general(a, b, (dims, ((), ())), preferred_element_type=jnp.float32)


def round_bf16(x):
    return x.astype(jnp.bfloat16).astype(jnp.float32)


class Plan:
    def __init__(self, devices, width):
        lanes = devices // 2
        self.per_head = per_head = lanes // KEY_HEADS
        self.heads, self.chunks = QUERY_HEADS // devices, width // HEAD_WIDTH
        self.single = 1
        self.pairs = [(m, m + 1) for m in range(lanes - 2, 0, -2)]
        self.pairs[:2] = self.pairs[1::-1]
        size = self.heads + self.chunks
        self.own = ((0, 0), ((0, 0), (1, 0)))
        self.one = ((self.single,) * 2, ((2, 0), (3, 0)))
        self.mine, self.theirs = [], []
        for k, (a, b) in enumerate(self.pairs):
            at = size + 2 * size * k
            self.mine.append(((a, b), ((2, at), (2, at + size))))
            self.theirs.append(((b, a), ((3, at + size), (3, at))))

    def head_masks(self, unit):
        return tuple(mask // self.per_head for mask in unit[0][0])

    def units(self, keep):
        if keep:
            units = [(self.own, 0), (self.one, 0)]
            units += [(slot, side) for slot in self.mine for side in (0, 1)]
        else:
            units = [(self.own, 1), (self.one, 1)]
            units += [(slot, side) for slot in self.theirs for side in (1, 0)]
        if self.per_head > 1:
            units.sort(key=self.head_masks)
        return units

    def attention_chunks(self, slot_rows, keep):
        units = self.units(keep)
        count = HEAD_WIDTH // slot_rows
        chunks = []
        for at in range(0, len(units), count):
            runs = []
            for unit in units[at : at + count]:
                if runs and self.head_masks(runs[-1][0]) == self.head_masks(unit):
                    runs[-1].append(unit)
                else:
                    runs.append([unit])
            chunks.append(runs)
        return chunks

    def slots(self):
        return [self.own, self.one] + self.mine + self.theirs


def here_mask(masks, here):
    return masks[0] if masks[0] == masks[1] else jnp.where(here % 2 == 0, masks[0], masks[1])


def head_columns(head):
    return pl.ds(pl.multiple_of(head * HEAD_WIDTH, HEAD_WIDTH), HEAD_WIDTH)


def sources_of(plan):
    sources = [
        (array, tile + plan.heads, masks, side)
        for masks, places in plan.slots()
        for side, (array, tile) in enumerate(places)
    ]
    return sorted(sources, key=lambda source: source[0] % 2)


def streams(sources, index_ref, down_ref, halves, sems):
    count, depth = halves[0].shape[:2]
    here = index_ref[0]
    copies = []
    for at, (_, _, masks, side) in enumerate(sources):
        source = here ^ (2 * here_mask(masks, here) + side)
        rows = pl.ds(pl.multiple_of(source * depth, depth), depth)
        place = halves[at // count].at[at % count]
        copies.append(pltpu.make_async_copy(down_ref.at[rows], place, sems.at[at]))
    return copies


def lower(sources, arrays, half_ref):
    total = None
    depth = half_ref.shape[1]
    for at, (array, first, _, _) in enumerate(sources):
        tiles = range(first, first + depth // HEAD_WIDTH)
        hidden = jnp.concatenate([arrays[array][c] for c in tiles], axis=1)
        term = dot(hidden, half_ref[at], ((1,), (0,)))
        total = term if total is None else total + term
    return total


def tiles_of(refs, requests, out_ref, at):
    for ref in refs:
        rows = jnp.concatenate([ref[b].astype(jnp.float32) for b in range(requests)], axis=0)
        for c in range(rows.shape[1] // HEAD_WIDTH):
            tile = rows[:, c * HEAD_WIDTH : (c + 1) * HEAD_WIDTH]
            out_ref[at] = tile.astype(jnp.bfloat16)
            at += 1


def pack_kernel(requests, query_ref, hidden_ref, own_ref, query_buf, hidden_buf, sems):
    loads = [
        pltpu.make_async_copy(query_ref, query_buf, sems.at[0]),
        pltpu.make_async_copy(hidden_ref, hidden_buf, sems.at[1]),
    ]
    for load in loads:
        load.start()
    for load in loads:
        load.wait()
    tiles_of((query_buf, hidden_buf), requests, own_ref, 0)


def pack_other_kernel(requests, own_ref, query_ref, hidden_ref, other_ref, both_ref):
    size = own_ref.shape[0]
    both_ref[:size] = own_ref[...]
    tiles_of((query_ref, hidden_ref), requests, both_ref, size)
    other_ref[...] = both_ref[size:]


def base_kernel(sizes, plan, *refs):
    index_ref, *scalars = refs[:5]
    (own_ref, weight_ref, down_ref, *sources) = refs[5:11]
    (base_ref, bias_ref, mask_ref, *held) = refs[11:17]
    *halves, buffer, length_ref, adapter_ref, rank_ref, pool_ref, sems, row_sems, scalar_sems = refs[17:]
    requests, tokens, devices = sizes
    rows = requests * tokens
    here = index_ref[0]
    parts, depth = buffer.shape[:2]
    loads = [
        pltpu.make_async_copy(weight_ref.at[pl.ds(p * depth, depth)], buffer.at[p], sems.at[p])
        for p in range(parts)
    ]
    others = [
        pltpu.make_async_copy(source, place, sems.at[parts + i])
        for i, (source, place) in enumerate(zip(sources, held))
    ]
    others += streams(sources_of(plan), index_ref, down_ref, halves, row_sems)
    scalars = [
        pltpu.make_async_copy(source, place, scalar_sems.at[i])
        for i, (source, place) in enumerate(
            zip(scalars, (length_ref, adapter_ref, rank_ref, pool_ref))
        )
    ]
    for load in scalars + loads + others:
        load.start()
    tiles = depth // HEAD_WIDTH
    total = jnp.zeros(base_ref.shape, jnp.float32)
    for p in range(parts):
        first = plan.heads + p * tiles
        hidden = jnp.concatenate([own_ref[first + c] for c in range(tiles)], axis=1)
        loads[p].wait()
        total += dot(hidden, buffer[p], ((1,), (0,)))
    base_ref[...] = total
    for load in scalars:
        load.wait()
    positions = bias_ref.shape[0] // requests
    place = lax.broadcasted_iota(jnp.int32, bias_ref.shape, 0)
    column = lax.broadcasted_iota(jnp.int32, bias_ref.shape, 1)
    place_request = place // positions
    limit = jnp.zeros_like(place)
    for b in range(requests):
        limit = jnp.where(place_request == b, length_ref[b], limit)
    allowed = (here * positions + place % positions < limit) & (
        place_request == (column // tokens) % requests
    )
    bias_ref[...] = jnp.where(allowed, 0.0, NEG_FILL)
    row_request = lax.broadcasted_iota(jnp.int32, (rows, HEAD_WIDTH), 0) // tokens
    ranks = jnp.zeros((rows, HEAD_WIDTH), jnp.int32)
    owners = jnp.zeros((rows, HEAD_WIDTH), jnp.int32)
    for b in range(requests):
        adapter = adapter_ref[b]
        ranks = jnp.where(row_request == b, rank_ref[adapter], ranks)
        owners = jnp.where(row_request == b, pool_ref[adapter], owners)
    column = lax.broadcasted_iota(jnp.int32, ranks.shape, 1)
    mask_ref[0] = jnp.where(column < ranks, 1.0, 0.0)
    mask_ref[1] = jnp.where(owners == here, 1.0, 0.0)
    for load in others:
        load.wait()


def attend(sizes, plan, keep, numbers, index_ref, bias_ref, arrays, key_ref, value_ref, put):
    requests, tokens, devices = sizes
    here = index_ref[0]
    chip = here // 2
    per_head = plan.per_head
    slot_rows = plan.heads * requests * tokens
    bias = bias_ref[...]
    column = lax.broadcasted_iota(jnp.int32, bias.shape, 1)
    chunks = plan.attention_chunks(slot_rows, keep)
    chunks = [chunks[i] for i in numbers]
    spots, scores = [], []
    for runs in chunks:
        places = [slot[1][side] for run in runs for slot, side in run]
        query = jnp.concatenate(
            [arrays[array][tile + h] for array, tile in places for h in range(plan.heads)], axis=0
        )
        spots.append(
            [
                head_columns((chip // per_head) ^ (here_mask(run[0][0][0], here) // per_head))
                for run in runs
            ]
        )
        share = HEAD_WIDTH // len(runs)
        score = None
        for i, spot in enumerate(spots[-1]):
            part = dot(key_ref[:, spot], query, ((1,), (1,)))
            score = part if score is None else jnp.where(column < i * share, score, part)
        scores.append(score * SCALE + bias)
    peaks = [round_bf16(jnp.max(score, axis=0, keepdims=True)) for score in scores]
    weights = [jnp.exp(score - peak) for score, peak in zip(scores, peaks)]
    totals = [jnp.sum(weight, axis=0, keepdims=True) for weight in weights]
    weights = [jnp.transpose(weight.astype(jnp.bfloat16)) for weight in weights]
    for number, weight in enumerate(weights):
        share = HEAD_WIDTH // len(spots[number])
        for i, spot in enumerate(spots[number]):
            own = slice(i * share, (i + 1) * share)
            put(number, i * share, dot(weight[own], value_ref[:, spot], ((1,), (0,))))
    return peaks, totals


def rows_of(items, count):
    row = lax.broadcasted_iota(jnp.int32, (count, HEAD_WIDTH), 0)
    out = jnp.zeros((count, HEAD_WIDTH), jnp.float32)
    for i, item in enumerate(items):
        out = jnp.where(row == i, item, out)
    return out


def send_kernel(sizes, plan, *refs):
    (index_ref, bias_ref, *arrays) = refs[:6]
    (key_ref, value_ref, base_ref, up_ref, half_ref, lowered_ref, mask_ref) = refs[6:13]
    (send_ref, own_ref) = refs[13:]
    requests, tokens, devices = sizes

    def put(chunk, row, mix):
        at = chunk * 128 + row
        send_ref[at : at + mix.shape[0]] = mix.astype(jnp.bfloat16)

    peaks, totals = attend(
        sizes, plan, False, range(CHUNKS), index_ref, bias_ref, arrays, key_ref, value_ref, put
    )
    highs = [round_bf16(total) for total in totals]
    lows = [total - high for total, high in zip(totals, highs)]
    send_ref[-STAT_ROWS:] = rows_of(peaks + highs + lows, STAT_ROWS).astype(jnp.bfloat16)

    rows = requests * tokens
    sources = sources_of(plan)
    lowered = lowered_ref[...] + lower(sources[devices // 2 :], arrays, half_ref)
    lowered = jnp.where(mask_ref[0] > 0.0, lowered, 0.0).astype(jnp.bfloat16)
    lifted = dot(lowered, up_ref[...], ((1,), (0,)))
    projected = base_ref[...] + jnp.where(mask_ref[1][:, :1] > 0.0, lifted, 0.0)
    split = KEY_HEADS * HEAD_WIDTH
    step = KEY_HEADS * rows
    keys, values = [
        jnp.concatenate(
            [projected[:, at + j * HEAD_WIDTH : at + (j + 1) * HEAD_WIDTH] for j in range(KEY_HEADS)],
            axis=0,
        )
        for at in (0, split)
    ]
    own_ref[0] = keys
    own_ref[1] = values
    high = keys.astype(jnp.bfloat16)
    send_ref[MIX_ROWS : MIX_ROWS + step] = high
    send_ref[MIX_ROWS + step : MIX_ROWS + 2 * step] = (keys - high.astype(jnp.float32)).astype(
        jnp.bfloat16
    )
    send_ref[MIX_ROWS + 2 * step : MIX_ROWS + 3 * step] = values.astype(jnp.bfloat16)


def keep_kernel(sizes, plan, numbers, *refs):
    (index_ref, bias_ref, own_ref, near_ref, key_ref, value_ref) = refs[:6]
    arrays = {0: own_ref, 2: near_ref}
    if len(refs) > 8:
        half_ref, mix_ref, stat_ref, lowered_ref = refs[6:]
        lowered_ref[...] = lower(sources_of(plan)[: half_ref.shape[0]], arrays, half_ref)
    else:
        mix_ref, stat_ref = refs[6:]

    def put(chunk, row, mix):
        at = chunk * 128 + row
        mix_ref[at : at + mix.shape[0]] = mix

    peaks, totals = attend(
        sizes, plan, True, numbers, index_ref, bias_ref, arrays, key_ref, value_ref, put
    )
    stat_ref[...] = rows_of(peaks + totals, 8)


def join_kernel(sizes, plan, index_ref, *refs):
    mix_refs, stat_refs, (proj_ref, got_ref) = refs[:2], refs[2:4], refs[4:6]
    packet_refs, tail_ref = refs[6:-1], refs[-1]
    requests, tokens, devices = sizes
    here = index_ref[0]
    chip = here // 2
    per_head = plan.per_head
    rows = requests * tokens
    slot_rows = plan.heads * rows
    step = KEY_HEADS * rows
    got = got_ref[MIX_ROWS + 3 * step :].astype(jnp.float32)
    half = CHUNKS // 2
    own_peak = jnp.concatenate([ref[:half] for ref in stat_refs], axis=0)
    own_total = jnp.concatenate([ref[half : 2 * half] for ref in stat_refs], axis=0)
    got_peak = got[:CHUNKS]
    peak = jnp.maximum(own_peak, got_peak)
    own_factor = jnp.exp(own_peak - peak)
    got_factor = jnp.exp(got_peak - peak)
    total = own_factor * own_total + got_factor * (
        got[CHUNKS : 2 * CHUNKS] + got[2 * CHUNKS : 3 * CHUNKS]
    )
    high = round_bf16(total)
    low = total - high
    filler = jnp.zeros((128 - 2 * CHUNKS, 128), jnp.float32)
    table = jnp.transpose(jnp.concatenate([own_factor, got_factor, filler], axis=0))
    parts = got_ref[MIX_ROWS : MIX_ROWS + 3 * step].astype(jnp.float32)
    keys = proj_ref[0] + parts[:step] + parts[step : 2 * step]
    values = proj_ref[1] + parts[2 * step :]
    keys_high = round_bf16(keys)
    for j in range(KEY_HEADS):
        part = slice(j * rows, (j + 1) * rows)
        tail_ref[j, :rows] = keys_high[part]
        tail_ref[j, rows : 2 * rows] = (keys - keys_high)[part]
        tail_ref[j, 2 * rows :] = values[part]
    stat_row = lax.broadcasted_iota(jnp.int32, (rows, HEAD_WIDTH), 0)
    packet = {id(slot): ref for slot, ref in zip([plan.own, plan.one] + plan.mine, packet_refs)}
    for c, runs in enumerate(plan.attention_chunks(slot_rows, True)):
        span = slice(c * 128, c * 128 + 128)
        at = c % half * 128
        mix = mix_refs[c // half][at : at + 128] * table[:, c : c + 1]
        mix += got_ref[span].astype(jnp.float32) * table[:, CHUNKS + c : CHUNKS + c + 1]
        stats = jnp.where(
            stat_row == 0,
            peak[c : c + 1],
            jnp.where(
                stat_row == 1, high[c : c + 1], jnp.where(stat_row == 2, low[c : c + 1], 0.0)
            ),
        )
        for t, (slot, side) in enumerate(unit for run in runs for unit in run):
            packet_ref = packet[id(slot)]
            at = side * slot_rows
            packet_ref[at : at + slot_rows] = mix[t * slot_rows : (t + 1) * slot_rows].astype(
                jnp.bfloat16
            )
            if side == 0:
                shifted = stats if t == 0 else pltpu.roll(stats, HEAD_WIDTH - t * slot_rows, 1)
                head = (chip // per_head) ^ (here_mask(slot[0], here) // per_head)
                tail = jnp.concatenate([tail_ref[head], shifted], axis=0)
                packet_ref[packet_ref.shape[0] - 4 * rows :] = tail.astype(jnp.bfloat16)


def merge_kernel(devices, requests, tokens, swapped, own_ref, cos_ref, sin_ref, *refs):
    got_refs, out_ref = refs[:-1], refs[-1]
    rows = requests * tokens
    heads = QUERY_HEADS // devices
    mix_rows = heads * rows
    sources = len(got_refs)
    tails = [ref[ref.shape[0] - 4 * rows :].astype(jnp.float32) for ref in got_refs]
    sums = functools.reduce(jnp.add, [tail[: 3 * rows] for tail in tails])
    keys = sums[:rows] + sums[rows : 2 * rows]
    values = sums[2 * rows :].astype(jnp.bfloat16)
    turned = pltpu.roll(keys, HEAD_WIDTH // 2, 1)
    keys = (keys * cos_ref[...] + turned * sin_ref[...]).astype(jnp.bfloat16)
    query = jnp.concatenate([own_ref[h] for h in range(heads)], axis=0)
    if mix_rows < 128:
        query = jnp.concatenate(
            [query, jnp.zeros((128 - mix_rows, HEAD_WIDTH), jnp.bfloat16)], axis=0
        )
    fresh = dot(keys, query, ((1,), (1,))) * SCALE
    source = lax.broadcasted_iota(jnp.int32, fresh.shape, 0)
    column = lax.broadcasted_iota(jnp.int32, fresh.shape, 1) % rows
    allowed = (source // tokens == column // tokens) & (source % tokens <= column % tokens)
    fresh_peak = jnp.max(jnp.where(allowed, fresh, NEG_FILL), axis=0, keepdims=True)
    stats = [tail[3 * rows :] for tail in tails]
    for s in range(swapped, sources):
        stats[s] = pltpu.roll(stats[s], HEAD_WIDTH - mix_rows, 1)
    past_peak = functools.reduce(jnp.maximum, [stat[0:1] for stat in stats])
    factors = [jnp.exp(stat[0:1] - past_peak) for stat in stats]
    past_total = functools.reduce(
        jnp.add, [factor * (stat[1:2] + stat[2:3]) for factor, stat in zip(factors, stats)]
    )
    table = jnp.concatenate(factors + [jnp.zeros((128 - sources, 128), jnp.float32)], axis=0)
    table = jnp.transpose(table)[:mix_rows]
    mix = None
    for s, ref in enumerate(got_refs):
        term = ref[:mix_rows].astype(jnp.float32) * table[:, s : s + 1]
        mix = term if mix is None else mix + term
    peak = jnp.maximum(past_peak, fresh_peak)
    scale = jnp.exp(past_peak - peak)
    weights = jnp.where(allowed, jnp.exp(fresh - peak), 0.0)
    inverse = 1.0 / (past_total * scale + jnp.sum(weights, axis=0, keepdims=True))
    table = jnp.concatenate(
        [
            scale * inverse,
            inverse,
            jnp.zeros((rows - 2, 128), jnp.float32),
            weights,
            jnp.zeros((128 - 2 * rows, 128), jnp.float32),
        ],
        axis=0,
    )
    table = jnp.transpose(table)[:mix_rows]
    lane = lax.broadcasted_iota(jnp.int32, table.shape, 1)
    weights = jnp.where((lane >= rows) & (lane < 2 * rows), table, 0.0).astype(jnp.bfloat16)
    values = jnp.concatenate(
        [
            jnp.zeros((rows, HEAD_WIDTH), jnp.bfloat16),
            values,
            jnp.zeros((128 - 2 * rows, HEAD_WIDTH), jnp.bfloat16),
        ],
        axis=0,
    )
    mix = mix * table[:, 0:1] + dot(weights, values, ((1,), (0,))) * table[:, 1:2]
    for h in range(heads):
        tile = mix[h * rows : (h + 1) * rows]
        for b in range(requests):
            out_ref[b, :, h * HEAD_WIDTH : (h + 1) * HEAD_WIDTH] = tile[
                b * tokens : (b + 1) * tokens
            ].astype(jnp.bfloat16)


def rotation(lengths, tokens):
    half = HEAD_WIDTH // 2
    places = (lengths[:, None] + jnp.arange(tokens, dtype=jnp.int32)[None, :]).astype(jnp.float32)
    inverse_freq = jnp.exp(
        jnp.arange(half, dtype=jnp.float32) * (-2.0 * math.log(ROPE_BASE) / HEAD_WIDTH)
    )
    angles = places.reshape(-1, 1) * inverse_freq[None, :]
    cosine, sine = jnp.cos(angles), jnp.sin(angles)
    return jnp.concatenate([cosine, cosine], axis=1), jnp.concatenate([-sine, sine], axis=1)


def vmem():
    return pl.BlockSpec(memory_space=pltpu.VMEM)


def smem():
    return pl.BlockSpec(memory_space=pltpu.SMEM)


def hbm():
    return pl.BlockSpec(memory_space=pltpu.HBM)


def pinned(x):
    return pltpu.with_memory_space_constraint(x, pltpu.HBM)


def cost(flops, moved):
    return pl.CostEstimate(flops=int(flops), bytes_accessed=int(moved), transcendentals=0)


def trade(x, devices, even, odd, core=0):
    pairs = [(d, d ^ (2 * (odd if d % 2 else even) + core)) for d in range(devices)]
    return lax.ppermute(x, "tensor", pairs)


def per_device(
    hidden,
    queries,
    key_value_weight,
    adapter_down_weight,
    adapter_up_weight,
    cached_key_rows,
    cached_value_rows,
    request_adapter,
    adapter_rank_list,
    adapter_pool_row,
    lengths,
):
    requests, tokens, width = hidden.shape
    rows = requests * tokens
    devices = lax.axis_size("tensor")
    sizes = (requests, tokens, devices)
    plan = Plan(devices, width)
    heads, chunks = plan.heads, plan.chunks
    slot_rows = heads * rows
    index = lax.axis_index("tensor").reshape(1).astype(jnp.int32)

    def call(kernel, operands, in_specs, out_shape, scratch, name):
        return pl.pallas_call(
            kernel,
            out_shape=tuple(out_shape),
            in_specs=in_specs,
            out_specs=(vmem(),) * len(out_shape),
            scratch_shapes=scratch,
            compiler_params=pltpu.CompilerParams(vmem_limit_bytes=12 * MIB),
            cost_estimate=cost(10**6, 0),
            name=name,
        )(*operands)

    def core_swap(x):
        return trade(x, devices, 0, 0, core=1)

    flat = requests * cached_key_rows.shape[1]
    keys = cached_key_rows.reshape(flat, -1)
    values = cached_value_rows.reshape(flat, -1)
    (own,) = call(
        functools.partial(pack_kernel, requests),
        (pinned(queries), pinned(hidden)),
        [hbm()] * 2,
        [pltpu.VMEM((heads + chunks, rows, HEAD_WIDTH), jnp.bfloat16)],
        [
            pltpu.VMEM(queries.shape, jnp.bfloat16),
            pltpu.VMEM(hidden.shape, jnp.bfloat16),
            pltpu.SemaphoreType.DMA((2,)),
        ],
        "pack",
    )
    other_queries, other_hidden = core_swap(queries), core_swap(hidden)
    other_queries, late_own = lax.optimization_barrier((other_queries, own))
    shape = (heads + chunks, rows, HEAD_WIDTH)
    other, both = call(
        functools.partial(pack_other_kernel, requests),
        (late_own, other_queries, other_hidden),
        [vmem()] * 3,
        [pltpu.VMEM(shape, jnp.bfloat16), pltpu.VMEM((2 * shape[0],) + shape[1:], jnp.bfloat16)],
        [],
        "pack_other",
    )
    both, late_own = lax.optimization_barrier((both, late_own))
    one = trade(late_own, devices, plan.single, plan.single)
    mine = [trade(both, devices, a, b) for a, b in plan.pairs]

    out_width = key_value_weight.shape[1]
    parts = 4 if width % (4 * HEAD_WIDTH) == 0 else 1
    down = pinned(adapter_down_weight[0])
    rank = down.shape[1]
    up = adapter_up_weight[0]
    big = (keys, values, up)
    scalars = (lengths, request_adapter, adapter_rank_list, adapter_pool_row)
    base, bias, masks, keys, values, up, *halves = call(
        functools.partial(base_kernel, sizes, plan),
        (index,)
        + tuple(pinned(x) for x in scalars)
        + (late_own, pinned(key_value_weight), down)
        + tuple(pinned(x) for x in big),
        [smem()] + [hbm()] * 4 + [vmem()] + [hbm()] * 5,
        [
            pltpu.VMEM((rows, out_width), jnp.float32),
            pltpu.VMEM((flat, HEAD_WIDTH), jnp.float32),
            pltpu.VMEM((2, rows, HEAD_WIDTH), jnp.float32),
        ]
        + [pltpu.VMEM(x.shape, x.dtype) for x in big]
        + [pltpu.VMEM((devices // 2, width, rank), jnp.bfloat16)] * 2,
        [
            pltpu.VMEM((parts, width // parts, out_width), jnp.bfloat16),
            *[pltpu.SMEM(x.shape, x.dtype) for x in scalars],
            pltpu.SemaphoreType.DMA((parts + 3,)),
            pltpu.SemaphoreType.DMA((devices,)),
            pltpu.SemaphoreType.DMA((4,)),
        ],
        "base",
    )
    near = jnp.concatenate([one] + mine, axis=0)
    near, base = lax.optimization_barrier((near, base))
    other_near = core_swap(near)

    def keep(numbers, *half):
        return call(
            functools.partial(keep_kernel, sizes, plan, numbers),
            (index, bias, own, near, keys, values) + half,
            [smem()] + [vmem()] * (5 + len(half)),
            [
                pltpu.VMEM((MIX_ROWS // 2, HEAD_WIDTH), jnp.float32),
                pltpu.VMEM((8, HEAD_WIDTH), jnp.float32),
            ]
            + [pltpu.VMEM((rows, rank), jnp.float32)] * len(half),
            [],
            "keep_states",
        )

    first_mix, first_stats, lowered = keep(range(CHUNKS // 2), halves[0])
    other_near, first_mix = lax.optimization_barrier((other_near, first_mix))
    arrays = (own, other, near, other_near)
    step = KEY_HEADS * rows
    send, proj = call(
        functools.partial(send_kernel, sizes, plan),
        (index, bias) + arrays + (keys, values, base, up, halves[1], lowered, masks),
        [smem()] + [vmem()] * 12,
        [
            pltpu.VMEM((MIX_ROWS + 3 * step + STAT_ROWS, HEAD_WIDTH), jnp.bfloat16),
            pltpu.VMEM((2, step, HEAD_WIDTH), jnp.float32),
        ],
        [],
        "send_states",
    )
    got = core_swap(send)
    second_mix, second_stats = keep(range(CHUNKS // 2, CHUNKS))
    packets = call(
        functools.partial(join_kernel, sizes, plan),
        (index, first_mix, second_mix, first_stats, second_stats, proj, got),
        [smem()] + [vmem()] * 6,
        [pltpu.VMEM((slot_rows + 4 * rows, HEAD_WIDTH), jnp.bfloat16)] * 2
        + [pltpu.VMEM((2 * slot_rows + 4 * rows, HEAD_WIDTH), jnp.bfloat16)] * len(plan.pairs),
        [pltpu.VMEM((KEY_HEADS, 3 * rows, HEAD_WIDTH), jnp.float32)],
        "join",
    )
    sent = sorted(zip(packets[2:], plan.pairs), key=lambda item: -sum(item[1]))
    back = [trade(x, devices, a, b) for x, (a, b) in sent]
    back[0], late_lengths = lax.optimization_barrier((back[0], lengths))
    cosine, sine = rotation(late_lengths, tokens)
    heard = [packets[0], trade(packets[1], devices, plan.single, plan.single)] + back
    heard += [core_swap(x[slot_rows:]) for x in back]
    return pl.pallas_call(
        functools.partial(merge_kernel, devices, requests, tokens, 2 + len(plan.pairs)),
        out_shape=jax.ShapeDtypeStruct((requests, tokens, heads * HEAD_WIDTH), jnp.bfloat16),
        in_specs=[vmem()] * (3 + len(heard)),
        out_specs=vmem(),
        compiler_params=pltpu.CompilerParams(vmem_limit_bytes=8 * MIB),
        name="merge_states",
    )(own, cosine, sine, *heard)


def solution(mesh):
    in_specs = (
        P("groups", None, "tensor"),
        P("groups", None, "tensor"),
        P("tensor", None),
        P("tensor", None, None),
        P("tensor", None, None),
        P("groups", "tensor", None),
        P("groups", "tensor", None),
        P("groups"),
        P(),
        P(),
        P("groups"),
    )
    out_specs = P("groups", None, "tensor")
    return jax.shard_map(
        per_device, mesh=mesh, in_specs=in_specs, out_specs=out_specs, check_vma=False
    )
```

```python
import functools
import math

import jax
import jax.numpy as jnp
from jax import lax
from jax.experimental import pallas as pl
from jax.experimental.pallas import tpu as pltpu
from jax.sharding import PartitionSpec as P

QUERY_HEADS = 128
KEY_HEADS = 8
HEAD_WIDTH = 128
ROPE_BASE = 500000.0
NEG_FILL = -(2.0**100)
SCALE = 1.0 / math.sqrt(HEAD_WIDTH)
CHUNKS = KEY_HEADS // 2
MIX_ROWS = CHUNKS * 128
STAT_ROWS = 16
MIB = 2**20


def dot(a, b, dims):
    return lax.dot_general(a, b, (dims, ((), ())), preferred_element_type=jnp.float32)


def round_bf16(x):
    return x.astype(jnp.bfloat16).astype(jnp.float32)


class Plan:
    def __init__(self, devices, width):
        lanes = devices // 2
        self.per_head = per_head = lanes // KEY_HEADS
        self.heads, self.chunks = QUERY_HEADS // devices, width // HEAD_WIDTH
        self.single = 1
        self.pairs = [(m, m + 1) for m in range(lanes - 2, 0, -2)]
        self.pairs[:2] = self.pairs[1::-1]
        size = self.heads + self.chunks
        self.own = ((0, 0), ((0, 0), (1, 0)))
        self.one = ((self.single,) * 2, ((2, 0), (3, 0)))
        self.mine, self.theirs = [], []
        for k, (a, b) in enumerate(self.pairs):
            at = size + 2 * size * k
            self.mine.append(((a, b), ((2, at), (2, at + size))))
            self.theirs.append(((b, a), ((3, at + size), (3, at))))

    def head_masks(self, unit):
        return tuple(mask // self.per_head for mask in unit[0][0])

    def units(self, keep):
        if keep:
            units = [(self.own, 0), (self.one, 0)]
            units += [(slot, side) for slot in self.mine for side in (0, 1)]
        else:
            units = [(self.own, 1), (self.one, 1)]
            units += [(slot, side) for slot in self.theirs for side in (1, 0)]
        if self.per_head > 1:
            units.sort(key=self.head_masks)
        return units

    def attention_chunks(self, slot_rows, keep):
        units = self.units(keep)
        count = HEAD_WIDTH // slot_rows
        chunks = []
        for at in range(0, len(units), count):
            runs = []
            for unit in units[at : at + count]:
                if runs and self.head_masks(runs[-1][0]) == self.head_masks(unit):
                    runs[-1].append(unit)
                else:
                    runs.append([unit])
            chunks.append(runs)
        return chunks

    def slots(self):
        return [self.own, self.one] + self.mine + self.theirs


def here_mask(masks, here):
    return masks[0] if masks[0] == masks[1] else jnp.where(here % 2 == 0, masks[0], masks[1])


def head_columns(head):
    return pl.ds(pl.multiple_of(head * HEAD_WIDTH, HEAD_WIDTH), HEAD_WIDTH)


def sources_of(plan):
    sources = [
        (array, tile + plan.heads, masks, side)
        for masks, places in plan.slots()
        for side, (array, tile) in enumerate(places)
    ]
    return sorted(sources, key=lambda source: source[0] % 2)


def streams(sources, index_ref, down_ref, halves, sems):
    count, depth = halves[0].shape[:2]
    here = index_ref[0]
    copies = []
    for at, (_, _, masks, side) in enumerate(sources):
        source = here ^ (2 * here_mask(masks, here) + side)
        rows = pl.ds(pl.multiple_of(source * depth, depth), depth)
        place = halves[at // count].at[at % count]
        copies.append(pltpu.make_async_copy(down_ref.at[rows], place, sems.at[at]))
    return copies


def lower(sources, arrays, half_ref):
    total = None
    depth = half_ref.shape[1]
    for at, (array, first, _, _) in enumerate(sources):
        tiles = range(first, first + depth // HEAD_WIDTH)
        hidden = jnp.concatenate([arrays[array][c] for c in tiles], axis=1)
        term = dot(hidden, half_ref[at], ((1,), (0,)))
        total = term if total is None else total + term
    return total


def tiles_of(refs, requests, out_ref, at):
    for ref in refs:
        rows = jnp.concatenate([ref[b].astype(jnp.float32) for b in range(requests)], axis=0)
        for c in range(rows.shape[1] // HEAD_WIDTH):
            tile = rows[:, c * HEAD_WIDTH : (c + 1) * HEAD_WIDTH]
            out_ref[at] = tile.astype(jnp.bfloat16)
            at += 1


def pack_kernel(requests, query_ref, hidden_ref, own_ref, query_buf, hidden_buf, sems):
    loads = [
        pltpu.make_async_copy(query_ref, query_buf, sems.at[0]),
        pltpu.make_async_copy(hidden_ref, hidden_buf, sems.at[1]),
    ]
    for load in loads:
        load.start()
    for load in loads:
        load.wait()
    tiles_of((query_buf, hidden_buf), requests, own_ref, 0)


def pack_other_kernel(requests, own_ref, query_ref, hidden_ref, other_ref, both_ref):
    size = own_ref.shape[0]
    both_ref[:size] = own_ref[...]
    tiles_of((query_ref, hidden_ref), requests, both_ref, size)
    other_ref[...] = both_ref[size:]


def base_kernel(sizes, plan, *refs):
    index_ref, *scalars = refs[:5]
    (own_ref, weight_ref, down_ref, *sources) = refs[5:11]
    (base_ref, bias_ref, mask_ref, *held) = refs[11:17]
    *halves, buffer, length_ref, adapter_ref, rank_ref, pool_ref, sems, row_sems, scalar_sems = refs[17:]
    requests, tokens, devices = sizes
    rows = requests * tokens
    here = index_ref[0]
    parts, depth = buffer.shape[:2]
    loads = [
        pltpu.make_async_copy(weight_ref.at[pl.ds(p * depth, depth)], buffer.at[p], sems.at[p])
        for p in range(parts)
    ]
    others = [
        pltpu.make_async_copy(source, place, sems.at[parts + i])
        for i, (source, place) in enumerate(zip(sources, held))
    ]
    others += streams(sources_of(plan), index_ref, down_ref, halves, row_sems)
    scalars = [
        pltpu.make_async_copy(source, place, scalar_sems.at[i])
        for i, (source, place) in enumerate(
            zip(scalars, (length_ref, adapter_ref, rank_ref, pool_ref))
        )
    ]
    for load in scalars + loads + others:
        load.start()
    tiles = depth // HEAD_WIDTH
    total = jnp.zeros(base_ref.shape, jnp.float32)
    for p in range(parts):
        first = plan.heads + p * tiles
        hidden = jnp.concatenate([own_ref[first + c] for c in range(tiles)], axis=1)
        loads[p].wait()
        total += dot(hidden, buffer[p], ((1,), (0,)))
    base_ref[...] = total
    for load in scalars:
        load.wait()
    positions = bias_ref.shape[0] // requests
    place = lax.broadcasted_iota(jnp.int32, bias_ref.shape, 0)
    column = lax.broadcasted_iota(jnp.int32, bias_ref.shape, 1)
    place_request = place // positions
    limit = jnp.zeros_like(place)
    for b in range(requests):
        limit = jnp.where(place_request == b, length_ref[b], limit)
    allowed = (here * positions + place % positions < limit) & (
        place_request == (column // tokens) % requests
    )
    bias_ref[...] = jnp.where(allowed, 0.0, NEG_FILL)
    row_request = lax.broadcasted_iota(jnp.int32, (rows, HEAD_WIDTH), 0) // tokens
    ranks = jnp.zeros((rows, HEAD_WIDTH), jnp.int32)
    owners = jnp.zeros((rows, HEAD_WIDTH), jnp.int32)
    for b in range(requests):
        adapter = adapter_ref[b]
        ranks = jnp.where(row_request == b, rank_ref[adapter], ranks)
        owners = jnp.where(row_request == b, pool_ref[adapter], owners)
    column = lax.broadcasted_iota(jnp.int32, ranks.shape, 1)
    mask_ref[0] = jnp.where(column < ranks, 1.0, 0.0)
    mask_ref[1] = jnp.where(owners == here, 1.0, 0.0)
    for load in others:
        load.wait()


def attend(sizes, plan, keep, numbers, index_ref, bias_ref, arrays, key_ref, value_ref, put):
    requests, tokens, devices = sizes
    here = index_ref[0]
    chip = here // 2
    per_head = plan.per_head
    slot_rows = plan.heads * requests * tokens
    bias = bias_ref[...]
    column = lax.broadcasted_iota(jnp.int32, bias.shape, 1)
    chunks = plan.attention_chunks(slot_rows, keep)
    chunks = [chunks[i] for i in numbers]
    spots, scores = [], []
    for runs in chunks:
        places = [slot[1][side] for run in runs for slot, side in run]
        query = jnp.concatenate(
            [arrays[array][tile + h] for array, tile in places for h in range(plan.heads)], axis=0
        )
        spots.append(
            [
                head_columns((chip // per_head) ^ (here_mask(run[0][0][0], here) // per_head))
                for run in runs
            ]
        )
        share = HEAD_WIDTH // len(runs)
        score = None
        for i, spot in enumerate(spots[-1]):
            part = dot(key_ref[:, spot], query, ((1,), (1,)))
            score = part if score is None else jnp.where(column < i * share, score, part)
        scores.append(score * SCALE + bias)
    peaks = [round_bf16(jnp.max(score, axis=0, keepdims=True)) for score in scores]
    weights = [jnp.exp(score - peak) for score, peak in zip(scores, peaks)]
    totals = [jnp.sum(weight, axis=0, keepdims=True) for weight in weights]
    weights = [jnp.transpose(weight.astype(jnp.bfloat16)) for weight in weights]
    for number, weight in enumerate(weights):
        share = HEAD_WIDTH // len(spots[number])
        for i, spot in enumerate(spots[number]):
            own = slice(i * share, (i + 1) * share)
            put(number, i * share, dot(weight[own], value_ref[:, spot], ((1,), (0,))))
    return peaks, totals


def rows_of(items, count):
    row = lax.broadcasted_iota(jnp.int32, (count, HEAD_WIDTH), 0)
    out = jnp.zeros((count, HEAD_WIDTH), jnp.float32)
    for i, item in enumerate(items):
        out = jnp.where(row == i, item, out)
    return out


def send_kernel(sizes, plan, *refs):
    (index_ref, bias_ref, *arrays) = refs[:6]
    (key_ref, value_ref, base_ref, up_ref, half_ref, lowered_ref, mask_ref) = refs[6:13]
    (send_ref, own_ref) = refs[13:]
    requests, tokens, devices = sizes

    def put(chunk, row, mix):
        at = chunk * 128 + row
        send_ref[at : at + mix.shape[0]] = mix.astype(jnp.bfloat16)

    peaks, totals = attend(
        sizes, plan, False, range(CHUNKS), index_ref, bias_ref, arrays, key_ref, value_ref, put
    )
    highs = [round_bf16(total) for total in totals]
    lows = [total - high for total, high in zip(totals, highs)]
    send_ref[-STAT_ROWS:] = rows_of(peaks + highs + lows, STAT_ROWS).astype(jnp.bfloat16)

    rows = requests * tokens
    sources = sources_of(plan)
    lowered = lowered_ref[...] + lower(sources[devices // 2 :], arrays, half_ref)
    lowered = jnp.where(mask_ref[0] > 0.0, lowered, 0.0).astype(jnp.bfloat16)
    lifted = dot(lowered, up_ref[...], ((1,), (0,)))
    projected = base_ref[...] + jnp.where(mask_ref[1][:, :1] > 0.0, lifted, 0.0)
    split = KEY_HEADS * HEAD_WIDTH
    step = KEY_HEADS * rows
    keys, values = [
        jnp.concatenate(
            [projected[:, at + j * HEAD_WIDTH : at + (j + 1) * HEAD_WIDTH] for j in range(KEY_HEADS)],
            axis=0,
        )
        for at in (0, split)
    ]
    own_ref[0] = keys
    own_ref[1] = values
    high = keys.astype(jnp.bfloat16)
    send_ref[MIX_ROWS : MIX_ROWS + step] = high
    send_ref[MIX_ROWS + step : MIX_ROWS + 2 * step] = (keys - high.astype(jnp.float32)).astype(
        jnp.bfloat16
    )
    send_ref[MIX_ROWS + 2 * step : MIX_ROWS + 3 * step] = values.astype(jnp.bfloat16)


def keep_kernel(sizes, plan, numbers, *refs):
    (index_ref, bias_ref, own_ref, near_ref, key_ref, value_ref) = refs[:6]
    arrays = {0: own_ref, 2: near_ref}
    if len(refs) > 8:
        half_ref, mix_ref, stat_ref, lowered_ref = refs[6:]
        lowered_ref[...] = lower(sources_of(plan)[: half_ref.shape[0]], arrays, half_ref)
    else:
        mix_ref, stat_ref = refs[6:]

    def put(chunk, row, mix):
        at = chunk * 128 + row
        mix_ref[at : at + mix.shape[0]] = mix

    peaks, totals = attend(
        sizes, plan, True, numbers, index_ref, bias_ref, arrays, key_ref, value_ref, put
    )
    stat_ref[...] = rows_of(peaks + totals, 8)


def join_kernel(sizes, plan, index_ref, *refs):
    mix_refs, stat_refs, (proj_ref, got_ref) = refs[:2], refs[2:4], refs[4:6]
    packet_refs, tail_ref = refs[6:-1], refs[-1]
    requests, tokens, devices = sizes
    here = index_ref[0]
    chip = here // 2
    per_head = plan.per_head
    rows = requests * tokens
    slot_rows = plan.heads * rows
    step = KEY_HEADS * rows
    got = got_ref[MIX_ROWS + 3 * step :].astype(jnp.float32)
    half = CHUNKS // 2
    own_peak = jnp.concatenate([ref[:half] for ref in stat_refs], axis=0)
    own_total = jnp.concatenate([ref[half : 2 * half] for ref in stat_refs], axis=0)
    got_peak = got[:CHUNKS]
    peak = jnp.maximum(own_peak, got_peak)
    own_factor = jnp.exp(own_peak - peak)
    got_factor = jnp.exp(got_peak - peak)
    total = own_factor * own_total + got_factor * (
        got[CHUNKS : 2 * CHUNKS] + got[2 * CHUNKS : 3 * CHUNKS]
    )
    high = round_bf16(total)
    low = total - high
    filler = jnp.zeros((128 - 2 * CHUNKS, 128), jnp.float32)
    table = jnp.transpose(jnp.concatenate([own_factor, got_factor, filler], axis=0))
    parts = got_ref[MIX_ROWS : MIX_ROWS + 3 * step].astype(jnp.float32)
    keys = proj_ref[0] + parts[:step] + parts[step : 2 * step]
    values = proj_ref[1] + parts[2 * step :]
    keys_high = round_bf16(keys)
    for j in range(KEY_HEADS):
        part = slice(j * rows, (j + 1) * rows)
        tail_ref[j, :rows] = keys_high[part]
        tail_ref[j, rows : 2 * rows] = (keys - keys_high)[part]
        tail_ref[j, 2 * rows :] = values[part]
    stat_row = lax.broadcasted_iota(jnp.int32, (rows, HEAD_WIDTH), 0)
    packet = {id(slot): ref for slot, ref in zip([plan.own, plan.one] + plan.mine, packet_refs)}
    for c, runs in enumerate(plan.attention_chunks(slot_rows, True)):
        span = slice(c * 128, c * 128 + 128)
        at = c % half * 128
        mix = mix_refs[c // half][at : at + 128] * table[:, c : c + 1]
        mix += got_ref[span].astype(jnp.float32) * table[:, CHUNKS + c : CHUNKS + c + 1]
        stats = jnp.where(
            stat_row == 0,
            peak[c : c + 1],
            jnp.where(
                stat_row == 1, high[c : c + 1], jnp.where(stat_row == 2, low[c : c + 1], 0.0)
            ),
        )
        for t, (slot, side) in enumerate(unit for run in runs for unit in run):
            packet_ref = packet[id(slot)]
            at = side * slot_rows
            packet_ref[at : at + slot_rows] = mix[t * slot_rows : (t + 1) * slot_rows].astype(
                jnp.bfloat16
            )
            if side == 0:
                shifted = stats if t == 0 else pltpu.roll(stats, HEAD_WIDTH - t * slot_rows, 1)
                head = (chip // per_head) ^ (here_mask(slot[0], here) // per_head)
                tail = jnp.concatenate([tail_ref[head], shifted], axis=0)
                packet_ref[packet_ref.shape[0] - 4 * rows :] = tail.astype(jnp.bfloat16)


def fold_states(states, mix_rows):
    peak = functools.reduce(jnp.maximum, [state[0] for state in states])
    factors = [jnp.exp(state[0] - peak) for state in states]
    total = functools.reduce(jnp.add, [f * state[1] for f, state in zip(factors, states)])
    table = jnp.concatenate(factors + [jnp.zeros((128 - len(states), 128), jnp.float32)], axis=0)
    table = jnp.transpose(table)[:mix_rows]
    mix = None
    for s, state in enumerate(states):
        term = state[2].astype(jnp.float32) * table[:, s : s + 1]
        mix = term if mix is None else mix + term
    return peak, total, mix


def packet_states(refs, rows, mix_rows, shift):
    states, sums = [], None
    for ref in refs:
        tail = ref[ref.shape[0] - 4 * rows :].astype(jnp.float32)
        stat = tail[3 * rows :]
        if shift:
            stat = pltpu.roll(stat, HEAD_WIDTH - shift, 1)
        states.append((stat[0:1], stat[1:2] + stat[2:3], ref[:mix_rows]))
        sums = tail[: 3 * rows] if sums is None else sums + tail[: 3 * rows]
    return states, sums


def fold_kernel(rows, mix_rows, *refs):
    *got_refs, mix_ref, stat_ref, sum_ref = refs
    states, sums = packet_states(got_refs, rows, mix_rows, 0)
    peak, total, mix = fold_states(states, mix_rows)
    mix_ref[...] = mix
    stat_ref[...] = rows_of([peak, total], 8)
    sum_ref[...] = sums


def merge_kernel(devices, requests, tokens, own_ref, cos_ref, sin_ref, *refs):
    mix_ref, stat_ref, sum_ref, *got_refs, out_ref = refs
    rows = requests * tokens
    heads = QUERY_HEADS // devices
    mix_rows = heads * rows
    states, sums = packet_states(got_refs, rows, mix_rows, mix_rows)
    sums += sum_ref[...]
    keys = sums[:rows] + sums[rows : 2 * rows]
    values = sums[2 * rows :].astype(jnp.bfloat16)
    turned = pltpu.roll(keys, HEAD_WIDTH // 2, 1)
    keys = (keys * cos_ref[...] + turned * sin_ref[...]).astype(jnp.bfloat16)
    query = jnp.concatenate([own_ref[h] for h in range(heads)], axis=0)
    if mix_rows < 128:
        query = jnp.concatenate(
            [query, jnp.zeros((128 - mix_rows, HEAD_WIDTH), jnp.bfloat16)], axis=0
        )
    fresh = dot(keys, query, ((1,), (1,))) * SCALE
    source = lax.broadcasted_iota(jnp.int32, fresh.shape, 0)
    column = lax.broadcasted_iota(jnp.int32, fresh.shape, 1) % rows
    allowed = (source // tokens == column // tokens) & (source % tokens <= column % tokens)
    fresh_peak = jnp.max(jnp.where(allowed, fresh, NEG_FILL), axis=0, keepdims=True)
    states = [(stat_ref[0:1], stat_ref[1:2], mix_ref[...])] + states
    past_peak, past_total, mix = fold_states(states, mix_rows)
    peak = jnp.maximum(past_peak, fresh_peak)
    scale = jnp.exp(past_peak - peak)
    weights = jnp.where(allowed, jnp.exp(fresh - peak), 0.0)
    inverse = 1.0 / (past_total * scale + jnp.sum(weights, axis=0, keepdims=True))
    table = jnp.concatenate(
        [
            scale * inverse,
            inverse,
            jnp.zeros((rows - 2, 128), jnp.float32),
            weights,
            jnp.zeros((128 - 2 * rows, 128), jnp.float32),
        ],
        axis=0,
    )
    table = jnp.transpose(table)[:mix_rows]
    lane = lax.broadcasted_iota(jnp.int32, table.shape, 1)
    weights = jnp.where((lane >= rows) & (lane < 2 * rows), table, 0.0).astype(jnp.bfloat16)
    values = jnp.concatenate(
        [
            jnp.zeros((rows, HEAD_WIDTH), jnp.bfloat16),
            values,
            jnp.zeros((128 - 2 * rows, HEAD_WIDTH), jnp.bfloat16),
        ],
        axis=0,
    )
    mix = mix * table[:, 0:1] + dot(weights, values, ((1,), (0,))) * table[:, 1:2]
    for h in range(heads):
        tile = mix[h * rows : (h + 1) * rows]
        for b in range(requests):
            out_ref[b, :, h * HEAD_WIDTH : (h + 1) * HEAD_WIDTH] = tile[
                b * tokens : (b + 1) * tokens
            ].astype(jnp.bfloat16)


def rotation(lengths, tokens):
    half = HEAD_WIDTH // 2
    places = (lengths[:, None] + jnp.arange(tokens, dtype=jnp.int32)[None, :]).astype(jnp.float32)
    inverse_freq = jnp.exp(
        jnp.arange(half, dtype=jnp.float32) * (-2.0 * math.log(ROPE_BASE) / HEAD_WIDTH)
    )
    angles = places.reshape(-1, 1) * inverse_freq[None, :]
    cosine, sine = jnp.cos(angles), jnp.sin(angles)
    return jnp.concatenate([cosine, cosine], axis=1), jnp.concatenate([-sine, sine], axis=1)


def vmem():
    return pl.BlockSpec(memory_space=pltpu.VMEM)


def smem():
    return pl.BlockSpec(memory_space=pltpu.SMEM)


def hbm():
    return pl.BlockSpec(memory_space=pltpu.HBM)


def pinned(x):
    return pltpu.with_memory_space_constraint(x, pltpu.HBM)


def cost(flops, moved):
    return pl.CostEstimate(flops=int(flops), bytes_accessed=int(moved), transcendentals=0)


def trade(x, devices, even, odd, core=0):
    pairs = [(d, d ^ (2 * (odd if d % 2 else even) + core)) for d in range(devices)]
    return lax.ppermute(x, "tensor", pairs)


def per_device(
    hidden,
    queries,
    key_value_weight,
    adapter_down_weight,
    adapter_up_weight,
    cached_key_rows,
    cached_value_rows,
    request_adapter,
    adapter_rank_list,
    adapter_pool_row,
    lengths,
):
    requests, tokens, width = hidden.shape
    rows = requests * tokens
    devices = lax.axis_size("tensor")
    sizes = (requests, tokens, devices)
    plan = Plan(devices, width)
    heads, chunks = plan.heads, plan.chunks
    slot_rows = heads * rows
    index = lax.axis_index("tensor").reshape(1).astype(jnp.int32)

    def call(kernel, operands, in_specs, out_shape, scratch, name):
        return pl.pallas_call(
            kernel,
            out_shape=tuple(out_shape),
            in_specs=in_specs,
            out_specs=(vmem(),) * len(out_shape),
            scratch_shapes=scratch,
            compiler_params=pltpu.CompilerParams(vmem_limit_bytes=12 * MIB),
            cost_estimate=cost(10**6, 0),
            name=name,
        )(*operands)

    def core_swap(x):
        return trade(x, devices, 0, 0, core=1)

    flat = requests * cached_key_rows.shape[1]
    keys = cached_key_rows.reshape(flat, -1)
    values = cached_value_rows.reshape(flat, -1)
    (own,) = call(
        functools.partial(pack_kernel, requests),
        (pinned(queries), pinned(hidden)),
        [hbm()] * 2,
        [pltpu.VMEM((heads + chunks, rows, HEAD_WIDTH), jnp.bfloat16)],
        [
            pltpu.VMEM(queries.shape, jnp.bfloat16),
            pltpu.VMEM(hidden.shape, jnp.bfloat16),
            pltpu.SemaphoreType.DMA((2,)),
        ],
        "pack",
    )
    other_queries, other_hidden = core_swap(queries), core_swap(hidden)
    other_queries, late_own = lax.optimization_barrier((other_queries, own))
    shape = (heads + chunks, rows, HEAD_WIDTH)
    other, both = call(
        functools.partial(pack_other_kernel, requests),
        (late_own, other_queries, other_hidden),
        [vmem()] * 3,
        [pltpu.VMEM(shape, jnp.bfloat16), pltpu.VMEM((2 * shape[0],) + shape[1:], jnp.bfloat16)],
        [],
        "pack_other",
    )
    both, late_own = lax.optimization_barrier((both, late_own))
    one = trade(late_own, devices, plan.single, plan.single)
    mine = [trade(both, devices, a, b) for a, b in plan.pairs]

    out_width = key_value_weight.shape[1]
    parts = 4 if width % (4 * HEAD_WIDTH) == 0 else 1
    down = pinned(adapter_down_weight[0])
    rank = down.shape[1]
    up = adapter_up_weight[0]
    big = (keys, values, up)
    scalars = (lengths, request_adapter, adapter_rank_list, adapter_pool_row)
    base, bias, masks, keys, values, up, *halves = call(
        functools.partial(base_kernel, sizes, plan),
        (index,)
        + tuple(pinned(x) for x in scalars)
        + (late_own, pinned(key_value_weight), down)
        + tuple(pinned(x) for x in big),
        [smem()] + [hbm()] * 4 + [vmem()] + [hbm()] * 5,
        [
            pltpu.VMEM((rows, out_width), jnp.float32),
            pltpu.VMEM((flat, HEAD_WIDTH), jnp.float32),
            pltpu.VMEM((2, rows, HEAD_WIDTH), jnp.float32),
        ]
        + [pltpu.VMEM(x.shape, x.dtype) for x in big]
        + [pltpu.VMEM((devices // 2, width, rank), jnp.bfloat16)] * 2,
        [
            pltpu.VMEM((parts, width // parts, out_width), jnp.bfloat16),
            *[pltpu.SMEM(x.shape, x.dtype) for x in scalars],
            pltpu.SemaphoreType.DMA((parts + 3,)),
            pltpu.SemaphoreType.DMA((devices,)),
            pltpu.SemaphoreType.DMA((4,)),
        ],
        "base",
    )
    near = jnp.concatenate([one] + mine, axis=0)
    near, base = lax.optimization_barrier((near, base))
    other_near = core_swap(near)

    def keep(numbers, *half):
        return call(
            functools.partial(keep_kernel, sizes, plan, numbers),
            (index, bias, own, near, keys, values) + half,
            [smem()] + [vmem()] * (5 + len(half)),
            [
                pltpu.VMEM((MIX_ROWS // 2, HEAD_WIDTH), jnp.float32),
                pltpu.VMEM((8, HEAD_WIDTH), jnp.float32),
            ]
            + [pltpu.VMEM((rows, rank), jnp.float32)] * len(half),
            [],
            "keep_states",
        )

    first_mix, first_stats, lowered = keep(range(CHUNKS // 2), halves[0])
    other_near, first_mix = lax.optimization_barrier((other_near, first_mix))
    arrays = (own, other, near, other_near)
    step = KEY_HEADS * rows
    send, proj = call(
        functools.partial(send_kernel, sizes, plan),
        (index, bias) + arrays + (keys, values, base, up, halves[1], lowered, masks),
        [smem()] + [vmem()] * 12,
        [
            pltpu.VMEM((MIX_ROWS + 3 * step + STAT_ROWS, HEAD_WIDTH), jnp.bfloat16),
            pltpu.VMEM((2, step, HEAD_WIDTH), jnp.float32),
        ],
        [],
        "send_states",
    )
    got = core_swap(send)
    second_mix, second_stats = keep(range(CHUNKS // 2, CHUNKS))
    packets = call(
        functools.partial(join_kernel, sizes, plan),
        (index, first_mix, second_mix, first_stats, second_stats, proj, got),
        [smem()] + [vmem()] * 6,
        [pltpu.VMEM((slot_rows + 4 * rows, HEAD_WIDTH), jnp.bfloat16)] * 2
        + [pltpu.VMEM((2 * slot_rows + 4 * rows, HEAD_WIDTH), jnp.bfloat16)] * len(plan.pairs),
        [pltpu.VMEM((KEY_HEADS, 3 * rows, HEAD_WIDTH), jnp.float32)],
        "join",
    )
    sent = sorted(zip(packets[2:], plan.pairs), key=lambda item: -sum(item[1]))
    sent[1:] = sent[:0:-1]
    back = [trade(x, devices, a, b) for x, (a, b) in sent]
    back[0], late_lengths = lax.optimization_barrier((back[0], lengths))
    cosine, sine = rotation(late_lengths, tokens)
    heard = [packets[0], trade(packets[1], devices, plan.single, plan.single)] + back
    folded = call(
        functools.partial(fold_kernel, rows, slot_rows),
        tuple(heard),
        [vmem()] * len(heard),
        [
            pltpu.VMEM((slot_rows, HEAD_WIDTH), jnp.float32),
            pltpu.VMEM((8, HEAD_WIDTH), jnp.float32),
            pltpu.VMEM((3 * rows, HEAD_WIDTH), jnp.float32),
        ],
        [],
        "fold",
    )
    swapped = [core_swap(x[slot_rows:]) for x in back]
    return pl.pallas_call(
        functools.partial(merge_kernel, devices, requests, tokens),
        out_shape=jax.ShapeDtypeStruct((requests, tokens, heads * HEAD_WIDTH), jnp.bfloat16),
        in_specs=[vmem()] * (6 + len(swapped)),
        out_specs=vmem(),
        compiler_params=pltpu.CompilerParams(vmem_limit_bytes=8 * MIB),
        name="merge_states",
    )(own, cosine, sine, *folded, *swapped)


def solution(mesh):
    in_specs = (
        P("groups", None, "tensor"),
        P("groups", None, "tensor"),
        P("tensor", None),
        P("tensor", None, None),
        P("tensor", None, None),
        P("groups", "tensor", None),
        P("groups", "tensor", None),
        P("groups"),
        P(),
        P(),
        P("groups"),
    )
    out_specs = P("groups", None, "tensor")
    return jax.shard_map(
        per_device, mesh=mesh, in_specs=in_specs, out_specs=out_specs, check_vma=False
    )
```
